32 devices in a mesh: dp: 8 (over z, y), tensor: 4 (over x, core).
Axes of the slice: x: 2, y: 2, z: 4, core: 2. Of those that a mesh axis runs over, the one named last changes fastest.
Arguments:
- kept_rows: bfloat16 [4096, 1152], P('dp', 'tensor'), may hold values from -6 to 6
- owner_index: int32 [4096], P('dp'), may hold values from 0 to 7, as said below
- kept_position: int32 [4096], P('dp'), may hold values from 0 to 1023, as said below
- resolution: int32 [8], P('dp'), may hold values from 0 to 1, as said below
- mask_token: bfloat16 [1152], replicated, may hold values from -6 to 6
- condition: bfloat16 [32, 1152], P('dp'), may hold values from -3 to 3, as said below
- modulate_weight: bfloat16 [1152, 6912], P('tensor'), may hold values from -0.1875 to 0.1875
- entry_weight: bfloat16 [1152, 3, 1152], P(None, None, 'tensor'), may hold values from -3 to 3, as said below
- output_weight: bfloat16 [1152, 1152], P('tensor'), may hold values from -0.75 to 0.75
- expand_weight: bfloat16 [1152, 4608], P(None, 'tensor'), may hold values from -0.1875 to 0.1875
- shrink_weight: bfloat16 [4608, 1152], P('tensor'), may hold values from -0.09375 to 0.09375
- cotangent: bfloat16 [8192, 1152], P('dp'), may hold values from -6 to 6
Outputs:
- layer_out: bfloat16 [8192, 1152], P('dp', 'tensor')
- kept_grad: bfloat16 [4096, 1152], P('dp', 'tensor')
- mask_grad: float32 [1152], P('dp')
- condition_grad: float32 [32, 1152], P('dp', 'tensor')
- modulate_grad: float32 [1152, 6912], P('tensor', 'dp')
- entry_grad: float32 [1152, 3, 1152], P('dp', None, 'tensor')
- output_grad: float32 [1152, 1152], P('tensor', 'dp')
- expand_grad: float32 [1152, 4608], P('dp', 'tensor')
- shrink_grad: float32 [4608, 1152], P('tensor', 'dp')
The draws below stay inside these ranges and needn't reach their ends.
Inputs may be any that keep to these rules, and one draw needn't show every extreme that they name: `owner_index`: every owner receives exactly 512 kept rows in all. The kept rows of one index of dp going to one owner number at most 128, and in every draw some pair of a sender and an owner has exactly 128. `kept_position`: the kept rows of one owner have distinct positions, exactly half of the positions of each of its images. `resolution`: one entry a region of an owner, regions in order: 1 means the region is one image of 1024 tokens that uses the first of the region's four condition rows; 0 means four images of a quarter of 1024 tokens each, one after another, using the region's four condition rows in order. `condition`: independent entries of mean zero. `entry_weight`: independent entries of mean zero.
All inputs are finite; a program needn't handle non-finite values.
Results may differ from the reference program's by a relative error of at most 0.017.
Values may be sent and summed in bfloat16 or wider, within the bound.
No kernel may reach another device: no remote copies, remote signals or barrier semaphores. Data moves between devices by JAX's collectives and lax.ppermute only.
A program may use at most 256 MiB of HBM per device.

```python
from functools import partial
import jax
import jax.numpy as jnp
from jax import lax

D = 1152
FF = 4608
HEADS = 16
HEAD = 72
IMG_TOK = 1024
BLOCKS = 1
KEPT_DEV = 512
TOKENS = 8192
KEPT_ALL = 4096
CONDS = 32
N_DP = 8


def routing_tables(key):
    owners = N_DP
    mean_rows = KEPT_DEV // owners
    half = owners // 2
    split_keys = jax.random.split(key, 8)
    resolution = jax.random.randint(split_keys[0], (owners * BLOCKS,), 0, 2, dtype=jnp.int32)
    lifts = jax.random.randint(split_keys[1], (half,), 0, mean_rows + 1, dtype=jnp.int32)
    peak = jax.random.randint(split_keys[2], (), 0, half, dtype=jnp.int32)
    lifts = jnp.where(jnp.arange(half) == peak, mean_rows, lifts)
    offsets = jnp.concatenate([lifts, -lifts])
    source_order = jax.random.permutation(split_keys[3], owners)
    owner_order = jax.random.permutation(split_keys[4], owners)
    counts = mean_rows + offsets[(owner_order[None, :] - source_order[:, None]) % owners]
    bounds = jnp.cumsum(counts, axis=1)
    row_ids = jnp.arange(KEPT_DEV)
    sorted_owner = jnp.sum(row_ids[None, :, None] >= bounds[:, None, :], axis=2).astype(jnp.int32)
    starts = bounds - counts
    sorted_slot = row_ids[None, :] - jnp.take_along_axis(starts, sorted_owner, axis=1)
    shuffles = jax.vmap(lambda single_key: jax.random.permutation(single_key, KEPT_DEV))(jax.random.split(split_keys[5], owners))
    row_owner = jnp.take_along_axis(sorted_owner, shuffles, axis=1)
    row_slot = jnp.take_along_axis(sorted_slot, shuffles, axis=1)
    quarter = IMG_TOK // 4

    def region_places(single_key, large):
        whole_key, part_key = jax.random.split(single_key)
        whole = jax.random.permutation(whole_key, IMG_TOK)[:IMG_TOK // 2]
        parts = jax.vmap(lambda inner_key: jax.random.permutation(inner_key, quarter)[:quarter // 2])(jax.random.split(part_key, 4))
        parts = (parts + quarter * jnp.arange(4)[:, None]).reshape(IMG_TOK // 2)
        return jnp.where(large == 1, whole, parts)
    regions = owners * BLOCKS
    chosen = jax.vmap(region_places)(jax.random.split(split_keys[6], regions), resolution)
    chosen = chosen + IMG_TOK * (jnp.arange(regions) % BLOCKS)[:, None]
    per_owner = chosen.reshape(owners, KEPT_DEV)
    mixes = jax.vmap(lambda single_key: jax.random.permutation(single_key, KEPT_DEV))(jax.random.split(split_keys[7], owners))
    per_owner = jnp.take_along_axis(per_owner, mixes, axis=1)
    receive_start = jnp.cumsum(counts, axis=0) - counts
    order_in_owner = receive_start[jnp.arange(owners)[:, None], row_owner] + row_slot
    position = per_owner[row_owner, order_in_owner]
    return (resolution, row_owner.reshape(-1).astype(jnp.int32), position.reshape(-1).astype(jnp.int32))


def draw_owner_index(key, part):
    tables = routing_tables(key)
    return tables[1]


def draw_kept_position(key, part):
    tables = routing_tables(key)
    return tables[2]


def draw_resolution(key, part):
    tables = routing_tables(key)
    return tables[0]


def draw_condition(key, part):
    key = jax.random.fold_in(key, 21)
    values = jax.random.normal(key, (CONDS, D), dtype=jnp.float32)
    return jnp.clip(values, -3.0, 3.0).astype(jnp.bfloat16)


def draw_entry_weight(key, part):
    key = jax.random.fold_in(key, 22)
    values = jax.random.normal(key, (D, 3, D), dtype=jnp.float32)
    return (jnp.clip(values, -3.0, 3.0) * D ** (-0.5)).astype(jnp.bfloat16)


def raised(entries, key, source, target, blocks, factor):
    def block_of(dim):
        return (jnp.arange(entries.shape[dim]) // (entries.shape[dim] // blocks)).reshape((-1,) + (1,) * (entries.ndim - 1 - dim))

    one_side = jax.random.permutation(key, blocks)[block_of(target)]
    far = (block_of(target) + blocks // 2) % blocks
    return jnp.where((block_of(source) == one_side) | (block_of(source) == far), factor * entries, entries)


def block_levels(stream_key, extent, cuts, low, top_value):
    def one(axis_at, blocks):
        steps = jax.random.uniform(jax.random.fold_in(jax.random.fold_in(stream_key, 6), axis_at), (blocks,), jnp.float32, low / len(cuts), top_value / len(cuts))
        return jnp.repeat(jnp.exp(steps), extent[axis_at] // blocks).reshape((-1,) + (1,) * (len(extent) - axis_at - 1))

    gain = one(*cuts[0])
    for cut in cuts[1:]:
        gain = gain * one(*cut)
    return gain


def bell_draw(key, shape, spread, limit, cuts=(), kind=jnp.bfloat16):
    array = jax.random.normal(key, shape, jnp.float32) * spread
    if len(cuts) > 0:
        array = block_levels(key, shape, cuts, -0.22, 0.18) * array
    return jnp.clip(array, min=-limit, max=limit).astype(kind)


def heavy_noise(key, extent, scale, most, cuts, heavy, kind=jnp.bfloat16):
    values = scale * jax.random.normal(key, extent, jnp.float32)
    if cuts:
        values = values * block_levels(key, extent, cuts, -0.22, 0.18)
    return jnp.clip(raised(values, jax.random.fold_in(key, 3), *heavy), -most, most).astype(kind)


def setup_inputs(seed: int = 0) -> dict:
    arg_keys = jax.random.split(jax.random.key(seed), 13)
    kept_rows = bell_draw(arg_keys[0], (KEPT_ALL, D), 1.0, 6.0, ((0, 8), (1, 4)))
    owner_index = draw_owner_index(jax.random.fold_in(arg_keys[12], 71), 0)
    kept_position = draw_kept_position(jax.random.fold_in(arg_keys[12], 71), 0)
    resolution = draw_resolution(jax.random.fold_in(arg_keys[12], 71), 0)
    mask_token = bell_draw(arg_keys[4], (D,), 1.0, 6.0)
    condition = draw_condition(jax.random.fold_in(arg_keys[12], 71), 0)
    modulate_weight = bell_draw(arg_keys[6], (D, 6 * D), D ** -0.5, 0.1875, ((0, 4),))
    entry_weight = draw_entry_weight(jax.random.fold_in(arg_keys[12], 71), 0)
    output_weight = bell_draw(arg_keys[8], (D, D), (D // 16) ** -0.5, 0.75, ((0, 4),))
    expand_weight = bell_draw(arg_keys[9], (D, FF), D ** -0.5, 0.1875, ((1, 4),))
    shrink_weight = bell_draw(arg_keys[10], (FF, D), FF ** -0.5, 0.09375, ((0, 4),))
    cotangent = heavy_noise(arg_keys[11], (TOKENS, D), 1.0, 6.0, ((0, 8),), (0, 1, 8, 2.0))
    return {"kept_rows": kept_rows, "owner_index": owner_index, "kept_position": kept_position, "resolution": resolution, "mask_token": mask_token, "condition": condition, "modulate_weight": modulate_weight, "entry_weight": entry_weight, "output_weight": output_weight, "expand_weight": expand_weight, "shrink_weight": shrink_weight, "cotangent": cotangent}


highest = lax.Precision.HIGHEST
epsilon = 1e-06

@jax.custom_vjp
def low(v):
    return lax.optimization_barrier(v.astype(jnp.bfloat16)).astype(jnp.float32)

@jax.custom_vjp
def low_back(v):
    return v

def low_keep(v):
    return (low(v), None)

def low_pass(kept, grad):
    return (grad,)

def back_keep(v):
    return (v, None)

def back_low(kept, grad):
    return (low(grad),)
low.defvjp(low_keep, low_pass)
low_back.defvjp(back_keep, back_low)

def normalize(rows):
    centered = rows - lax.optimization_barrier(jnp.mean(rows, axis=-1, keepdims=True))
    return centered * lax.rsqrt(lax.optimization_barrier(jnp.mean(centered * centered, axis=-1, keepdims=True)) + epsilon)

def gelu_tanh(value):
    inner = 0.7978845608028654 * (value + 0.044715 * value * value * value)
    return 0.5 * value * (1.0 + jnp.tanh(inner))

def block_layer(fields, weights):
    tokens, table, large = fields
    entry, output, expand, shrink = weights
    quarter = IMG_TOK // 4
    chosen = jnp.where(large == 1, table[0:1], table)
    per_token = jnp.repeat(chosen, quarter, axis=0)
    normed = low(normalize(tokens) * (1.0 + per_token[:, 1]) + per_token[:, 0])
    projected = jnp.einsum('td,dsf->tsf', normed, entry, precision=highest)
    projected = low(low_back(projected)).reshape(IMG_TOK, 3, HEADS, HEAD)
    queries = projected[:, 0]
    keys_all = projected[:, 1]
    values_all = projected[:, 2]
    image = jnp.where(large == 1, 0, jnp.arange(IMG_TOK) // quarter)
    same = image[:, None] == image[None, :]
    scores = jnp.einsum('qhe,khe->hqk', queries, keys_all, precision=highest) * HEAD ** (-0.5)
    scores = low_back(jnp.where(same[None], scores, -1e+30))
    probs = low(jax.nn.softmax(scores, axis=-1))
    attended = jnp.einsum('hqk,khe->qhe', probs, values_all, precision=highest)
    attended = low(low_back(attended.reshape(IMG_TOK, D)))
    branch = low_back(jnp.dot(attended, output, precision=highest))
    middle = tokens + per_token[:, 2] * branch
    normed_two = low(normalize(middle) * (1.0 + per_token[:, 4]) + per_token[:, 3])
    hidden = low_back(jnp.dot(normed_two, expand, precision=highest))
    activated = low(gelu_tanh(hidden))
    feed = low_back(jnp.dot(activated, shrink, precision=highest))
    return middle + per_token[:, 5] * feed

def reference(kept_rows, owner_index, kept_position, resolution, mask_token, condition, modulate_weight, entry_weight, output_weight, expand_weight, shrink_weight, cotangent):
    own_tokens = BLOCKS * IMG_TOK
    total = own_tokens * N_DP
    places = (owner_index * own_tokens + kept_position).astype(jnp.int32)

    def forward(rows, token, context, modulate, entry, output, expand, shrink):
        spatial = jnp.broadcast_to(token[None, :], (total, D))
        spatial = spatial.at[places].set(rows)
        lifted = low(jax.nn.silu(context))
        table = low_back(jnp.dot(lifted, modulate, precision=highest))
        table = table.reshape(BLOCKS * N_DP, 4, 6, D)
        stepper = jax.checkpoint(partial(block_layer, weights=(entry, output, expand, shrink)))
        result = lax.map(stepper, (spatial.reshape(BLOCKS * N_DP, IMG_TOK, D), table, resolution))
        return result.reshape(total, D)
    primals = tuple((item.astype(jnp.float32) for item in (kept_rows, mask_token, condition, modulate_weight, entry_weight, output_weight, expand_weight, shrink_weight)))
    result, pullback = jax.vjp(forward, *primals)
    grads = pullback(cotangent.astype(jnp.float32))
    return (result.astype(jnp.bfloat16), grads[0].astype(jnp.bfloat16), grads[1], grads[2], grads[3], grads[4], grads[5], grads[6], grads[7])
```

```python
from functools import partial

import jax
import jax.numpy as jnp
from jax import lax
from jax.experimental import pallas as pl
from jax.experimental.pallas import tpu as pltpu
from jax.sharding import PartitionSpec as P

HEAD = 72
QUARTERS = 4
SPARE = 8
scale = HEAD ** (-0.5)
epsilon = 1e-06
gelu_coeff = 0.7978845608028654
low = jnp.bfloat16
full = jnp.float32
VMEM_ASK = 48 * 1024 * 1024


def dot(a, b, dims=((1,), (0,))):
    return lax.dot_general(a, b, (dims, ((), ())), preferred_element_type=full)


def normalize(rows):
    centered = rows - jnp.mean(rows, axis=-1, keepdims=True)
    inverse = lax.rsqrt(jnp.mean(centered * centered, axis=-1, keepdims=True) + epsilon)
    return (centered * inverse, inverse)


def normalize_back(unit, inverse, grad):
    return inverse * (
        grad
        - jnp.mean(grad, axis=-1, keepdims=True)
        - unit * jnp.mean(grad * unit, axis=-1, keepdims=True)
    )


def gelu_both(value):
    square = value * value
    curve = jnp.tanh(gelu_coeff * (value + 0.044715 * square * value))
    slope = 0.5 * (1.0 + curve) + 0.5 * value * (1.0 - curve * curve) * gelu_coeff * (
        1.0 + 3.0 * 0.044715 * square
    )
    return (0.5 * value * (1.0 + curve), slope)


def swap(value, axis, bit):
    size = lax.axis_size(axis)
    return lax.ppermute(value, axis, [(index, index ^ bit) for index in range(size)])


def gather_blocks(own):
    near = swap(own, "tensor", 1)
    across = swap(own, "tensor", 2)
    return [own, near, across, swap(across, "tensor", 1)]


def sum_blocks(parts):
    got = swap(parts[3], "tensor", 1)
    far = (parts[2].astype(full) + got.astype(full)).astype(low)
    across = swap(far, "tensor", 2)
    got = swap(parts[1], "tensor", 1)
    return parts[0].astype(full) + got.astype(full) + across.astype(full)


def sum_owners(partial_sum):
    owners = lax.axis_size("dp")
    me = lax.axis_index("dp")
    rows, columns = partial_sum.shape
    step = 1
    held = partial_sum.reshape(owners, rows // owners, columns)
    while step < owners:
        pairs = held.reshape(held.shape[0] // 2, 2, held.shape[1], columns)
        mine = (me // step) % 2
        given = lax.dynamic_index_in_dim(pairs, 1 - mine, 1, keepdims=False)
        kept = lax.dynamic_index_in_dim(pairs, mine, 1, keepdims=False)
        got = swap(given, "dp", step)
        total = kept.astype(full) + got.astype(full)
        step *= 2
        held = total if step >= owners else total.astype(low)
    return held.reshape(rows // owners, columns)


def exchange_owners(slabs):
    owners = slabs.shape[0]
    if owners <= 8:
        return jnp.stack(
            [slabs[0]] + [swap(slabs[index], "dp", index) for index in range(1, owners)]
        )
    order = jnp.arange(owners, dtype=jnp.int32) ^ lax.axis_index("dp")
    sent = jnp.take(slabs, order, axis=0)
    got = lax.all_to_all(sent, "dp", split_axis=0, concat_axis=0, tiled=True)
    return jnp.take(got, order, axis=0)


def attend_kernel(projected_ref, bias_ref, output_ref, attended_ref, part_ref):
    rows, width_part = attended_ref.shape
    half = rows // 2
    for chunk in (1, 0):
        span = slice(chunk * half, (chunk + 1) * half)
        pieces = []
        for head in range(width_part // HEAD):
            at = head * HEAD
            queries = projected_ref[span, at : at + HEAD]
            keys = projected_ref[:, width_part + at : width_part + at + HEAD]
            values = projected_ref[:, 2 * width_part + at : 2 * width_part + at + HEAD]
            scores = dot(queries, keys, ((1,), (1,))) * scale + bias_ref[span, :]
            spread = jnp.exp(scores - jnp.max(scores, axis=1, keepdims=True))
            probs = spread * (1.0 / jnp.sum(spread, axis=1, keepdims=True))
            pieces.append(dot(probs.astype(low), values))
        attended = jnp.concatenate(pieces, axis=1).astype(low)
        attended_ref[span, :] = attended
        part_ref[span, :] = dot(attended, output_ref[...]).astype(low)


def attend_back_kernel(projected_ref, bias_ref, output_ref, branch_grad_ref, grad_ref):
    rows, width_all = projected_ref.shape
    width_part = width_all // 3
    attended_grad = dot(branch_grad_ref[...], output_ref[...], ((1,), (1,))).astype(low)
    pieces = [[], [], []]
    for head in range(width_part // HEAD):
        at = head * HEAD
        queries = projected_ref[:, at : at + HEAD]
        keys = projected_ref[:, width_part + at : width_part + at + HEAD]
        values = projected_ref[:, 2 * width_part + at : 2 * width_part + at + HEAD]
        grad = attended_grad[:, at : at + HEAD]
        scores = dot(keys, queries, ((1,), (1,))) * scale + bias_ref[...]
        spread = jnp.exp(scores - jnp.max(scores, axis=0, keepdims=True))
        probs = spread * (1.0 / jnp.sum(spread, axis=0, keepdims=True))
        pieces[2].append(dot(probs.astype(low), grad))
        prob_grad = dot(values, grad, ((1,), (1,)))
        delta = jnp.sum(probs * prob_grad, axis=0, keepdims=True)
        score_grad = (probs * (prob_grad - delta)).astype(low)
        pieces[1].append(dot(score_grad, queries) * scale)
        pieces[0].append(dot(score_grad, keys, ((0,), (0,))) * scale)
    grad_ref[...] = jnp.concatenate(pieces[0] + pieces[1] + pieces[2], axis=1).astype(low)


def body(
    kept_rows,
    owner_index,
    kept_position,
    resolution,
    mask_token,
    condition,
    modulate_weight,
    entry_weight,
    output_weight,
    expand_weight,
    shrink_weight,
    cotangent,
):
    owners = lax.axis_size("dp")
    me = lax.axis_index("dp")
    lane = lax.axis_index("tensor")
    kept_count, width_part = kept_rows.shape
    width = mask_token.shape[0]
    own_tokens = cotangent.shape[0]
    quarter = own_tokens // QUARTERS
    group = quarter // 2
    arrived_count = own_tokens // 2
    block = group + SPARE
    rows = QUARTERS * block
    capacity = 2 * kept_count // owners
    slots_all = owners * capacity
    big = resolution[0] == 1

    owner_local = owner_index ^ me
    owner_hot = (owner_local[:, None] == jnp.arange(owners, dtype=jnp.int32)[None, :]).astype(low)
    earlier = (jnp.arange(kept_count)[:, None] > jnp.arange(kept_count)[None, :]).astype(low)
    before = dot(earlier, owner_hot)
    ranking = jnp.sum(before * owner_hot.astype(full), axis=1).astype(jnp.int32)
    slot_index = owner_local * capacity + ranking
    pack_matrix = (
        slot_index[:, None] == jnp.arange(slots_all, dtype=jnp.int32)[None, :]
    ).astype(low)
    context_part = lax.dynamic_slice_in_dim(
        condition.astype(full), lane * width_part, width_part, 1
    )
    lifted = jax.nn.silu(context_part).astype(low)
    coded = kept_position + 1
    tags = jnp.stack([coded // 32, coded % 32]).astype(low)
    tags = jnp.concatenate([tags, jnp.zeros((6, kept_count), low)])
    packed = dot(jnp.concatenate([kept_rows.T, tags]), pack_matrix).astype(low)
    packed = jnp.transpose(packed.reshape(width_part + 8, owners, capacity), (1, 0, 2))
    riders = lifted.reshape(-1, capacity)
    packed = jnp.concatenate(
        [packed, jnp.broadcast_to(riders[None], (owners,) + riders.shape)], axis=1
    )
    arrived = exchange_owners(packed)
    lifted_all = arrived[:, width_part + 8 :].reshape(owners * QUARTERS, width_part)
    arrived_rows = jnp.transpose(arrived[:, : width_part + 2], (1, 0, 2)).reshape(
        width_part + 2, slots_all
    )
    place = (
        arrived_rows[width_part].astype(full) * 32.0 + arrived_rows[width_part + 1].astype(full)
    ).astype(jnp.int32) - 1
    arrived_rows = arrived_rows[:width_part]

    place_column = place[:, None]
    there = place_column >= 0
    slot_rank = jnp.sum((there & (place_column < place[None, :])).astype(jnp.int32), axis=0)
    slot_rank = jnp.where(place >= 0, slot_rank, -1)
    positions = jnp.arange(own_tokens, dtype=jnp.int32)[None, :]
    token_rank = jnp.sum((there & (place_column < positions)).astype(jnp.int32), axis=0)
    filled = jnp.sum((place_column == positions).astype(jnp.int32), axis=0) > 0

    def row_of(rank):
        return ((rank // group) ^ lane) * block + rank % group

    spare_row = ((jnp.arange(own_tokens, dtype=jnp.int32) // quarter) ^ lane) * block + group
    token_row = jnp.where(filled, row_of(token_rank), spare_row)
    row_ids = jnp.arange(rows, dtype=jnp.int32)
    row_inner = row_ids % block
    row_rank = jnp.where(
        row_inner < group, ((row_ids // block) ^ lane) * group + row_inner, own_tokens
    )
    is_spare = row_inner == group
    spread_matrix = (row_ids[:, None] == token_row[None, :]).astype(low)
    slot_matrix = (row_rank[:, None] == slot_rank[None, :]).astype(low)
    rank_matrix = (
        slot_rank[:, None] == jnp.arange(arrived_count, dtype=jnp.int32)[None, :]
    ).astype(low)
    compact = dot(arrived_rows, rank_matrix).astype(low)
    gathered = jnp.zeros((width, arrived_count), low)
    for index, piece in enumerate(gather_blocks(compact)):
        gathered = lax.dynamic_update_slice(gathered, piece, ((lane ^ index) * width_part, 0))
    select_matrix = (
        row_rank[:, None] == jnp.arange(arrived_count, dtype=jnp.int32)[None, :]
    ).astype(low)
    spatial = dot(select_matrix, gathered, ((1,), (1,)))
    spatial = jnp.where(is_spare[:, None], mask_token.astype(full)[None, :], spatial)

    table = dot(lifted, modulate_weight)
    table = table + swap(table, "tensor", 1)
    table = table + swap(table, "tensor", 2)
    local_rows = jnp.arange(QUARTERS, dtype=jnp.int32) ^ lane
    chosen = jnp.where(big, table[0:1], jnp.take(table, local_rows, axis=0))

    def per_row(index):
        piece = chosen[:, index * width : (index + 1) * width]
        return jnp.broadcast_to(piece[:, None, :], (QUARTERS, block, width)).reshape(rows, width)

    def own_row(index):
        return chosen[0:1, index * width : (index + 1) * width]

    upstream = dot(spread_matrix, cotangent)
    feed_grad = (per_row(5) * upstream).astype(low)
    upstream_own = upstream[:block]

    key_block = row_ids // block
    same = key_block[:, None] == key_block[None, :]
    kept_key = (row_inner < group)[None, :]
    spare_key = is_spare[None, :]
    allowed_small = same & (kept_key | spare_key)
    allowed_big = kept_key | (spare_key & (key_block == 0)[None, :])
    allowed = jnp.where(big, allowed_big, allowed_small)
    weight_log = jnp.where(
        spare_key, jnp.log(jnp.where(big, float(arrived_count), float(group))), 0.0
    )
    bias = jnp.where(allowed, weight_log, -1e30)

    unit_one, inverse_one = normalize(spatial)
    normed_one = (unit_one * (1.0 + per_row(1)) + per_row(0)).astype(low)
    entry_flat = jnp.transpose(entry_weight, (1, 2, 0)).reshape(3 * width_part, width)
    projected = dot(normed_one, entry_flat, ((1,), (1,))).astype(low)
    attended, branch_part = pl.pallas_call(
        attend_kernel,
        out_shape=(
            jax.ShapeDtypeStruct((rows, width_part), low),
            jax.ShapeDtypeStruct((rows, width), low),
        ),
        compiler_params=pltpu.CompilerParams(vmem_limit_bytes=VMEM_ASK),
    )(projected, bias, output_weight)
    branch = sum_blocks(branch_part.reshape(QUARTERS, block, width))
    middle = spatial[:block] + own_row(2) * branch
    unit_two, inverse_two = normalize(middle)
    normed_two = (unit_two * (1.0 + own_row(4)) + own_row(3)).astype(low)
    normed_two = jnp.concatenate(gather_blocks(normed_two))
    hidden = dot(normed_two, expand_weight)
    activated, slope = gelu_both(hidden)
    activated = activated.astype(low)
    hidden_grad = (dot(feed_grad, shrink_weight, ((1,), (1,))) * slope).astype(low)
    normed_two_grad = sum_blocks(
        dot(hidden_grad, expand_weight, ((1,), (1,))).astype(low).reshape(QUARTERS, block, width)
    )
    middle_grad = upstream_own + normalize_back(
        unit_two, inverse_two, normed_two_grad * (1.0 + own_row(4))
    )
    branch_grad = (own_row(2) * middle_grad).astype(low)
    branch_grad = jnp.concatenate(gather_blocks(branch_grad))

    feed = sum_blocks(dot(activated, shrink_weight).astype(low).reshape(QUARTERS, block, width))
    out_own = (middle + own_row(5) * feed).astype(low)
    shrink_grad = sum_owners(dot(feed_grad, activated, ((0,), (0,))).astype(low))
    expand_grad = sum_owners(dot(normed_two, hidden_grad, ((0,), (0,))).astype(low))
    column_ids = jnp.arange(width, dtype=jnp.int32)
    column_from = ((column_ids // width_part) ^ lane) * width_part + column_ids % width_part
    column_matrix = (column_ids[:, None] == column_from[None, :]).astype(low)

    def to_columns(own):
        moved = dot(own, column_matrix).astype(low)
        pieces = [
            moved[:, index * width_part : (index + 1) * width_part] for index in range(QUARTERS)
        ]
        return jnp.concatenate(
            [pieces[0]] + [swap(pieces[index], "tensor", index) for index in range(1, QUARTERS)]
        )

    layer_out = dot(to_columns(out_own), spread_matrix, ((0,), (0,))).astype(low).T

    output_grad = sum_owners(dot(branch_grad, attended, ((0,), (0,))).astype(low))
    projected_grad = pl.pallas_call(
        attend_back_kernel,
        out_shape=jax.ShapeDtypeStruct((rows, 3 * width_part), low),
        compiler_params=pltpu.CompilerParams(vmem_limit_bytes=VMEM_ASK),
    )(projected, bias.T, output_weight, branch_grad)
    normed_one_grad = sum_blocks(
        dot(projected_grad, entry_flat).astype(low).reshape(QUARTERS, block, width)
    )
    entry_grad = sum_owners(dot(normed_one, projected_grad, ((0,), (0,))).astype(low))
    unit_own = unit_one[:block]
    spatial_grad = middle_grad + normalize_back(
        unit_own, inverse_one[:block], normed_one_grad * (1.0 + own_row(1))
    )
    back = to_columns(spatial_grad.astype(low))
    slots_back = dot(back, slot_matrix, ((0,), (0,))).astype(low)

    sums = jnp.concatenate(
        [
            jnp.sum(field, axis=0)
            for field in (
                normed_one_grad,
                normed_one_grad * unit_own,
                middle_grad * branch,
                normed_two_grad,
                normed_two_grad * unit_two,
                upstream_own * feed,
            )
        ]
    )
    mask_sum = spatial_grad[group]
    mask_high = mask_sum.astype(low)
    mask_rest = (mask_sum - mask_high.astype(full)).astype(low)
    sums = jnp.concatenate([sums.astype(low), mask_high, mask_rest])
    sums = jnp.stack(gather_blocks(sums.reshape(-1, 128))).reshape(QUARTERS, 8 * width)
    table_local = sums[:, : 6 * width]
    mask_total = jnp.sum(
        sums[:, 6 * width : 7 * width].astype(full) + sums[:, 7 * width :].astype(full), axis=0
    )
    first = jnp.arange(QUARTERS, dtype=jnp.int32)[:, None] == 0
    table_small = jnp.take(table_local, local_rows, axis=0)
    table_big = jnp.where(first, jnp.sum(table_local.astype(full), axis=0, keepdims=True), 0.0)
    table_grad = jnp.where(big, table_big, table_small.astype(full)).astype(low)
    logistic = jax.nn.sigmoid(context_part)
    condition_grad = (
        dot(table_grad, modulate_weight, ((1,), (1,)))
        * logistic
        * (1.0 + context_part * (1.0 - logistic))
    )
    table_part = 6 * width // owners
    mask_part = width // owners
    mask_high = mask_total.astype(low)
    mask_rest = (mask_total - mask_high.astype(full)).astype(low)
    riders = jnp.concatenate(
        [
            jnp.transpose(table_grad.reshape(QUARTERS, owners, table_part), (1, 0, 2)).reshape(
                owners, QUARTERS * table_part
            ),
            mask_high.reshape(owners, mask_part),
            mask_rest.reshape(owners, mask_part),
        ],
        axis=1,
    )
    rider_rows = -(-riders.shape[1] // capacity)
    riders = jnp.pad(riders, ((0, 0), (0, rider_rows * capacity - riders.shape[1])))
    owner_order = jnp.arange(owners, dtype=jnp.int32) ^ me
    riders = jnp.take(riders, owner_order, axis=0).reshape(owners, rider_rows, capacity)
    slabs = jnp.transpose(slots_back.reshape(width_part, owners, capacity), (1, 0, 2))
    returned = exchange_owners(jnp.concatenate([slabs, riders], axis=1))
    riders = returned[:, width_part:].reshape(owners, rider_rows * capacity)
    table_all = riders[:, : QUARTERS * table_part].reshape(owners * QUARTERS, table_part)
    modulate_grad = dot(lifted_all, table_all, ((0,), (0,)))
    mask_pieces = riders[:, QUARTERS * table_part :].astype(full)
    mask_grad = jnp.sum(
        mask_pieces[:, :mask_part] + mask_pieces[:, mask_part : 2 * mask_part], axis=0
    )
    returned = jnp.transpose(returned[:, :width_part], (1, 0, 2)).reshape(width_part, slots_all)
    kept_grad = dot(returned, pack_matrix, ((1,), (1,))).astype(low).T

    return (
        layer_out,
        kept_grad,
        mask_grad,
        condition_grad,
        modulate_grad,
        entry_grad.reshape(entry_grad.shape[0], 3, width_part),
        output_grad.T,
        expand_grad,
        shrink_grad.T,
    )


def solution(mesh):
    return jax.shard_map(
        body,
        mesh=mesh,
        in_specs=(
            P("dp", "tensor"),
            P("dp"),
            P("dp"),
            P("dp"),
            P(),
            P("dp", None),
            P("tensor", None),
            P(None, None, "tensor"),
            P("tensor", None),
            P(None, "tensor"),
            P("tensor", None),
            P("dp", None),
        ),
        out_specs=(
            P("dp", "tensor"),
            P("dp", "tensor"),
            P("dp"),
            P("dp", "tensor"),
            P("tensor", "dp"),
            P("dp", None, "tensor"),
            P("tensor", "dp"),
            P("dp", "tensor"),
            P("tensor", "dp"),
        ),
        check_vma=False,
    )
```

```python
from functools import partial

import jax
import jax.numpy as jnp
from jax import lax
from jax.experimental import pallas as pl
from jax.experimental.pallas import tpu as pltpu
from jax.sharding import PartitionSpec as P

HEAD = 72
QUARTERS = 4
SPARE = 8
scale = HEAD ** (-0.5)
epsilon = 1e-06
gelu_coeff = 0.7978845608028654
low = jnp.bfloat16
full = jnp.float32
VMEM_ASK = 32 * 1024 * 1024
RIDERS = 48
SWAP_OWNERS = 8


def dot(a, b, dims=((1,), (0,))):
    return lax.dot_general(a, b, (dims, ((), ())), preferred_element_type=full)


def normalize(rows):
    centered = rows - jnp.mean(rows, axis=-1, keepdims=True)
    inverse = lax.rsqrt(jnp.mean(centered * centered, axis=-1, keepdims=True) + epsilon)
    return (centered * inverse, inverse)


def normalize_back(unit, inverse, grad):
    return inverse * (
        grad
        - jnp.mean(grad, axis=-1, keepdims=True)
        - unit * jnp.mean(grad * unit, axis=-1, keepdims=True)
    )


def gelu_both(value):
    square = value * value
    curve = jnp.tanh(gelu_coeff * (value + 0.044715 * square * value))
    slope = 0.5 * (1.0 + curve) + 0.5 * value * (1.0 - curve * curve) * gelu_coeff * (
        1.0 + 3.0 * 0.044715 * square
    )
    return (0.5 * value * (1.0 + curve), slope)


def swap(value, axis, bit):
    size = lax.axis_size(axis)
    return lax.ppermute(value, axis, [(index, index ^ bit) for index in range(size)])


def gather_blocks(own):
    near = swap(own, "tensor", 1)
    across = swap(own, "tensor", 2)
    return [own, near, across, swap(across, "tensor", 1)]


def sum_far(part_2, part_3):
    got = swap(part_3, "tensor", 1)
    far = (part_2.astype(full) + got.astype(full)).astype(low)
    return far, swap(far, "tensor", 2)


class OwnerSum:
    def __init__(self, partial_sum, order):
        owners = lax.axis_size("dp")
        self.bits = owners.bit_length() - 1
        rows, columns = partial_sum.shape
        self.held = partial_sum.reshape((2,) * self.bits + (rows // owners, columns))
        self.left = list(range(self.bits - 1, -1, -1))
        self.order = list(order) + [bit for bit in range(self.bits) if bit not in order]
        self.send()

    def send(self):
        bit = self.order.pop(0)
        axis = self.left.index(bit)
        self.left.remove(bit)
        mine = (lax.axis_index("dp") >> bit) % 2
        given = lax.dynamic_index_in_dim(self.held, 1 - mine, axis, keepdims=False)
        self.kept = lax.dynamic_index_in_dim(self.held, mine, axis, keepdims=False)
        self.got = swap(given, "dp", 1 << bit)

    def step(self, *events):
        got = after(self.got, *events)
        total = self.kept.astype(full) + got.astype(full)
        if not self.order:
            self.held = total
            return total
        self.held = total.astype(low)
        self.send()
        return self.held

    def finish(self, *events):
        while True:
            last = not self.order
            total = self.step(*events)
            if last:
                return total


def exchange_owners(slabs):
    if len(slabs) > 1:
        return [slabs[0]] + [swap(slab, "dp", index) for index, slab in enumerate(slabs) if index]
    return [lax.all_to_all(slabs[0], "dp", split_axis=0, concat_axis=0, tiled=True)]


def attend(projected_ref, bias_ref, output_ref, attended_ref, chunk, half, width_part):
    span = slice(chunk * half, (chunk + 1) * half)
    pieces = []
    for head in range(width_part // HEAD):
        at = head * HEAD
        queries = projected_ref[span, at : at + HEAD]
        keys = projected_ref[:, width_part + at : width_part + at + HEAD]
        values = projected_ref[:, 2 * width_part + at : 2 * width_part + at + HEAD]
        scores = dot(queries, keys, ((1,), (1,))) * scale + bias_ref[span, :]
        spread = jnp.exp(scores - jnp.max(scores, axis=1, keepdims=True))
        probs = spread * (1.0 / jnp.sum(spread, axis=1, keepdims=True))
        pieces.append(dot(probs.astype(low), values))
    attended = jnp.concatenate(pieces, axis=1).astype(low)
    attended_ref[...] = attended
    return dot(attended, output_ref[...])


def entry_kernel(
    lane_ref,
    piece_0,
    piece_1,
    piece_2,
    piece_3,
    mask_ref,
    chosen_ref,
    entry_ref,
    bias_ref,
    output_ref,
    spatial_ref,
    normed_ref,
    projected_ref,
    attended_ref,
    part_0,
    part_1,
    gathered,
):
    lane = lane_ref[0]
    width_part = piece_0.shape[0]
    block, width = spatial_ref.shape
    group = block - SPARE
    half = 2 * block
    for index, piece in enumerate((piece_0, piece_1, piece_2, piece_3)):
        at = pl.multiple_of((lane ^ index) * width_part, 16)
        gathered[pl.ds(at, width_part), :] = piece[...]
    row_id = lax.broadcasted_iota(jnp.int32, (group, group), 0)
    column_id = lax.broadcasted_iota(jnp.int32, (group, group), 1)
    eye = (row_id == column_id).astype(full).astype(low)
    spare_id = lax.broadcasted_iota(jnp.int32, (SPARE, width), 0)
    spare = jnp.where(spare_id == 0, mask_ref[...].astype(full), 0.0)
    for chunk in (1, 0):
        span = slice(chunk * half, (chunk + 1) * half)
        normed = []
        for index in (2 * chunk, 2 * chunk + 1):
            at = pl.multiple_of((lane ^ index) * group, 128)
            kept = dot(eye, gathered[:, pl.ds(at, group)], ((1,), (1,)))
            rows = jnp.concatenate([kept, spare], axis=0)
            if index == 0:
                spatial_ref[...] = rows.astype(low)
            unit, inverse = normalize(rows)
            shift = chosen_ref[index : index + 1, :width]
            gain = chosen_ref[index : index + 1, width : 2 * width]
            normed.append(unit * (1.0 + gain) + shift)
        normed = jnp.concatenate(normed, axis=0).astype(low)
        normed_ref[span, :] = normed
        projected_ref[span, :] = dot(normed, entry_ref[...], ((1,), (1,))).astype(low)
    part = attend(projected_ref, bias_ref, output_ref, attended_ref, 1, half, width_part)
    part_0[...] = part[:block].astype(low)
    part_1[...] = part[block:].astype(low)


def attend_kernel(projected_ref, bias_ref, output_ref, attended_ref, part_0, part_1):
    block = part_0.shape[0]
    part = attend(
        projected_ref, bias_ref, output_ref, attended_ref, 0, 2 * block, output_ref.shape[0]
    )
    part_0[...] = part[:block].astype(low)
    part_1[...] = part[block:].astype(low)


def middle_kernel(
    part_0, part_1, part_2, spatial_ref, chosen_ref, branch_ref, middle_ref, normed_ref
):
    width = spatial_ref.shape[1]
    branch = part_0[...].astype(full) + part_1[...].astype(full) + part_2[...].astype(full)
    branch_ref[...] = branch
    middle = spatial_ref[...].astype(full) + chosen_ref[0:1, 2 * width : 3 * width] * branch
    middle_ref[...] = middle
    unit, inverse = normalize(middle)
    shift = chosen_ref[0:1, 3 * width : 4 * width]
    gain = chosen_ref[0:1, 4 * width : 5 * width]
    normed_ref[...] = (unit * (1.0 + gain) + shift).astype(low)


def feed_kernel(
    piece_0,
    piece_1,
    back_ref,
    expand_ref,
    normed_ref,
    activated_ref,
    hidden_grad_ref,
    part_0,
    part_1,
):
    block = piece_0.shape[0]
    normed = jnp.concatenate([piece_0[...].astype(full), piece_1[...].astype(full)], axis=0)
    normed = normed.astype(low)
    normed_ref[...] = normed
    hidden = dot(normed, expand_ref[...])
    activated, slope = gelu_both(hidden)
    activated_ref[...] = activated.astype(low)
    hidden_grad = (back_ref[...] * slope).astype(low)
    hidden_grad_ref[...] = hidden_grad
    part = dot(hidden_grad, expand_ref[...], ((1,), (1,)))
    part_0[...] = part[:block].astype(low)
    part_1[...] = part[block:].astype(low)


def middle_back_kernel(
    part_0,
    part_1,
    part_2,
    middle_ref,
    branch_ref,
    upstream_ref,
    chosen_ref,
    middle_grad_ref,
    branch_grad_ref,
    sums_ref,
):
    width = middle_ref.shape[1]
    normed_grad = part_0[...].astype(full) + part_1[...].astype(full) + part_2[...].astype(full)
    unit, inverse = normalize(middle_ref[...])
    gain = chosen_ref[0:1, 4 * width : 5 * width]
    middle_grad = upstream_ref[...] + normalize_back(unit, inverse, normed_grad * (1.0 + gain))
    middle_grad_ref[...] = middle_grad
    branch_grad_ref[...] = (chosen_ref[0:1, 2 * width : 3 * width] * middle_grad).astype(low)
    sums_ref[0:1, :] = jnp.sum(middle_grad * branch_ref[...], axis=0, keepdims=True)
    sums_ref[1:2, :] = jnp.sum(normed_grad, axis=0, keepdims=True)
    sums_ref[2:3, :] = jnp.sum(normed_grad * unit, axis=0, keepdims=True)


def attend_back_kernel(
    projected_ref,
    bias_ref,
    output_ref,
    entry_ref,
    piece_0,
    piece_1,
    piece_2,
    piece_3,
    branch_grad_ref,
    grad_ref,
    part_0,
    part_1,
):
    rows, width_all = projected_ref.shape
    width_part = width_all // 3
    block = piece_0.shape[0]
    half = 2 * block
    for chunk, pair in enumerate(((piece_0, piece_1), (piece_2, piece_3))):
        branch_grad_ref[chunk * half : (chunk + 1) * half, :] = jnp.concatenate(
            [piece[...].astype(full) for piece in pair], axis=0
        ).astype(low)
    attended_grad = dot(branch_grad_ref[...], output_ref[...], ((1,), (1,))).astype(low)
    pieces = [[], [], []]
    for head in range(width_part // HEAD):
        at = head * HEAD
        queries = projected_ref[:, at : at + HEAD]
        keys = projected_ref[:, width_part + at : width_part + at + HEAD]
        values = projected_ref[:, 2 * width_part + at : 2 * width_part + at + HEAD]
        grad = attended_grad[:, at : at + HEAD]
        scores = dot(keys, queries, ((1,), (1,))) * scale + bias_ref[...]
        spread = jnp.exp(scores - jnp.max(scores, axis=0, keepdims=True))
        probs = spread * (1.0 / jnp.sum(spread, axis=0, keepdims=True))
        pieces[2].append(dot(probs.astype(low), grad))
        prob_grad = dot(values, grad, ((1,), (1,)))
        delta = jnp.sum(probs * prob_grad, axis=0, keepdims=True)
        score_grad = (probs * (prob_grad - delta)).astype(low)
        pieces[1].append(dot(score_grad, queries) * scale)
        pieces[0].append(dot(score_grad, keys, ((0,), (0,))) * scale)
    grad_ref[...] = jnp.concatenate(pieces[0] + pieces[1] + pieces[2], axis=1).astype(low)
    part = dot(grad_ref[half:, :], entry_ref[...])
    part_0[...] = part[:block].astype(low)
    part_1[...] = part[block:].astype(low)


def entry_back_kernel(grad_ref, entry_ref, part_0, part_1):
    block = part_0.shape[0]
    part = dot(grad_ref[: 2 * block, :], entry_ref[...])
    part_0[...] = part[:block].astype(low)
    part_1[...] = part[block:].astype(low)


def pack_kernel(owners, me_ref, kept_ref, owner_ref, position_ref, riders_ref, *out_refs):
    slot_ref = out_refs[-1]
    extra, capacity = riders_ref.shape
    kept_count = kept_ref.shape[1]
    owner_local = owner_ref[...] ^ me_ref[0]
    owner_id = lax.broadcasted_iota(jnp.int32, (owners, kept_count), 0)
    hot = (owner_id == owner_local).astype(full)
    row_id = lax.broadcasted_iota(jnp.int32, (kept_count, kept_count), 0)
    column_id = lax.broadcasted_iota(jnp.int32, (kept_count, kept_count), 1)
    before = dot(hot.astype(low), (row_id < column_id).astype(full).astype(low))
    rank = jnp.sum(hot * before, axis=0, keepdims=True).astype(jnp.int32)
    slot = owner_local * capacity + rank
    slot_ref[...] = slot
    coded = position_ref[...] + 1
    tag_id = lax.broadcasted_iota(jnp.int32, (extra, kept_count), 0)
    tags = jnp.where(tag_id == 0, coded >> 5, jnp.where(tag_id == 1, coded & 31, 0))
    rows = jnp.concatenate([kept_ref[...], tags.astype(full).astype(low)], axis=0)
    slot_id = lax.broadcasted_iota(jnp.int32, (capacity, kept_count), 0)
    for index in range(owners):
        matrix = (slot_id + index * capacity == slot).astype(full).astype(low)
        slab = dot(rows, matrix, ((1,), (1,)))
        split = kept_ref.shape[0]
        slab = jnp.concatenate([slab[:split], slab[split:] + riders_ref[...].astype(full)], axis=0)
        if len(out_refs) == 2:
            out_refs[0][me_ref[0] ^ index] = slab.astype(low)
        else:
            out_refs[index][...] = slab.astype(low)


def unpack_kernel(owners, me_ref, *refs):
    slab_refs, (compact_ref, slot_rank_ref, token_rank_ref, arrived) = refs[:-4], refs[-4:]
    width_part, arrived_count = compact_ref.shape
    slots_all = arrived.shape[1]
    own_tokens = token_rank_ref.shape[1]
    capacity = slots_all // owners
    for index in range(owners):
        slab = slab_refs[0][me_ref[0] ^ index] if len(slab_refs) == 1 else slab_refs[index][...]
        arrived[:, index * capacity : (index + 1) * capacity] = slab
    tags = arrived[width_part : width_part + 16, :].astype(full)
    place = tags[0:1] * 32.0 + tags[1:2] - 1.0
    turned = jnp.transpose(jnp.broadcast_to(place, (8, slots_all)))[:, 0:1]
    turned = jnp.where(turned < 0.0, 1e9, turned)
    slot_rank = jnp.sum(jnp.where(turned < place, 1.0, 0.0), axis=0, keepdims=True)
    slot_rank = jnp.where(place < 0.0, -1.0, slot_rank).astype(jnp.int32)
    slot_rank_ref[...] = slot_rank
    spot = lax.broadcasted_iota(jnp.int32, (1, own_tokens), 1).astype(full)
    token_rank = jnp.sum(jnp.where(turned < spot, 1.0, 0.0), axis=0, keepdims=True)
    filled = jnp.sum(jnp.where(turned == spot, 1.0, 0.0), axis=0, keepdims=True)
    token_rank_ref[...] = jnp.where(filled > 0.0, token_rank, -1.0).astype(jnp.int32)
    rank_id = lax.broadcasted_iota(jnp.int32, (arrived_count, slots_all), 0)
    matrix = (rank_id == slot_rank).astype(full).astype(low)
    compact_ref[...] = dot(arrived[:width_part, :], matrix, ((1,), (1,))).astype(low)


def back_kernel(
    lane_ref,
    part_0,
    part_1,
    part_2,
    spatial_ref,
    middle_grad_ref,
    chosen_ref,
    sums_ref,
    feed_sum_ref,
    piece_0,
    piece_1,
    piece_2,
    piece_3,
    turned,
    riders,
):
    lane = lane_ref[0]
    block, width = spatial_ref.shape
    group = block - SPARE
    width_part = width // QUARTERS
    normed_grad = part_0[...].astype(full) + part_1[...].astype(full) + part_2[...].astype(full)
    unit, inverse = normalize(spatial_ref[...].astype(full))
    gain = chosen_ref[0:1, width : 2 * width]
    grad = middle_grad_ref[...] + normalize_back(unit, inverse, normed_grad * (1.0 + gain))
    turned[...] = jnp.transpose(grad[:group]).astype(low)
    mask_sum = grad[group : group + 1]
    mask_high = mask_sum.astype(low).astype(full)
    fields = [
        jnp.sum(normed_grad, axis=0, keepdims=True),
        jnp.sum(normed_grad * unit, axis=0, keepdims=True),
        sums_ref[0:1, :],
        sums_ref[1:2, :],
        sums_ref[2:3, :],
        feed_sum_ref[...],
        mask_high,
        mask_sum - mask_high,
    ]
    chunks = width // 128
    riders[...] = jnp.zeros_like(riders)
    for number, field in enumerate(fields):
        for chunk in range(chunks):
            at = number * chunks + chunk
            riders[at : at + 1, :] = field[:, chunk * 128 : (chunk + 1) * 128]
    rider_rows = riders[...].astype(low)
    for index, piece in enumerate((piece_0, piece_1, piece_2, piece_3)):
        at = pl.multiple_of((lane ^ index) * width_part, 16)
        piece[:width_part, :] = turned[pl.ds(at, width_part), :]
        piece[width_part:, :] = rider_rows


def slots_kernel(
    owners, lane_ref, me_ref, big_ref, rank_ref, piece_0, piece_1, piece_2, piece_3, *refs
):
    slab_refs, (table_ref, table, mask_total) = refs[:-3], refs[-3:]
    lane = lane_ref[0]
    me = me_ref[0]
    group = piece_0.shape[1]
    slots_all = rank_ref.shape[1]
    capacity = slots_all // owners
    chunks = table_ref.shape[1]
    width_part = slab_refs[0].shape[0] - RIDERS
    pieces = [piece_0, piece_1, piece_2, piece_3]
    rows = jnp.concatenate([piece[:width_part, :] for piece in pieces], axis=1)
    row_id = lax.broadcasted_iota(jnp.int32, (group, slots_all), 0)
    matrix = jnp.concatenate(
        [
            (row_id + (lane ^ index) * group == rank_ref[...]).astype(full).astype(low)
            for index in range(QUARTERS)
        ],
        axis=0,
    )
    slots = dot(rows, matrix)
    table[...] = jnp.zeros_like(table)
    summed = jnp.zeros((chunks, 128), full)
    mask_sum = jnp.zeros((16, 128), full)
    mask_rows = chunks // 6
    for index, piece in enumerate(pieces):
        field = piece[width_part : width_part + chunks, :].astype(full)
        summed = summed + field
        rest = piece[width_part + chunks - chunks % 16 :, :].astype(full)
        table[lane ^ index, :chunks, :] = field
        at = chunks % 16
        mask_sum = mask_sum + jnp.concatenate(
            [
                rest[at : at + mask_rows] + rest[at + mask_rows : at + 2 * mask_rows],
                jnp.zeros((16 - mask_rows, 128), full),
            ],
            axis=0,
        )
    mask_total[...] = mask_sum

    @pl.when(big_ref[0] == 1)
    def _():
        table[...] = jnp.zeros_like(table)
        table[0, :chunks, :] = summed

    table_ref[...] = table[:, :chunks, :].astype(low)
    for index in range(owners):
        owner = me ^ index
        start = (owner * chunks) // owners
        fields = [table[row, pl.ds(start, 8), :] for row in range(QUARTERS)]
        mask_start = (owner * mask_rows) // owners
        mask_part = mask_total[pl.ds(mask_start, 2), :]
        mask_high = mask_part.astype(low).astype(full)
        fields += [mask_high, mask_part - mask_high, jnp.zeros((RIDERS - 36, 128), full)]
        slab = jnp.concatenate([slots[:, index * capacity : (index + 1) * capacity]] + fields, axis=0)
        slab_refs[index][...] = slab.astype(low)


def kept_kernel(owners, me_ref, slot_ref, lifted_ref, *refs):
    slab_refs = refs[:owners]
    kept_ref, modulate_ref, mask_ref, table = refs[owners:]
    width_part, kept_count = kept_ref.shape
    capacity = slab_refs[0].shape[1]
    table_part = modulate_ref.shape[1]
    mask_part = mask_ref.shape[1]
    me = me_ref[0]
    rows = jnp.concatenate([slab[:width_part, :] for slab in slab_refs], axis=1)
    slot_id = lax.broadcasted_iota(jnp.int32, (owners * capacity, kept_count), 0)
    matrix = (slot_id == slot_ref[...]).astype(full).astype(low)
    kept_ref[...] = dot(rows, matrix).astype(low)
    mask_sum = jnp.zeros((1, 256), full)
    for index, slab in enumerate(slab_refs):
        rider = slab[width_part:, :].astype(full)
        for row in range(QUARTERS):
            at = index * QUARTERS + row
            for chunk in range(8):
                from_row = row * 8 + chunk
                table[at : at + 1, chunk * 128 : (chunk + 1) * 128] = rider[
                    from_row : from_row + 1
                ]
        high, rest = rider[32:34], rider[34:36]
        both = high + rest
        mask_sum = mask_sum + jnp.concatenate([both[0:1], both[1:2]], axis=1)
    shift = (me * table_part) % 128
    field = pltpu.roll(table[...], (1024 - shift) % 1024, 1)[:, :table_part]
    modulate_ref[...] = dot(lifted_ref[...], field.astype(low), ((0,), (0,)))
    shift = (me * mask_part) % 128
    mask_sum = jnp.broadcast_to(mask_sum, (8, 256))
    mask_ref[...] = pltpu.roll(mask_sum, (256 - shift) % 256, 1)[0:1, :mask_part]


def out_kernel(
    lane_ref,
    part_0,
    part_1,
    part_2,
    middle_ref,
    upstream_ref,
    chosen_ref,
    feed_sum_ref,
    piece_0,
    piece_1,
    piece_2,
    piece_3,
    turned,
    riders,
):
    lane = lane_ref[0]
    block, width = middle_ref.shape
    group = block - SPARE
    width_part = width // QUARTERS
    feed = part_0[...].astype(full) + part_1[...].astype(full) + part_2[...].astype(full)
    feed_sum_ref[...] = jnp.sum(feed * upstream_ref[...], axis=0, keepdims=True)
    out = middle_ref[...] + chosen_ref[0:1, 5 * width : 6 * width] * feed
    turned[...] = jnp.transpose(out[:group]).astype(low)
    riders[...] = jnp.zeros_like(riders)
    for chunk in range(width // 128):
        riders[chunk : chunk + 1, :] = out[group : group + 1, chunk * 128 : (chunk + 1) * 128]
    rider_rows = riders[...].astype(low)
    for index, piece in enumerate((piece_0, piece_1, piece_2, piece_3)):
        at = pl.multiple_of((lane ^ index) * width_part, 16)
        piece[:width_part, :] = turned[pl.ds(at, width_part), :]
        piece[width_part:, :] = rider_rows


def layer_kernel(
    lane_ref, rank_ref, piece_0, piece_1, piece_2, piece_3, out_ref, spare, turned
):
    lane = lane_ref[0]
    width_part, own_tokens = out_ref.shape
    group = piece_0.shape[1]
    quarter = own_tokens // QUARTERS
    pieces = (piece_0, piece_1, piece_2, piece_3)
    rows = jnp.concatenate([piece[:width_part, :] for piece in pieces], axis=1)
    row_id = lax.broadcasted_iota(jnp.int32, (group, own_tokens), 0)
    matrix = jnp.concatenate(
        [
            (row_id + (lane ^ index) * group == rank_ref[...]).astype(full).astype(low)
            for index in range(QUARTERS)
        ],
        axis=0,
    )
    spare[...] = jnp.zeros_like(spare)
    for index, piece in enumerate(pieces):
        rider = piece[width_part:, :].astype(full)
        for chunk in range(spare.shape[1] // 128):
            spare[index : index + 1, chunk * 128 : (chunk + 1) * 128] = rider[chunk : chunk + 1]
    turned[...] = jnp.transpose(spare[...])
    columns = turned[pl.ds(pl.multiple_of(lane * width_part, 16), width_part), :].astype(low)
    spare_id = lax.broadcasted_iota(jnp.int32, (8, own_tokens), 0)
    spot = lax.broadcasted_iota(jnp.int32, (8, own_tokens), 1) // quarter
    empty = rank_ref[...] < 0
    spots = jnp.where(((spare_id ^ lane) == spot) & (spare_id < QUARTERS) & empty, 1.0, 0.0)
    out_ref[...] = (dot(rows, matrix) + dot(columns, spots.astype(low))).astype(low)


def call(kernel, outs, *operands, **options):
    return pl.pallas_call(
        kernel,
        out_shape=tuple(jax.ShapeDtypeStruct(shape, kind) for shape, kind in outs),
        compiler_params=pltpu.CompilerParams(vmem_limit_bytes=VMEM_ASK),
        **options,
    )(*operands)


def after(value, *others):
    return lax.optimization_barrier((value,) + others)[0]


def body(
    kept_rows,
    owner_index,
    kept_position,
    resolution,
    mask_token,
    condition,
    modulate_weight,
    entry_weight,
    output_weight,
    expand_weight,
    shrink_weight,
    cotangent,
):
    owners = lax.axis_size("dp")
    me = lax.axis_index("dp")
    lane = lax.axis_index("tensor")
    kept_count, width_part = kept_rows.shape
    width = mask_token.shape[0]
    own_tokens = cotangent.shape[0]
    quarter = own_tokens // QUARTERS
    group = quarter // 2
    arrived_count = own_tokens // 2
    block = group + SPARE
    rows = QUARTERS * block
    capacity = 2 * kept_count // owners
    slots_all = owners * capacity
    big = resolution[0] == 1

    direct = owners <= SWAP_OWNERS
    small = pl.BlockSpec(memory_space=pltpu.SMEM)
    plain = pl.BlockSpec(memory_space=pltpu.VMEM)
    lane_word = lane.reshape(1).astype(jnp.int32)
    me_word = me.reshape(1).astype(jnp.int32)
    context_part = lax.dynamic_slice_in_dim(
        condition.astype(full), lane * width_part, width_part, 1
    )
    lifted = jax.nn.silu(context_part).astype(low)
    riders = lifted.reshape(-1, capacity)
    rider_count = riders.shape[0]
    extra = -(-(rider_count + 2) // 16) * 16
    riders = jnp.pad(riders, ((2, extra - 2 - rider_count), (0, 0)))
    slab_rows = width_part + extra
    if direct:
        slab_shapes = (((slab_rows, capacity), low),) * owners
    else:
        slab_shapes = (((owners, slab_rows, capacity), low),)
    *slabs, slot_index = call(
        partial(pack_kernel, owners),
        slab_shapes + (((1, kept_count), jnp.int32),),
        me_word,
        kept_rows.T,
        owner_index[None, :],
        kept_position[None, :],
        riders,
        in_specs=[small] + [plain] * 4,
    )
    slabs = exchange_owners(slabs)
    if direct:
        lifted_all = jnp.stack([slab[width_part + 2 : width_part + 2 + rider_count] for slab in slabs])
    else:
        owner_order = jnp.arange(owners, dtype=jnp.int32) ^ me
        lifted_all = slabs[0][:, width_part + 2 : width_part + 2 + rider_count]
    lifted_all = lifted_all.reshape(owners * QUARTERS, width_part)
    compact, slot_rank, token_rank = call(
        partial(unpack_kernel, owners),
        (
            ((width_part, arrived_count), low),
            ((1, slots_all), jnp.int32),
            ((1, own_tokens), jnp.int32),
        ),
        me_word,
        *slabs,
        in_specs=[small] + [plain] * len(slabs),
        scratch_shapes=[pltpu.VMEM((slab_rows, slots_all), low)],
    )
    spatial_pieces = gather_blocks(compact)
    token_flat = token_rank[0]
    spare_row = ((jnp.arange(own_tokens, dtype=jnp.int32) // quarter) ^ lane) * block + group
    token_row = jnp.where(
        token_flat >= 0,
        ((token_flat // group) ^ lane) * block + token_flat % group,
        spare_row,
    )
    row_ids = jnp.arange(rows, dtype=jnp.int32)
    row_inner = row_ids % block
    is_spare = row_inner == group
    spread_matrix = (row_ids[:, None] == token_row[None, :]).astype(low)

    table = dot(lifted, modulate_weight)
    table = table + swap(table, "tensor", 1)
    table = table + swap(table, "tensor", 2)
    local_rows = jnp.arange(QUARTERS, dtype=jnp.int32) ^ lane
    chosen = jnp.where(big, table[0:1], jnp.take(table, local_rows, axis=0))

    def per_row(index):
        piece = chosen[:, index * width : (index + 1) * width]
        return jnp.broadcast_to(piece[:, None, :], (QUARTERS, block, width)).reshape(rows, width)

    def own_row(index):
        return chosen[0:1, index * width : (index + 1) * width]

    upstream = dot(spread_matrix, cotangent)
    feed_grad = (per_row(5) * upstream).astype(low)
    upstream_own = upstream[:block]

    key_block = row_ids // block
    same = key_block[:, None] == key_block[None, :]
    kept_key = (row_inner < group)[None, :]
    spare_key = is_spare[None, :]
    allowed_small = same & (kept_key | spare_key)
    allowed_big = kept_key | (spare_key & (key_block == 0)[None, :])
    allowed = jnp.where(big, allowed_big, allowed_small)
    weight_log = jnp.where(
        spare_key, jnp.log(jnp.where(big, float(arrived_count), float(group))), 0.0
    )
    bias = jnp.where(allowed, weight_log, -1e30)
    bias_turned = bias.T

    entry_flat = jnp.transpose(entry_weight, (1, 2, 0)).reshape(3 * width_part, width)
    token_shape = ((block, width), low)
    half = 2 * block
    spatial_own, normed_one, projected, attended_far, part_2, part_3 = call(
        entry_kernel,
        (
            token_shape,
            ((rows, width), low),
            ((rows, 3 * width_part), low),
            ((half, width_part), low),
            token_shape,
            token_shape,
        ),
        lane_word,
        *spatial_pieces,
        mask_token[None, :],
        chosen[:, : 2 * width],
        entry_flat,
        bias,
        output_weight,
        in_specs=[small] + [plain] * 9,
        scratch_shapes=[pltpu.VMEM((width, arrived_count), low)],
    )
    far, across = sum_far(part_2, part_3)
    attended_near, part_0, part_1 = call(
        attend_kernel,
        (((half, width_part), low), token_shape, token_shape),
        after(projected, far),
        bias,
        output_weight,
    )
    got = swap(part_1, "tensor", 1)
    hidden_back = dot(after(feed_grad, part_0), shrink_weight, ((1,), (1,)))
    branch, middle, normed_two_own = call(
        middle_kernel,
        (((block, width), full), ((block, width), full), token_shape),
        part_0,
        got,
        after(across, hidden_back),
        spatial_own,
        chosen,
    )

    def feed_call(piece_0, piece_1, back):
        return call(
            feed_kernel,
            (((half, width), low), ((half, width), low), ((half, width), low))
            + (token_shape, token_shape),
            piece_0,
            piece_1,
            back,
            expand_weight,
        )

    near_piece = swap(normed_two_own, "tensor", 1)
    across = swap(normed_two_own, "tensor", 2)
    normed_near, activated_near, hidden_near, part_0, part_1 = feed_call(
        normed_two_own, near_piece, hidden_back[:half]
    )
    last_piece = swap(after(across, part_0), "tensor", 1)
    normed_far, activated_far, hidden_far, part_2, part_3 = feed_call(
        across, last_piece, hidden_back[half:]
    )
    far, across = sum_far(part_2, part_3)
    got = swap(part_1, "tensor", 1)
    activated = jnp.concatenate([after(activated_near, far), activated_far])
    shrink_partial = dot(feed_grad, activated, ((0,), (0,))).astype(low)
    shrink_sum = OwnerSum(shrink_partial, (0, 1, 2))
    normed_two = jnp.concatenate([after(normed_near, shrink_partial), normed_far])
    hidden_grad = jnp.concatenate([hidden_near, hidden_far])
    expand_partial = dot(normed_two, hidden_grad, ((0,), (0,))).astype(low)
    expand_sum = OwnerSum(expand_partial, (1, 0, 2))
    middle_grad, branch_grad_own, sums = call(
        middle_back_kernel,
        (((block, width), full), token_shape, ((SPARE, width), full)),
        part_0,
        got,
        after(across, expand_partial),
        middle,
        branch,
        upstream_own,
        chosen,
    )
    branch_pieces = gather_blocks(branch_grad_own)
    feed_parts = dot(after(activated, branch_grad_own), shrink_weight).astype(low)
    feed_parts = feed_parts.reshape(QUARTERS, block, width)
    feed_far = swap(feed_parts[3], "tensor", 1)
    feed_got = swap(feed_parts[1], "tensor", 1)
    feed_far = (feed_parts[2].astype(full) + feed_far.astype(full)).astype(low)
    branch_grad, projected_grad, part_2, part_3 = call(
        attend_back_kernel,
        (((rows, width), low), ((rows, 3 * width_part), low), token_shape, token_shape),
        projected,
        bias_turned,
        output_weight,
        entry_flat,
        *branch_pieces[:3],
        after(branch_pieces[3], feed_far),
    )
    feed_across = swap(after(feed_far, branch_pieces[3]), "tensor", 2)
    far, across = sum_far(part_2, after(part_3, feed_across))
    part_0, part_1 = call(
        entry_back_kernel, (token_shape, token_shape), after(projected_grad, far), entry_flat
    )
    got = swap(part_1, "tensor", 1)
    entry_partial = dot(
        after(normed_one, part_1), projected_grad, ((0,), (0,))
    ).astype(low)
    entry_sum = OwnerSum(entry_partial, (0, 1, 2))
    shrink_sum.step(entry_partial)
    expand_sum.step(entry_partial)
    piece_shape = ((width_part + 80, group), low)
    out_shape = ((width_part + 16, group), low)
    feed_sum, *out_pieces = call(
        out_kernel,
        (((1, width), full),) + (out_shape,) * QUARTERS,
        lane_word,
        feed_parts[0],
        feed_got,
        after(feed_across, entry_partial),
        middle,
        upstream_own,
        chosen,
        in_specs=[small] + [plain] * 6,
        scratch_shapes=[pltpu.VMEM((width, group), low), pltpu.VMEM((16, 128), full)],
    )
    back_pieces = call(
        back_kernel,
        (piece_shape,) * QUARTERS,
        lane_word,
        part_0,
        got,
        across,
        spatial_own,
        middle_grad,
        chosen,
        sums,
        feed_sum,
        in_specs=[small] + [plain] * 8,
        scratch_shapes=[pltpu.VMEM((width, group), low), pltpu.VMEM((80, 128), full)],
    )
    back_pieces = [back_pieces[0]] + [
        swap(back_pieces[index], "tensor", index) for index in range(1, QUARTERS)
    ]
    output_partial = dot(
        after(branch_grad, entry_partial),
        jnp.concatenate([attended_near, attended_far]),
        ((0,), (0,)),
    ).astype(low)
    output_sum = OwnerSum(output_partial, (0, 1, 2))
    chunks = 6 * width // 128
    big_word = resolution[:1]
    logistic = jax.nn.sigmoid(context_part)
    logistic = logistic * (1.0 + context_part * (1.0 - logistic))
    if direct:
        *slabs, table_grad = call(
            partial(slots_kernel, owners),
            (((width_part + RIDERS, capacity), low),) * owners
            + (((QUARTERS, chunks, 128), low),),
            lane_word,
            me_word,
            big_word,
            slot_rank,
            *back_pieces,
            in_specs=[small] * 3 + [plain] * 5,
            scratch_shapes=[
                pltpu.VMEM((QUARTERS, chunks + 2, 128), full),
                pltpu.VMEM((16, 128), full),
            ],
        )
        slabs = exchange_owners(slabs)
        table_grad = table_grad.reshape(QUARTERS, 6 * width)
        kept_grad, modulate_grad, mask_grad = call(
            partial(kept_kernel, owners),
            (
                ((width_part, kept_count), low),
                ((width_part, 6 * width // owners), full),
                ((1, width // owners), full),
            ),
            me_word,
            slot_index,
            lifted_all,
            *slabs,
            in_specs=[small] + [plain] * (2 + owners),
            scratch_shapes=[pltpu.VMEM((owners * QUARTERS, 1024), full)],
        )
        mask_grad = mask_grad[0]
    else:
        rows_back = jnp.concatenate([piece[:width_part] for piece in back_pieces], axis=1)
        rank_ids = jnp.arange(arrived_count, dtype=jnp.int32)
        rank_ids = ((rank_ids // group) ^ lane) * group + rank_ids % group
        matrix = (rank_ids[:, None] == slot_rank).astype(low)
        slabs = dot(rows_back, matrix).astype(low).reshape(width_part, owners, capacity)
        slabs = jnp.take(jnp.transpose(slabs, (1, 0, 2)), owner_order, axis=0)
        slabs = jnp.take(exchange_owners([slabs])[0], owner_order, axis=0)
        slabs = jnp.transpose(slabs, (1, 0, 2)).reshape(width_part, slots_all)
        slot_ids = jnp.arange(slots_all, dtype=jnp.int32)[:, None]
        kept_grad = dot(slabs, (slot_ids == slot_index).astype(low)).astype(low)
        riders = jnp.stack([piece[width_part : width_part + 8 * width // 128] for piece in back_pieces])
        riders = riders.reshape(QUARTERS, 8, width).astype(full)
        mask_total = jnp.sum(riders[:, 6] + riders[:, 7], axis=0)
        table_local = riders[:, :6].reshape(QUARTERS, 6 * width)
        table_small = jnp.take(table_local, jnp.arange(QUARTERS, dtype=jnp.int32) ^ lane, axis=0)
        first = jnp.arange(QUARTERS, dtype=jnp.int32)[:, None] == 0
        table_big = jnp.where(first, jnp.sum(table_local, axis=0, keepdims=True), 0.0)
        table_grad = jnp.where(big, table_big, table_small).astype(low)
        sent = jnp.transpose(table_grad.reshape(QUARTERS, owners, -1), (1, 0, 2))
        table_all = exchange_owners([sent])[0].reshape(owners * QUARTERS, -1)
        modulate_grad = dot(lifted_all, table_all, ((0,), (0,)))
        mask_grad = lax.psum_scatter(mask_total, "dp", scatter_dimension=0, tiled=True)
    condition_grad = dot(table_grad, modulate_weight, ((1,), (1,))) * logistic
    out_pieces = [out_pieces[0]] + [
        swap(after(out_pieces[index], *slabs[:1]), "tensor", index) for index in range(1, QUARTERS)
    ]
    layer_out = call(
        layer_kernel,
        (((width_part, own_tokens), low),),
        lane_word,
        token_rank,
        *out_pieces,
        in_specs=[small] + [plain] * 5,
        scratch_shapes=[pltpu.VMEM((8, width), full), pltpu.VMEM((width, 8), full)],
    )[0]
    shrink_grad = shrink_sum.finish()
    expand_grad = expand_sum.finish()
    entry_grad = entry_sum.finish()
    output_grad = output_sum.finish()

    return (
        layer_out.T,
        kept_grad.T,
        mask_grad,
        condition_grad,
        modulate_grad,
        entry_grad.reshape(entry_grad.shape[0], 3, width_part),
        output_grad.T,
        expand_grad,
        shrink_grad.T,
    )


def solution(mesh):
    return jax.shard_map(
        body,
        mesh=mesh,
        in_specs=(
            P("dp", "tensor"),
            P("dp"),
            P("dp"),
            P("dp"),
            P(),
            P("dp", None),
            P("tensor", None),
            P(None, None, "tensor"),
            P("tensor", None),
            P(None, "tensor"),
            P("tensor", None),
            P("dp", None),
        ),
        out_specs=(
            P("dp", "tensor"),
            P("dp", "tensor"),
            P("dp"),
            P("dp", "tensor"),
            P("tensor", "dp"),
            P("dp", None, "tensor"),
            P("tensor", "dp"),
            P("dp", "tensor"),
            P("tensor", "dp"),
        ),
        check_vma=False,
    )
```

```python
from functools import partial

import jax
import jax.numpy as jnp
from jax import lax
from jax.experimental import pallas as pl
from jax.experimental.pallas import tpu as pltpu
from jax.sharding import PartitionSpec as P

HEAD = 72
QUARTERS = 4
SPARE = 8
scale = HEAD ** (-0.5)
epsilon = 1e-06
gelu_coeff = 0.7978845608028654
low = jnp.bfloat16
full = jnp.float32
VMEM_ASK = 24 * 1024 * 1024
RIDERS = 48
SWAP_OWNERS = 8
SPLIT = 72
FAR = (6, 7, 4, 5)
NEAR = (2, 3, 1, 0)
SMALL = pl.BlockSpec(memory_space=pltpu.SMEM)
PLAIN = pl.BlockSpec(memory_space=pltpu.VMEM)


def dot(a, b, dims=((1,), (0,))):
    return lax.dot_general(a, b, (dims, ((), ())), preferred_element_type=full)


def normalize(rows):
    centered = rows - jnp.mean(rows, axis=-1, keepdims=True)
    inverse = lax.rsqrt(jnp.mean(centered * centered, axis=-1, keepdims=True) + epsilon)
    return (centered * inverse, inverse)


def normalize_back(unit, inverse, grad):
    return inverse * (
        grad
        - jnp.mean(grad, axis=-1, keepdims=True)
        - unit * jnp.mean(grad * unit, axis=-1, keepdims=True)
    )


def gelu_both(value):
    square = value * value
    curve = jnp.tanh(gelu_coeff * (value + 0.044715 * square * value))
    slope = 0.5 * (1.0 + curve) + 0.5 * value * (1.0 - curve * curve) * gelu_coeff * (
        1.0 + 3.0 * 0.044715 * square
    )
    return (0.5 * value * (1.0 + curve), slope)


def swap(value, axis, bit):
    size = lax.axis_size(axis)
    return lax.ppermute(value, axis, [(index, index ^ bit) for index in range(size)])


def gather_blocks(own):
    near = swap(own, "tensor", 1)
    across = swap(own, "tensor", 2)
    return [own, near, across, swap(across, "tensor", 1)]


def sum_far(part_2, part_3):
    got = swap(part_3, "tensor", 1)
    far, token = call(add_kernel, ((part_2.shape, low),), part_2, got, time=0.4, token=True)
    return far, swap(far, "tensor", 2), turn(token)


def sum_owners(total):
    owners, rows, columns = total.shape
    me = lax.axis_index("dp")
    step = 1
    while step < owners:
        pairs = total.reshape(-1, 2, rows, columns)
        mine = (me // step) % 2
        given = lax.dynamic_index_in_dim(pairs, 1 - mine, 1, keepdims=False)
        kept = lax.dynamic_index_in_dim(pairs, mine, 1, keepdims=False)
        total = kept.astype(full) + swap(given, "dp", step).astype(full)
        step *= 2
        total = total if step == owners else total.astype(low)
    return total[0]


def part_shapes(count, rows, columns):
    return [((count, SPLIT, columns), low), ((count, rows - SPLIT, columns), low)]


def start_sums(groups, deps=(), time=3.0):
    width = groups[0][0][0][0].shape[1]
    columns = sum(rhs[0].shape[1] for _, rhs in groups[0])
    rows = width // 8
    shapes = part_shapes(4 * len(groups), rows, columns)
    counts = [[(len(lhs), len(rhs)) for lhs, rhs in pairs] for pairs in groups]
    given_0, given_1, kept_0, kept_1, token = call(
        partial(weight_kernel, counts),
        shapes + shapes,
        lax.axis_index("dp").reshape(1).astype(jnp.int32),
        *[value for pairs in groups for lhs, rhs in pairs for value in (*lhs, *rhs)],
        words=1,
        deps=deps,
        time=time,
        scratch=[pltpu.VMEM((width, columns), full)],
        token=True,
    )
    return (given_0, given_1), (kept_0, kept_1), token


def cross(given, first, second):
    return swap(given[0], "dp", first), swap(given[1], "dp", second)


def halve_sums(kept, got, deps=()):
    count, _, columns = kept[0].shape
    shapes = part_shapes(count // 2, SPLIT + kept[1].shape[1], columns)
    given_0, given_1, kept_0, kept_1, token = call(
        halve_kernel,
        shapes + shapes,
        lax.axis_index("dp").reshape(1).astype(jnp.int32),
        *kept,
        *got,
        words=1,
        deps=deps,
        time=0.8,
        token=True,
    )
    return (given_0, given_1), (kept_0, kept_1), token


def join_sums(kept, got, deps=()):
    count, _, columns = kept[0].shape
    shape = ((count // 2, SPLIT + kept[1].shape[1], columns), low)
    given, kept, token = call(
        join_kernel,
        (shape, shape),
        lax.axis_index("dp").reshape(1).astype(jnp.int32),
        *kept,
        *got,
        words=1,
        deps=deps,
        time=0.8,
        token=True,
    )
    return swap(given, "dp", 4), kept, token


def exchange_owners(slabs):
    if isinstance(slabs, dict):
        return {index: swap(slab, "dp", index) if index else slab for index, slab in slabs.items()}
    return [lax.all_to_all(slabs[0], "dp", split_axis=0, concat_axis=0, tiled=True)]


def attend(projected_ref, bias_ref, output_ref, attended_ref, chunk, half, width_part):
    span = slice(chunk * half, (chunk + 1) * half)
    pieces = []
    for head in range(width_part // HEAD):
        at = head * HEAD
        queries = projected_ref[span, at : at + HEAD]
        keys = projected_ref[:, width_part + at : width_part + at + HEAD]
        values = projected_ref[:, 2 * width_part + at : 2 * width_part + at + HEAD]
        scores = dot(queries, keys, ((1,), (1,))) * scale + bias_ref[span, :]
        spread = jnp.exp(scores - jnp.max(scores, axis=1, keepdims=True))
        probs = spread * (1.0 / jnp.sum(spread, axis=1, keepdims=True))
        pieces.append(dot(probs.astype(low), values))
    attended = jnp.concatenate(pieces, axis=1).astype(low)
    attended_ref[...] = attended
    return dot(attended, output_ref[...])


def entry_kernel(
    lane_ref,
    piece_0,
    piece_1,
    piece_2,
    piece_3,
    mask_ref,
    chosen_ref,
    entry_ref,
    bias_ref,
    output_ref,
    spatial_ref,
    normed_ref,
    projected_ref,
    attended_ref,
    part_0,
    part_1,
    gathered,
):
    lane = lane_ref[0]
    width_part = piece_0.shape[0]
    block, width = spatial_ref.shape
    group = block - SPARE
    half = 2 * block
    for index, piece in enumerate((piece_0, piece_1, piece_2, piece_3)):
        at = pl.multiple_of((lane ^ index) * width_part, 16)
        gathered[pl.ds(at, width_part), :] = piece[...]
    row_id = lax.broadcasted_iota(jnp.int32, (group, group), 0)
    column_id = lax.broadcasted_iota(jnp.int32, (group, group), 1)
    eye = (row_id == column_id).astype(full).astype(low)
    spare_id = lax.broadcasted_iota(jnp.int32, (SPARE, width), 0)
    spare = jnp.where(spare_id == 0, mask_ref[...].astype(full), 0.0)
    for chunk in (1, 0):
        span = slice(chunk * half, (chunk + 1) * half)
        normed = []
        for index in (2 * chunk, 2 * chunk + 1):
            at = pl.multiple_of((lane ^ index) * group, 128)
            kept = dot(eye, gathered[:, pl.ds(at, group)], ((1,), (1,)))
            rows = jnp.concatenate([kept, spare], axis=0)
            if index == 0:
                spatial_ref[...] = rows.astype(low)
            unit, inverse = normalize(rows)
            shift = chosen_ref[index : index + 1, :width]
            gain = chosen_ref[index : index + 1, width : 2 * width]
            normed.append(unit * (1.0 + gain) + shift)
        normed = jnp.concatenate(normed, axis=0).astype(low)
        normed_ref[span, :] = normed
        projected_ref[span, :] = dot(normed, entry_ref[...], ((1,), (1,))).astype(low)
    part = attend(projected_ref, bias_ref, output_ref, attended_ref, 1, half, width_part)
    part_0[...] = part[:block].astype(low)
    part_1[...] = part[block:].astype(low)


def attend_kernel(projected_ref, bias_ref, output_ref, attended_ref, part_0, part_1):
    block = part_0.shape[0]
    part = attend(
        projected_ref, bias_ref, output_ref, attended_ref, 0, 2 * block, output_ref.shape[0]
    )
    part_0[...] = part[:block].astype(low)
    part_1[...] = part[block:].astype(low)


def middle_kernel(
    part_0, part_1, part_2, spatial_ref, chosen_ref, branch_ref, middle_ref, normed_ref
):
    width = spatial_ref.shape[1]
    branch = part_0[...].astype(full) + part_1[...].astype(full) + part_2[...].astype(full)
    branch_ref[...] = branch
    middle = spatial_ref[...].astype(full) + chosen_ref[0:1, 2 * width : 3 * width] * branch
    middle_ref[...] = middle
    unit, inverse = normalize(middle)
    shift = chosen_ref[0:1, 3 * width : 4 * width]
    gain = chosen_ref[0:1, 4 * width : 5 * width]
    normed_ref[...] = (unit * (1.0 + gain) + shift).astype(low)


def feed_kernel(
    piece_0,
    piece_1,
    back_ref,
    expand_ref,
    normed_ref,
    activated_ref,
    hidden_grad_ref,
    part_0,
    part_1,
):
    block = piece_0.shape[0]
    normed = jnp.concatenate([piece_0[...].astype(full), piece_1[...].astype(full)], axis=0)
    normed = normed.astype(low)
    normed_ref[...] = normed
    hidden = dot(normed, expand_ref[...])
    activated, slope = gelu_both(hidden)
    activated_ref[...] = activated.astype(low)
    hidden_grad = (back_ref[...] * slope).astype(low)
    hidden_grad_ref[...] = hidden_grad
    part = dot(hidden_grad, expand_ref[...], ((1,), (1,)))
    part_0[...] = part[:block].astype(low)
    part_1[...] = part[block:].astype(low)


def middle_back_kernel(
    part_0,
    part_1,
    part_2,
    middle_ref,
    branch_ref,
    upstream_ref,
    chosen_ref,
    middle_grad_ref,
    branch_grad_ref,
    sums_ref,
):
    width = middle_ref.shape[1]
    normed_grad = part_0[...].astype(full) + part_1[...].astype(full) + part_2[...].astype(full)
    unit, inverse = normalize(middle_ref[...])
    gain = chosen_ref[0:1, 4 * width : 5 * width]
    middle_grad = upstream_ref[...] + normalize_back(unit, inverse, normed_grad * (1.0 + gain))
    middle_grad_ref[...] = middle_grad
    branch_grad_ref[...] = (chosen_ref[0:1, 2 * width : 3 * width] * middle_grad).astype(low)
    sums_ref[0:1, :] = jnp.sum(middle_grad * branch_ref[...], axis=0, keepdims=True)
    sums_ref[1:2, :] = jnp.sum(normed_grad, axis=0, keepdims=True)
    sums_ref[2:3, :] = jnp.sum(normed_grad * unit, axis=0, keepdims=True)


def probs_kernel(projected_ref, bias_ref, probs_ref):
    width_part = projected_ref.shape[1] // 3
    for head in range(width_part // HEAD):
        at = head * HEAD
        queries = projected_ref[:, at : at + HEAD]
        keys = projected_ref[:, width_part + at : width_part + at + HEAD]
        scores = dot(keys, queries, ((1,), (1,))) * scale + bias_ref[...]
        spread = jnp.exp(scores - jnp.max(scores, axis=0, keepdims=True))
        probs = spread * (1.0 / jnp.sum(spread, axis=0, keepdims=True))
        probs_ref[head] = probs.astype(low)


def attend_back_kernel(
    projected_ref,
    probs_ref,
    output_ref,
    entry_ref,
    piece_0,
    piece_1,
    piece_2,
    piece_3,
    branch_grad_ref,
    grad_ref,
    part_0,
    part_1,
):
    rows, width_all = projected_ref.shape
    width_part = width_all // 3
    block = piece_0.shape[0]
    half = 2 * block
    for chunk, pair in enumerate(((piece_0, piece_1), (piece_2, piece_3))):
        branch_grad_ref[chunk * half : (chunk + 1) * half, :] = jnp.concatenate(
            [piece[...].astype(full) for piece in pair], axis=0
        ).astype(low)
    attended_grad = dot(branch_grad_ref[...], output_ref[...], ((1,), (1,))).astype(low)
    pieces = [[], [], []]
    for head in range(width_part // HEAD):
        at = head * HEAD
        queries = projected_ref[:, at : at + HEAD]
        keys = projected_ref[:, width_part + at : width_part + at + HEAD]
        values = projected_ref[:, 2 * width_part + at : 2 * width_part + at + HEAD]
        grad = attended_grad[:, at : at + HEAD]
        probs = probs_ref[head]
        pieces[2].append(dot(probs, grad))
        probs = probs.astype(full)
        prob_grad = dot(values, grad, ((1,), (1,)))
        delta = jnp.sum(probs * prob_grad, axis=0, keepdims=True)
        score_grad = (probs * (prob_grad - delta)).astype(low)
        pieces[1].append(dot(score_grad, queries) * scale)
        pieces[0].append(dot(score_grad, keys, ((0,), (0,))) * scale)
    grad_ref[...] = jnp.concatenate(pieces[0] + pieces[1] + pieces[2], axis=1).astype(low)
    part = dot(grad_ref[half:, :], entry_ref[...])
    part_0[...] = part[:block].astype(low)
    part_1[...] = part[block:].astype(low)


def entry_back_kernel(grad_ref, entry_ref, part_0, part_1):
    block = part_0.shape[0]
    part = dot(grad_ref[: 2 * block, :], entry_ref[...])
    part_0[...] = part[:block].astype(low)
    part_1[...] = part[block:].astype(low)


def pack_kernel(owners, chosen, me_ref, kept_ref, owner_ref, position_ref, riders_ref, *out_refs):
    slot_ref = out_refs[-1]
    extra, capacity = riders_ref.shape
    kept_count = kept_ref.shape[1]
    owner_local = owner_ref[...] ^ me_ref[0]
    owner_id = lax.broadcasted_iota(jnp.int32, (owners, kept_count), 0)
    hot = (owner_id == owner_local).astype(full)
    row_id = lax.broadcasted_iota(jnp.int32, (kept_count, kept_count), 0)
    column_id = lax.broadcasted_iota(jnp.int32, (kept_count, kept_count), 1)
    before = dot(hot.astype(low), (row_id < column_id).astype(full).astype(low))
    rank = jnp.sum(hot * before, axis=0, keepdims=True).astype(jnp.int32)
    slot = owner_local * capacity + rank
    slot_ref[...] = slot
    coded = position_ref[...] + 1
    tag_id = lax.broadcasted_iota(jnp.int32, (extra, kept_count), 0)
    tags = jnp.where(tag_id == 0, coded >> 5, jnp.where(tag_id == 1, coded & 31, 0))
    rows = jnp.concatenate([kept_ref[...], tags.astype(full).astype(low)], axis=0)
    slot_id = lax.broadcasted_iota(jnp.int32, (capacity, kept_count), 0)
    for number, index in enumerate(chosen):
        matrix = (slot_id + index * capacity == slot).astype(full).astype(low)
        slab = dot(rows, matrix, ((1,), (1,)))
        split = kept_ref.shape[0]
        slab = jnp.concatenate([slab[:split], slab[split:] + riders_ref[...].astype(full)], axis=0)
        if len(out_refs) == 2:
            out_refs[0][me_ref[0] ^ index] = slab.astype(low)
        else:
            out_refs[number][...] = slab.astype(low)


def unpack_kernel(owners, me_ref, *refs):
    slab_refs, outs = refs[:-5], refs[-5:]
    compact_ref, slot_rank_ref, token_rank_ref, lifted_ref, arrived = outs
    width_part, arrived_count = compact_ref.shape
    slots_all = arrived.shape[1]
    own_tokens = token_rank_ref.shape[1]
    capacity = slots_all // owners
    for index in range(owners):
        if len(slab_refs) == 1:
            slab = slab_refs[0][me_ref[0] ^ index]
        else:
            slab = slab_refs[(FAR + NEAR).index(index)][...]
        arrived[:, index * capacity : (index + 1) * capacity] = slab
    tags = arrived[width_part : width_part + 16, :].astype(full)
    place = tags[0:1] * 32.0 + tags[1:2] - 1.0
    turned = jnp.transpose(jnp.broadcast_to(place, (8, slots_all)))[:, 0:1]
    turned = jnp.where(turned < 0.0, 1e9, turned)
    slot_rank = jnp.sum(jnp.where(turned < place, 1.0, 0.0), axis=0, keepdims=True)
    slot_rank = jnp.where(place < 0.0, -1.0, slot_rank).astype(jnp.int32)
    slot_rank_ref[...] = slot_rank
    rank_id = lax.broadcasted_iota(jnp.int32, (arrived_count, slots_all), 0)
    matrix = (rank_id == slot_rank).astype(full).astype(low)
    compact_ref[...] = dot(arrived[:width_part, :], matrix, ((1,), (1,))).astype(low)
    spot = lax.broadcasted_iota(jnp.int32, (1, own_tokens), 1).astype(full)
    token_rank = jnp.sum(jnp.where(turned < spot, 1.0, 0.0), axis=0, keepdims=True)
    filled = jnp.sum(jnp.where(turned == spot, 1.0, 0.0), axis=0, keepdims=True)
    token_rank_ref[...] = jnp.where(filled > 0.0, token_rank, -1.0).astype(jnp.int32)
    if len(slab_refs) > 1:
        chunks = lifted_ref.shape[1] // capacity
        for index in range(owners):
            for row in range(QUARTERS):
                for chunk in range(chunks):
                    lifted_ref[
                        index * QUARTERS + row : index * QUARTERS + row + 1,
                        chunk * capacity : (chunk + 1) * capacity,
                    ] = tags[
                        2 + row * chunks + chunk : 3 + row * chunks + chunk,
                        index * capacity : (index + 1) * capacity,
                    ]
    else:
        lifted_ref[...] = jnp.zeros_like(lifted_ref)


def choose_kernel(lane_ref, big_ref, table_0, table_1, chosen_ref, table):
    table[:QUARTERS, :] = table_0[...] + table_1[...]
    for index in range(QUARTERS):
        row = jnp.where(big_ref[0] == 1, 0, lane_ref[0] ^ index)
        chosen_ref[index : index + 1, :] = table[pl.ds(row, 1), :]


def back_kernel(
    lane_ref,
    part_0,
    part_1,
    part_2,
    spatial_ref,
    middle_grad_ref,
    chosen_ref,
    sums_ref,
    feed_0,
    feed_1,
    feed_2,
    upstream_ref,
    piece_0,
    piece_1,
    piece_2,
    piece_3,
    turned,
    riders,
):
    lane = lane_ref[0]
    block, width = spatial_ref.shape
    group = block - SPARE
    width_part = width // QUARTERS
    normed_grad = part_0[...].astype(full) + part_1[...].astype(full) + part_2[...].astype(full)
    unit, inverse = normalize(spatial_ref[...].astype(full))
    gain = chosen_ref[0:1, width : 2 * width]
    grad = middle_grad_ref[...] + normalize_back(unit, inverse, normed_grad * (1.0 + gain))
    turned[...] = jnp.transpose(grad[:group]).astype(low)
    feed = feed_0[...].astype(full) + feed_1[...].astype(full) + feed_2[...].astype(full)
    mask_sum = grad[group : group + 1]
    mask_high = mask_sum.astype(low).astype(full)
    fields = [
        jnp.sum(normed_grad, axis=0, keepdims=True),
        jnp.sum(normed_grad * unit, axis=0, keepdims=True),
        sums_ref[0:1, :],
        sums_ref[1:2, :],
        sums_ref[2:3, :],
        jnp.sum(feed * upstream_ref[...], axis=0, keepdims=True),
        mask_high,
        mask_sum - mask_high,
    ]
    chunks = width // 128
    riders[...] = jnp.zeros_like(riders)
    for number, field in enumerate(fields):
        for chunk in range(chunks):
            at = number * chunks + chunk
            riders[at : at + 1, :] = field[:, chunk * 128 : (chunk + 1) * 128]
    rider_rows = riders[...].astype(low)
    for index, piece in enumerate((piece_0, piece_1, piece_2, piece_3)):
        at = pl.multiple_of((lane ^ index) * width_part, 16)
        piece[:width_part, :] = turned[pl.ds(at, width_part), :]
        piece[width_part:, :] = rider_rows


def slots_kernel(
    owners, lane_ref, me_ref, big_ref, rank_ref, piece_0, piece_1, piece_2, piece_3, *refs
):
    slab_refs, (table_ref, table, mask_total) = refs[:-3], refs[-3:]
    lane = lane_ref[0]
    me = me_ref[0]
    group = piece_0.shape[1]
    slots_all = rank_ref.shape[1]
    capacity = slots_all // owners
    chunks = table_ref.shape[1]
    width_part = slab_refs[0].shape[0] - RIDERS
    pieces = [piece_0, piece_1, piece_2, piece_3]
    rows = jnp.concatenate([piece[:width_part, :] for piece in pieces], axis=1)
    row_id = lax.broadcasted_iota(jnp.int32, (group, slots_all), 0)
    matrix = jnp.concatenate(
        [
            (row_id + (lane ^ index) * group == rank_ref[...]).astype(full).astype(low)
            for index in range(QUARTERS)
        ],
        axis=0,
    )
    slots = dot(rows, matrix)
    table[...] = jnp.zeros_like(table)
    summed = jnp.zeros((chunks, 128), full)
    mask_sum = jnp.zeros((16, 128), full)
    mask_rows = chunks // 6
    for index, piece in enumerate(pieces):
        field = piece[width_part : width_part + chunks, :].astype(full)
        summed = summed + field
        rest = piece[width_part + chunks - chunks % 16 :, :].astype(full)
        table[lane ^ index, :chunks, :] = field
        at = chunks % 16
        mask_sum = mask_sum + jnp.concatenate(
            [
                rest[at : at + mask_rows] + rest[at + mask_rows : at + 2 * mask_rows],
                jnp.zeros((16 - mask_rows, 128), full),
            ],
            axis=0,
        )
    mask_total[...] = mask_sum

    @pl.when(big_ref[0] == 1)
    def _():
        table[...] = jnp.zeros_like(table)
        table[0, :chunks, :] = summed

    table_ref[...] = table[:, :chunks, :].astype(low)
    for number, index in enumerate(FAR + NEAR):
        owner = me ^ index
        start = (owner * chunks) // owners
        fields = [table[row, pl.ds(start, 8), :] for row in range(QUARTERS)]
        mask_start = (owner * mask_rows) // owners
        mask_part = mask_total[pl.ds(mask_start, 2), :]
        mask_high = mask_part.astype(low).astype(full)
        fields += [mask_high, mask_part - mask_high, jnp.zeros((RIDERS - 36, 128), full)]
        slab = jnp.concatenate([slots[:, index * capacity : (index + 1) * capacity]] + fields, axis=0)
        slab_refs[number][...] = slab.astype(low)


def kept_kernel(owners, me_ref, slot_ref, lifted_ref, *refs):
    slab_refs = refs[:owners]
    kept_ref, modulate_ref, mask_ref, table = refs[owners:]
    width_part, kept_count = kept_ref.shape
    capacity = slab_refs[0].shape[1]
    table_part = modulate_ref.shape[1]
    mask_part = mask_ref.shape[1]
    me = me_ref[0]
    slab_refs = [slab_refs[(FAR + NEAR).index(index)] for index in range(owners)]
    rows = jnp.concatenate([slab[:width_part, :] for slab in slab_refs], axis=1)
    slot_id = lax.broadcasted_iota(jnp.int32, (owners * capacity, kept_count), 0)
    matrix = (slot_id == slot_ref[...]).astype(full).astype(low)
    kept_ref[...] = dot(rows, matrix).astype(low)
    mask_sum = jnp.zeros((1, 256), full)
    for index, slab in enumerate(slab_refs):
        rider = slab[width_part:, :].astype(full)
        for row in range(QUARTERS):
            at = index * QUARTERS + row
            for chunk in range(8):
                from_row = row * 8 + chunk
                table[at : at + 1, chunk * 128 : (chunk + 1) * 128] = rider[
                    from_row : from_row + 1
                ]
        high, rest = rider[32:34], rider[34:36]
        both = high + rest
        mask_sum = mask_sum + jnp.concatenate([both[0:1], both[1:2]], axis=1)
    shift = (me * table_part) % 128
    field = pltpu.roll(table[...], (1024 - shift) % 1024, 1)[:, :table_part]
    lifted = lifted_ref[...].astype(low)[:, :width_part]
    modulate_ref[...] = dot(lifted, field.astype(low), ((0,), (0,)))
    shift = (me * mask_part) % 128
    mask_sum = jnp.broadcast_to(mask_sum, (8, 256))
    mask_ref[...] = pltpu.roll(mask_sum, (256 - shift) % 256, 1)[0:1, :mask_part]


def out_kernel(
    lane_ref,
    part_0,
    part_1,
    part_2,
    middle_ref,
    chosen_ref,
    piece_0,
    piece_1,
    piece_2,
    piece_3,
    turned,
    riders,
):
    lane = lane_ref[0]
    block, width = middle_ref.shape
    group = block - SPARE
    width_part = width // QUARTERS
    feed = part_0[...].astype(full) + part_1[...].astype(full) + part_2[...].astype(full)
    out = middle_ref[...] + chosen_ref[0:1, 5 * width : 6 * width] * feed
    turned[...] = jnp.transpose(out[:group]).astype(low)
    riders[...] = jnp.zeros_like(riders)
    for chunk in range(width // 128):
        riders[chunk : chunk + 1, :] = out[group : group + 1, chunk * 128 : (chunk + 1) * 128]
    rider_rows = riders[...].astype(low)
    for index, piece in enumerate((piece_0, piece_1, piece_2, piece_3)):
        at = pl.multiple_of((lane ^ index) * width_part, 16)
        piece[:width_part, :] = turned[pl.ds(at, width_part), :]
        piece[width_part:, :] = rider_rows


def layer_kernel(
    lane_ref, rank_ref, piece_0, piece_1, piece_2, piece_3, out_ref, spare, turned
):
    lane = lane_ref[0]
    width_part, own_tokens = out_ref.shape
    group = piece_0.shape[1]
    quarter = own_tokens // QUARTERS
    pieces = (piece_0, piece_1, piece_2, piece_3)
    rows = jnp.concatenate([piece[:width_part, :] for piece in pieces], axis=1)
    row_id = lax.broadcasted_iota(jnp.int32, (group, own_tokens), 0)
    matrix = jnp.concatenate(
        [
            (row_id + (lane ^ index) * group == rank_ref[...]).astype(full).astype(low)
            for index in range(QUARTERS)
        ],
        axis=0,
    )
    spare[...] = jnp.zeros_like(spare)
    for index, piece in enumerate(pieces):
        rider = piece[width_part:, :].astype(full)
        for chunk in range(spare.shape[1] // 128):
            spare[index : index + 1, chunk * 128 : (chunk + 1) * 128] = rider[chunk : chunk + 1]
    turned[...] = jnp.transpose(spare[...])
    columns = turned[pl.ds(pl.multiple_of(lane * width_part, 16), width_part), :].astype(low)
    spare_id = lax.broadcasted_iota(jnp.int32, (8, own_tokens), 0)
    spot = lax.broadcasted_iota(jnp.int32, (8, own_tokens), 1) // quarter
    empty = rank_ref[...] < 0
    spots = jnp.where(((spare_id ^ lane) == spot) & (spare_id < QUARTERS) & empty, 1.0, 0.0)
    out_ref[...] = (dot(rows, matrix) + dot(columns, spots.astype(low))).astype(low)


def table_kernel(big_ref, lifted_ref, modulate_ref, table_ref, bias_ref, turned_ref):
    table_ref[...] = dot(lifted_ref[...], modulate_ref[...])
    rows = bias_ref.shape[0]
    block = rows // QUARTERS
    group = block - SPARE
    big = big_ref[0] == 1
    spare_small = jnp.log(jnp.full((1, 1), float(group), full))
    spare_big = jnp.log(jnp.full((1, 1), float(QUARTERS * group), full))

    def bias_of(query, key):
        query_block, key_block, key_inner = query // block, key // block, key % block
        small = jnp.where(key_inner < group, 0.0, jnp.where(key_inner == group, spare_small, -1e30))
        small = jnp.where(query_block == key_block, small, -1e30)
        large = jnp.where(key_inner < group, 0.0, jnp.where(key == group, spare_big, -1e30))
        return jnp.where(big, large, small)

    row_id = lax.broadcasted_iota(jnp.int32, (rows, rows), 0)
    column_id = lax.broadcasted_iota(jnp.int32, (rows, rows), 1)
    bias_ref[...] = bias_of(row_id, column_id)
    turned_ref[...] = bias_of(column_id, row_id)


def add_kernel(left_ref, right_ref, out_ref):
    out_ref[...] = (left_ref[...].astype(full) + right_ref[...].astype(full)).astype(low)


def copy_kernel(*refs):
    for index in range(len(refs) // 2):
        refs[len(refs) // 2 + index][...] = refs[index][...]


def upstream_kernel(
    lane_ref,
    rank_ref,
    chosen_ref,
    cotangent_ref,
    shrink_ref,
    feed_grad_ref,
    upstream_ref,
    back_near,
    back_far,
):
    lane = lane_ref[0]
    block, width = upstream_ref.shape
    own_tokens = rank_ref.shape[1]
    group = block - SPARE
    half = 2 * block
    rank = rank_ref[...]
    row_id = lax.broadcasted_iota(jnp.int32, (group, own_tokens), 0)
    spare_id = lax.broadcasted_iota(jnp.int32, (SPARE, own_tokens), 0)
    spot = lax.broadcasted_iota(jnp.int32, (SPARE, own_tokens), 1) // (own_tokens // QUARTERS)
    for chunk, back in ((0, back_near), (1, back_far)):
        matrix = []
        for index in (2 * chunk, 2 * chunk + 1):
            matrix.append(jnp.where(row_id + (lane ^ index) * group == rank, 1.0, 0.0))
            matrix.append(
                jnp.where((spare_id == 0) & (spot == (lane ^ index)) & (rank < 0), 1.0, 0.0)
            )
        upstream = dot(jnp.concatenate(matrix, axis=0).astype(low), cotangent_ref[...])
        if chunk == 0:
            upstream_ref[...] = upstream[:block]
        gates = [chosen_ref[index : index + 1, 5 * width :] for index in (2 * chunk, 2 * chunk + 1)]
        feed_grad = jnp.concatenate(
            [gates[0] * upstream[:block], gates[1] * upstream[block:]], axis=0
        ).astype(low)
        feed_grad_ref[chunk * half : (chunk + 1) * half, :] = feed_grad
        back[...] = dot(feed_grad, shrink_ref[...], ((1,), (1,)))


def feed_out_kernel(near_ref, far_ref, shrink_ref, part_0, part_1, part_2, part_3):
    block = part_0.shape[0]
    for activated, pair in ((far_ref, (part_2, part_3)), (near_ref, (part_0, part_1))):
        part = dot(activated[...], shrink_ref[...])
        pair[0][...] = part[:block].astype(low)
        pair[1][...] = part[block:].astype(low)


def weight_kernel(counts, me_ref, *refs):
    given_0, given_1, kept_0, kept_1, product = refs[-5:]
    operands = list(refs[:-5])
    rows = given_0.shape[1] + given_1.shape[1]
    chunk = product.shape[0] // 3
    for group, pairs in enumerate(counts):
        products = []
        for lefts, rights in pairs:
            lhs = [operands.pop(0) for _ in range(lefts)]
            right = jnp.concatenate([operands.pop(0)[...] for _ in range(rights)], axis=0)
            products.append((lhs, right))
        for number in range(3):
            span = slice(number * chunk, (number + 1) * chunk)
            parts = [
                dot(jnp.concatenate([ref[:, span] for ref in lhs], axis=0), right, ((0,), (0,)))
                for lhs, right in products
            ]
            product[span, :] = jnp.concatenate(parts, axis=1)
        for bit, start, given, kept in (
            (0, 0, given_0, kept_0),
            (1, given_0.shape[1], given_1, kept_1),
        ):
            mine = (me_ref[0] >> bit) & 1
            for index in range(4):
                for value, ref in ((1 - mine, given), (mine, kept)):
                    above = (index >> bit) << (bit + 1)
                    at = (above + (value << bit) + (index & bit)) * rows + start
                    at = pl.multiple_of(at, 8)
                    ref[4 * group + index] = product[pl.ds(at, ref.shape[1]), :].astype(low)


def halve_kernel(
    me_ref, held_0, held_1, got_0, got_1, given_0, given_1, kept_0, kept_1
):
    for bit, held, got, given, kept in (
        (1, held_0, got_0, given_0, kept_0),
        (0, held_1, got_1, given_1, kept_1),
    ):
        mine = (me_ref[0] >> bit) & 1
        for index in range(given.shape[0]):
            for value, ref in ((1 - mine, given), (mine, kept)):
                at = 2 * index + value
                ref[index] = (held[at].astype(full) + got[at].astype(full)).astype(low)


def join_kernel(me_ref, held_0, held_1, got_0, got_1, given, kept):
    mine = (me_ref[0] >> 2) & 1
    for index in range(given.shape[0]):
        for value, ref in ((1 - mine, given), (mine, kept)):
            at = 2 * index + value
            upper = held_0[at].astype(full) + got_0[at].astype(full)
            lower = held_1[at].astype(full) + got_1[at].astype(full)
            ref[index] = jnp.concatenate([upper, lower], axis=0).astype(low)


def total_kernel(held_ref, got_ref, *out_refs):
    if len(out_refs[0].shape) == 2:
        for index, out_ref in enumerate(out_refs):
            out_ref[...] = held_ref[index].astype(full) + got_ref[index].astype(full)
        return
    entry_ref, output_ref = out_refs
    total = held_ref[0].astype(full) + got_ref[0].astype(full)
    parts, _, columns = entry_ref.shape
    for index in range(parts):
        entry_ref[index] = total[:, index * columns : (index + 1) * columns]
    output_ref[...] = total[:, parts * columns :]


def call(
    kernel, outs, *operands, words=0, deps=(), time=1.0, scratch=(), token=False, loose=False
):
    count = len(operands)
    deps = tuple(deps)
    outs = tuple(outs)
    if token:
        outs += (((8, 128), full),)

    def run(*refs):
        outs_at = count + len(deps)
        rest = list(refs[outs_at:])
        if token:
            last = rest.pop(len(outs) - 1)
            last[...] = jnp.zeros_like(last)
        kernel(*refs[:count], *rest)

    return pl.pallas_call(
        run,
        out_shape=tuple(jax.ShapeDtypeStruct(shape, kind) for shape, kind in outs),
        in_specs=[SMALL] * words
        + [pl.BlockSpec() if loose else PLAIN] * (count - words)
        + [pl.BlockSpec(memory_space=pl.ANY)] * len(deps),
        scratch_shapes=list(scratch),
        compiler_params=pltpu.CompilerParams(vmem_limit_bytes=VMEM_ASK),
        cost_estimate=pl.CostEstimate(
            flops=int(time * 1.15e9), bytes_accessed=1024, transcendentals=0
        ),
    )(*operands, *deps)


def turn(token):
    return swap(token, "tensor", 1)


def body(
    kept_rows,
    owner_index,
    kept_position,
    resolution,
    mask_token,
    condition,
    modulate_weight,
    entry_weight,
    output_weight,
    expand_weight,
    shrink_weight,
    cotangent,
):
    owners = lax.axis_size("dp")
    me = lax.axis_index("dp")
    lane = lax.axis_index("tensor")
    kept_count, width_part = kept_rows.shape
    width = mask_token.shape[0]
    own_tokens = cotangent.shape[0]
    ff_part = expand_weight.shape[1]
    quarter = own_tokens // QUARTERS
    group = quarter // 2
    arrived_count = own_tokens // 2
    block = group + SPARE
    rows = QUARTERS * block
    capacity = 2 * kept_count // owners
    slots_all = owners * capacity
    direct = owners == SWAP_OWNERS
    lane_word = lane.reshape(1).astype(jnp.int32)
    me_word = me.reshape(1).astype(jnp.int32)
    big_word = resolution[:1]
    context_part = lax.dynamic_slice_in_dim(
        condition.astype(full), lane * width_part, width_part, 1
    )
    lifted = jax.nn.silu(context_part).astype(low)
    if direct:
        padded = -(-width_part // capacity) * capacity
        riders = jnp.pad(lifted, ((0, 0), (0, padded - width_part))).reshape(-1, capacity)
    else:
        padded = 128
        riders = lifted.reshape(-1, capacity)
    rider_count = riders.shape[0]
    extra = -(-(rider_count + 2) // 16) * 16
    riders = jnp.pad(riders, ((2, extra - 2 - rider_count), (0, 0)))
    slab_rows = width_part + extra
    def pack(chosen, count, deps):
        shape = (slab_rows, capacity)
        if not direct:
            shape, count = (owners,) + shape, 1
        *slabs, slot_index = call(
            partial(pack_kernel, owners, chosen),
            ((shape, low),) * count + (((1, kept_count), jnp.int32),),
            me_word,
            kept_rows.T,
            owner_index[None, :],
            kept_position[None, :],
            riders,
            words=1,
            deps=deps,
            time=1.0,
        )
        return slabs, slot_index

    far_slabs, slot_index = pack(FAR if direct else range(owners), len(FAR), ())

    table, bias, bias_turned = call(
        table_kernel,
        (
            ((QUARTERS, 6 * width), full),
            ((rows, rows), full),
            ((rows, rows), full),
        ),
        big_word,
        lifted,
        modulate_weight,
        words=1,
        deps=[slot_index],
        time=2.0,
    )
    table = table + swap(table, "tensor", 1)
    table_across = swap(table, "tensor", 2)
    (chosen,) = call(
        choose_kernel,
        (((QUARTERS, 6 * width), full),),
        lane_word,
        big_word,
        table,
        table_across,
        words=2,
        time=0.6,
        scratch=[pltpu.VMEM((8, 6 * width), full)],
    )
    if direct:
        near_slabs = pack(NEAR, len(NEAR), [chosen])[0]
        slabs = exchange_owners(dict(zip(FAR + NEAR, far_slabs + near_slabs)))
        slabs = list(slabs.values())
    else:
        slabs = exchange_owners(far_slabs)
    compact, slot_rank, token_rank, lifted_all = call(
        partial(unpack_kernel, owners),
        (
            ((width_part, arrived_count), low),
            ((1, slots_all), jnp.int32),
            ((1, own_tokens), jnp.int32),
            ((owners * QUARTERS, padded), full),
        ),
        me_word,
        *slabs,
        words=1,
        time=2.4,
        scratch=[pltpu.VMEM((slab_rows, slots_all), low)],
    )
    if not direct:
        owner_order = jnp.arange(owners, dtype=jnp.int32) ^ me
        lifted_all = slabs[0][:, width_part + 2 : width_part + 2 + rider_count]
        lifted_all = lifted_all.reshape(owners * QUARTERS, width_part)
    spatial_pieces = gather_blocks(compact)
    entry_flat = jnp.transpose(entry_weight, (1, 2, 0)).reshape(3 * width_part, width)
    token_shape = ((block, width), low)
    half = 2 * block
    spatial_own, normed_one, projected, attended_far, part_2, part_3 = call(
        entry_kernel,
        (
            token_shape,
            ((rows, width), low),
            ((rows, 3 * width_part), low),
            ((half, width_part), low),
            token_shape,
            token_shape,
        ),
        lane_word,
        *spatial_pieces,
        mask_token[None, :],
        chosen,
        entry_flat,
        bias,
        output_weight,
        words=1,
        time=5.0,
        scratch=[pltpu.VMEM((width, arrived_count), low)],
    )
    far, across, start = sum_far(part_2, part_3)
    attended_near, part_0, part_1 = call(
        attend_kernel,
        (((half, width_part), low), token_shape, token_shape),
        projected,
        bias,
        output_weight,
        deps=[start],
        time=3.0,
    )
    got = swap(part_1, "tensor", 1)
    feed_grad, upstream_own, back_near, back_far = call(
        upstream_kernel,
        (
            ((rows, width), low),
            ((block, width), full),
            ((half, width), full),
            ((half, width), full),
        ),
        lane_word,
        token_rank,
        chosen,
        cotangent,
        shrink_weight,
        words=1,
        deps=[part_1],
        time=3.6,
    )
    branch, middle, normed_two_own = call(
        middle_kernel,
        (((block, width), full), ((block, width), full), token_shape),
        part_0,
        got,
        across,
        spatial_own,
        chosen,
        deps=[back_far],
        time=0.6,
    )

    def feed_call(piece_0, piece_1, back, *deps):
        return call(
            feed_kernel,
            (((half, width), low), ((half, width), low), ((half, width), low))
            + (token_shape, token_shape),
            piece_0,
            piece_1,
            back,
            expand_weight,
            deps=deps,
            time=2.4,
        )

    near_piece = swap(normed_two_own, "tensor", 1)
    across = swap(normed_two_own, "tensor", 2)
    normed_near, activated_near, hidden_near, part_0, part_1 = feed_call(
        normed_two_own, near_piece, back_near
    )
    (across,) = call(copy_kernel, (token_shape,), across, deps=[part_0], time=0.3)
    last_piece = swap(across, "tensor", 1)
    normed_far, activated_far, hidden_far, part_2, part_3 = feed_call(
        across, last_piece, back_far
    )
    far, across, start = sum_far(part_2, part_3)
    got = swap(part_1, "tensor", 1)
    feed_groups = [
        [([feed_grad], [activated_near, activated_far])],
        [([normed_near, normed_far], [hidden_near, hidden_far])],
    ]
    event = start
    if direct:
        feed_given, feed_kept, event = start_sums(feed_groups, [start], 5.8)
        feed_got = cross(feed_given, 1, 2)
    middle_grad, branch_grad_own, sums, start = call(
        middle_back_kernel,
        (((block, width), full), token_shape, ((SPARE, width), full)),
        part_0,
        got,
        across,
        middle,
        branch,
        upstream_own,
        chosen,
        deps=[event],
        time=0.7,
        token=True,
    )
    branch_pieces = gather_blocks(branch_grad_own)
    feed_parts = call(
        feed_out_kernel,
        (token_shape,) * QUARTERS,
        activated_near,
        activated_far,
        shrink_weight,
        deps=[turn(start)],
        time=2.0,
    )
    (probs,) = call(
        probs_kernel,
        (((width_part // HEAD, rows, rows), low),),
        projected,
        bias_turned,
        deps=[feed_parts[0]],
        time=2.5,
    )
    feed_far = swap(feed_parts[3], "tensor", 1)
    feed_near = swap(feed_parts[1], "tensor", 1)
    feed_far, start = call(
        add_kernel,
        (token_shape,),
        feed_parts[2],
        feed_far,
        deps=[branch_pieces[2], probs],
        time=0.4,
        token=True,
    )
    branch_grad, projected_grad, part_2, part_3 = call(
        attend_back_kernel,
        (((rows, width), low), ((rows, 3 * width_part), low), token_shape, token_shape),
        projected,
        probs,
        output_weight,
        entry_flat,
        *branch_pieces,
        deps=[turn(start)],
        time=4.0,
    )
    feed_across = swap(feed_far, "tensor", 2)
    far, across, start = sum_far(part_2, part_3)
    part_0, part_1 = call(
        entry_back_kernel,
        (token_shape, token_shape),
        projected_grad,
        entry_flat,
        deps=[start, feed_across],
        time=1.0,
    )
    got = swap(part_1, "tensor", 1)
    entry_groups = [
        [([normed_one], [projected_grad]), ([branch_grad], [attended_near, attended_far])]
    ]
    event = part_1
    if direct:
        entry_given, entry_kept, entry_token = start_sums(entry_groups, [part_1], 2.5)
        feed_given, feed_kept, event = halve_sums(feed_kept, feed_got, [entry_token])
        feed_got = cross(feed_given, 2, 1)
        event = turn(event)
    back_pieces = call(
        back_kernel,
        (((width_part + 80, group), low),) * QUARTERS,
        lane_word,
        part_0,
        got,
        across,
        spatial_own,
        middle_grad,
        chosen,
        sums,
        feed_parts[0],
        feed_near,
        feed_across,
        upstream_own,
        words=1,
        deps=[event],
        time=1.0,
        scratch=[pltpu.VMEM((width, group), low), pltpu.VMEM((80, 128), full)],
    )
    back_pieces = [back_pieces[0]] + [
        swap(back_pieces[index], "tensor", index) for index in range(1, QUARTERS)
    ]
    chunks = 6 * width // 128
    logistic = jax.nn.sigmoid(context_part)
    logistic = logistic * (1.0 + context_part * (1.0 - logistic))
    if direct:
        *slabs, table_grad = call(
            partial(slots_kernel, owners),
            (((width_part + RIDERS, capacity), low),) * owners
            + (((QUARTERS, chunks, 128), low),),
            lane_word,
            me_word,
            big_word,
            slot_rank,
            *back_pieces,
            words=3,
            time=0.8,
            scratch=[
                pltpu.VMEM((QUARTERS, chunks + 2, 128), full),
                pltpu.VMEM((16, 128), full),
            ],
        )
        event = slabs[0]
        slabs = list(exchange_owners(dict(zip(FAR + NEAR, slabs))).values())
        feed_got, feed_kept, start = join_sums(feed_kept, feed_got, [event])
        table_grad = table_grad.reshape(QUARTERS, 6 * width)
        kept_grad, modulate_grad, mask_grad = call(
            partial(kept_kernel, owners),
            (
                ((width_part, kept_count), low),
                ((width_part, 6 * width // owners), full),
                ((1, width // owners), full),
            ),
            me_word,
            slot_index,
            lifted_all,
            *slabs,
            words=1,
            deps=[start],
            time=1.6,
            scratch=[pltpu.VMEM((owners * QUARTERS, 1024), full)],
        )
        mask_grad = mask_grad[0]
    else:
        event = back_pieces[1]
        rows_back = jnp.concatenate([piece[:width_part] for piece in back_pieces], axis=1)
        rank_ids = jnp.arange(arrived_count, dtype=jnp.int32)
        rank_ids = ((rank_ids // group) ^ lane) * group + rank_ids % group
        matrix = (rank_ids[:, None] == slot_rank).astype(low)
        slabs = dot(rows_back, matrix).astype(low).reshape(width_part, owners, capacity)
        slabs = jnp.take(jnp.transpose(slabs, (1, 0, 2)), owner_order, axis=0)
        slabs = jnp.take(exchange_owners([slabs])[0], owner_order, axis=0)
        slabs = jnp.transpose(slabs, (1, 0, 2)).reshape(width_part, slots_all)
        slot_ids = jnp.arange(slots_all, dtype=jnp.int32)[:, None]
        kept_grad = dot(slabs, (slot_ids == slot_index).astype(low)).astype(low)
        riders = jnp.stack(
            [piece[width_part : width_part + 8 * width // 128] for piece in back_pieces]
        )
        riders = riders.reshape(QUARTERS, 8, width).astype(full)
        mask_total = jnp.sum(riders[:, 6] + riders[:, 7], axis=0)
        table_local = riders[:, :6].reshape(QUARTERS, 6 * width)
        table_small = jnp.take(table_local, jnp.arange(QUARTERS, dtype=jnp.int32) ^ lane, axis=0)
        first = jnp.arange(QUARTERS, dtype=jnp.int32)[:, None] == 0
        table_big = jnp.where(first, jnp.sum(table_local, axis=0, keepdims=True), 0.0)
        table_grad = jnp.where(big_word[0] == 1, table_big, table_small).astype(low)
        sent = jnp.transpose(table_grad.reshape(QUARTERS, owners, -1), (1, 0, 2))
        table_all = exchange_owners([sent])[0].reshape(owners * QUARTERS, -1)
        modulate_grad = dot(lifted_all, table_all, ((0,), (0,)))
        mask_grad = lax.psum_scatter(mask_total, "dp", scatter_dimension=0, tiled=True)
    condition_grad = dot(table_grad, modulate_weight, ((1,), (1,))) * logistic
    out_pieces = call(
        out_kernel,
        (((width_part + 16, group), low),) * QUARTERS,
        lane_word,
        feed_parts[0],
        feed_near,
        feed_across,
        middle,
        chosen,
        words=1,
        deps=[event],
        time=1.0,
        scratch=[pltpu.VMEM((width, group), low), pltpu.VMEM((16, 128), full)],
    )
    out_pieces = [out_pieces[0]] + [
        swap(out_pieces[index], "tensor", index) for index in range(1, QUARTERS)
    ]
    (layer_out,) = call(
        layer_kernel,
        (((width_part, own_tokens), low),),
        lane_word,
        token_rank,
        *out_pieces,
        words=1,
        deps=[kept_grad],
        time=1.6,
        scratch=[pltpu.VMEM((8, width), full), pltpu.VMEM((width, 8), full)],
    )
    if direct:
        entry_given = call(
            copy_kernel,
            [(value.shape, low) for value in entry_given],
            *entry_given,
            deps=[kept_grad],
            time=0.8,
        )
        entry_got = cross(entry_given, 1, 2)
        entry_given, entry_kept, event = halve_sums(entry_kept, entry_got, [layer_out])
        entry_got = cross(entry_given, 2, 1)
    rows_part = width // owners
    if direct:
        shrink_grad, expand_grad = call(
            total_kernel,
            (((rows_part, ff_part), full),) * 2,
            feed_kept,
            feed_got,
            deps=[entry_kept[0]],
            time=0.8,
        )
        entry_got, entry_kept, event = join_sums(entry_kept, entry_got, [shrink_grad])
        entry_grad, output_grad = call(
            total_kernel,
            (((3, rows_part, width_part), full), ((rows_part, width_part), full)),
            entry_kept,
            entry_got,
            time=0.8,
        )
    else:
        totals = [
            sum_owners(
                jnp.concatenate(
                    [
                        dot(jnp.concatenate(lhs), jnp.concatenate(rhs), ((0,), (0,)))
                        for lhs, rhs in pairs
                    ],
                    axis=1,
                )
                .astype(low)
                .reshape(owners, rows_part, -1)
            )
            for pairs in feed_groups + entry_groups
        ]
        shrink_grad, expand_grad, entry_grad = totals
        output_grad = entry_grad[:, 3 * width_part :]
        entry_grad = entry_grad[:, : 3 * width_part].reshape(rows_part, 3, width_part)
        entry_grad = jnp.transpose(entry_grad, (1, 0, 2))

    return (
        layer_out.T,
        kept_grad.T,
        mask_grad,
        condition_grad,
        modulate_grad,
        jnp.transpose(entry_grad, (1, 0, 2)),
        output_grad.T,
        expand_grad,
        shrink_grad.T,
    )


def solution(mesh):
    return jax.shard_map(
        body,
        mesh=mesh,
        in_specs=(
            P("dp", "tensor"),
            P("dp"),
            P("dp"),
            P("dp"),
            P(),
            P("dp", None),
            P("tensor", None),
            P(None, None, "tensor"),
            P("tensor", None),
            P(None, "tensor"),
            P("tensor", None),
            P("dp", None),
        ),
        out_specs=(
            P("dp", "tensor"),
            P("dp", "tensor"),
            P("dp"),
            P("dp", "tensor"),
            P("tensor", "dp"),
            P("dp", None, "tensor"),
            P("tensor", "dp"),
            P("dp", "tensor"),
            P("tensor", "dp"),
        ),
        check_vma=False,
    )
```

```python
from functools import partial

import jax
import jax.numpy as jnp
from jax import lax
from jax.experimental import pallas as pl
from jax.experimental.pallas import tpu as pltpu
from jax.sharding import PartitionSpec as P

HEAD = 72
QUARTERS = 4
SPARE = 8
scale = HEAD ** (-0.5)
epsilon = 1e-06
gelu_coeff = 0.7978845608028654
low = jnp.bfloat16
full = jnp.float32
VMEM_ASK = 12 * 1024 * 1024
RIDERS = 48
SWAP_OWNERS = 8
FEED_SPLIT = 72
ENTRY_SPLIT = 88
FAR = (6, 7, 4, 5)
NEAR = (2, 3, 1, 0)
JOIN_TIME = 14.0
KEPT_TIME = 1.0
BACK_TIME = 8.0
SMALL = pl.BlockSpec(memory_space=pltpu.SMEM)
PLAIN = pl.BlockSpec(memory_space=pltpu.VMEM)


def dot(a, b, dims=((1,), (0,))):
    return lax.dot_general(a, b, (dims, ((), ())), preferred_element_type=full)


def normalize(rows):
    centered = rows - jnp.mean(rows, axis=-1, keepdims=True)
    inverse = lax.rsqrt(jnp.mean(centered * centered, axis=-1, keepdims=True) + epsilon)
    return (centered * inverse, inverse)


def normalize_back(unit, inverse, grad):
    return inverse * (
        grad
        - jnp.mean(grad, axis=-1, keepdims=True)
        - unit * jnp.mean(grad * unit, axis=-1, keepdims=True)
    )


def gelu_both(value):
    square = value * value
    curve = jnp.tanh(gelu_coeff * (value + 0.044715 * square * value))
    slope = 0.5 * (1.0 + curve) + 0.5 * value * (1.0 - curve * curve) * gelu_coeff * (
        1.0 + 3.0 * 0.044715 * square
    )
    return (0.5 * value * (1.0 + curve), slope)


def swap(value, axis, bit):
    size = lax.axis_size(axis)
    return lax.ppermute(value, axis, [(index, index ^ bit) for index in range(size)])


def swap_pair(pieces):
    came = swap(jnp.stack(pieces), "tensor", 2)
    return came[0], swap(came[1], "tensor", 1)


def gather_blocks(own):
    near = swap(own, "tensor", 1)
    across = swap(own, "tensor", 2)
    return [own, near, across, swap(across, "tensor", 1)]


def sum_far(part_2, part_3):
    got = swap(part_3, "tensor", 1)
    far, token = call(add_kernel, ((part_2.shape, low),), part_2, got, time=0.4, token=True)
    return far, swap(far, "tensor", 2), turn(token)


def sum_owners(total):
    owners, rows, columns = total.shape
    me = lax.axis_index("dp")
    step = 1
    while step < owners:
        pairs = total.reshape(-1, 2, rows, columns)
        mine = (me // step) % 2
        given = lax.dynamic_index_in_dim(pairs, 1 - mine, 1, keepdims=False)
        kept = lax.dynamic_index_in_dim(pairs, mine, 1, keepdims=False)
        total = kept.astype(full) + swap(given, "dp", step).astype(full)
        step *= 2
        total = total if step == owners else total.astype(low)
    return total[0]


def part_shapes(count, upper, lower, columns):
    return [((count, upper, columns), low), ((count, lower, columns), low)]


def start_sums(groups, split, deps=(), time=3.0):
    width = groups[0][0][0][0].shape[1]
    columns = sum(rhs[0].shape[1] for _, rhs in groups[0])
    rows = width // 8
    shapes = part_shapes(4 * len(groups), split, rows - split, columns)
    counts = [[(len(lhs), len(rhs)) for lhs, rhs in pairs] for pairs in groups]
    given_0, given_1, kept_0, kept_1, token = call(
        partial(weight_kernel, counts),
        shapes + shapes,
        lax.axis_index("dp").reshape(1).astype(jnp.int32),
        *[value for pairs in groups for lhs, rhs in pairs for value in (*lhs, *rhs)],
        words=1,
        deps=deps,
        time=time,
        scratch=[pltpu.VMEM((width, columns), full)],
        token=True,
    )
    return (given_0, given_1), (kept_0, kept_1), token


def cross(given, first, second):
    return swap(given[0], "dp", first), swap(given[1], "dp", second)


def halve_sums(kept, got, deps=()):
    count, _, columns = kept[0].shape
    shapes = part_shapes(count // 2, kept[0].shape[1], kept[1].shape[1], columns)
    given_0, given_1, kept_0, kept_1, token = call(
        halve_kernel,
        shapes + shapes,
        lax.axis_index("dp").reshape(1).astype(jnp.int32),
        *kept,
        *got,
        words=1,
        deps=deps,
        time=0.1,
        token=True,
    )
    return (given_0, given_1), (kept_0, kept_1), token


def join_sums(kept, got, deps=()):
    count, _, columns = kept[0].shape
    shape = ((count // 2, kept[0].shape[1] + kept[1].shape[1], columns), low)
    given, kept, token = call(
        join_kernel,
        (shape, shape),
        lax.axis_index("dp").reshape(1).astype(jnp.int32),
        *kept,
        *got,
        words=1,
        deps=deps,
        time=JOIN_TIME,
        token=True,
    )
    return swap(given, "dp", 4), kept, token


def exchange_owners(slabs):
    if isinstance(slabs, dict):
        return {index: swap(slab, "dp", index) if index else slab for index, slab in slabs.items()}
    return [lax.all_to_all(slabs[0], "dp", split_axis=0, concat_axis=0, tiled=True)]


def attend(projected_ref, bias_ref, output_ref, attended_ref, chunk, half, width_part):
    span = slice(chunk * half, (chunk + 1) * half)
    pieces = []
    for head in range(width_part // HEAD):
        at = head * HEAD
        queries = projected_ref[span, at : at + HEAD]
        keys = projected_ref[:, width_part + at : width_part + at + HEAD]
        values = projected_ref[:, 2 * width_part + at : 2 * width_part + at + HEAD]
        scores = dot(queries, keys, ((1,), (1,))) * scale + bias_ref[span, :]
        spread = jnp.exp(scores - jnp.max(scores, axis=1, keepdims=True))
        probs = spread * (1.0 / jnp.sum(spread, axis=1, keepdims=True))
        pieces.append(dot(probs.astype(low), values))
    attended = jnp.concatenate(pieces, axis=1).astype(low)
    attended_ref[...] = attended
    return dot(attended, output_ref[...])


def entry_kernel(
    lane_ref,
    big_ref,
    piece_0,
    piece_1,
    piece_2,
    piece_3,
    mask_ref,
    entry_ref,
    bias_ref,
    output_ref,
    chosen_ref,
    spatial_ref,
    normed_ref,
    projected_ref,
    attended_ref,
    part_0,
    part_1,
    gathered,
    table,
):
    lane = lane_ref[0]
    block, width = spatial_ref.shape
    width_part = width // QUARTERS
    group = block - SPARE
    half = 2 * block
    pieces = (piece_0, piece_1, piece_2, piece_3)
    for index, piece in enumerate(pieces):
        at = pl.multiple_of((lane ^ index) * width_part, 16)
        gathered[pl.ds(at, width_part), :] = piece[:width_part, :]
    summed = pieces[0][width_part:, :].astype(full)
    for piece in pieces[1:]:
        summed = summed + piece[width_part:, :].astype(full)
    span = summed.shape[1]
    steps = summed.shape[0] // QUARTERS
    for row in range(QUARTERS):
        for step in range(steps):
            from_row = row * steps + step
            table[row : row + 1, step * span : (step + 1) * span] = summed[from_row : from_row + 1]
    for index in range(QUARTERS):
        row = jnp.where(big_ref[0] == 1, 0, lane ^ index)
        chosen_ref[index : index + 1, :] = table[pl.ds(row, 1), : 6 * width]
    row_id = lax.broadcasted_iota(jnp.int32, (group, group), 0)
    column_id = lax.broadcasted_iota(jnp.int32, (group, group), 1)
    eye = (row_id == column_id).astype(full).astype(low)
    spare_id = lax.broadcasted_iota(jnp.int32, (SPARE, width), 0)
    spare = jnp.where(spare_id == 0, mask_ref[...].astype(full), 0.0)
    for chunk in (1, 0):
        span = slice(chunk * half, (chunk + 1) * half)
        normed = []
        for index in (2 * chunk, 2 * chunk + 1):
            at = pl.multiple_of((lane ^ index) * group, 128)
            kept = dot(eye, gathered[:, pl.ds(at, group)], ((1,), (1,)))
            rows = jnp.concatenate([kept, spare], axis=0)
            if index == 0:
                spatial_ref[...] = rows.astype(low)
            unit, inverse = normalize(rows)
            shift = chosen_ref[index : index + 1, :width]
            gain = chosen_ref[index : index + 1, width : 2 * width]
            normed.append(unit * (1.0 + gain) + shift)
        normed = jnp.concatenate(normed, axis=0).astype(low)
        normed_ref[span, :] = normed
        projected_ref[span, :] = dot(normed, entry_ref[...], ((1,), (1,))).astype(low)
    part = attend(projected_ref, bias_ref, output_ref, attended_ref, 1, half, width_part)
    part_0[...] = part[:block].astype(low)
    part_1[...] = part[block:].astype(low)


def attend_kernel(projected_ref, bias_ref, output_ref, attended_ref, part_0, part_1):
    block = part_0.shape[0]
    part = attend(
        projected_ref, bias_ref, output_ref, attended_ref, 0, 2 * block, output_ref.shape[0]
    )
    part_0[...] = part[:block].astype(low)
    part_1[...] = part[block:].astype(low)


def middle_kernel(
    part_0, part_1, part_2, spatial_ref, chosen_ref, branch_ref, middle_ref, normed_ref
):
    width = spatial_ref.shape[1]
    branch = part_0[...].astype(full) + part_1[...].astype(full) + part_2[...].astype(full)
    branch_ref[...] = branch
    middle = spatial_ref[...].astype(full) + chosen_ref[0:1, 2 * width : 3 * width] * branch
    middle_ref[...] = middle
    unit, inverse = normalize(middle)
    shift = chosen_ref[0:1, 3 * width : 4 * width]
    gain = chosen_ref[0:1, 4 * width : 5 * width]
    normed_ref[...] = (unit * (1.0 + gain) + shift).astype(low)


def feed_kernel(
    piece_0,
    piece_1,
    back_ref,
    expand_ref,
    normed_ref,
    activated_ref,
    hidden_grad_ref,
    part_0,
    part_1,
):
    block = piece_0.shape[0]
    normed = jnp.concatenate([piece_0[...].astype(full), piece_1[...].astype(full)], axis=0)
    normed = normed.astype(low)
    normed_ref[...] = normed
    hidden = dot(normed, expand_ref[...])
    activated, slope = gelu_both(hidden)
    activated_ref[...] = activated.astype(low)
    hidden_grad = (back_ref[...] * slope).astype(low)
    hidden_grad_ref[...] = hidden_grad
    part = dot(hidden_grad, expand_ref[...], ((1,), (1,)))
    part_0[...] = part[:block].astype(low)
    part_1[...] = part[block:].astype(low)


def middle_back_kernel(
    part_0,
    part_1,
    part_2,
    middle_ref,
    branch_ref,
    upstream_ref,
    chosen_ref,
    middle_grad_ref,
    branch_grad_ref,
    sums_ref,
):
    width = middle_ref.shape[1]
    normed_grad = part_0[...].astype(full) + part_1[...].astype(full) + part_2[...].astype(full)
    unit, inverse = normalize(middle_ref[...])
    gain = chosen_ref[0:1, 4 * width : 5 * width]
    middle_grad = upstream_ref[...] + normalize_back(unit, inverse, normed_grad * (1.0 + gain))
    middle_grad_ref[...] = middle_grad
    branch_grad_ref[...] = (chosen_ref[0:1, 2 * width : 3 * width] * middle_grad).astype(low)
    sums_ref[0:1, :] = jnp.sum(middle_grad * branch_ref[...], axis=0, keepdims=True)
    sums_ref[1:2, :] = jnp.sum(normed_grad, axis=0, keepdims=True)
    sums_ref[2:3, :] = jnp.sum(normed_grad * unit, axis=0, keepdims=True)


def probs_kernel(projected_ref, bias_ref, probs_ref):
    width_part = projected_ref.shape[1] // 3
    for head in range(width_part // HEAD):
        at = head * HEAD
        queries = projected_ref[:, at : at + HEAD]
        keys = projected_ref[:, width_part + at : width_part + at + HEAD]
        scores = dot(keys, queries, ((1,), (1,))) * scale + bias_ref[...]
        spread = jnp.exp(scores - jnp.max(scores, axis=0, keepdims=True))
        probs = spread * (1.0 / jnp.sum(spread, axis=0, keepdims=True))
        probs_ref[head] = probs.astype(low)


def attend_back_kernel(
    projected_ref,
    probs_ref,
    output_ref,
    piece_0,
    piece_1,
    piece_2,
    piece_3,
    branch_grad_ref,
    grad_ref,
):
    rows, width_all = projected_ref.shape
    width_part = width_all // 3
    block = piece_0.shape[0]
    half = 2 * block
    for chunk, pair in enumerate(((piece_0, piece_1), (piece_2, piece_3))):
        branch_grad_ref[chunk * half : (chunk + 1) * half, :] = jnp.concatenate(
            [piece[...].astype(full) for piece in pair], axis=0
        ).astype(low)
    attended_grad = dot(branch_grad_ref[...], output_ref[...], ((1,), (1,))).astype(low)
    pieces = [[], [], []]
    for head in range(width_part // HEAD):
        at = head * HEAD
        queries = projected_ref[:, at : at + HEAD]
        keys = projected_ref[:, width_part + at : width_part + at + HEAD]
        values = projected_ref[:, 2 * width_part + at : 2 * width_part + at + HEAD]
        grad = attended_grad[:, at : at + HEAD]
        probs = probs_ref[head]
        pieces[2].append(dot(probs, grad))
        probs = probs.astype(full)
        prob_grad = dot(values, grad, ((1,), (1,)))
        delta = jnp.sum(probs * prob_grad, axis=0, keepdims=True)
        score_grad = (probs * (prob_grad - delta)).astype(low)
        pieces[1].append(dot(score_grad, queries) * scale)
        pieces[0].append(dot(score_grad, keys, ((0,), (0,))) * scale)
    grad_ref[...] = jnp.concatenate(pieces[0] + pieces[1] + pieces[2], axis=1).astype(low)


def entry_back_kernel(chunk, grad_ref, entry_ref, part_0, part_1):
    block = part_0.shape[0]
    part = dot(grad_ref[2 * chunk * block : 2 * (chunk + 1) * block, :], entry_ref[...])
    part_0[...] = part[:block].astype(low)
    part_1[...] = part[block:].astype(low)


def pack_kernel(owners, chosen, me_ref, kept_ref, owner_ref, position_ref, riders_ref, *out_refs):
    slot_ref = out_refs[-1]
    extra, capacity = riders_ref.shape
    kept_count = kept_ref.shape[1]
    owner_local = owner_ref[...] ^ me_ref[0]
    owner_id = lax.broadcasted_iota(jnp.int32, (owners, kept_count), 0)
    hot = (owner_id == owner_local).astype(full)
    row_id = lax.broadcasted_iota(jnp.int32, (kept_count, kept_count), 0)
    column_id = lax.broadcasted_iota(jnp.int32, (kept_count, kept_count), 1)
    before = dot(hot.astype(low), (row_id < column_id).astype(full).astype(low))
    rank = jnp.sum(hot * before, axis=0, keepdims=True).astype(jnp.int32)
    slot = owner_local * capacity + rank
    slot_ref[...] = slot
    coded = position_ref[...] + 1
    tag_id = lax.broadcasted_iota(jnp.int32, (extra, kept_count), 0)
    tags = jnp.where(tag_id == 0, coded >> 5, jnp.where(tag_id == 1, coded & 31, 0))
    rows = jnp.concatenate([kept_ref[...], tags.astype(full).astype(low)], axis=0)
    slot_id = lax.broadcasted_iota(jnp.int32, (capacity, kept_count), 0)
    for number, index in enumerate(chosen):
        matrix = (slot_id + index * capacity == slot).astype(full).astype(low)
        slab = dot(rows, matrix, ((1,), (1,)))
        split = kept_ref.shape[0]
        slab = jnp.concatenate([slab[:split], slab[split:] + riders_ref[...].astype(full)], axis=0)
        if len(out_refs) == 2:
            out_refs[0][me_ref[0] ^ index] = slab.astype(low)
        else:
            out_refs[number][...] = slab.astype(low)


def unpack_kernel(owners, me_ref, *refs):
    slab_refs, outs = refs[:-5], refs[-5:]
    compact_ref, slot_rank_ref, token_rank_ref, lifted_ref, arrived = outs
    table_ref, slab_refs = slab_refs[0], slab_refs[1:]
    arrived_count = compact_ref.shape[1]
    width_part = compact_ref.shape[0] - table_ref.shape[0]
    slots_all = arrived.shape[1]
    own_tokens = token_rank_ref.shape[1]
    capacity = slots_all // owners
    for index in range(owners):
        if len(slab_refs) == 1:
            slab = slab_refs[0][me_ref[0] ^ index]
        else:
            slab = slab_refs[(FAR + NEAR).index(index)][...]
        arrived[:, index * capacity : (index + 1) * capacity] = slab
    tags = arrived[width_part : width_part + 16, :].astype(full)
    place = tags[0:1] * 32.0 + tags[1:2] - 1.0
    turned = jnp.transpose(jnp.broadcast_to(place, (8, slots_all)))[:, 0:1]
    turned = jnp.where(turned < 0.0, 1e9, turned)
    slot_rank = jnp.sum(jnp.where(turned < place, 1.0, 0.0), axis=0, keepdims=True)
    slot_rank = jnp.where(place < 0.0, -1.0, slot_rank).astype(jnp.int32)
    slot_rank_ref[...] = slot_rank
    rank_id = lax.broadcasted_iota(jnp.int32, (arrived_count, slots_all), 0)
    matrix = (rank_id == slot_rank).astype(full).astype(low)
    compact_ref[:width_part, :] = dot(arrived[:width_part, :], matrix, ((1,), (1,))).astype(low)
    compact_ref[width_part:, :] = table_ref[...]
    spot = lax.broadcasted_iota(jnp.int32, (1, own_tokens), 1).astype(full)
    token_rank = jnp.sum(jnp.where(turned < spot, 1.0, 0.0), axis=0, keepdims=True)
    filled = jnp.sum(jnp.where(turned == spot, 1.0, 0.0), axis=0, keepdims=True)
    token_rank_ref[...] = jnp.where(filled > 0.0, token_rank, -1.0).astype(jnp.int32)
    if len(slab_refs) > 1:
        chunks = lifted_ref.shape[1] // capacity
        for index in range(owners):
            for row in range(QUARTERS):
                for chunk in range(chunks):
                    lifted_ref[
                        index * QUARTERS + row : index * QUARTERS + row + 1,
                        chunk * capacity : (chunk + 1) * capacity,
                    ] = tags[
                        2 + row * chunks + chunk : 3 + row * chunks + chunk,
                        index * capacity : (index + 1) * capacity,
                    ]
    else:
        lifted_ref[...] = jnp.zeros_like(lifted_ref)


def back_kernel(
    lane_ref,
    part_0,
    part_1,
    part_2,
    spatial_ref,
    middle_grad_ref,
    chosen_ref,
    sums_ref,
    feed_0,
    feed_1,
    feed_2,
    upstream_ref,
    piece_0,
    piece_1,
    piece_2,
    piece_3,
    turned,
    riders,
):
    lane = lane_ref[0]
    block, width = spatial_ref.shape
    group = block - SPARE
    width_part = width // QUARTERS
    normed_grad = part_0[...].astype(full) + part_1[...].astype(full) + part_2[...].astype(full)
    unit, inverse = normalize(spatial_ref[...].astype(full))
    gain = chosen_ref[0:1, width : 2 * width]
    grad = middle_grad_ref[...] + normalize_back(unit, inverse, normed_grad * (1.0 + gain))
    turned[...] = jnp.transpose(grad[:group]).astype(low)
    feed = feed_0[...].astype(full) + feed_1[...].astype(full) + feed_2[...].astype(full)
    mask_sum = grad[group : group + 1]
    mask_high = mask_sum.astype(low).astype(full)
    fields = [
        jnp.sum(normed_grad, axis=0, keepdims=True),
        jnp.sum(normed_grad * unit, axis=0, keepdims=True),
        sums_ref[0:1, :],
        sums_ref[1:2, :],
        sums_ref[2:3, :],
        jnp.sum(feed * upstream_ref[...], axis=0, keepdims=True),
        mask_high,
        mask_sum - mask_high,
    ]
    chunks = width // 128
    riders[...] = jnp.zeros_like(riders)
    for number, field in enumerate(fields):
        for chunk in range(chunks):
            at = number * chunks + chunk
            riders[at : at + 1, :] = field[:, chunk * 128 : (chunk + 1) * 128]
    rider_rows = riders[...].astype(low)
    for index, piece in enumerate((piece_0, piece_1, piece_2, piece_3)):
        at = pl.multiple_of((lane ^ index) * width_part, 16)
        piece[:width_part, :] = turned[pl.ds(at, width_part), :]
        piece[width_part:, :] = rider_rows


def slots_kernel(
    owners,
    lane_ref,
    me_ref,
    big_ref,
    rank_ref,
    piece_0,
    piece_1,
    piece_2,
    piece_3,
    slabs_ref,
    table_ref,
    table,
    mask_total,
):
    lane = lane_ref[0]
    me = me_ref[0]
    group = piece_0.shape[1]
    slots_all = rank_ref.shape[1]
    capacity = slots_all // owners
    chunks = table_ref.shape[1]
    width_part = slabs_ref.shape[1] - RIDERS
    pieces = [piece_0, piece_1, piece_2, piece_3]
    rows = jnp.concatenate([piece[:width_part, :] for piece in pieces], axis=1)
    row_id = lax.broadcasted_iota(jnp.int32, (group, slots_all), 0)
    matrix = jnp.concatenate(
        [
            (row_id + (lane ^ index) * group == rank_ref[...]).astype(full).astype(low)
            for index in range(QUARTERS)
        ],
        axis=0,
    )
    slots = dot(rows, matrix)
    table[...] = jnp.zeros_like(table)
    summed = jnp.zeros((chunks, 128), full)
    mask_sum = jnp.zeros((16, 128), full)
    mask_rows = chunks // 6
    for index, piece in enumerate(pieces):
        field = piece[width_part : width_part + chunks, :].astype(full)
        summed = summed + field
        rest = piece[width_part + chunks - chunks % 16 :, :].astype(full)
        table[lane ^ index, :chunks, :] = field
        at = chunks % 16
        mask_sum = mask_sum + jnp.concatenate(
            [
                rest[at : at + mask_rows] + rest[at + mask_rows : at + 2 * mask_rows],
                jnp.zeros((16 - mask_rows, 128), full),
            ],
            axis=0,
        )
    mask_total[...] = mask_sum

    @pl.when(big_ref[0] == 1)
    def _():
        table[...] = jnp.zeros_like(table)
        table[0, :chunks, :] = summed

    table_ref[...] = table[:, :chunks, :].astype(low)
    for index in range(owners):
        owner = me ^ index
        start = (owner * chunks) // owners
        fields = [table[row, pl.ds(start, 8), :] for row in range(QUARTERS)]
        mask_start = (owner * mask_rows) // owners
        mask_part = mask_total[pl.ds(mask_start, 2), :]
        mask_high = mask_part.astype(low).astype(full)
        fields += [mask_high, mask_part - mask_high, jnp.zeros((RIDERS - 36, 128), full)]
        slab = jnp.concatenate([slots[:, index * capacity : (index + 1) * capacity]] + fields, axis=0)
        slabs_ref[owner] = slab.astype(low)


def kept_kernel(
    owners, me_ref, slot_ref, lifted_ref, slabs_ref, kept_ref, modulate_ref, mask_ref, table
):
    width_part, kept_count = kept_ref.shape
    capacity = slabs_ref.shape[2]
    table_part = modulate_ref.shape[1]
    mask_part = mask_ref.shape[1]
    me = me_ref[0]
    slabs = [slabs_ref[me ^ index] for index in range(owners)]
    rows = jnp.concatenate([slab[:width_part] for slab in slabs], axis=1)
    slot_id = lax.broadcasted_iota(jnp.int32, (owners * capacity, kept_count), 0)
    matrix = (slot_id == slot_ref[...]).astype(full).astype(low)
    kept_ref[...] = dot(rows, matrix).astype(low)
    mask_sum = jnp.zeros((1, 256), full)
    for index, slab in enumerate(slabs):
        rider = slab[width_part:].astype(full)
        for row in range(QUARTERS):
            at = index * QUARTERS + row
            for chunk in range(8):
                from_row = row * 8 + chunk
                table[at : at + 1, chunk * 128 : (chunk + 1) * 128] = rider[
                    from_row : from_row + 1
                ]
        high, rest = rider[32:34], rider[34:36]
        both = high + rest
        mask_sum = mask_sum + jnp.concatenate([both[0:1], both[1:2]], axis=1)
    shift = (me * table_part) % 128
    field = pltpu.roll(table[...], (1024 - shift) % 1024, 1)[:, :table_part]
    lifted = lifted_ref[...].astype(low)[:, :width_part]
    modulate_ref[...] = dot(lifted, field.astype(low), ((0,), (0,)))
    shift = (me * mask_part) % 128
    mask_sum = jnp.broadcast_to(mask_sum, (8, 256))
    mask_ref[...] = pltpu.roll(mask_sum, (256 - shift) % 256, 1)[0:1, :mask_part]


def out_kernel(
    lane_ref,
    part_0,
    part_1,
    part_2,
    middle_ref,
    chosen_ref,
    piece_0,
    piece_1,
    piece_2,
    piece_3,
    turned,
    riders,
):
    lane = lane_ref[0]
    block, width = middle_ref.shape
    group = block - SPARE
    width_part = width // QUARTERS
    feed = part_0[...].astype(full) + part_1[...].astype(full) + part_2[...].astype(full)
    out = middle_ref[...] + chosen_ref[0:1, 5 * width : 6 * width] * feed
    turned[...] = jnp.transpose(out[:group]).astype(low)
    riders[...] = jnp.zeros_like(riders)
    for chunk in range(width // 128):
        riders[chunk : chunk + 1, :] = out[group : group + 1, chunk * 128 : (chunk + 1) * 128]
    rider_rows = riders[...].astype(low)
    for index, piece in enumerate((piece_0, piece_1, piece_2, piece_3)):
        at = pl.multiple_of((lane ^ index) * width_part, 16)
        piece[:width_part, :] = turned[pl.ds(at, width_part), :]
        piece[width_part:, :] = rider_rows


def layer_kernel(
    lane_ref, rank_ref, piece_0, piece_1, piece_2, piece_3, out_ref, spare, turned
):
    lane = lane_ref[0]
    width_part, own_tokens = out_ref.shape
    group = piece_0.shape[1]
    quarter = own_tokens // QUARTERS
    pieces = (piece_0, piece_1, piece_2, piece_3)
    rows = jnp.concatenate([piece[:width_part, :] for piece in pieces], axis=1)
    row_id = lax.broadcasted_iota(jnp.int32, (group, own_tokens), 0)
    matrix = jnp.concatenate(
        [
            (row_id + (lane ^ index) * group == rank_ref[...]).astype(full).astype(low)
            for index in range(QUARTERS)
        ],
        axis=0,
    )
    spare[...] = jnp.zeros_like(spare)
    for index, piece in enumerate(pieces):
        rider = piece[width_part:, :].astype(full)
        for chunk in range(spare.shape[1] // 128):
            spare[index : index + 1, chunk * 128 : (chunk + 1) * 128] = rider[chunk : chunk + 1]
    turned[...] = jnp.transpose(spare[...])
    columns = turned[pl.ds(pl.multiple_of(lane * width_part, 16), width_part), :].astype(low)
    spare_id = lax.broadcasted_iota(jnp.int32, (8, own_tokens), 0)
    spot = lax.broadcasted_iota(jnp.int32, (8, own_tokens), 1) // quarter
    empty = rank_ref[...] < 0
    spots = jnp.where(((spare_id ^ lane) == spot) & (spare_id < QUARTERS) & empty, 1.0, 0.0)
    out_ref[...] = (dot(rows, matrix) + dot(columns, spots.astype(low))).astype(low)


def table_kernel(big_ref, lifted_ref, modulate_ref, table_ref, bias_ref, turned_ref, table):
    span = table_ref.shape[1]
    steps = table_ref.shape[0] // QUARTERS
    table[...] = jnp.zeros_like(table)
    table[:QUARTERS, : modulate_ref.shape[1]] = dot(lifted_ref[...], modulate_ref[...])
    table_ref[...] = jnp.concatenate(
        [
            table[row : row + 1, step * span : (step + 1) * span]
            for row in range(QUARTERS)
            for step in range(steps)
        ],
        axis=0,
    ).astype(low)
    rows = bias_ref.shape[0]
    block = rows // QUARTERS
    group = block - SPARE
    big = big_ref[0] == 1
    spare_small = jnp.log(jnp.full((1, 1), float(group), full))
    spare_big = jnp.log(jnp.full((1, 1), float(QUARTERS * group), full))

    def bias_of(query, key):
        query_block, key_block, key_inner = query // block, key // block, key % block
        small = jnp.where(key_inner < group, 0.0, jnp.where(key_inner == group, spare_small, -1e30))
        small = jnp.where(query_block == key_block, small, -1e30)
        large = jnp.where(key_inner < group, 0.0, jnp.where(key == group, spare_big, -1e30))
        return jnp.where(big, large, small)

    row_id = lax.broadcasted_iota(jnp.int32, (rows, rows), 0)
    column_id = lax.broadcasted_iota(jnp.int32, (rows, rows), 1)
    bias_ref[...] = bias_of(row_id, column_id)
    turned_ref[...] = bias_of(column_id, row_id)


def add_kernel(left_ref, right_ref, out_ref):
    out_ref[...] = (left_ref[...].astype(full) + right_ref[...].astype(full)).astype(low)


def copy_kernel(*refs):
    for index in range(len(refs) // 2):
        refs[len(refs) // 2 + index][...] = refs[index][...]


def upstream_kernel(
    lane_ref,
    rank_ref,
    chosen_ref,
    cotangent_ref,
    shrink_ref,
    feed_grad_ref,
    upstream_ref,
    back_near,
    back_far,
):
    lane = lane_ref[0]
    block, width = upstream_ref.shape
    own_tokens = rank_ref.shape[1]
    group = block - SPARE
    half = 2 * block
    rank = rank_ref[...]
    row_id = lax.broadcasted_iota(jnp.int32, (group, own_tokens), 0)
    spare_id = lax.broadcasted_iota(jnp.int32, (SPARE, own_tokens), 0)
    spot = lax.broadcasted_iota(jnp.int32, (SPARE, own_tokens), 1) // (own_tokens // QUARTERS)
    for chunk, back in ((0, back_near), (1, back_far)):
        matrix = []
        for index in (2 * chunk, 2 * chunk + 1):
            matrix.append(jnp.where(row_id + (lane ^ index) * group == rank, 1.0, 0.0))
            matrix.append(
                jnp.where((spare_id == 0) & (spot == (lane ^ index)) & (rank < 0), 1.0, 0.0)
            )
        upstream = dot(jnp.concatenate(matrix, axis=0).astype(low), cotangent_ref[...])
        if chunk == 0:
            upstream_ref[...] = upstream[:block]
        gates = [chosen_ref[index : index + 1, 5 * width :] for index in (2 * chunk, 2 * chunk + 1)]
        feed_grad = jnp.concatenate(
            [gates[0] * upstream[:block], gates[1] * upstream[block:]], axis=0
        ).astype(low)
        feed_grad_ref[chunk * half : (chunk + 1) * half, :] = feed_grad
        back[...] = dot(feed_grad, shrink_ref[...], ((1,), (1,)))


def feed_out_kernel(near_ref, far_ref, shrink_ref, part_0, part_1, part_2, part_3):
    block = part_0.shape[0]
    for activated, pair in ((far_ref, (part_2, part_3)), (near_ref, (part_0, part_1))):
        part = dot(activated[...], shrink_ref[...])
        pair[0][...] = part[:block].astype(low)
        pair[1][...] = part[block:].astype(low)


def weight_kernel(counts, me_ref, *refs):
    given_0, given_1, kept_0, kept_1, product = refs[-5:]
    operands = list(refs[:-5])
    rows = given_0.shape[1] + given_1.shape[1]
    chunk = product.shape[0] // 3
    for group, pairs in enumerate(counts):
        products = []
        for lefts, rights in pairs:
            lhs = [operands.pop(0) for _ in range(lefts)]
            right = jnp.concatenate([operands.pop(0)[...] for _ in range(rights)], axis=0)
            products.append((lhs, right))
        for number in range(3):
            span = slice(number * chunk, (number + 1) * chunk)
            parts = [
                dot(jnp.concatenate([ref[:, span] for ref in lhs], axis=0), right, ((0,), (0,)))
                for lhs, right in products
            ]
            product[span, :] = jnp.concatenate(parts, axis=1)
        for bit, start, given, kept in (
            (0, 0, given_0, kept_0),
            (1, given_0.shape[1], given_1, kept_1),
        ):
            mine = (me_ref[0] >> bit) & 1
            for index in range(4):
                for value, ref in ((1 - mine, given), (mine, kept)):
                    above = (index >> bit) << (bit + 1)
                    at = (above + (value << bit) + (index & bit)) * rows + start
                    at = pl.multiple_of(at, 8)
                    ref[4 * group + index] = product[pl.ds(at, ref.shape[1]), :].astype(low)


def halve_kernel(
    me_ref, held_0, held_1, got_0, got_1, given_0, given_1, kept_0, kept_1
):
    for bit, held, got, given, kept in (
        (1, held_0, got_0, given_0, kept_0),
        (0, held_1, got_1, given_1, kept_1),
    ):
        mine = (me_ref[0] >> bit) & 1
        for index in range(given.shape[0]):
            for value, ref in ((1 - mine, given), (mine, kept)):
                at = 2 * index + value
                ref[index] = (held[at].astype(full) + got[at].astype(full)).astype(low)


def join_kernel(me_ref, held_0, held_1, got_0, got_1, given, kept):
    mine = (me_ref[0] >> 2) & 1
    for index in range(given.shape[0]):
        for value, ref in ((1 - mine, given), (mine, kept)):
            at = 2 * index + value
            upper = held_0[at].astype(full) + got_0[at].astype(full)
            lower = held_1[at].astype(full) + got_1[at].astype(full)
            ref[index] = jnp.concatenate([upper, lower], axis=0).astype(low)


def total_kernel(held_ref, got_ref, *out_refs):
    if len(out_refs[0].shape) == 2:
        for index, out_ref in enumerate(out_refs):
            out_ref[...] = held_ref[index].astype(full) + got_ref[index].astype(full)
        return
    entry_ref, output_ref = out_refs
    total = held_ref[0].astype(full) + got_ref[0].astype(full)
    parts, _, columns = entry_ref.shape
    for index in range(parts):
        entry_ref[index] = total[:, index * columns : (index + 1) * columns]
    output_ref[...] = total[:, parts * columns :]


def call(
    kernel, outs, *operands, words=0, deps=(), time=1.0, scratch=(), token=False, loose=False
):
    count = len(operands)
    deps = tuple(deps)
    outs = tuple(outs)
    if token:
        outs += (((8, 128), full),)

    def run(*refs):
        outs_at = count + len(deps)
        rest = list(refs[outs_at:])
        if token:
            last = rest.pop(len(outs) - 1)
            last[...] = jnp.zeros_like(last)
        kernel(*refs[:count], *rest)

    return pl.pallas_call(
        run,
        out_shape=tuple(jax.ShapeDtypeStruct(shape, kind) for shape, kind in outs),
        in_specs=[SMALL] * words
        + [pl.BlockSpec() if loose else PLAIN] * (count - words)
        + [pl.BlockSpec(memory_space=pl.ANY)] * len(deps),
        scratch_shapes=list(scratch),
        compiler_params=pltpu.CompilerParams(vmem_limit_bytes=VMEM_ASK),
        cost_estimate=pl.CostEstimate(
            flops=int(time * 1.15e9), bytes_accessed=1024, transcendentals=0
        ),
    )(*operands, *deps)


def turn(token):
    return swap(token, "tensor", 1)


def body(
    kept_rows,
    owner_index,
    kept_position,
    resolution,
    mask_token,
    condition,
    modulate_weight,
    entry_weight,
    output_weight,
    expand_weight,
    shrink_weight,
    cotangent,
):
    owners = lax.axis_size("dp")
    me = lax.axis_index("dp")
    lane = lax.axis_index("tensor")
    kept_count, width_part = kept_rows.shape
    width = mask_token.shape[0]
    own_tokens = cotangent.shape[0]
    ff_part = expand_weight.shape[1]
    quarter = own_tokens // QUARTERS
    group = quarter // 2
    arrived_count = own_tokens // 2
    block = group + SPARE
    rows = QUARTERS * block
    capacity = 2 * kept_count // owners
    slots_all = owners * capacity
    direct = owners == SWAP_OWNERS
    lane_word = lane.reshape(1).astype(jnp.int32)
    me_word = me.reshape(1).astype(jnp.int32)
    big_word = resolution[:1]
    context_part = lax.dynamic_slice_in_dim(
        condition.astype(full), lane * width_part, width_part, 1
    )
    lifted = jax.nn.silu(context_part).astype(low)
    if direct:
        padded = -(-width_part // capacity) * capacity
        riders = jnp.pad(lifted, ((0, 0), (0, padded - width_part))).reshape(-1, capacity)
    else:
        padded = 128
        riders = lifted.reshape(-1, capacity)
    rider_count = riders.shape[0]
    extra = -(-(rider_count + 2) // 16) * 16
    riders = jnp.pad(riders, ((2, extra - 2 - rider_count), (0, 0)))
    slab_rows = width_part + extra
    slab_shape = (slab_rows, capacity)
    if not direct:
        slab_shape = (owners,) + slab_shape
    *slabs, slot_index = call(
        partial(pack_kernel, owners, FAR + NEAR if direct else range(owners)),
        ((slab_shape, low),) * (owners if direct else 1) + (((1, kept_count), jnp.int32),),
        me_word,
        kept_rows.T,
        owner_index[None, :],
        kept_position[None, :],
        riders,
        words=1,
        time=1.0,
        loose=direct,
    )

    steps = -(-6 * width // arrived_count)
    table, bias, bias_turned = call(
        table_kernel,
        (
            ((QUARTERS * steps, arrived_count), low),
            ((rows, rows), full),
            ((rows, rows), full),
        ),
        big_word,
        lifted,
        modulate_weight,
        words=1,
        deps=[slot_index],
        time=2.0,
        scratch=[pltpu.VMEM((8, steps * arrived_count), full)],
    )
    if direct:
        slabs = exchange_owners(dict(zip(FAR + NEAR, slabs)))
        slabs = list(slabs.values())
    else:
        slabs = exchange_owners(slabs)
    compact, slot_rank, token_rank, lifted_all = call(
        partial(unpack_kernel, owners),
        (
            ((width_part + QUARTERS * steps, arrived_count), low),
            ((1, slots_all), jnp.int32),
            ((1, own_tokens), jnp.int32),
            ((owners * QUARTERS, padded), full),
        ),
        me_word,
        table,
        *slabs,
        words=1,
        time=2.4,
        scratch=[pltpu.VMEM((slab_rows, slots_all), low)],
    )
    if not direct:
        owner_order = jnp.arange(owners, dtype=jnp.int32) ^ me
        lifted_all = slabs[0][:, width_part + 2 : width_part + 2 + rider_count]
        lifted_all = lifted_all.reshape(owners * QUARTERS, width_part)
    spatial_pieces = gather_blocks(compact)
    entry_flat = jnp.transpose(entry_weight, (1, 2, 0)).reshape(3 * width_part, width)
    token_shape = ((block, width), low)
    half = 2 * block
    chosen, spatial_own, normed_one, projected, attended_far, part_2, part_3 = call(
        entry_kernel,
        (
            ((QUARTERS, 6 * width), full),
            token_shape,
            ((rows, width), low),
            ((rows, 3 * width_part), low),
            ((half, width_part), low),
            token_shape,
            token_shape,
        ),
        lane_word,
        big_word,
        *spatial_pieces,
        mask_token[None, :],
        entry_flat,
        bias,
        output_weight,
        words=2,
        time=5.0,
        scratch=[
            pltpu.VMEM((width, arrived_count), low),
            pltpu.VMEM((8, steps * arrived_count), full),
        ],
    )
    far, across, start = sum_far(part_2, part_3)
    attended_near, part_0, part_1 = call(
        attend_kernel,
        (((half, width_part), low), token_shape, token_shape),
        projected,
        bias,
        output_weight,
        deps=[start],
        time=3.0,
    )
    got = swap(part_1, "tensor", 1)
    feed_grad, upstream_own, back_near, back_far = call(
        upstream_kernel,
        (
            ((rows, width), low),
            ((block, width), full),
            ((half, width), full),
            ((half, width), full),
        ),
        lane_word,
        token_rank,
        chosen,
        cotangent,
        shrink_weight,
        words=1,
        deps=[part_1],
        time=3.6,
    )
    branch, middle, normed_two_own = call(
        middle_kernel,
        (((block, width), full), ((block, width), full), token_shape),
        part_0,
        got,
        across,
        spatial_own,
        chosen,
        deps=[back_far],
        time=0.6,
    )

    def feed_call(piece_0, piece_1, back, *deps):
        return call(
            feed_kernel,
            (((half, width), low), ((half, width), low), ((half, width), low))
            + (token_shape, token_shape),
            piece_0,
            piece_1,
            back,
            expand_weight,
            deps=deps,
            time=2.4,
        )

    near_piece = swap(normed_two_own, "tensor", 1)
    across = swap(normed_two_own, "tensor", 2)
    normed_near, activated_near, hidden_near, part_0, part_1 = feed_call(
        normed_two_own, near_piece, back_near
    )
    (across,) = call(copy_kernel, (token_shape,), across, deps=[part_0], time=0.3)
    last_piece = swap(across, "tensor", 1)
    normed_far, activated_far, hidden_far, part_2, part_3 = feed_call(
        across, last_piece, back_far
    )
    far, across, start = sum_far(part_2, part_3)
    got = swap(part_1, "tensor", 1)
    feed_groups = [
        [([feed_grad], [activated_near, activated_far])],
        [([normed_near, normed_far], [hidden_near, hidden_far])],
    ]
    event = start
    if direct:
        feed_given, feed_kept, event = start_sums(feed_groups, FEED_SPLIT, [start], 5.8)
        feed_got = cross(feed_given, 1, 2)
    middle_grad, branch_grad_own, sums, start = call(
        middle_back_kernel,
        (((block, width), full), token_shape, ((SPARE, width), full)),
        part_0,
        got,
        across,
        middle,
        branch,
        upstream_own,
        chosen,
        deps=[event],
        time=0.7,
        token=True,
    )
    branch_pieces = gather_blocks(branch_grad_own)
    feed_parts = call(
        feed_out_kernel,
        (token_shape,) * QUARTERS,
        activated_near,
        activated_far,
        shrink_weight,
        deps=[turn(start)],
        time=0.1,
    )
    feed_far = swap(feed_parts[3], "tensor", 1)
    feed_near = swap(feed_parts[1], "tensor", 1)
    feed_far, start = call(
        add_kernel,
        (token_shape,),
        feed_parts[2],
        feed_far,
        deps=[branch_pieces[2]],
        time=0.1,
        token=True,
    )
    (probs,) = call(
        probs_kernel,
        (((width_part // HEAD, rows, rows), low),),
        projected,
        bias_turned,
        deps=[feed_far],
        time=0.1,
    )
    branch_grad, projected_grad = call(
        attend_back_kernel,
        (((rows, width), low), ((rows, 3 * width_part), low)),
        projected,
        probs,
        output_weight,
        *branch_pieces,
        deps=[turn(start)],
        time=0.1,
    )
    feed_across = swap(feed_far, "tensor", 2)
    part_2, part_3 = call(
        partial(entry_back_kernel, 1),
        (token_shape, token_shape),
        projected_grad,
        entry_flat,
        deps=[feed_across, feed_near],
        time=0.1,
    )
    far, across, start = sum_far(part_2, part_3)
    part_0, part_1 = call(
        partial(entry_back_kernel, 0),
        (token_shape, token_shape),
        projected_grad,
        entry_flat,
        deps=[start],
        time=0.2,
    )
    got = swap(part_1, "tensor", 1)
    entry_groups = [
        [([normed_one], [projected_grad]), ([branch_grad], [attended_near, attended_far])]
    ]
    event = part_1
    if direct:
        feed_given, feed_kept, event = halve_sums(feed_kept, feed_got, [part_1])
        feed_got = cross(feed_given, 2, 1)
        entry_given, entry_kept, event = start_sums(entry_groups, ENTRY_SPLIT, [event], 0.2)
        entry_got = cross(entry_given, 1, 2)
    back_pieces = call(
        back_kernel,
        (((width_part + 80, group), low),) * QUARTERS,
        lane_word,
        part_0,
        got,
        across,
        spatial_own,
        middle_grad,
        chosen,
        sums,
        feed_parts[0],
        feed_near,
        feed_across,
        upstream_own,
        words=1,
        deps=[event],
        time=BACK_TIME,
        scratch=[pltpu.VMEM((width, group), low), pltpu.VMEM((80, 128), full)],
    )
    back_pieces = [
        back_pieces[0],
        swap(back_pieces[1], "tensor", 1),
        *swap_pair(back_pieces[2:]),
    ]
    chunks = 6 * width // 128
    logistic = jax.nn.sigmoid(context_part)
    logistic = logistic * (1.0 + context_part * (1.0 - logistic))
    if direct:
        slabs, table_grad, event = call(
            partial(slots_kernel, owners),
            (
                ((owners, width_part + RIDERS, capacity), low),
                ((QUARTERS, chunks, 128), low),
            ),
            lane_word,
            me_word,
            big_word,
            slot_rank,
            *back_pieces,
            words=3,
            time=0.8,
            token=True,
            scratch=[
                pltpu.VMEM((QUARTERS, chunks + 2, 128), full),
                pltpu.VMEM((16, 128), full),
            ],
        )
        (slabs,) = exchange_owners([slabs])
        table_grad = table_grad.reshape(QUARTERS, 6 * width)
        feed_got, feed_kept, joined = join_sums(feed_kept, feed_got, [event])
        entry_given, entry_kept, halved = halve_sums(entry_kept, entry_got, [joined])
        entry_got = cross(entry_given, 2, 1)
        kept_grad, modulate_grad, mask_grad, kept_token = call(
            partial(kept_kernel, owners),
            (
                ((width_part, kept_count), low),
                ((width_part, 6 * width // owners), full),
                ((1, width // owners), full),
            ),
            me_word,
            slot_index,
            lifted_all,
            slabs,
            words=1,
            deps=[halved],
            time=KEPT_TIME,
            token=True,
            scratch=[pltpu.VMEM((owners * QUARTERS, 1024), full)],
        )
        mask_grad = mask_grad[0]
    else:
        event = back_pieces[1]
        rows_back = jnp.concatenate([piece[:width_part] for piece in back_pieces], axis=1)
        rank_ids = jnp.arange(arrived_count, dtype=jnp.int32)
        rank_ids = ((rank_ids // group) ^ lane) * group + rank_ids % group
        matrix = (rank_ids[:, None] == slot_rank).astype(low)
        slabs = dot(rows_back, matrix).astype(low).reshape(width_part, owners, capacity)
        slabs = jnp.take(jnp.transpose(slabs, (1, 0, 2)), owner_order, axis=0)
        slabs = jnp.take(exchange_owners([slabs])[0], owner_order, axis=0)
        slabs = jnp.transpose(slabs, (1, 0, 2)).reshape(width_part, slots_all)
        slot_ids = jnp.arange(slots_all, dtype=jnp.int32)[:, None]
        kept_grad = dot(slabs, (slot_ids == slot_index).astype(low)).astype(low)
        riders = jnp.stack(
            [piece[width_part : width_part + 8 * width // 128] for piece in back_pieces]
        )
        riders = riders.reshape(QUARTERS, 8, width).astype(full)
        mask_total = jnp.sum(riders[:, 6] + riders[:, 7], axis=0)
        table_local = riders[:, :6].reshape(QUARTERS, 6 * width)
        table_small = jnp.take(table_local, jnp.arange(QUARTERS, dtype=jnp.int32) ^ lane, axis=0)
        first = jnp.arange(QUARTERS, dtype=jnp.int32)[:, None] == 0
        table_big = jnp.where(first, jnp.sum(table_local, axis=0, keepdims=True), 0.0)
        table_grad = jnp.where(big_word[0] == 1, table_big, table_small).astype(low)
        sent = jnp.transpose(table_grad.reshape(QUARTERS, owners, -1), (1, 0, 2))
        table_all = exchange_owners([sent])[0].reshape(owners * QUARTERS, -1)
        modulate_grad = dot(lifted_all, table_all, ((0,), (0,)))
        mask_grad = lax.psum_scatter(mask_total, "dp", scatter_dimension=0, tiled=True)
    condition_grad = dot(table_grad, modulate_weight, ((1,), (1,))) * logistic
    out_pieces = call(
        out_kernel,
        (((width_part + 16, group), low),) * QUARTERS,
        lane_word,
        feed_parts[0],
        feed_near,
        feed_across,
        middle,
        chosen,
        words=1,
        deps=[event],
        time=1.0,
        scratch=[pltpu.VMEM((width, group), low), pltpu.VMEM((16, 128), full)],
    )
    out_pieces = [out_pieces[0]] + [
        swap(out_pieces[index], "tensor", index) for index in range(1, QUARTERS)
    ]
    layer_out, layer_token = call(
        layer_kernel,
        (((width_part, own_tokens), low),),
        lane_word,
        token_rank,
        *out_pieces,
        words=1,
        deps=[kept_token] if direct else [],
        time=0.1,
        token=True,
        scratch=[pltpu.VMEM((8, width), full), pltpu.VMEM((width, 8), full)],
    )
    rows_part = width // owners
    if direct:
        shrink_grad, expand_grad, total_token = call(
            total_kernel,
            (((rows_part, ff_part), full),) * 2,
            feed_kept,
            feed_got,
            deps=[layer_token],
            time=0.8,
            token=True,
        )
        entry_got, entry_kept, _ = join_sums(entry_kept, entry_got, [total_token])
        entry_grad, output_grad = call(
            total_kernel,
            (((3, rows_part, width_part), full), ((rows_part, width_part), full)),
            entry_kept,
            entry_got,
            time=0.8,
        )
    else:
        totals = [
            sum_owners(
                jnp.concatenate(
                    [
                        dot(jnp.concatenate(lhs), jnp.concatenate(rhs), ((0,), (0,)))
                        for lhs, rhs in pairs
                    ],
                    axis=1,
                )
                .astype(low)
                .reshape(owners, rows_part, -1)
            )
            for pairs in feed_groups + entry_groups
        ]
        shrink_grad, expand_grad, entry_grad = totals
        output_grad = entry_grad[:, 3 * width_part :]
        entry_grad = entry_grad[:, : 3 * width_part].reshape(rows_part, 3, width_part)
        entry_grad = jnp.transpose(entry_grad, (1, 0, 2))

    return (
        layer_out.T,
        kept_grad.T,
        mask_grad,
        condition_grad,
        modulate_grad,
        jnp.transpose(entry_grad, (1, 0, 2)),
        output_grad.T,
        expand_grad,
        shrink_grad.T,
    )


def solution(mesh):
    return jax.shard_map(
        body,
        mesh=mesh,
        in_specs=(
            P("dp", "tensor"),
            P("dp"),
            P("dp"),
            P("dp"),
            P(),
            P("dp", None),
            P("tensor", None),
            P(None, None, "tensor"),
            P("tensor", None),
            P(None, "tensor"),
            P("tensor", None),
            P("dp", None),
        ),
        out_specs=(
            P("dp", "tensor"),
            P("dp", "tensor"),
            P("dp"),
            P("dp", "tensor"),
            P("tensor", "dp"),
            P("dp", None, "tensor"),
            P("tensor", "dp"),
            P("dp", "tensor"),
            P("tensor", "dp"),
        ),
        check_vma=False,
    )
```

```python
from functools import partial

import jax
import jax.numpy as jnp
from jax import lax
from jax.experimental import pallas as pl
from jax.experimental.pallas import tpu as pltpu
from jax.sharding import PartitionSpec as P

HEAD = 72
QUARTERS = 4
SPARE = 8
scale = HEAD ** (-0.5)
epsilon = 1e-06
gelu_coeff = 0.7978845608028654
low = jnp.bfloat16
full = jnp.float32
VMEM_ASK = 12 * 1024 * 1024
RIDERS = 48
SWAP_OWNERS = 8
FEED_SPLIT = 72
ENTRY_SPLIT = 72
FAR = (6, 7, 4, 5)
NEAR = (2, 3, 1, 0)
JOIN_TIME = 0.1
KEPT_TIME = 0.1
TOTAL_TIME = 14.0
HALVE_TIME = 0.35
BACK_TIME = 0.1
SMALL = pl.BlockSpec(memory_space=pltpu.SMEM)
PLAIN = pl.BlockSpec(memory_space=pltpu.VMEM)


def dot(a, b, dims=((1,), (0,))):
    return lax.dot_general(a, b, (dims, ((), ())), preferred_element_type=full)


def normalize(rows):
    centered = rows - jnp.mean(rows, axis=-1, keepdims=True)
    inverse = lax.rsqrt(jnp.mean(centered * centered, axis=-1, keepdims=True) + epsilon)
    return (centered * inverse, inverse)


def normalize_back(unit, inverse, grad):
    return inverse * (
        grad
        - jnp.mean(grad, axis=-1, keepdims=True)
        - unit * jnp.mean(grad * unit, axis=-1, keepdims=True)
    )


def gelu_both(value):
    square = value * value
    curve = jnp.tanh(gelu_coeff * (value + 0.044715 * square * value))
    slope = 0.5 * (1.0 + curve) + 0.5 * value * (1.0 - curve * curve) * gelu_coeff * (
        1.0 + 3.0 * 0.044715 * square
    )
    return (0.5 * value * (1.0 + curve), slope)


def swap(value, axis, bit):
    size = lax.axis_size(axis)
    return lax.ppermute(value, axis, [(index, index ^ bit) for index in range(size)])


def swap_pair(pieces):
    came = swap(jnp.stack(pieces), "tensor", 2)
    return came[0], swap(came[1], "tensor", 1)


def gather_blocks(own):
    near = swap(own, "tensor", 1)
    across = swap(own, "tensor", 2)
    return [own, near, across, swap(across, "tensor", 1)]


def sum_far(part_2, part_3, deps=()):
    got = swap(part_3, "tensor", 1)
    far, token = call(
        add_kernel, ((part_2.shape, low),), part_2, got, deps=deps, time=0.1, token=True
    )
    return far, swap(far, "tensor", 2), turn(token)


def sum_owners(total):
    owners, rows, columns = total.shape
    me = lax.axis_index("dp")
    step = 1
    while step < owners:
        pairs = total.reshape(-1, 2, rows, columns)
        mine = (me // step) % 2
        given = lax.dynamic_index_in_dim(pairs, 1 - mine, 1, keepdims=False)
        kept = lax.dynamic_index_in_dim(pairs, mine, 1, keepdims=False)
        total = kept.astype(full) + swap(given, "dp", step).astype(full)
        step *= 2
        total = total if step == owners else total.astype(low)
    return total[0]


def part_shapes(count, upper, lower, columns):
    return [((count, upper, columns), low), ((count, lower, columns), low)]


def start_sums(groups, split, deps=(), time=3.0, bases=()):
    width = groups[0][0][0][0].shape[1]
    columns = sum(rhs[0].shape[1] for _, rhs in groups[0])
    rows = width // 8
    shapes = part_shapes(4 * len(groups), split, rows - split, columns)
    counts = [[(len(lhs), len(rhs)) for lhs, rhs in pairs] for pairs in groups]
    given_0, given_1, kept_0, kept_1, token = call(
        partial(weight_kernel, counts, len(bases)),
        shapes + shapes,
        lax.axis_index("dp").reshape(1).astype(jnp.int32),
        *[value for pairs in groups for lhs, rhs in pairs for value in (*lhs, *rhs)],
        *bases,
        words=1,
        deps=deps,
        time=time,
        scratch=[pltpu.VMEM((width, columns), full)],
        token=True,
    )
    return (given_0, given_1), (kept_0, kept_1), token


def cross(given, first, second):
    return swap(given[0], "dp", first), swap(given[1], "dp", second)


def halve_sums(kept, got, deps=(), time=0.1):
    count, _, columns = kept[0].shape
    shapes = part_shapes(count // 2, kept[0].shape[1], kept[1].shape[1], columns)
    given_0, given_1, kept_0, kept_1, token = call(
        halve_kernel,
        shapes + shapes,
        lax.axis_index("dp").reshape(1).astype(jnp.int32),
        *kept,
        *got,
        words=1,
        deps=deps,
        time=time,
        token=True,
    )
    return (given_0, given_1), (kept_0, kept_1), token


def join_sums(kept, got, deps=()):
    count, _, columns = kept[0].shape
    shape = ((count // 2, kept[0].shape[1] + kept[1].shape[1], columns), low)
    given, kept, token = call(
        join_kernel,
        (shape, shape),
        lax.axis_index("dp").reshape(1).astype(jnp.int32),
        *kept,
        *got,
        words=1,
        deps=deps,
        time=JOIN_TIME,
        token=True,
    )
    return swap(given, "dp", 4), kept, token


def exchange_owners(slabs):
    if isinstance(slabs, dict):
        return {index: swap(slab, "dp", index) if index else slab for index, slab in slabs.items()}
    return [lax.all_to_all(slabs[0], "dp", split_axis=0, concat_axis=0, tiled=True)]


def attend(projected_ref, bias_ref, output_ref, attended_ref, chunk, half, width_part):
    span = slice(chunk * half, (chunk + 1) * half)
    pieces = []
    for head in range(width_part // HEAD):
        at = head * HEAD
        queries = projected_ref[span, at : at + HEAD]
        keys = projected_ref[:, width_part + at : width_part + at + HEAD]
        values = projected_ref[:, 2 * width_part + at : 2 * width_part + at + HEAD]
        scores = dot(queries, keys, ((1,), (1,))) * scale + bias_ref[span, :]
        spread = jnp.exp(scores - jnp.max(scores, axis=1, keepdims=True))
        probs = spread * (1.0 / jnp.sum(spread, axis=1, keepdims=True))
        pieces.append(dot(probs.astype(low), values))
    attended = jnp.concatenate(pieces, axis=1).astype(low)
    attended_ref[...] = attended
    return dot(attended, output_ref[...])


def entry_kernel(
    lane_ref,
    big_ref,
    piece_0,
    piece_1,
    piece_2,
    piece_3,
    mask_ref,
    entry_ref,
    bias_ref,
    output_ref,
    chosen_ref,
    spatial_ref,
    normed_ref,
    projected_ref,
    attended_ref,
    part_0,
    part_1,
    gathered,
    table,
):
    lane = lane_ref[0]
    block, width = spatial_ref.shape
    width_part = width // QUARTERS
    group = block - SPARE
    half = 2 * block
    pieces = (piece_0, piece_1, piece_2, piece_3)
    for index, piece in enumerate(pieces):
        at = pl.multiple_of((lane ^ index) * width_part, 16)
        gathered[pl.ds(at, width_part), :] = piece[:width_part, :]
    summed = pieces[0][width_part:, :].astype(full)
    for piece in pieces[1:]:
        summed = summed + piece[width_part:, :].astype(full)
    span = summed.shape[1]
    steps = summed.shape[0] // QUARTERS
    for row in range(QUARTERS):
        for step in range(steps):
            from_row = row * steps + step
            table[row : row + 1, step * span : (step + 1) * span] = summed[from_row : from_row + 1]
    for index in range(QUARTERS):
        row = jnp.where(big_ref[0] == 1, 0, lane ^ index)
        chosen_ref[index : index + 1, :] = table[pl.ds(row, 1), : 6 * width]
    row_id = lax.broadcasted_iota(jnp.int32, (group, group), 0)
    column_id = lax.broadcasted_iota(jnp.int32, (group, group), 1)
    eye = (row_id == column_id).astype(full).astype(low)
    spare_id = lax.broadcasted_iota(jnp.int32, (SPARE, width), 0)
    spare = jnp.where(spare_id == 0, mask_ref[...].astype(full), 0.0)
    for chunk in (1, 0):
        span = slice(chunk * half, (chunk + 1) * half)
        normed = []
        for index in (2 * chunk, 2 * chunk + 1):
            at = pl.multiple_of((lane ^ index) * group, 128)
            kept = dot(eye, gathered[:, pl.ds(at, group)], ((1,), (1,)))
            rows = jnp.concatenate([kept, spare], axis=0)
            if index == 0:
                spatial_ref[...] = rows.astype(low)
            unit, inverse = normalize(rows)
            shift = chosen_ref[index : index + 1, :width]
            gain = chosen_ref[index : index + 1, width : 2 * width]
            normed.append(unit * (1.0 + gain) + shift)
        normed = jnp.concatenate(normed, axis=0).astype(low)
        normed_ref[span, :] = normed
        projected_ref[span, :] = dot(normed, entry_ref[...], ((1,), (1,))).astype(low)
    part = attend(projected_ref, bias_ref, output_ref, attended_ref, 1, half, width_part)
    part_0[...] = part[:block].astype(low)
    part_1[...] = part[block:].astype(low)


def attend_kernel(projected_ref, bias_ref, output_ref, attended_ref, part_0, part_1):
    block = part_0.shape[0]
    part = attend(
        projected_ref, bias_ref, output_ref, attended_ref, 0, 2 * block, output_ref.shape[0]
    )
    part_0[...] = part[:block].astype(low)
    part_1[...] = part[block:].astype(low)


def middle_kernel(
    part_0, part_1, part_2, spatial_ref, chosen_ref, branch_ref, middle_ref, normed_ref
):
    width = spatial_ref.shape[1]
    branch = part_0[...].astype(full) + part_1[...].astype(full) + part_2[...].astype(full)
    branch_ref[...] = branch
    middle = spatial_ref[...].astype(full) + chosen_ref[0:1, 2 * width : 3 * width] * branch
    middle_ref[...] = middle
    unit, inverse = normalize(middle)
    shift = chosen_ref[0:1, 3 * width : 4 * width]
    gain = chosen_ref[0:1, 4 * width : 5 * width]
    normed_ref[...] = (unit * (1.0 + gain) + shift).astype(low)


def feed_kernel(
    piece_0,
    piece_1,
    back_ref,
    expand_ref,
    normed_ref,
    activated_ref,
    hidden_grad_ref,
    part_0,
    part_1,
):
    block = piece_0.shape[0]
    normed = jnp.concatenate([piece_0[...].astype(full), piece_1[...].astype(full)], axis=0)
    normed = normed.astype(low)
    normed_ref[...] = normed
    hidden = dot(normed, expand_ref[...])
    activated, slope = gelu_both(hidden)
    activated_ref[...] = activated.astype(low)
    hidden_grad = (back_ref[...] * slope).astype(low)
    hidden_grad_ref[...] = hidden_grad
    part = dot(hidden_grad, expand_ref[...], ((1,), (1,)))
    part_0[...] = part[:block].astype(low)
    part_1[...] = part[block:].astype(low)


def middle_back_kernel(
    part_0,
    part_1,
    part_2,
    middle_ref,
    branch_ref,
    upstream_ref,
    chosen_ref,
    middle_grad_ref,
    branch_grad_ref,
    sums_ref,
):
    width = middle_ref.shape[1]
    normed_grad = part_0[...].astype(full) + part_1[...].astype(full) + part_2[...].astype(full)
    unit, inverse = normalize(middle_ref[...])
    gain = chosen_ref[0:1, 4 * width : 5 * width]
    middle_grad = upstream_ref[...] + normalize_back(unit, inverse, normed_grad * (1.0 + gain))
    middle_grad_ref[...] = middle_grad
    branch_grad_ref[...] = (chosen_ref[0:1, 2 * width : 3 * width] * middle_grad).astype(low)
    sums_ref[0:1, :] = jnp.sum(middle_grad * branch_ref[...], axis=0, keepdims=True)
    sums_ref[1:2, :] = jnp.sum(normed_grad, axis=0, keepdims=True)
    sums_ref[2:3, :] = jnp.sum(normed_grad * unit, axis=0, keepdims=True)


def probs_kernel(projected_ref, bias_ref, probs_ref):
    width_part = projected_ref.shape[1] // 3
    for head in range(width_part // HEAD):
        at = head * HEAD
        queries = projected_ref[:, at : at + HEAD]
        keys = projected_ref[:, width_part + at : width_part + at + HEAD]
        scores = dot(keys, queries, ((1,), (1,))) * scale + bias_ref[...]
        spread = jnp.exp(scores - jnp.max(scores, axis=0, keepdims=True))
        probs = spread * (1.0 / jnp.sum(spread, axis=0, keepdims=True))
        probs_ref[head] = probs.astype(low)


def attend_back_kernel(
    projected_ref,
    probs_ref,
    output_ref,
    piece_0,
    piece_1,
    piece_2,
    piece_3,
    branch_grad_ref,
    grad_ref,
):
    rows, width_all = projected_ref.shape
    width_part = width_all // 3
    block = piece_0.shape[0]
    half = 2 * block
    for chunk, pair in enumerate(((piece_0, piece_1), (piece_2, piece_3))):
        branch_grad_ref[chunk * half : (chunk + 1) * half, :] = jnp.concatenate(
            [piece[...].astype(full) for piece in pair], axis=0
        ).astype(low)
    attended_grad = dot(branch_grad_ref[...], output_ref[...], ((1,), (1,))).astype(low)
    pieces = [[], [], []]
    for head in range(width_part // HEAD):
        at = head * HEAD
        queries = projected_ref[:, at : at + HEAD]
        keys = projected_ref[:, width_part + at : width_part + at + HEAD]
        values = projected_ref[:, 2 * width_part + at : 2 * width_part + at + HEAD]
        grad = attended_grad[:, at : at + HEAD]
        probs = probs_ref[head]
        pieces[2].append(dot(probs, grad))
        probs = probs.astype(full)
        prob_grad = dot(values, grad, ((1,), (1,)))
        delta = jnp.sum(probs * prob_grad, axis=0, keepdims=True)
        score_grad = (probs * (prob_grad - delta)).astype(low)
        pieces[1].append(dot(score_grad, queries) * scale)
        pieces[0].append(dot(score_grad, keys, ((0,), (0,))) * scale)
    grad_ref[...] = jnp.concatenate(pieces[0] + pieces[1] + pieces[2], axis=1).astype(low)


def entry_back_kernel(chunk, grad_ref, entry_ref, part_0, part_1):
    block = part_0.shape[0]
    part = dot(grad_ref[2 * chunk * block : 2 * (chunk + 1) * block, :], entry_ref[...])
    part_0[...] = part[:block].astype(low)
    part_1[...] = part[block:].astype(low)


def pack_kernel(owners, chosen, me_ref, kept_ref, owner_ref, position_ref, riders_ref, *out_refs):
    slot_ref = out_refs[-1]
    extra, capacity = riders_ref.shape
    kept_count = kept_ref.shape[1]
    owner_local = owner_ref[...] ^ me_ref[0]
    owner_id = lax.broadcasted_iota(jnp.int32, (owners, kept_count), 0)
    hot = (owner_id == owner_local).astype(full)
    row_id = lax.broadcasted_iota(jnp.int32, (kept_count, kept_count), 0)
    column_id = lax.broadcasted_iota(jnp.int32, (kept_count, kept_count), 1)
    before = dot(hot.astype(low), (row_id < column_id).astype(full).astype(low))
    rank = jnp.sum(hot * before, axis=0, keepdims=True).astype(jnp.int32)
    slot = owner_local * capacity + rank
    slot_ref[...] = slot
    coded = position_ref[...] + 1
    tag_id = lax.broadcasted_iota(jnp.int32, (extra, kept_count), 0)
    tags = jnp.where(tag_id == 0, coded >> 5, jnp.where(tag_id == 1, coded & 31, 0))
    rows = jnp.concatenate([kept_ref[...], tags.astype(full).astype(low)], axis=0)
    slot_id = lax.broadcasted_iota(jnp.int32, (capacity, kept_count), 0)
    for number, index in enumerate(chosen):
        matrix = (slot_id + index * capacity == slot).astype(full).astype(low)
        slab = dot(rows, matrix, ((1,), (1,)))
        split = kept_ref.shape[0]
        slab = jnp.concatenate([slab[:split], slab[split:] + riders_ref[...].astype(full)], axis=0)
        if len(out_refs) == 2:
            out_refs[0][me_ref[0] ^ index] = slab.astype(low)
        else:
            out_refs[number][...] = slab.astype(low)


def unpack_kernel(owners, me_ref, *refs):
    slab_refs, outs = refs[:-5], refs[-5:]
    compact_ref, slot_rank_ref, token_rank_ref, lifted_ref, arrived = outs
    table_ref, slab_refs = slab_refs[0], slab_refs[1:]
    arrived_count = compact_ref.shape[1]
    width_part = compact_ref.shape[0] - table_ref.shape[0]
    slots_all = arrived.shape[1]
    own_tokens = token_rank_ref.shape[1]
    capacity = slots_all // owners
    for index in range(owners):
        if len(slab_refs) == 1:
            slab = slab_refs[0][me_ref[0] ^ index]
        else:
            slab = slab_refs[(FAR + NEAR).index(index)][...]
        arrived[:, index * capacity : (index + 1) * capacity] = slab
    tags = arrived[width_part : width_part + 16, :].astype(full)
    place = tags[0:1] * 32.0 + tags[1:2] - 1.0
    turned = jnp.transpose(jnp.broadcast_to(place, (8, slots_all)))[:, 0:1]
    turned = jnp.where(turned < 0.0, 1e9, turned)
    slot_rank = jnp.sum(jnp.where(turned < place, 1.0, 0.0), axis=0, keepdims=True)
    slot_rank = jnp.where(place < 0.0, -1.0, slot_rank).astype(jnp.int32)
    slot_rank_ref[...] = slot_rank
    rank_id = lax.broadcasted_iota(jnp.int32, (arrived_count, slots_all), 0)
    matrix = (rank_id == slot_rank).astype(full).astype(low)
    compact_ref[:width_part, :] = dot(arrived[:width_part, :], matrix, ((1,), (1,))).astype(low)
    compact_ref[width_part:, :] = table_ref[...]
    spot = lax.broadcasted_iota(jnp.int32, (1, own_tokens), 1).astype(full)
    token_rank = jnp.sum(jnp.where(turned < spot, 1.0, 0.0), axis=0, keepdims=True)
    filled = jnp.sum(jnp.where(turned == spot, 1.0, 0.0), axis=0, keepdims=True)
    token_rank_ref[...] = jnp.where(filled > 0.0, token_rank, -1.0).astype(jnp.int32)
    if len(slab_refs) > 1:
        chunks = lifted_ref.shape[1] // capacity
        for index in range(owners):
            for row in range(QUARTERS):
                for chunk in range(chunks):
                    lifted_ref[
                        index * QUARTERS + row : index * QUARTERS + row + 1,
                        chunk * capacity : (chunk + 1) * capacity,
                    ] = tags[
                        2 + row * chunks + chunk : 3 + row * chunks + chunk,
                        index * capacity : (index + 1) * capacity,
                    ]
    else:
        lifted_ref[...] = jnp.zeros_like(lifted_ref)


def back_kernel(
    lane_ref,
    part_0,
    part_1,
    part_2,
    spatial_ref,
    middle_grad_ref,
    chosen_ref,
    sums_ref,
    feed_0,
    feed_1,
    feed_2,
    upstream_ref,
    piece_0,
    piece_1,
    piece_2,
    piece_3,
    turned,
    riders,
):
    lane = lane_ref[0]
    block, width = spatial_ref.shape
    group = block - SPARE
    width_part = width // QUARTERS
    normed_grad = part_0[...].astype(full) + part_1[...].astype(full) + part_2[...].astype(full)
    unit, inverse = normalize(spatial_ref[...].astype(full))
    gain = chosen_ref[0:1, width : 2 * width]
    grad = middle_grad_ref[...] + normalize_back(unit, inverse, normed_grad * (1.0 + gain))
    turned[...] = jnp.transpose(grad[:group]).astype(low)
    feed = feed_0[...].astype(full) + feed_1[...].astype(full) + feed_2[...].astype(full)
    mask_sum = grad[group : group + 1]
    mask_high = mask_sum.astype(low).astype(full)
    fields = [
        jnp.sum(normed_grad, axis=0, keepdims=True),
        jnp.sum(normed_grad * unit, axis=0, keepdims=True),
        sums_ref[0:1, :],
        sums_ref[1:2, :],
        sums_ref[2:3, :],
        jnp.sum(feed * upstream_ref[...], axis=0, keepdims=True),
        mask_high,
        mask_sum - mask_high,
    ]
    chunks = width // 128
    riders[...] = jnp.zeros_like(riders)
    for number, field in enumerate(fields):
        for chunk in range(chunks):
            at = number * chunks + chunk
            riders[at : at + 1, :] = field[:, chunk * 128 : (chunk + 1) * 128]
    rider_rows = riders[...].astype(low)
    for index, piece in enumerate((piece_0, piece_1, piece_2, piece_3)):
        at = pl.multiple_of((lane ^ index) * width_part, 16)
        piece[:width_part, :] = turned[pl.ds(at, width_part), :]
        piece[width_part:, :] = rider_rows


def slots_kernel(
    owners,
    lane_ref,
    me_ref,
    big_ref,
    rank_ref,
    piece_0,
    piece_1,
    piece_2,
    piece_3,
    slabs_ref,
    table_ref,
    table,
    mask_total,
):
    lane = lane_ref[0]
    me = me_ref[0]
    group = piece_0.shape[1]
    slots_all = rank_ref.shape[1]
    capacity = slots_all // owners
    chunks = table_ref.shape[1]
    width_part = slabs_ref.shape[1] - RIDERS
    pieces = [piece_0, piece_1, piece_2, piece_3]
    rows = jnp.concatenate([piece[:width_part, :] for piece in pieces], axis=1)
    row_id = lax.broadcasted_iota(jnp.int32, (group, slots_all), 0)
    matrix = jnp.concatenate(
        [
            (row_id + (lane ^ index) * group == rank_ref[...]).astype(full).astype(low)
            for index in range(QUARTERS)
        ],
        axis=0,
    )
    slots = dot(rows, matrix)
    table[...] = jnp.zeros_like(table)
    summed = jnp.zeros((chunks, 128), full)
    mask_sum = jnp.zeros((16, 128), full)
    mask_rows = chunks // 6
    for index, piece in enumerate(pieces):
        field = piece[width_part : width_part + chunks, :].astype(full)
        summed = summed + field
        rest = piece[width_part + chunks - chunks % 16 :, :].astype(full)
        table[lane ^ index, :chunks, :] = field
        at = chunks % 16
        mask_sum = mask_sum + jnp.concatenate(
            [
                rest[at : at + mask_rows] + rest[at + mask_rows : at + 2 * mask_rows],
                jnp.zeros((16 - mask_rows, 128), full),
            ],
            axis=0,
        )
    mask_total[...] = mask_sum

    @pl.when(big_ref[0] == 1)
    def _():
        table[...] = jnp.zeros_like(table)
        table[0, :chunks, :] = summed

    table_ref[...] = table[:, :chunks, :].astype(low)
    for index in range(owners):
        owner = me ^ index
        start = (owner * chunks) // owners
        fields = [table[row, pl.ds(start, 8), :] for row in range(QUARTERS)]
        mask_start = (owner * mask_rows) // owners
        mask_part = mask_total[pl.ds(mask_start, 2), :]
        mask_high = mask_part.astype(low).astype(full)
        fields += [mask_high, mask_part - mask_high, jnp.zeros((RIDERS - 36, 128), full)]
        slab = jnp.concatenate([slots[:, index * capacity : (index + 1) * capacity]] + fields, axis=0)
        slabs_ref[owner] = slab.astype(low)


def kept_kernel(
    owners, me_ref, slot_ref, lifted_ref, slabs_ref, kept_ref, modulate_ref, mask_ref, table
):
    width_part, kept_count = kept_ref.shape
    capacity = slabs_ref.shape[2]
    table_part = modulate_ref.shape[1]
    mask_part = mask_ref.shape[1]
    me = me_ref[0]
    slabs = [slabs_ref[me ^ index] for index in range(owners)]
    rows = jnp.concatenate([slab[:width_part] for slab in slabs], axis=1)
    slot_id = lax.broadcasted_iota(jnp.int32, (owners * capacity, kept_count), 0)
    matrix = (slot_id == slot_ref[...]).astype(full).astype(low)
    kept_ref[...] = dot(rows, matrix).astype(low)
    mask_sum = jnp.zeros((1, 256), full)
    for index, slab in enumerate(slabs):
        rider = slab[width_part:].astype(full)
        for row in range(QUARTERS):
            at = index * QUARTERS + row
            for chunk in range(8):
                from_row = row * 8 + chunk
                table[at : at + 1, chunk * 128 : (chunk + 1) * 128] = rider[
                    from_row : from_row + 1
                ]
        high, rest = rider[32:34], rider[34:36]
        both = high + rest
        mask_sum = mask_sum + jnp.concatenate([both[0:1], both[1:2]], axis=1)
    shift = (me * table_part) % 128
    field = pltpu.roll(table[...], (1024 - shift) % 1024, 1)[:, :table_part]
    lifted = lifted_ref[...].astype(low)[:, :width_part]
    modulate_ref[...] = dot(lifted, field.astype(low), ((0,), (0,)))
    shift = (me * mask_part) % 128
    mask_sum = jnp.broadcast_to(mask_sum, (8, 256))
    mask_ref[...] = pltpu.roll(mask_sum, (256 - shift) % 256, 1)[0:1, :mask_part]


def out_kernel(
    lane_ref,
    part_0,
    part_1,
    part_2,
    middle_ref,
    chosen_ref,
    piece_0,
    piece_1,
    piece_2,
    piece_3,
    turned,
    riders,
):
    lane = lane_ref[0]
    block, width = middle_ref.shape
    group = block - SPARE
    width_part = width // QUARTERS
    feed = part_0[...].astype(full) + part_1[...].astype(full) + part_2[...].astype(full)
    out = middle_ref[...] + chosen_ref[0:1, 5 * width : 6 * width] * feed
    turned[...] = jnp.transpose(out[:group]).astype(low)
    riders[...] = jnp.zeros_like(riders)
    for chunk in range(width // 128):
        riders[chunk : chunk + 1, :] = out[group : group + 1, chunk * 128 : (chunk + 1) * 128]
    rider_rows = riders[...].astype(low)
    for index, piece in enumerate((piece_0, piece_1, piece_2, piece_3)):
        at = pl.multiple_of((lane ^ index) * width_part, 16)
        piece[:width_part, :] = turned[pl.ds(at, width_part), :]
        piece[width_part:, :] = rider_rows


def layer_kernel(
    lane_ref, rank_ref, piece_0, piece_1, piece_2, piece_3, out_ref, spare, turned
):
    lane = lane_ref[0]
    width_part, own_tokens = out_ref.shape
    group = piece_0.shape[1]
    quarter = own_tokens // QUARTERS
    pieces = (piece_0, piece_1, piece_2, piece_3)
    rows = jnp.concatenate([piece[:width_part, :] for piece in pieces], axis=1)
    row_id = lax.broadcasted_iota(jnp.int32, (group, own_tokens), 0)
    matrix = jnp.concatenate(
        [
            (row_id + (lane ^ index) * group == rank_ref[...]).astype(full).astype(low)
            for index in range(QUARTERS)
        ],
        axis=0,
    )
    spare[...] = jnp.zeros_like(spare)
    for index, piece in enumerate(pieces):
        rider = piece[width_part:, :].astype(full)
        for chunk in range(spare.shape[1] // 128):
            spare[index : index + 1, chunk * 128 : (chunk + 1) * 128] = rider[chunk : chunk + 1]
    turned[...] = jnp.transpose(spare[...])
    columns = turned[pl.ds(pl.multiple_of(lane * width_part, 16), width_part), :].astype(low)
    spare_id = lax.broadcasted_iota(jnp.int32, (8, own_tokens), 0)
    spot = lax.broadcasted_iota(jnp.int32, (8, own_tokens), 1) // quarter
    empty = rank_ref[...] < 0
    spots = jnp.where(((spare_id ^ lane) == spot) & (spare_id < QUARTERS) & empty, 1.0, 0.0)
    out_ref[...] = (dot(rows, matrix) + dot(columns, spots.astype(low))).astype(low)


def table_kernel(big_ref, lifted_ref, modulate_ref, table_ref, bias_ref, turned_ref, table):
    span = table_ref.shape[1]
    steps = table_ref.shape[0] // QUARTERS
    table[...] = jnp.zeros_like(table)
    table[:QUARTERS, : modulate_ref.shape[1]] = dot(lifted_ref[...], modulate_ref[...])
    table_ref[...] = jnp.concatenate(
        [
            table[row : row + 1, step * span : (step + 1) * span]
            for row in range(QUARTERS)
            for step in range(steps)
        ],
        axis=0,
    ).astype(low)
    rows = bias_ref.shape[0]
    block = rows // QUARTERS
    group = block - SPARE
    big = big_ref[0] == 1
    spare_small = jnp.log(jnp.full((1, 1), float(group), full))
    spare_big = jnp.log(jnp.full((1, 1), float(QUARTERS * group), full))

    def bias_of(query, key):
        query_block, key_block, key_inner = query // block, key // block, key % block
        small = jnp.where(key_inner < group, 0.0, jnp.where(key_inner == group, spare_small, -1e30))
        small = jnp.where(query_block == key_block, small, -1e30)
        large = jnp.where(key_inner < group, 0.0, jnp.where(key == group, spare_big, -1e30))
        return jnp.where(big, large, small)

    row_id = lax.broadcasted_iota(jnp.int32, (rows, rows), 0)
    column_id = lax.broadcasted_iota(jnp.int32, (rows, rows), 1)
    bias_ref[...] = bias_of(row_id, column_id)
    turned_ref[...] = bias_of(column_id, row_id)


def add_kernel(left_ref, right_ref, out_ref):
    out_ref[...] = (left_ref[...].astype(full) + right_ref[...].astype(full)).astype(low)


def copy_kernel(*refs):
    for index in range(len(refs) // 2):
        refs[len(refs) // 2 + index][...] = refs[index][...]


def upstream_kernel(
    lane_ref,
    rank_ref,
    chosen_ref,
    cotangent_ref,
    shrink_ref,
    grad_near,
    grad_far,
    upstream_ref,
    back_near,
    back_far,
):
    lane = lane_ref[0]
    block, width = upstream_ref.shape
    own_tokens = rank_ref.shape[1]
    group = block - SPARE
    rank = rank_ref[...]
    row_id = lax.broadcasted_iota(jnp.int32, (group, own_tokens), 0)
    spare_id = lax.broadcasted_iota(jnp.int32, (SPARE, own_tokens), 0)
    spot = lax.broadcasted_iota(jnp.int32, (SPARE, own_tokens), 1) // (own_tokens // QUARTERS)
    for chunk, back, grad_ref in ((0, back_near, grad_near), (1, back_far, grad_far)):
        matrix = []
        for index in (2 * chunk, 2 * chunk + 1):
            matrix.append(jnp.where(row_id + (lane ^ index) * group == rank, 1.0, 0.0))
            matrix.append(
                jnp.where((spare_id == 0) & (spot == (lane ^ index)) & (rank < 0), 1.0, 0.0)
            )
        upstream = dot(jnp.concatenate(matrix, axis=0).astype(low), cotangent_ref[...])
        if chunk == 0:
            upstream_ref[...] = upstream[:block]
        gates = [chosen_ref[index : index + 1, 5 * width :] for index in (2 * chunk, 2 * chunk + 1)]
        feed_grad = jnp.concatenate(
            [gates[0] * upstream[:block], gates[1] * upstream[block:]], axis=0
        ).astype(low)
        grad_ref[...] = feed_grad
        back[...] = dot(feed_grad, shrink_ref[...], ((1,), (1,)))


def feed_out_kernel(near_ref, far_ref, shrink_ref, part_0, part_1, part_2, part_3):
    block = part_0.shape[0]
    for activated, pair in ((far_ref, (part_2, part_3)), (near_ref, (part_0, part_1))):
        part = dot(activated[...], shrink_ref[...])
        pair[0][...] = part[:block].astype(low)
        pair[1][...] = part[block:].astype(low)


def partial_kernel(lhs_0, rhs_0, lhs_1, rhs_1, out_0, out_1):
    for lhs, rhs, out in ((lhs_0, rhs_0, out_0), (lhs_1, rhs_1, out_1)):
        chunk = lhs.shape[1] // 3
        for number in range(3):
            span = slice(number * chunk, (number + 1) * chunk)
            out[span, :] = dot(lhs[:, span], rhs[...], ((0,), (0,))).astype(low)


def weight_kernel(counts, bases, me_ref, *refs):
    given_0, given_1, kept_0, kept_1, product = refs[-5:]
    operands = list(refs[:-5])
    base_refs = [operands.pop() for _ in range(bases)][::-1]
    rows = given_0.shape[1] + given_1.shape[1]
    chunk = product.shape[0] // 3
    for group, pairs in enumerate(counts):
        products = []
        for lefts, rights in pairs:
            lhs = [operands.pop(0) for _ in range(lefts)]
            right = jnp.concatenate([operands.pop(0)[...] for _ in range(rights)], axis=0)
            products.append((lhs, right))
        for number in range(3):
            span = slice(number * chunk, (number + 1) * chunk)
            parts = [
                dot(jnp.concatenate([ref[:, span] for ref in lhs], axis=0), right, ((0,), (0,)))
                for lhs, right in products
            ]
            value = jnp.concatenate(parts, axis=1)
            if bases:
                value = value + base_refs[group][span, :].astype(full)
            product[span, :] = value
        for bit, start, given, kept in (
            (0, 0, given_0, kept_0),
            (1, given_0.shape[1], given_1, kept_1),
        ):
            mine = (me_ref[0] >> bit) & 1
            for index in range(4):
                for value, ref in ((1 - mine, given), (mine, kept)):
                    above = (index >> bit) << (bit + 1)
                    at = (above + (value << bit) + (index & bit)) * rows + start
                    at = pl.multiple_of(at, 8)
                    ref[4 * group + index] = product[pl.ds(at, ref.shape[1]), :].astype(low)


def halve_kernel(
    me_ref, held_0, held_1, got_0, got_1, given_0, given_1, kept_0, kept_1
):
    for bit, held, got, given, kept in (
        (1, held_0, got_0, given_0, kept_0),
        (0, held_1, got_1, given_1, kept_1),
    ):
        mine = (me_ref[0] >> bit) & 1
        for index in range(given.shape[0]):
            for value, ref in ((1 - mine, given), (mine, kept)):
                at = 2 * index + value
                ref[index] = (held[at].astype(full) + got[at].astype(full)).astype(low)


def join_kernel(me_ref, held_0, held_1, got_0, got_1, given, kept):
    mine = (me_ref[0] >> 2) & 1
    for index in range(given.shape[0]):
        for value, ref in ((1 - mine, given), (mine, kept)):
            at = 2 * index + value
            upper = held_0[at].astype(full) + got_0[at].astype(full)
            lower = held_1[at].astype(full) + got_1[at].astype(full)
            ref[index] = jnp.concatenate([upper, lower], axis=0).astype(low)


def total_kernel(held_ref, got_ref, *out_refs):
    if len(out_refs[0].shape) == 2:
        for index, out_ref in enumerate(out_refs):
            out_ref[...] = held_ref[index].astype(full) + got_ref[index].astype(full)
        return
    entry_ref, output_ref = out_refs
    total = held_ref[0].astype(full) + got_ref[0].astype(full)
    parts, _, columns = entry_ref.shape
    for index in range(parts):
        entry_ref[index] = total[:, index * columns : (index + 1) * columns]
    output_ref[...] = total[:, parts * columns :]


def call(
    kernel, outs, *operands, words=0, deps=(), time=1.0, scratch=(), token=False, loose=False
):
    count = len(operands)
    deps = tuple(deps)
    outs = tuple(outs)
    if token:
        outs += (((8, 128), full),)

    def run(*refs):
        outs_at = count + len(deps)
        rest = list(refs[outs_at:])
        if token:
            last = rest.pop(len(outs) - 1)
            last[...] = jnp.zeros_like(last)
        kernel(*refs[:count], *rest)

    return pl.pallas_call(
        run,
        out_shape=tuple(jax.ShapeDtypeStruct(shape, kind) for shape, kind in outs),
        in_specs=[SMALL] * words
        + [pl.BlockSpec() if loose else PLAIN] * (count - words)
        + [pl.BlockSpec(memory_space=pl.ANY)] * len(deps),
        scratch_shapes=list(scratch),
        compiler_params=pltpu.CompilerParams(vmem_limit_bytes=VMEM_ASK),
        cost_estimate=pl.CostEstimate(
            flops=int(time * 1.15e9), bytes_accessed=1024, transcendentals=0
        ),
    )(*operands, *deps)


def turn(token):
    return swap(token, "tensor", 1)


def body(
    kept_rows,
    owner_index,
    kept_position,
    resolution,
    mask_token,
    condition,
    modulate_weight,
    entry_weight,
    output_weight,
    expand_weight,
    shrink_weight,
    cotangent,
):
    owners = lax.axis_size("dp")
    me = lax.axis_index("dp")
    lane = lax.axis_index("tensor")
    kept_count, width_part = kept_rows.shape
    width = mask_token.shape[0]
    own_tokens = cotangent.shape[0]
    ff_part = expand_weight.shape[1]
    quarter = own_tokens // QUARTERS
    group = quarter // 2
    arrived_count = own_tokens // 2
    block = group + SPARE
    rows = QUARTERS * block
    capacity = 2 * kept_count // owners
    slots_all = owners * capacity
    direct = owners == SWAP_OWNERS
    lane_word = lane.reshape(1).astype(jnp.int32)
    me_word = me.reshape(1).astype(jnp.int32)
    big_word = resolution[:1]
    context_part = lax.dynamic_slice_in_dim(
        condition.astype(full), lane * width_part, width_part, 1
    )
    lifted = jax.nn.silu(context_part).astype(low)
    if direct:
        padded = -(-width_part // capacity) * capacity
        riders = jnp.pad(lifted, ((0, 0), (0, padded - width_part))).reshape(-1, capacity)
    else:
        padded = 128
        riders = lifted.reshape(-1, capacity)
    rider_count = riders.shape[0]
    extra = -(-(rider_count + 2) // 16) * 16
    riders = jnp.pad(riders, ((2, extra - 2 - rider_count), (0, 0)))
    slab_rows = width_part + extra
    slab_shape = (slab_rows, capacity)
    if not direct:
        slab_shape = (owners,) + slab_shape
    *slabs, slot_index = call(
        partial(pack_kernel, owners, FAR + NEAR if direct else range(owners)),
        ((slab_shape, low),) * (owners if direct else 1) + (((1, kept_count), jnp.int32),),
        me_word,
        kept_rows.T,
        owner_index[None, :],
        kept_position[None, :],
        riders,
        words=1,
        time=1.0,
        loose=direct,
    )

    steps = -(-6 * width // arrived_count)
    table, bias, bias_turned = call(
        table_kernel,
        (
            ((QUARTERS * steps, arrived_count), low),
            ((rows, rows), full),
            ((rows, rows), full),
        ),
        big_word,
        lifted,
        modulate_weight,
        words=1,
        deps=[slot_index],
        time=2.0,
        scratch=[pltpu.VMEM((8, steps * arrived_count), full)],
    )
    if direct:
        slabs = exchange_owners(dict(zip(FAR + NEAR, slabs)))
        slabs = list(slabs.values())
    else:
        slabs = exchange_owners(slabs)
    compact, slot_rank, token_rank, lifted_all = call(
        partial(unpack_kernel, owners),
        (
            ((width_part + QUARTERS * steps, arrived_count), low),
            ((1, slots_all), jnp.int32),
            ((1, own_tokens), jnp.int32),
            ((owners * QUARTERS, padded), full),
        ),
        me_word,
        table,
        *slabs,
        words=1,
        time=2.4,
        scratch=[pltpu.VMEM((slab_rows, slots_all), low)],
    )
    if not direct:
        owner_order = jnp.arange(owners, dtype=jnp.int32) ^ me
        lifted_all = slabs[0][:, width_part + 2 : width_part + 2 + rider_count]
        lifted_all = lifted_all.reshape(owners * QUARTERS, width_part)
    spatial_pieces = gather_blocks(compact)
    entry_flat = jnp.transpose(entry_weight, (1, 2, 0)).reshape(3 * width_part, width)
    token_shape = ((block, width), low)
    half = 2 * block
    chosen, spatial_own, normed_one, projected, attended_far, part_2, part_3 = call(
        entry_kernel,
        (
            ((QUARTERS, 6 * width), full),
            token_shape,
            ((rows, width), low),
            ((rows, 3 * width_part), low),
            ((half, width_part), low),
            token_shape,
            token_shape,
        ),
        lane_word,
        big_word,
        *spatial_pieces,
        mask_token[None, :],
        entry_flat,
        bias,
        output_weight,
        words=2,
        time=5.0,
        scratch=[
            pltpu.VMEM((width, arrived_count), low),
            pltpu.VMEM((8, steps * arrived_count), full),
        ],
    )
    far, across, start = sum_far(part_2, part_3)
    attended_near, part_0, part_1 = call(
        attend_kernel,
        (((half, width_part), low), token_shape, token_shape),
        projected,
        bias,
        output_weight,
        deps=[start],
        time=3.0,
    )
    got = swap(part_1, "tensor", 1)
    feed_grad_near, feed_grad_far, upstream_own, back_near, back_far = call(
        upstream_kernel,
        (
            ((half, width), low),
            ((half, width), low),
            ((block, width), full),
            ((half, width), full),
            ((half, width), full),
        ),
        lane_word,
        token_rank,
        chosen,
        cotangent,
        shrink_weight,
        words=1,
        deps=[part_1],
        time=3.6,
    )
    branch, middle, normed_two_own = call(
        middle_kernel,
        (((block, width), full), ((block, width), full), token_shape),
        part_0,
        got,
        across,
        spatial_own,
        chosen,
        deps=[back_far],
        time=0.6,
    )

    def feed_call(piece_0, piece_1, back, *deps):
        return call(
            feed_kernel,
            (((half, width), low), ((half, width), low), ((half, width), low))
            + (token_shape, token_shape),
            piece_0,
            piece_1,
            back,
            expand_weight,
            deps=deps,
            time=2.4,
        )

    near_piece = swap(normed_two_own, "tensor", 1)
    across = swap(normed_two_own, "tensor", 2)
    normed_near, activated_near, hidden_near, part_0, part_1 = feed_call(
        normed_two_own, near_piece, back_near
    )
    *partials, event = call(
        partial_kernel,
        (((width, ff_part), low),) * 2,
        feed_grad_near,
        activated_near,
        normed_near,
        hidden_near,
        time=2.5,
        token=True,
    )
    (across,) = call(copy_kernel, (token_shape,), across, deps=[event], time=0.3)
    last_piece = swap(across, "tensor", 1)
    normed_far, activated_far, hidden_far, part_2, part_3 = feed_call(
        across, last_piece, back_far
    )
    feed_groups = [
        [([feed_grad_far], [activated_far])],
        [([normed_far], [hidden_far])],
    ]
    event = part_0
    if direct:
        feed_given, feed_kept, event = start_sums(feed_groups, FEED_SPLIT, (), 3.5, partials)
        feed_got = cross(feed_given, 1, 2)
    far, across, start = sum_far(part_2, part_3, [event])
    got = swap(part_1, "tensor", 1)
    middle_grad, branch_grad_own, sums, start = call(
        middle_back_kernel,
        (((block, width), full), token_shape, ((SPARE, width), full)),
        part_0,
        got,
        across,
        middle,
        branch,
        upstream_own,
        chosen,
        deps=[start],
        time=0.7,
        token=True,
    )
    branch_pieces = gather_blocks(branch_grad_own)
    feed_parts = call(
        feed_out_kernel,
        (token_shape,) * QUARTERS,
        activated_near,
        activated_far,
        shrink_weight,
        deps=[turn(start)],
        time=0.1,
    )
    feed_far = swap(feed_parts[3], "tensor", 1)
    feed_near = swap(feed_parts[1], "tensor", 1)
    feed_far, start = call(
        add_kernel,
        (token_shape,),
        feed_parts[2],
        feed_far,
        deps=[branch_pieces[2]],
        time=0.1,
        token=True,
    )
    (probs,) = call(
        probs_kernel,
        (((width_part // HEAD, rows, rows), low),),
        projected,
        bias_turned,
        deps=[feed_far],
        time=0.1,
    )
    branch_grad, projected_grad, event = call(
        attend_back_kernel,
        (((rows, width), low), ((rows, 3 * width_part), low)),
        projected,
        probs,
        output_weight,
        *branch_pieces,
        deps=[turn(start)],
        time=0.1,
        token=True,
    )
    feed_across = swap(feed_far, "tensor", 2)
    if direct:
        feed_given, feed_kept, event = halve_sums(feed_kept, feed_got, [event])
        feed_got = cross(feed_given, 2, 1)
    part_2, part_3 = call(
        partial(entry_back_kernel, 1),
        (token_shape, token_shape),
        projected_grad,
        entry_flat,
        deps=[feed_across, feed_near, event],
        time=0.1,
    )
    far, across, start = sum_far(part_2, part_3)
    part_0, part_1 = call(
        partial(entry_back_kernel, 0),
        (token_shape, token_shape),
        projected_grad,
        entry_flat,
        deps=[start],
        time=0.2,
    )
    got = swap(part_1, "tensor", 1)
    entry_groups = [
        [([normed_one], [projected_grad]), ([branch_grad], [attended_near, attended_far])]
    ]
    event = part_1
    if direct:
        entry_given, entry_kept, event = start_sums(entry_groups, ENTRY_SPLIT, [got], 0.2)
        entry_got = cross(entry_given, 1, 2)
        feed_got, feed_kept, event = join_sums(feed_kept, feed_got, [event])
    *back_pieces, back_token = call(
        back_kernel,
        (((width_part + 80, group), low),) * QUARTERS,
        lane_word,
        part_0,
        got,
        across,
        spatial_own,
        middle_grad,
        chosen,
        sums,
        feed_parts[0],
        feed_near,
        feed_across,
        upstream_own,
        words=1,
        deps=[event],
        time=BACK_TIME,
        token=True,
        scratch=[pltpu.VMEM((width, group), low), pltpu.VMEM((80, 128), full)],
    )
    back_pieces = [
        back_pieces[0],
        swap(back_pieces[1], "tensor", 1),
        *swap_pair(back_pieces[2:]),
    ]
    chunks = 6 * width // 128
    logistic = jax.nn.sigmoid(context_part)
    logistic = logistic * (1.0 + context_part * (1.0 - logistic))
    if direct:
        entry_given, entry_kept, halved = halve_sums(entry_kept, entry_got, [back_token], HALVE_TIME)
        entry_got = cross(entry_given, 2, 1)
        shrink_grad, expand_grad, total_token = call(
            total_kernel,
            (((width // owners, ff_part), full),) * 2,
            feed_kept,
            feed_got,
            deps=[halved],
            time=TOTAL_TIME,
            token=True,
        )
        slabs, table_grad, event = call(
            partial(slots_kernel, owners),
            (
                ((owners, width_part + RIDERS, capacity), low),
                ((QUARTERS, chunks, 128), low),
            ),
            lane_word,
            me_word,
            big_word,
            slot_rank,
            *back_pieces,
            words=3,
            time=0.1,
            token=True,
            scratch=[
                pltpu.VMEM((QUARTERS, chunks + 2, 128), full),
                pltpu.VMEM((16, 128), full),
            ],
        )
        (slabs,) = exchange_owners([slabs])
        table_grad = table_grad.reshape(QUARTERS, 6 * width)
        entry_got, entry_kept, event = join_sums(entry_kept, entry_got, [total_token])
        out_pieces = call(
            out_kernel,
            (((width_part + 16, group), low),) * QUARTERS,
            lane_word,
            feed_parts[0],
            feed_near,
            feed_across,
            middle,
            chosen,
            words=1,
            deps=[event],
            time=0.1,
            scratch=[pltpu.VMEM((width, group), low), pltpu.VMEM((16, 128), full)],
        )
        out_pieces = [
            out_pieces[0],
            swap(out_pieces[1], "tensor", 1),
            *swap_pair(out_pieces[2:]),
        ]
        layer_out, layer_token = call(
            layer_kernel,
            (((width_part, own_tokens), low),),
            lane_word,
            token_rank,
            *out_pieces,
            words=1,
            deps=[event],
            time=0.1,
            token=True,
            scratch=[pltpu.VMEM((8, width), full), pltpu.VMEM((width, 8), full)],
        )
        kept_grad, modulate_grad, mask_grad, kept_token = call(
            partial(kept_kernel, owners),
            (
                ((width_part, kept_count), low),
                ((width_part, 6 * width // owners), full),
                ((1, width // owners), full),
            ),
            me_word,
            slot_index,
            lifted_all,
            slabs,
            words=1,
            deps=[layer_token],
            time=KEPT_TIME,
            token=True,
            scratch=[pltpu.VMEM((owners * QUARTERS, 1024), full)],
        )
        mask_grad = mask_grad[0]
    else:
        event = back_pieces[1]
        rows_back = jnp.concatenate([piece[:width_part] for piece in back_pieces], axis=1)
        rank_ids = jnp.arange(arrived_count, dtype=jnp.int32)
        rank_ids = ((rank_ids // group) ^ lane) * group + rank_ids % group
        matrix = (rank_ids[:, None] == slot_rank).astype(low)
        slabs = dot(rows_back, matrix).astype(low).reshape(width_part, owners, capacity)
        slabs = jnp.take(jnp.transpose(slabs, (1, 0, 2)), owner_order, axis=0)
        slabs = jnp.take(exchange_owners([slabs])[0], owner_order, axis=0)
        slabs = jnp.transpose(slabs, (1, 0, 2)).reshape(width_part, slots_all)
        slot_ids = jnp.arange(slots_all, dtype=jnp.int32)[:, None]
        kept_grad = dot(slabs, (slot_ids == slot_index).astype(low)).astype(low)
        riders = jnp.stack(
            [piece[width_part : width_part + 8 * width // 128] for piece in back_pieces]
        )
        riders = riders.reshape(QUARTERS, 8, width).astype(full)
        mask_total = jnp.sum(riders[:, 6] + riders[:, 7], axis=0)
        table_local = riders[:, :6].reshape(QUARTERS, 6 * width)
        table_small = jnp.take(table_local, jnp.arange(QUARTERS, dtype=jnp.int32) ^ lane, axis=0)
        first = jnp.arange(QUARTERS, dtype=jnp.int32)[:, None] == 0
        table_big = jnp.where(first, jnp.sum(table_local, axis=0, keepdims=True), 0.0)
        table_grad = jnp.where(big_word[0] == 1, table_big, table_small).astype(low)
        sent = jnp.transpose(table_grad.reshape(QUARTERS, owners, -1), (1, 0, 2))
        table_all = exchange_owners([sent])[0].reshape(owners * QUARTERS, -1)
        modulate_grad = dot(lifted_all, table_all, ((0,), (0,)))
        mask_grad = lax.psum_scatter(mask_total, "dp", scatter_dimension=0, tiled=True)
    condition_grad = dot(table_grad, modulate_weight, ((1,), (1,))) * logistic
    if not direct:
        out_pieces = call(
            out_kernel,
            (((width_part + 16, group), low),) * QUARTERS,
            lane_word,
            feed_parts[0],
            feed_near,
            feed_across,
            middle,
            chosen,
            words=1,
            deps=[],
            time=0.1,
            scratch=[pltpu.VMEM((width, group), low), pltpu.VMEM((16, 128), full)],
        )
        out_pieces = [
            out_pieces[0],
            swap(out_pieces[1], "tensor", 1),
            *swap_pair(out_pieces[2:]),
        ]
        layer_out, layer_token = call(
            layer_kernel,
            (((width_part, own_tokens), low),),
            lane_word,
            token_rank,
            *out_pieces,
            words=1,
            deps=[],
            time=0.1,
            token=True,
            scratch=[pltpu.VMEM((8, width), full), pltpu.VMEM((width, 8), full)],
        )
    rows_part = width // owners
    if direct:
        entry_grad, output_grad = call(
            total_kernel,
            (((3, rows_part, width_part), full), ((rows_part, width_part), full)),
            entry_kept,
            entry_got,
            deps=[kept_token],
            time=0.8,
        )
    else:
        totals = [
            sum_owners(
                jnp.concatenate(
                    [
                        dot(jnp.concatenate(lhs), jnp.concatenate(rhs), ((0,), (0,)))
                        for lhs, rhs in pairs
                    ],
                    axis=1,
                )
                .astype(low)
                .reshape(owners, rows_part, -1)
            )
            for pairs in feed_groups + entry_groups
        ]
        shrink_grad, expand_grad, entry_grad = totals
        output_grad = entry_grad[:, 3 * width_part :]
        entry_grad = entry_grad[:, : 3 * width_part].reshape(rows_part, 3, width_part)
        entry_grad = jnp.transpose(entry_grad, (1, 0, 2))

    return (
        layer_out.T,
        kept_grad.T,
        mask_grad,
        condition_grad,
        modulate_grad,
        jnp.transpose(entry_grad, (1, 0, 2)),
        output_grad.T,
        expand_grad,
        shrink_grad.T,
    )


def solution(mesh):
    return jax.shard_map(
        body,
        mesh=mesh,
        in_specs=(
            P("dp", "tensor"),
            P("dp"),
            P("dp"),
            P("dp"),
            P(),
            P("dp", None),
            P("tensor", None),
            P(None, None, "tensor"),
            P("tensor", None),
            P(None, "tensor"),
            P("tensor", None),
            P("dp", None),
        ),
        out_specs=(
            P("dp", "tensor"),
            P("dp", "tensor"),
            P("dp"),
            P("dp", "tensor"),
            P("tensor", "dp"),
            P("dp", None, "tensor"),
            P("tensor", "dp"),
            P("dp", "tensor"),
            P("tensor", "dp"),
        ),
        check_vma=False,
    )
```

```python
from functools import partial

import jax
import jax.numpy as jnp
from jax import lax
from jax.experimental import pallas as pl
from jax.experimental.pallas import tpu as pltpu
from jax.sharding import PartitionSpec as P

HEAD = 72
QUARTERS = 4
SPARE = 8
scale = HEAD ** (-0.5)
epsilon = 1e-06
gelu_coeff = 0.7978845608028654
low = jnp.bfloat16
full = jnp.float32
VMEM_ASK = 12 * 1024 * 1024
RIDERS = 48
SWAP_OWNERS = 8
FEED_SPLIT = 72
ENTRY_SPLIT = 72
FAR = (6, 7, 4, 5)
NEAR = (2, 3, 1, 0)
JOIN_TIME = 0.1
KEPT_TIME = 0.1
TOTAL_TIME = 14.0
HALVE_TIME = 0.35
BACK_TIME = 0.1
SMALL = pl.BlockSpec(memory_space=pltpu.SMEM)
PLAIN = pl.BlockSpec(memory_space=pltpu.VMEM)


def dot(a, b, dims=((1,), (0,))):
    return lax.dot_general(a, b, (dims, ((), ())), preferred_element_type=full)


def normalize(rows):
    centered = rows - jnp.mean(rows, axis=-1, keepdims=True)
    inverse = lax.rsqrt(jnp.mean(centered * centered, axis=-1, keepdims=True) + epsilon)
    return (centered * inverse, inverse)


def normalize_back(unit, inverse, grad):
    return inverse * (
        grad
        - jnp.mean(grad, axis=-1, keepdims=True)
        - unit * jnp.mean(grad * unit, axis=-1, keepdims=True)
    )


def gelu_both(value):
    square = value * value
    curve = jnp.tanh(gelu_coeff * (value + 0.044715 * square * value))
    slope = 0.5 * (1.0 + curve) + 0.5 * value * (1.0 - curve * curve) * gelu_coeff * (
        1.0 + 3.0 * 0.044715 * square
    )
    return (0.5 * value * (1.0 + curve), slope)


def swap(value, axis, bit):
    size = lax.axis_size(axis)
    return lax.ppermute(value, axis, [(index, index ^ bit) for index in range(size)])


def swap_pair(pieces):
    came = swap(jnp.stack(pieces), "tensor", 2)
    return came[0], swap(came[1], "tensor", 1)


def gather_blocks(own):
    near = swap(own, "tensor", 1)
    across = swap(own, "tensor", 2)
    return [own, near, across, swap(across, "tensor", 1)]


def sum_far(part_2, part_3, deps=()):
    got = swap(part_3, "tensor", 1)
    far, token = call(
        add_kernel, ((part_2.shape, low),), part_2, got, deps=deps, time=0.1, token=True
    )
    return far, swap(far, "tensor", 2), turn(token)


def sum_owners(total):
    owners, rows, columns = total.shape
    me = lax.axis_index("dp")
    step = 1
    while step < owners:
        pairs = total.reshape(-1, 2, rows, columns)
        mine = (me // step) % 2
        given = lax.dynamic_index_in_dim(pairs, 1 - mine, 1, keepdims=False)
        kept = lax.dynamic_index_in_dim(pairs, mine, 1, keepdims=False)
        total = kept.astype(full) + swap(given, "dp", step).astype(full)
        step *= 2
        total = total if step == owners else total.astype(low)
    return total[0]


def part_shapes(count, upper, lower, columns):
    return [((count, upper, columns), low), ((count, lower, columns), low)]


def start_sums(groups, split, deps=(), time=3.0, bases=()):
    width = groups[0][0][0][0].shape[1]
    columns = sum(rhs[0].shape[1] for _, rhs in groups[0])
    rows = width // 8
    shapes = part_shapes(4 * len(groups), split, rows - split, columns)
    counts = [[(len(lhs), len(rhs)) for lhs, rhs in pairs] for pairs in groups]
    given_0, given_1, kept_0, kept_1, token = call(
        partial(weight_kernel, counts, len(bases)),
        shapes + shapes,
        lax.axis_index("dp").reshape(1).astype(jnp.int32),
        *[value for pairs in groups for lhs, rhs in pairs for value in (*lhs, *rhs)],
        *bases,
        words=1,
        deps=deps,
        time=time,
        scratch=[pltpu.VMEM((width, columns), full)],
        token=True,
    )
    return (given_0, given_1), (kept_0, kept_1), token


def cross(given, first, second):
    return swap(given[0], "dp", first), swap(given[1], "dp", second)


def halve_sums(kept, got, deps=(), time=0.1):
    count, _, columns = kept[0].shape
    shapes = part_shapes(count // 2, kept[0].shape[1], kept[1].shape[1], columns)
    given_0, given_1, kept_0, kept_1, token = call(
        halve_kernel,
        shapes + shapes,
        lax.axis_index("dp").reshape(1).astype(jnp.int32),
        *kept,
        *got,
        words=1,
        deps=deps,
        time=time,
        token=True,
    )
    return (given_0, given_1), (kept_0, kept_1), token


def join_sums(kept, got, deps=()):
    count, _, columns = kept[0].shape
    shape = ((count // 2, kept[0].shape[1] + kept[1].shape[1], columns), low)
    given, kept, token = call(
        join_kernel,
        (shape, shape),
        lax.axis_index("dp").reshape(1).astype(jnp.int32),
        *kept,
        *got,
        words=1,
        deps=deps,
        time=JOIN_TIME,
        token=True,
    )
    return swap(given, "dp", 4), kept, token


def exchange_owners(slabs):
    if isinstance(slabs, dict):
        return {index: swap(slab, "dp", index) if index else slab for index, slab in slabs.items()}
    return [lax.all_to_all(slabs[0], "dp", split_axis=0, concat_axis=0, tiled=True)]


def attend(projected_ref, bias_ref, output_ref, attended_ref, chunk, half, width_part):
    span = slice(chunk * half, (chunk + 1) * half)
    pieces = []
    for head in range(width_part // HEAD):
        at = head * HEAD
        queries = projected_ref[span, at : at + HEAD]
        keys = projected_ref[:, width_part + at : width_part + at + HEAD]
        values = projected_ref[:, 2 * width_part + at : 2 * width_part + at + HEAD]
        scores = dot(queries, keys, ((1,), (1,))) * scale + bias_ref[span, :]
        spread = jnp.exp(scores - jnp.max(scores, axis=1, keepdims=True))
        probs = spread * (1.0 / jnp.sum(spread, axis=1, keepdims=True))
        pieces.append(dot(probs.astype(low), values))
    attended = jnp.concatenate(pieces, axis=1).astype(low)
    attended_ref[...] = attended
    return dot(attended, output_ref[...])


def entry_kernel(
    lane_ref,
    big_ref,
    piece_0,
    piece_1,
    piece_2,
    piece_3,
    mask_ref,
    entry_ref,
    bias_ref,
    output_ref,
    chosen_ref,
    spatial_ref,
    normed_ref,
    projected_ref,
    attended_ref,
    part_0,
    part_1,
    gathered,
    table,
):
    lane = lane_ref[0]
    block, width = spatial_ref.shape
    width_part = width // QUARTERS
    group = block - SPARE
    half = 2 * block
    pieces = (piece_0, piece_1, piece_2, piece_3)
    for index, piece in enumerate(pieces):
        at = pl.multiple_of((lane ^ index) * width_part, 16)
        gathered[pl.ds(at, width_part), :] = piece[:width_part, :]
    summed = pieces[0][width_part:, :].astype(full)
    for piece in pieces[1:]:
        summed = summed + piece[width_part:, :].astype(full)
    span = summed.shape[1]
    steps = summed.shape[0] // QUARTERS
    for row in range(QUARTERS):
        for step in range(steps):
            from_row = row * steps + step
            table[row : row + 1, step * span : (step + 1) * span] = summed[from_row : from_row + 1]
    for index in range(QUARTERS):
        row = jnp.where(big_ref[0] == 1, 0, lane ^ index)
        chosen_ref[index : index + 1, :] = table[pl.ds(row, 1), : 6 * width]
    row_id = lax.broadcasted_iota(jnp.int32, (group, group), 0)
    column_id = lax.broadcasted_iota(jnp.int32, (group, group), 1)
    eye = (row_id == column_id).astype(full).astype(low)
    spare_id = lax.broadcasted_iota(jnp.int32, (SPARE, width), 0)
    spare = jnp.where(spare_id == 0, mask_ref[...].astype(full), 0.0)
    for chunk in (1, 0):
        span = slice(chunk * half, (chunk + 1) * half)
        normed = []
        for index in (2 * chunk, 2 * chunk + 1):
            at = pl.multiple_of((lane ^ index) * group, 128)
            kept = dot(eye, gathered[:, pl.ds(at, group)], ((1,), (1,)))
            rows = jnp.concatenate([kept, spare], axis=0)
            if index == 0:
                spatial_ref[...] = rows.astype(low)
            unit, inverse = normalize(rows)
            shift = chosen_ref[index : index + 1, :width]
            gain = chosen_ref[index : index + 1, width : 2 * width]
            normed.append(unit * (1.0 + gain) + shift)
        normed = jnp.concatenate(normed, axis=0).astype(low)
        normed_ref[span, :] = normed
        projected_ref[span, :] = dot(normed, entry_ref[...], ((1,), (1,))).astype(low)
    part = attend(projected_ref, bias_ref, output_ref, attended_ref, 1, half, width_part)
    part_0[...] = part[:block].astype(low)
    part_1[...] = part[block:].astype(low)


def attend_kernel(projected_ref, bias_ref, output_ref, attended_ref, part_0, part_1):
    block = part_0.shape[0]
    part = attend(
        projected_ref, bias_ref, output_ref, attended_ref, 0, 2 * block, output_ref.shape[0]
    )
    part_0[...] = part[:block].astype(low)
    part_1[...] = part[block:].astype(low)


def middle_kernel(
    part_0, part_1, part_2, spatial_ref, chosen_ref, branch_ref, middle_ref, normed_ref
):
    width = spatial_ref.shape[1]
    branch = part_0[...].astype(full) + part_1[...].astype(full) + part_2[...].astype(full)
    branch_ref[...] = branch
    middle = spatial_ref[...].astype(full) + chosen_ref[0:1, 2 * width : 3 * width] * branch
    middle_ref[...] = middle
    unit, inverse = normalize(middle)
    shift = chosen_ref[0:1, 3 * width : 4 * width]
    gain = chosen_ref[0:1, 4 * width : 5 * width]
    normed_ref[...] = (unit * (1.0 + gain) + shift).astype(low)


def feed_kernel(
    piece_0,
    piece_1,
    back_ref,
    expand_ref,
    normed_ref,
    activated_ref,
    hidden_grad_ref,
    part_0,
    part_1,
):
    block = piece_0.shape[0]
    normed = jnp.concatenate([piece_0[...].astype(full), piece_1[...].astype(full)], axis=0)
    normed = normed.astype(low)
    normed_ref[...] = normed
    hidden = dot(normed, expand_ref[...])
    activated, slope = gelu_both(hidden)
    activated_ref[...] = activated.astype(low)
    hidden_grad = (back_ref[...] * slope).astype(low)
    hidden_grad_ref[...] = hidden_grad
    part = dot(hidden_grad, expand_ref[...], ((1,), (1,)))
    part_0[...] = part[:block].astype(low)
    part_1[...] = part[block:].astype(low)


def middle_back_kernel(
    part_0,
    part_1,
    part_2,
    middle_ref,
    branch_ref,
    upstream_ref,
    chosen_ref,
    middle_grad_ref,
    branch_grad_ref,
    sums_ref,
):
    width = middle_ref.shape[1]
    normed_grad = part_0[...].astype(full) + part_1[...].astype(full) + part_2[...].astype(full)
    unit, inverse = normalize(middle_ref[...])
    gain = chosen_ref[0:1, 4 * width : 5 * width]
    middle_grad = upstream_ref[...] + normalize_back(unit, inverse, normed_grad * (1.0 + gain))
    middle_grad_ref[...] = middle_grad
    branch_grad_ref[...] = (chosen_ref[0:1, 2 * width : 3 * width] * middle_grad).astype(low)
    sums_ref[0:1, :] = jnp.sum(middle_grad * branch_ref[...], axis=0, keepdims=True)
    sums_ref[1:2, :] = jnp.sum(normed_grad, axis=0, keepdims=True)
    sums_ref[2:3, :] = jnp.sum(normed_grad * unit, axis=0, keepdims=True)


def probs_kernel(projected_ref, bias_ref, probs_ref):
    width_part = projected_ref.shape[1] // 3
    for head in range(width_part // HEAD):
        at = head * HEAD
        queries = projected_ref[:, at : at + HEAD]
        keys = projected_ref[:, width_part + at : width_part + at + HEAD]
        scores = dot(keys, queries, ((1,), (1,))) * scale + bias_ref[...]
        spread = jnp.exp(scores - jnp.max(scores, axis=0, keepdims=True))
        probs = spread * (1.0 / jnp.sum(spread, axis=0, keepdims=True))
        probs_ref[head] = probs.astype(low)


def attend_back_kernel(
    projected_ref,
    probs_ref,
    output_ref,
    piece_0,
    piece_1,
    piece_2,
    piece_3,
    branch_grad_ref,
    grad_ref,
):
    rows, width_all = projected_ref.shape
    width_part = width_all // 3
    block = piece_0.shape[0]
    half = 2 * block
    for chunk, pair in enumerate(((piece_0, piece_1), (piece_2, piece_3))):
        branch_grad_ref[chunk * half : (chunk + 1) * half, :] = jnp.concatenate(
            [piece[...].astype(full) for piece in pair], axis=0
        ).astype(low)
    attended_grad = dot(branch_grad_ref[...], output_ref[...], ((1,), (1,))).astype(low)
    pieces = [[], [], []]
    for head in range(width_part // HEAD):
        at = head * HEAD
        queries = projected_ref[:, at : at + HEAD]
        keys = projected_ref[:, width_part + at : width_part + at + HEAD]
        values = projected_ref[:, 2 * width_part + at : 2 * width_part + at + HEAD]
        grad = attended_grad[:, at : at + HEAD]
        probs = probs_ref[head]
        pieces[2].append(dot(probs, grad))
        probs = probs.astype(full)
        prob_grad = dot(values, grad, ((1,), (1,)))
        delta = jnp.sum(probs * prob_grad, axis=0, keepdims=True)
        score_grad = (probs * (prob_grad - delta)).astype(low)
        pieces[1].append(dot(score_grad, queries) * scale)
        pieces[0].append(dot(score_grad, keys, ((0,), (0,))) * scale)
    grad_ref[...] = jnp.concatenate(pieces[0] + pieces[1] + pieces[2], axis=1).astype(low)


def entry_back_kernel(chunk, grad_ref, entry_ref, part_0, part_1):
    block = part_0.shape[0]
    part = dot(grad_ref[2 * chunk * block : 2 * (chunk + 1) * block, :], entry_ref[...])
    part_0[...] = part[:block].astype(low)
    part_1[...] = part[block:].astype(low)


def pack_kernel(owners, chosen, shift, me_ref, kept_ref, spot_ref, riders_ref, *out_refs):
    slot_ref = out_refs[-1]
    extra, capacity = riders_ref.shape
    kept_count = kept_ref.shape[1]
    owner_local = (spot_ref[...] >> shift) ^ me_ref[0]
    owner_id = lax.broadcasted_iota(jnp.int32, (owners, kept_count), 0)
    hot = (owner_id == owner_local).astype(full)
    row_id = lax.broadcasted_iota(jnp.int32, (kept_count, kept_count), 0)
    column_id = lax.broadcasted_iota(jnp.int32, (kept_count, kept_count), 1)
    before = dot(hot.astype(low), (row_id < column_id).astype(full).astype(low))
    rank = jnp.sum(hot * before, axis=0, keepdims=True).astype(jnp.int32)
    slot = owner_local * capacity + rank
    slot_ref[...] = slot
    coded = (spot_ref[...] & ((1 << shift) - 1)) + 1
    tag_id = lax.broadcasted_iota(jnp.int32, (extra, kept_count), 0)
    tags = jnp.where(tag_id == 0, coded >> 5, jnp.where(tag_id == 1, coded & 31, 0))
    rows = jnp.concatenate([kept_ref[...], tags.astype(full).astype(low)], axis=0)
    slot_id = lax.broadcasted_iota(jnp.int32, (capacity, kept_count), 0)
    for number, index in enumerate(chosen):
        matrix = (slot_id + index * capacity == slot).astype(full).astype(low)
        slab = dot(rows, matrix, ((1,), (1,)))
        split = kept_ref.shape[0]
        slab = jnp.concatenate([slab[:split], slab[split:] + riders_ref[...].astype(full)], axis=0)
        if len(out_refs) == 2:
            out_refs[0][me_ref[0] ^ index] = slab.astype(low)
        else:
            out_refs[number][...] = slab.astype(low)


def places(owners, me_ref, slab_refs, arrived, width_part):
    slots_all = arrived.shape[1]
    capacity = slots_all // owners
    for index in range(owners):
        if len(slab_refs) == 1:
            slab = slab_refs[0][me_ref[0] ^ index]
        else:
            slab = slab_refs[(FAR + NEAR).index(index)][...]
        rows = arrived.shape[0]
        arrived[:, index * capacity : (index + 1) * capacity] = slab[slab.shape[0] - rows :]
    tags = arrived[width_part : width_part + 16, :].astype(full)
    place = tags[0:1] * 32.0 + tags[1:2] - 1.0
    turned = jnp.transpose(jnp.broadcast_to(place, (8, slots_all)))[:, 0:1]
    return tags, place, jnp.where(turned < 0.0, 1e9, turned)


def unpack_kernel(owners, me_ref, table_ref, *refs):
    slab_refs, (compact_ref, slot_rank_ref, arrived) = refs[:-3], refs[-3:]
    arrived_count = compact_ref.shape[1]
    width_part = compact_ref.shape[0] - table_ref.shape[0]
    _, place, turned = places(owners, me_ref, slab_refs, arrived, width_part)
    slot_rank = jnp.sum(jnp.where(turned < place, 1.0, 0.0), axis=0, keepdims=True)
    slot_rank = jnp.where(place < 0.0, -1.0, slot_rank).astype(jnp.int32)
    slot_rank_ref[...] = slot_rank
    rank_id = lax.broadcasted_iota(jnp.int32, (arrived_count, arrived.shape[1]), 0)
    matrix = (rank_id == slot_rank).astype(full).astype(low)
    compact_ref[:width_part, :] = dot(arrived[:width_part, :], matrix, ((1,), (1,))).astype(low)
    compact_ref[width_part:, :] = table_ref[...]


def spots_kernel(owners, me_ref, *refs):
    slab_refs, (token_rank_ref, lifted_ref, arrived) = refs[:-3], refs[-3:]
    own_tokens = token_rank_ref.shape[1]
    capacity = arrived.shape[1] // owners
    tags, _, turned = places(owners, me_ref, slab_refs, arrived, 0)
    spot = lax.broadcasted_iota(jnp.int32, (1, own_tokens), 1).astype(full)
    token_rank = jnp.sum(jnp.where(turned < spot, 1.0, 0.0), axis=0, keepdims=True)
    filled = jnp.sum(jnp.where(turned == spot, 1.0, 0.0), axis=0, keepdims=True)
    token_rank_ref[...] = jnp.where(filled > 0.0, token_rank, -1.0).astype(jnp.int32)
    if len(slab_refs) > 1:
        chunks = lifted_ref.shape[1] // capacity
        for index in range(owners):
            for row in range(QUARTERS):
                for chunk in range(chunks):
                    lifted_ref[
                        index * QUARTERS + row : index * QUARTERS + row + 1,
                        chunk * capacity : (chunk + 1) * capacity,
                    ] = tags[
                        2 + row * chunks + chunk : 3 + row * chunks + chunk,
                        index * capacity : (index + 1) * capacity,
                    ]
    else:
        lifted_ref[...] = jnp.zeros_like(lifted_ref)


def back_kernel(
    lane_ref,
    part_0,
    part_1,
    part_2,
    spatial_ref,
    middle_grad_ref,
    chosen_ref,
    sums_ref,
    feed_0,
    feed_1,
    feed_2,
    upstream_ref,
    piece_0,
    piece_1,
    piece_2,
    piece_3,
    turned,
    riders,
):
    lane = lane_ref[0]
    block, width = spatial_ref.shape
    group = block - SPARE
    width_part = width // QUARTERS
    normed_grad = part_0[...].astype(full) + part_1[...].astype(full) + part_2[...].astype(full)
    unit, inverse = normalize(spatial_ref[...].astype(full))
    gain = chosen_ref[0:1, width : 2 * width]
    grad = middle_grad_ref[...] + normalize_back(unit, inverse, normed_grad * (1.0 + gain))
    turned[...] = jnp.transpose(grad[:group]).astype(low)
    feed = feed_0[...].astype(full) + feed_1[...].astype(full) + feed_2[...].astype(full)
    mask_sum = grad[group : group + 1]
    mask_high = mask_sum.astype(low).astype(full)
    fields = [
        jnp.sum(normed_grad, axis=0, keepdims=True),
        jnp.sum(normed_grad * unit, axis=0, keepdims=True),
        sums_ref[0:1, :],
        sums_ref[1:2, :],
        sums_ref[2:3, :],
        jnp.sum(feed * upstream_ref[...], axis=0, keepdims=True),
        mask_high,
        mask_sum - mask_high,
    ]
    chunks = width // 128
    riders[...] = jnp.zeros_like(riders)
    for number, field in enumerate(fields):
        for chunk in range(chunks):
            at = number * chunks + chunk
            riders[at : at + 1, :] = field[:, chunk * 128 : (chunk + 1) * 128]
    rider_rows = riders[...].astype(low)
    for index, piece in enumerate((piece_0, piece_1, piece_2, piece_3)):
        at = pl.multiple_of((lane ^ index) * width_part, 16)
        piece[:width_part, :] = turned[pl.ds(at, width_part), :]
        piece[width_part:, :] = rider_rows


def slots_kernel(
    owners,
    lane_ref,
    me_ref,
    big_ref,
    rank_ref,
    piece_0,
    piece_1,
    piece_2,
    piece_3,
    slabs_ref,
    table_ref,
    table,
    mask_total,
):
    lane = lane_ref[0]
    me = me_ref[0]
    group = piece_0.shape[1]
    slots_all = rank_ref.shape[1]
    capacity = slots_all // owners
    chunks = table_ref.shape[1]
    width_part = slabs_ref.shape[1] - RIDERS
    pieces = [piece_0, piece_1, piece_2, piece_3]
    rows = jnp.concatenate([piece[:width_part, :] for piece in pieces], axis=1)
    row_id = lax.broadcasted_iota(jnp.int32, (group, slots_all), 0)
    matrix = jnp.concatenate(
        [
            (row_id + (lane ^ index) * group == rank_ref[...]).astype(full).astype(low)
            for index in range(QUARTERS)
        ],
        axis=0,
    )
    slots = dot(rows, matrix)
    table[...] = jnp.zeros_like(table)
    summed = jnp.zeros((chunks, 128), full)
    mask_sum = jnp.zeros((16, 128), full)
    mask_rows = chunks // 6
    for index, piece in enumerate(pieces):
        field = piece[width_part : width_part + chunks, :].astype(full)
        summed = summed + field
        rest = piece[width_part + chunks - chunks % 16 :, :].astype(full)
        table[lane ^ index, :chunks, :] = field
        at = chunks % 16
        mask_sum = mask_sum + jnp.concatenate(
            [
                rest[at : at + mask_rows] + rest[at + mask_rows : at + 2 * mask_rows],
                jnp.zeros((16 - mask_rows, 128), full),
            ],
            axis=0,
        )
    mask_total[...] = mask_sum

    @pl.when(big_ref[0] == 1)
    def _():
        table[...] = jnp.zeros_like(table)
        table[0, :chunks, :] = summed

    table_ref[...] = table[:, :chunks, :].astype(low)
    for index in range(owners):
        owner = me ^ index
        start = (owner * chunks) // owners
        fields = [table[row, pl.ds(start, 8), :] for row in range(QUARTERS)]
        mask_start = (owner * mask_rows) // owners
        mask_part = mask_total[pl.ds(mask_start, 2), :]
        mask_high = mask_part.astype(low).astype(full)
        fields += [mask_high, mask_part - mask_high, jnp.zeros((RIDERS - 36, 128), full)]
        slab = jnp.concatenate([slots[:, index * capacity : (index + 1) * capacity]] + fields, axis=0)
        slabs_ref[owner] = slab.astype(low)


def kept_kernel(
    owners, me_ref, slot_ref, lifted_ref, slabs_ref, kept_ref, modulate_ref, mask_ref, table
):
    width_part, kept_count = kept_ref.shape
    capacity = slabs_ref.shape[2]
    table_part = modulate_ref.shape[1]
    mask_part = mask_ref.shape[1]
    me = me_ref[0]
    slabs = [slabs_ref[me ^ index] for index in range(owners)]
    rows = jnp.concatenate([slab[:width_part] for slab in slabs], axis=1)
    slot_id = lax.broadcasted_iota(jnp.int32, (owners * capacity, kept_count), 0)
    matrix = (slot_id == slot_ref[...]).astype(full).astype(low)
    kept_ref[...] = dot(rows, matrix).astype(low)
    mask_sum = jnp.zeros((1, 256), full)
    for index, slab in enumerate(slabs):
        rider = slab[width_part:].astype(full)
        for row in range(QUARTERS):
            at = index * QUARTERS + row
            for chunk in range(8):
                from_row = row * 8 + chunk
                table[at : at + 1, chunk * 128 : (chunk + 1) * 128] = rider[
                    from_row : from_row + 1
                ]
        high, rest = rider[32:34], rider[34:36]
        both = high + rest
        mask_sum = mask_sum + jnp.concatenate([both[0:1], both[1:2]], axis=1)
    shift = (me * table_part) % 128
    field = pltpu.roll(table[...], (1024 - shift) % 1024, 1)[:, :table_part]
    lifted = lifted_ref[...].astype(low)[:, :width_part]
    modulate_ref[...] = dot(lifted, field.astype(low), ((0,), (0,)))
    shift = (me * mask_part) % 128
    mask_sum = jnp.broadcast_to(mask_sum, (8, 256))
    mask_ref[...] = pltpu.roll(mask_sum, (256 - shift) % 256, 1)[0:1, :mask_part]


def out_kernel(
    lane_ref,
    part_0,
    part_1,
    part_2,
    middle_ref,
    chosen_ref,
    piece_0,
    piece_1,
    piece_2,
    piece_3,
    turned,
    riders,
):
    lane = lane_ref[0]
    block, width = middle_ref.shape
    group = block - SPARE
    width_part = width // QUARTERS
    feed = part_0[...].astype(full) + part_1[...].astype(full) + part_2[...].astype(full)
    out = middle_ref[...] + chosen_ref[0:1, 5 * width : 6 * width] * feed
    turned[...] = jnp.transpose(out[:group]).astype(low)
    riders[...] = jnp.zeros_like(riders)
    for chunk in range(width // 128):
        riders[chunk : chunk + 1, :] = out[group : group + 1, chunk * 128 : (chunk + 1) * 128]
    rider_rows = riders[...].astype(low)
    for index, piece in enumerate((piece_0, piece_1, piece_2, piece_3)):
        at = pl.multiple_of((lane ^ index) * width_part, 16)
        piece[:width_part, :] = turned[pl.ds(at, width_part), :]
        piece[width_part:, :] = rider_rows


def layer_kernel(
    lane_ref, rank_ref, piece_0, piece_1, piece_2, piece_3, out_ref, spare, turned
):
    lane = lane_ref[0]
    width_part, own_tokens = out_ref.shape
    group = piece_0.shape[1]
    quarter = own_tokens // QUARTERS
    pieces = (piece_0, piece_1, piece_2, piece_3)
    rows = jnp.concatenate([piece[:width_part, :] for piece in pieces], axis=1)
    row_id = lax.broadcasted_iota(jnp.int32, (group, own_tokens), 0)
    matrix = jnp.concatenate(
        [
            (row_id + (lane ^ index) * group == rank_ref[...]).astype(full).astype(low)
            for index in range(QUARTERS)
        ],
        axis=0,
    )
    spare[...] = jnp.zeros_like(spare)
    for index, piece in enumerate(pieces):
        rider = piece[width_part:, :].astype(full)
        for chunk in range(spare.shape[1] // 128):
            spare[index : index + 1, chunk * 128 : (chunk + 1) * 128] = rider[chunk : chunk + 1]
    turned[...] = jnp.transpose(spare[...])
    columns = turned[pl.ds(pl.multiple_of(lane * width_part, 16), width_part), :].astype(low)
    spare_id = lax.broadcasted_iota(jnp.int32, (8, own_tokens), 0)
    spot = lax.broadcasted_iota(jnp.int32, (8, own_tokens), 1) // quarter
    empty = rank_ref[...] < 0
    spots = jnp.where(((spare_id ^ lane) == spot) & (spare_id < QUARTERS) & empty, 1.0, 0.0)
    out_ref[...] = (dot(rows, matrix) + dot(columns, spots.astype(low))).astype(low)


def table_kernel(big_ref, lifted_ref, modulate_ref, table_ref, bias_ref, turned_ref, table):
    span = table_ref.shape[1]
    steps = table_ref.shape[0] // QUARTERS
    table[...] = jnp.zeros_like(table)
    table[:QUARTERS, : modulate_ref.shape[1]] = dot(lifted_ref[...], modulate_ref[...])
    table_ref[...] = jnp.concatenate(
        [
            table[row : row + 1, step * span : (step + 1) * span]
            for row in range(QUARTERS)
            for step in range(steps)
        ],
        axis=0,
    ).astype(low)
    rows = bias_ref.shape[0]
    block = rows // QUARTERS
    group = block - SPARE
    big = big_ref[0] == 1
    spare_small = jnp.log(jnp.full((1, 1), float(group), full))
    spare_big = jnp.log(jnp.full((1, 1), float(QUARTERS * group), full))

    def bias_of(query, key):
        query_block, key_block, key_inner = query // block, key // block, key % block
        small = jnp.where(key_inner < group, 0.0, jnp.where(key_inner == group, spare_small, -1e30))
        small = jnp.where(query_block == key_block, small, -1e30)
        large = jnp.where(key_inner < group, 0.0, jnp.where(key == group, spare_big, -1e30))
        return jnp.where(big, large, small)

    row_id = lax.broadcasted_iota(jnp.int32, (rows, rows), 0)
    column_id = lax.broadcasted_iota(jnp.int32, (rows, rows), 1)
    bias_ref[...] = bias_of(row_id, column_id)
    turned_ref[...] = bias_of(column_id, row_id)


def add_kernel(left_ref, right_ref, out_ref):
    out_ref[...] = (left_ref[...].astype(full) + right_ref[...].astype(full)).astype(low)


def copy_kernel(*refs):
    for index in range(len(refs) // 2):
        refs[len(refs) // 2 + index][...] = refs[index][...]


def upstream_kernel(
    lane_ref,
    rank_ref,
    chosen_ref,
    cotangent_ref,
    shrink_ref,
    grad_near,
    grad_far,
    upstream_ref,
    back_near,
    back_far,
):
    lane = lane_ref[0]
    block, width = upstream_ref.shape
    own_tokens = rank_ref.shape[1]
    group = block - SPARE
    rank = rank_ref[...]
    row_id = lax.broadcasted_iota(jnp.int32, (group, own_tokens), 0)
    spare_id = lax.broadcasted_iota(jnp.int32, (SPARE, own_tokens), 0)
    spot = lax.broadcasted_iota(jnp.int32, (SPARE, own_tokens), 1) // (own_tokens // QUARTERS)
    for chunk, back, grad_ref in ((0, back_near, grad_near), (1, back_far, grad_far)):
        matrix = []
        for index in (2 * chunk, 2 * chunk + 1):
            matrix.append(jnp.where(row_id + (lane ^ index) * group == rank, 1.0, 0.0))
            matrix.append(
                jnp.where((spare_id == 0) & (spot == (lane ^ index)) & (rank < 0), 1.0, 0.0)
            )
        upstream = dot(jnp.concatenate(matrix, axis=0).astype(low), cotangent_ref[...])
        if chunk == 0:
            upstream_ref[...] = upstream[:block]
        gates = [chosen_ref[index : index + 1, 5 * width :] for index in (2 * chunk, 2 * chunk + 1)]
        feed_grad = jnp.concatenate(
            [gates[0] * upstream[:block], gates[1] * upstream[block:]], axis=0
        ).astype(low)
        grad_ref[...] = feed_grad
        back[...] = dot(feed_grad, shrink_ref[...], ((1,), (1,)))


def feed_out_kernel(near_ref, far_ref, shrink_ref, part_0, part_1, part_2, part_3):
    block = part_0.shape[0]
    for activated, pair in ((far_ref, (part_2, part_3)), (near_ref, (part_0, part_1))):
        part = dot(activated[...], shrink_ref[...])
        pair[0][...] = part[:block].astype(low)
        pair[1][...] = part[block:].astype(low)


def partial_kernel(lhs_0, rhs_0, lhs_1, rhs_1, out_0, out_1):
    for lhs, rhs, out in ((lhs_0, rhs_0, out_0), (lhs_1, rhs_1, out_1)):
        chunk = lhs.shape[1] // 3
        for number in range(3):
            span = slice(number * chunk, (number + 1) * chunk)
            out[span, :] = dot(lhs[:, span], rhs[...], ((0,), (0,))).astype(low)


def weight_kernel(counts, bases, me_ref, *refs):
    given_0, given_1, kept_0, kept_1, product = refs[-5:]
    operands = list(refs[:-5])
    base_refs = [operands.pop() for _ in range(bases)][::-1]
    rows = given_0.shape[1] + given_1.shape[1]
    chunk = product.shape[0] // 3
    for group, pairs in enumerate(counts):
        products = []
        for lefts, rights in pairs:
            lhs = [operands.pop(0) for _ in range(lefts)]
            right = jnp.concatenate([operands.pop(0)[...] for _ in range(rights)], axis=0)
            products.append((lhs, right))
        for number in range(3):
            span = slice(number * chunk, (number + 1) * chunk)
            parts = [
                dot(jnp.concatenate([ref[:, span] for ref in lhs], axis=0), right, ((0,), (0,)))
                for lhs, right in products
            ]
            value = jnp.concatenate(parts, axis=1)
            if bases:
                value = value + base_refs[group][span, :].astype(full)
            product[span, :] = value
        for bit, start, given, kept in (
            (0, 0, given_0, kept_0),
            (1, given_0.shape[1], given_1, kept_1),
        ):
            mine = (me_ref[0] >> bit) & 1
            for index in range(4):
                for value, ref in ((1 - mine, given), (mine, kept)):
                    above = (index >> bit) << (bit + 1)
                    at = (above + (value << bit) + (index & bit)) * rows + start
                    at = pl.multiple_of(at, 8)
                    ref[4 * group + index] = product[pl.ds(at, ref.shape[1]), :].astype(low)


def halve_kernel(
    me_ref, held_0, held_1, got_0, got_1, given_0, given_1, kept_0, kept_1
):
    for bit, held, got, given, kept in (
        (1, held_0, got_0, given_0, kept_0),
        (0, held_1, got_1, given_1, kept_1),
    ):
        mine = (me_ref[0] >> bit) & 1
        for index in range(given.shape[0]):
            for value, ref in ((1 - mine, given), (mine, kept)):
                at = 2 * index + value
                ref[index] = (held[at].astype(full) + got[at].astype(full)).astype(low)


def join_kernel(me_ref, held_0, held_1, got_0, got_1, given, kept):
    mine = (me_ref[0] >> 2) & 1
    for index in range(given.shape[0]):
        for value, ref in ((1 - mine, given), (mine, kept)):
            at = 2 * index + value
            upper = held_0[at].astype(full) + got_0[at].astype(full)
            lower = held_1[at].astype(full) + got_1[at].astype(full)
            ref[index] = jnp.concatenate([upper, lower], axis=0).astype(low)


def total_kernel(held_ref, got_ref, *out_refs):
    if len(out_refs[0].shape) == 2:
        for index, out_ref in enumerate(out_refs):
            out_ref[...] = held_ref[index].astype(full) + got_ref[index].astype(full)
        return
    entry_ref, output_ref = out_refs
    total = held_ref[0].astype(full) + got_ref[0].astype(full)
    parts, _, columns = entry_ref.shape
    for index in range(parts):
        entry_ref[index] = total[:, index * columns : (index + 1) * columns]
    output_ref[...] = total[:, parts * columns :]


def call(
    kernel, outs, *operands, words=0, deps=(), time=1.0, scratch=(), token=False, loose=False
):
    count = len(operands)
    deps = tuple(deps)
    outs = tuple(outs)
    if token:
        outs += (((8, 128), full),)

    def run(*refs):
        outs_at = count + len(deps)
        rest = list(refs[outs_at:])
        if token:
            last = rest.pop(len(outs) - 1)
            last[...] = jnp.zeros_like(last)
        kernel(*refs[:count], *rest)

    return pl.pallas_call(
        run,
        out_shape=tuple(jax.ShapeDtypeStruct(shape, kind) for shape, kind in outs),
        in_specs=[SMALL] * words
        + [pl.BlockSpec() if loose else PLAIN] * (count - words)
        + [pl.BlockSpec(memory_space=pl.ANY)] * len(deps),
        scratch_shapes=list(scratch),
        compiler_params=pltpu.CompilerParams(vmem_limit_bytes=VMEM_ASK),
        cost_estimate=pl.CostEstimate(
            flops=int(time * 1.15e9), bytes_accessed=1024, transcendentals=0
        ),
    )(*operands, *deps)


def turn(token):
    return swap(token, "tensor", 1)


def body(
    kept_rows,
    owner_index,
    kept_position,
    resolution,
    mask_token,
    condition,
    modulate_weight,
    entry_weight,
    output_weight,
    expand_weight,
    shrink_weight,
    cotangent,
):
    owners = lax.axis_size("dp")
    me = lax.axis_index("dp")
    lane = lax.axis_index("tensor")
    kept_count, width_part = kept_rows.shape
    width = mask_token.shape[0]
    own_tokens = cotangent.shape[0]
    ff_part = expand_weight.shape[1]
    quarter = own_tokens // QUARTERS
    group = quarter // 2
    arrived_count = own_tokens // 2
    block = group + SPARE
    rows = QUARTERS * block
    capacity = 2 * kept_count // owners
    slots_all = owners * capacity
    direct = owners == SWAP_OWNERS
    lane_word = lane.reshape(1).astype(jnp.int32)
    me_word = me.reshape(1).astype(jnp.int32)
    big_word = resolution[:1]
    context_part = lax.dynamic_slice_in_dim(
        condition.astype(full), lane * width_part, width_part, 1
    )
    lifted = jax.nn.silu(context_part).astype(low)
    if direct:
        padded = -(-width_part // capacity) * capacity
        riders = jnp.pad(lifted, ((0, 0), (0, padded - width_part))).reshape(-1, capacity)
    else:
        padded = 128
        riders = lifted.reshape(-1, capacity)
    rider_count = riders.shape[0]
    extra = -(-(rider_count + 2) // 16) * 16
    riders = jnp.pad(riders, ((2, extra - 2 - rider_count), (0, 0)))
    slab_rows = width_part + extra
    slab_shape = (slab_rows, capacity)
    if not direct:
        slab_shape = (owners,) + slab_shape
    *slabs, slot_index = call(
        partial(
            pack_kernel,
            owners,
            FAR + NEAR if direct else range(owners),
            own_tokens.bit_length() - 1,
        ),
        ((slab_shape, low),) * (owners if direct else 1) + (((1, kept_count), jnp.int32),),
        me_word,
        kept_rows.T,
        (owner_index * own_tokens + kept_position)[None, :],
        riders,
        words=1,
        time=1.0,
        loose=direct,
    )

    steps = -(-6 * width // arrived_count)
    table, bias, bias_turned = call(
        table_kernel,
        (
            ((QUARTERS * steps, arrived_count), low),
            ((rows, rows), full),
            ((rows, rows), full),
        ),
        big_word,
        lifted,
        modulate_weight,
        words=1,
        deps=[slot_index],
        time=2.0,
        scratch=[pltpu.VMEM((8, steps * arrived_count), full)],
    )
    if direct:
        slabs = exchange_owners(dict(zip(FAR + NEAR, slabs)))
        slabs = list(slabs.values())
    else:
        slabs = exchange_owners(slabs)
    compact, slot_rank, event = call(
        partial(unpack_kernel, owners),
        (
            ((width_part + QUARTERS * steps, arrived_count), low),
            ((1, slots_all), jnp.int32),
        ),
        me_word,
        table,
        *slabs,
        words=1,
        time=1.2,
        token=True,
        scratch=[pltpu.VMEM((slab_rows, slots_all), low)],
    )
    token_rank, lifted_all = call(
        partial(spots_kernel, owners),
        (((1, own_tokens), jnp.int32), ((owners * QUARTERS, padded), full)),
        me_word,
        *slabs,
        words=1,
        deps=[event],
        time=1.2,
        scratch=[pltpu.VMEM((extra, slots_all), low)],
    )
    if not direct:
        owner_order = jnp.arange(owners, dtype=jnp.int32) ^ me
        lifted_all = slabs[0][:, width_part + 2 : width_part + 2 + rider_count]
        lifted_all = lifted_all.reshape(owners * QUARTERS, width_part)
    spatial_pieces = gather_blocks(compact)
    entry_flat = jnp.transpose(entry_weight, (1, 2, 0)).reshape(3 * width_part, width)
    token_shape = ((block, width), low)
    half = 2 * block
    chosen, spatial_own, normed_one, projected, attended_far, part_2, part_3 = call(
        entry_kernel,
        (
            ((QUARTERS, 6 * width), full),
            token_shape,
            ((rows, width), low),
            ((rows, 3 * width_part), low),
            ((half, width_part), low),
            token_shape,
            token_shape,
        ),
        lane_word,
        big_word,
        *spatial_pieces,
        mask_token[None, :],
        entry_flat,
        bias,
        output_weight,
        words=2,
        deps=[token_rank],
        time=5.0,
        scratch=[
            pltpu.VMEM((width, arrived_count), low),
            pltpu.VMEM((8, steps * arrived_count), full),
        ],
    )
    far, across, start = sum_far(part_2, part_3)
    attended_near, part_0, part_1 = call(
        attend_kernel,
        (((half, width_part), low), token_shape, token_shape),
        projected,
        bias,
        output_weight,
        deps=[start],
        time=3.0,
    )
    got = swap(part_1, "tensor", 1)
    feed_grad_near, feed_grad_far, upstream_own, back_near, back_far = call(
        upstream_kernel,
        (
            ((half, width), low),
            ((half, width), low),
            ((block, width), full),
            ((half, width), full),
            ((half, width), full),
        ),
        lane_word,
        token_rank,
        chosen,
        cotangent,
        shrink_weight,
        words=1,
        deps=[part_1],
        time=3.6,
    )
    branch, middle, normed_two_own = call(
        middle_kernel,
        (((block, width), full), ((block, width), full), token_shape),
        part_0,
        got,
        across,
        spatial_own,
        chosen,
        deps=[back_far],
        time=0.6,
    )

    def feed_call(piece_0, piece_1, back, *deps):
        return call(
            feed_kernel,
            (((half, width), low), ((half, width), low), ((half, width), low))
            + (token_shape, token_shape),
            piece_0,
            piece_1,
            back,
            expand_weight,
            deps=deps,
            time=2.4,
        )

    near_piece = swap(normed_two_own, "tensor", 1)
    across = swap(normed_two_own, "tensor", 2)
    normed_near, activated_near, hidden_near, part_0, part_1 = feed_call(
        normed_two_own, near_piece, back_near
    )
    *partials, event = call(
        partial_kernel,
        (((width, ff_part), low),) * 2,
        feed_grad_near,
        activated_near,
        normed_near,
        hidden_near,
        time=2.5,
        token=True,
    )
    (across,) = call(copy_kernel, (token_shape,), across, deps=[event], time=0.3)
    last_piece = swap(across, "tensor", 1)
    normed_far, activated_far, hidden_far, part_2, part_3 = feed_call(
        across, last_piece, back_far
    )
    feed_groups = [
        [([feed_grad_far], [activated_far])],
        [([normed_far], [hidden_far])],
    ]
    event = part_0
    if direct:
        feed_given, feed_kept, event = start_sums(feed_groups, FEED_SPLIT, (), 3.5, partials)
        feed_got = cross(feed_given, 1, 2)
    far, across, start = sum_far(part_2, part_3, [event])
    got = swap(part_1, "tensor", 1)
    middle_grad, branch_grad_own, sums, start = call(
        middle_back_kernel,
        (((block, width), full), token_shape, ((SPARE, width), full)),
        part_0,
        got,
        across,
        middle,
        branch,
        upstream_own,
        chosen,
        deps=[start],
        time=0.7,
        token=True,
    )
    branch_pieces = gather_blocks(branch_grad_own)
    feed_parts = call(
        feed_out_kernel,
        (token_shape,) * QUARTERS,
        activated_near,
        activated_far,
        shrink_weight,
        deps=[turn(start)],
        time=0.1,
    )
    feed_far = swap(feed_parts[3], "tensor", 1)
    feed_near = swap(feed_parts[1], "tensor", 1)
    feed_far, start = call(
        add_kernel,
        (token_shape,),
        feed_parts[2],
        feed_far,
        deps=[branch_pieces[2]],
        time=0.1,
        token=True,
    )
    (probs,) = call(
        probs_kernel,
        (((width_part // HEAD, rows, rows), low),),
        projected,
        bias_turned,
        deps=[feed_far],
        time=0.1,
    )
    branch_grad, projected_grad, event = call(
        attend_back_kernel,
        (((rows, width), low), ((rows, 3 * width_part), low)),
        projected,
        probs,
        output_weight,
        *branch_pieces,
        deps=[turn(start)],
        time=0.1,
        token=True,
    )
    feed_across = swap(feed_far, "tensor", 2)
    if direct:
        feed_given, feed_kept, event = halve_sums(feed_kept, feed_got, [event])
        feed_got = cross(feed_given, 2, 1)
    part_2, part_3 = call(
        partial(entry_back_kernel, 1),
        (token_shape, token_shape),
        projected_grad,
        entry_flat,
        deps=[feed_across, feed_near, event],
        time=0.1,
    )
    far, across, start = sum_far(part_2, part_3)
    part_0, part_1 = call(
        partial(entry_back_kernel, 0),
        (token_shape, token_shape),
        projected_grad,
        entry_flat,
        deps=[start],
        time=0.2,
    )
    got = swap(part_1, "tensor", 1)
    entry_groups = [
        [([normed_one], [projected_grad]), ([branch_grad], [attended_near, attended_far])]
    ]
    event = part_1
    if direct:
        entry_given, entry_kept, event = start_sums(entry_groups, ENTRY_SPLIT, [got], 0.2)
        entry_got = cross(entry_given, 1, 2)
    *back_pieces, back_token = call(
        back_kernel,
        (((width_part + 80, group), low),) * QUARTERS,
        lane_word,
        part_0,
        got,
        across,
        spatial_own,
        middle_grad,
        chosen,
        sums,
        feed_parts[0],
        feed_near,
        feed_across,
        upstream_own,
        words=1,
        deps=[event],
        time=BACK_TIME,
        token=True,
        scratch=[pltpu.VMEM((width, group), low), pltpu.VMEM((80, 128), full)],
    )
    if direct:
        feed_got, feed_kept, joined = join_sums(feed_kept, feed_got, [back_token])
    back_pieces = [
        back_pieces[0],
        swap(back_pieces[1], "tensor", 1),
        *swap_pair(back_pieces[2:]),
    ]
    chunks = 6 * width // 128
    logistic = jax.nn.sigmoid(context_part)
    logistic = logistic * (1.0 + context_part * (1.0 - logistic))
    if direct:
        entry_given, entry_kept, halved = halve_sums(entry_kept, entry_got, [back_token], HALVE_TIME)
        entry_got = cross(entry_given, 2, 1)
        shrink_grad, expand_grad, total_token = call(
            total_kernel,
            (((width // owners, ff_part), full),) * 2,
            feed_kept,
            feed_got,
            deps=[halved],
            time=TOTAL_TIME,
            token=True,
        )
        slabs, table_grad, event = call(
            partial(slots_kernel, owners),
            (
                ((owners, width_part + RIDERS, capacity), low),
                ((QUARTERS, chunks, 128), low),
            ),
            lane_word,
            me_word,
            big_word,
            slot_rank,
            *back_pieces,
            words=3,
            time=0.1,
            token=True,
            scratch=[
                pltpu.VMEM((QUARTERS, chunks + 2, 128), full),
                pltpu.VMEM((16, 128), full),
            ],
        )
        (slabs,) = exchange_owners([slabs])
        table_grad = table_grad.reshape(QUARTERS, 6 * width)
        entry_got, entry_kept, event = join_sums(entry_kept, entry_got, [total_token])
        out_pieces = call(
            out_kernel,
            (((width_part + 16, group), low),) * QUARTERS,
            lane_word,
            feed_parts[0],
            feed_near,
            feed_across,
            middle,
            chosen,
            words=1,
            deps=[event],
            time=0.1,
            scratch=[pltpu.VMEM((width, group), low), pltpu.VMEM((16, 128), full)],
        )
        out_pieces = [
            out_pieces[0],
            swap(out_pieces[1], "tensor", 1),
            *swap_pair(out_pieces[2:]),
        ]
        layer_out, layer_token = call(
            layer_kernel,
            (((width_part, own_tokens), low),),
            lane_word,
            token_rank,
            *out_pieces,
            words=1,
            deps=[event],
            time=0.1,
            token=True,
            scratch=[pltpu.VMEM((8, width), full), pltpu.VMEM((width, 8), full)],
        )
        kept_grad, modulate_grad, mask_grad, kept_token = call(
            partial(kept_kernel, owners),
            (
                ((width_part, kept_count), low),
                ((width_part, 6 * width // owners), full),
                ((1, width // owners), full),
            ),
            me_word,
            slot_index,
            lifted_all,
            slabs,
            words=1,
            deps=[layer_token],
            time=KEPT_TIME,
            token=True,
            scratch=[pltpu.VMEM((owners * QUARTERS, 1024), full)],
        )
        mask_grad = mask_grad[0]
    else:
        event = back_pieces[1]
        rows_back = jnp.concatenate([piece[:width_part] for piece in back_pieces], axis=1)
        rank_ids = jnp.arange(arrived_count, dtype=jnp.int32)
        rank_ids = ((rank_ids // group) ^ lane) * group + rank_ids % group
        matrix = (rank_ids[:, None] == slot_rank).astype(low)
        slabs = dot(rows_back, matrix).astype(low).reshape(width_part, owners, capacity)
        slabs = jnp.take(jnp.transpose(slabs, (1, 0, 2)), owner_order, axis=0)
        slabs = jnp.take(exchange_owners([slabs])[0], owner_order, axis=0)
        slabs = jnp.transpose(slabs, (1, 0, 2)).reshape(width_part, slots_all)
        slot_ids = jnp.arange(slots_all, dtype=jnp.int32)[:, None]
        kept_grad = dot(slabs, (slot_ids == slot_index).astype(low)).astype(low)
        riders = jnp.stack(
            [piece[width_part : width_part + 8 * width // 128] for piece in back_pieces]
        )
        riders = riders.reshape(QUARTERS, 8, width).astype(full)
        mask_total = jnp.sum(riders[:, 6] + riders[:, 7], axis=0)
        table_local = riders[:, :6].reshape(QUARTERS, 6 * width)
        table_small = jnp.take(table_local, jnp.arange(QUARTERS, dtype=jnp.int32) ^ lane, axis=0)
        first = jnp.arange(QUARTERS, dtype=jnp.int32)[:, None] == 0
        table_big = jnp.where(first, jnp.sum(table_local, axis=0, keepdims=True), 0.0)
        table_grad = jnp.where(big_word[0] == 1, table_big, table_small).astype(low)
        sent = jnp.transpose(table_grad.reshape(QUARTERS, owners, -1), (1, 0, 2))
        table_all = exchange_owners([sent])[0].reshape(owners * QUARTERS, -1)
        modulate_grad = dot(lifted_all, table_all, ((0,), (0,)))
        mask_grad = lax.psum_scatter(mask_total, "dp", scatter_dimension=0, tiled=True)
    condition_grad = dot(table_grad, modulate_weight, ((1,), (1,))) * logistic
    if not direct:
        out_pieces = call(
            out_kernel,
            (((width_part + 16, group), low),) * QUARTERS,
            lane_word,
            feed_parts[0],
            feed_near,
            feed_across,
            middle,
            chosen,
            words=1,
            deps=[],
            time=0.1,
            scratch=[pltpu.VMEM((width, group), low), pltpu.VMEM((16, 128), full)],
        )
        out_pieces = [
            out_pieces[0],
            swap(out_pieces[1], "tensor", 1),
            *swap_pair(out_pieces[2:]),
        ]
        layer_out, layer_token = call(
            layer_kernel,
            (((width_part, own_tokens), low),),
            lane_word,
            token_rank,
            *out_pieces,
            words=1,
            deps=[],
            time=0.1,
            token=True,
            scratch=[pltpu.VMEM((8, width), full), pltpu.VMEM((width, 8), full)],
        )
    rows_part = width // owners
    if direct:
        entry_grad, output_grad = call(
            total_kernel,
            (((3, rows_part, width_part), full), ((rows_part, width_part), full)),
            entry_kept,
            entry_got,
            deps=[kept_token],
            time=0.8,
        )
    else:
        totals = []
        for number, pairs in enumerate(feed_groups + entry_groups):
            total = [
                dot(jnp.concatenate(lhs), jnp.concatenate(rhs), ((0,), (0,))) for lhs, rhs in pairs
            ]
            total = jnp.concatenate(total, axis=1)
            if number < len(partials):
                total = total + partials[number].astype(full)
            totals.append(sum_owners(total.astype(low).reshape(owners, rows_part, -1)))
        shrink_grad, expand_grad, entry_grad = totals
        output_grad = entry_grad[:, 3 * width_part :]
        entry_grad = entry_grad[:, : 3 * width_part].reshape(rows_part, 3, width_part)
        entry_grad = jnp.transpose(entry_grad, (1, 0, 2))

    return (
        layer_out.T,
        kept_grad.T,
        mask_grad,
        condition_grad,
        modulate_grad,
        jnp.transpose(entry_grad, (1, 0, 2)),
        output_grad.T,
        expand_grad,
        shrink_grad.T,
    )


def solution(mesh):
    return jax.shard_map(
        body,
        mesh=mesh,
        in_specs=(
            P("dp", "tensor"),
            P("dp"),
            P("dp"),
            P("dp"),
            P(),
            P("dp", None),
            P("tensor", None),
            P(None, None, "tensor"),
            P("tensor", None),
            P(None, "tensor"),
            P("tensor", None),
            P("dp", None),
        ),
        out_specs=(
            P("dp", "tensor"),
            P("dp", "tensor"),
            P("dp"),
            P("dp", "tensor"),
            P("tensor", "dp"),
            P("dp", None, "tensor"),
            P("tensor", "dp"),
            P("dp", "tensor"),
            P("tensor", "dp"),
        ),
        check_vma=False,
    )
```

```python
from functools import partial

import jax
import jax.numpy as jnp
from jax import lax
from jax.experimental import pallas as pl
from jax.experimental.pallas import tpu as pltpu
from jax.sharding import PartitionSpec as P

HEAD = 72
QUARTERS = 4
SPARE = 8
scale = HEAD ** (-0.5)
epsilon = 1e-06
gelu_coeff = 0.7978845608028654
low = jnp.bfloat16
full = jnp.float32
VMEM_ASK = 12 * 1024 * 1024
RIDERS = 48
SWAP_OWNERS = 8
FEED_SPLIT = 72
ENTRY_SPLIT = 72
FAR = (6, 7, 4, 5)
NEAR = (2, 3, 1, 0)
JOIN_TIME = 0.1
KEPT_TIME = 0.1
TOTAL_TIME = 14.0
HALVE_TIME = 0.35
BACK_TIME = 0.1
SMALL = pl.BlockSpec(memory_space=pltpu.SMEM)
PLAIN = pl.BlockSpec(memory_space=pltpu.VMEM)


def dot(a, b, dims=((1,), (0,))):
    return lax.dot_general(a, b, (dims, ((), ())), preferred_element_type=full)


def normalize(rows):
    centered = rows - jnp.mean(rows, axis=-1, keepdims=True)
    inverse = lax.rsqrt(jnp.mean(centered * centered, axis=-1, keepdims=True) + epsilon)
    return (centered * inverse, inverse)


def normalize_back(unit, inverse, grad):
    return inverse * (
        grad
        - jnp.mean(grad, axis=-1, keepdims=True)
        - unit * jnp.mean(grad * unit, axis=-1, keepdims=True)
    )


def gelu_both(value):
    square = value * value
    inner = value * (gelu_coeff + 0.044715 * gelu_coeff * square)
    half = 0.5 + 0.5 * jnp.tanh(inner)
    activated = value * half
    outer = 2.0 * gelu_coeff + 6.0 * 0.044715 * gelu_coeff * square
    return (activated, half + activated * (1.0 - half) * outer)


def swap(value, axis, bit):
    size = lax.axis_size(axis)
    return lax.ppermute(value, axis, [(index, index ^ bit) for index in range(size)])


def swap_pair(pieces):
    came = swap(jnp.stack(pieces), "tensor", 2)
    return came[0], swap(came[1], "tensor", 1)


def gather_blocks(own):
    near = swap(own, "tensor", 1)
    across = swap(own, "tensor", 2)
    return [own, near, across, swap(across, "tensor", 1)]


def sum_far(part_2, part_3, deps=()):
    got = swap(part_3, "tensor", 1)
    far, token = call(
        add_kernel, ((part_2.shape, low),), part_2, got, deps=deps, time=0.1, token=True
    )
    return far, swap(far, "tensor", 2), turn(token)


def sum_owners(total):
    owners, rows, columns = total.shape
    me = lax.axis_index("dp")
    step = 1
    while step < owners:
        pairs = total.reshape(-1, 2, rows, columns)
        mine = (me // step) % 2
        given = lax.dynamic_index_in_dim(pairs, 1 - mine, 1, keepdims=False)
        kept = lax.dynamic_index_in_dim(pairs, mine, 1, keepdims=False)
        total = kept.astype(full) + swap(given, "dp", step).astype(full)
        step *= 2
        total = total if step == owners else total.astype(low)
    return total[0]


def part_shapes(count, upper, lower, columns):
    return [((count, upper, columns), low), ((count, lower, columns), low)]


def start_sums(groups, split, deps=(), time=3.0, bases=()):
    width = groups[0][0][0][0].shape[1]
    columns = sum(rhs[0].shape[1] for _, rhs in groups[0])
    rows = width // 8
    shapes = part_shapes(4 * len(groups), split, rows - split, columns)
    counts = [[(len(lhs), len(rhs)) for lhs, rhs in pairs] for pairs in groups]
    given_0, given_1, kept_0, kept_1, token = call(
        partial(weight_kernel, counts, len(bases)),
        shapes + shapes,
        lax.axis_index("dp").reshape(1).astype(jnp.int32),
        *[value for pairs in groups for lhs, rhs in pairs for value in (*lhs, *rhs)],
        *bases,
        words=1,
        deps=deps,
        time=time,
        scratch=[pltpu.VMEM((width, columns), full)],
        token=True,
    )
    return (given_0, given_1), (kept_0, kept_1), token


def cross(given, first, second):
    return swap(given[0], "dp", first), swap(given[1], "dp", second)


def halve_sums(kept, got, deps=(), time=0.1):
    count, _, columns = kept[0].shape
    shapes = part_shapes(count // 2, kept[0].shape[1], kept[1].shape[1], columns)
    given_0, given_1, kept_0, kept_1, token = call(
        halve_kernel,
        shapes + shapes,
        lax.axis_index("dp").reshape(1).astype(jnp.int32),
        *kept,
        *got,
        words=1,
        deps=deps,
        time=time,
        token=True,
    )
    return (given_0, given_1), (kept_0, kept_1), token


def join_sums(kept, got, deps=()):
    count, _, columns = kept[0].shape
    shape = ((count // 2, kept[0].shape[1] + kept[1].shape[1], columns), low)
    given, kept, token = call(
        join_kernel,
        (shape, shape),
        lax.axis_index("dp").reshape(1).astype(jnp.int32),
        *kept,
        *got,
        words=1,
        deps=deps,
        time=JOIN_TIME,
        token=True,
    )
    return swap(given, "dp", 4), kept, token


def exchange_owners(slabs):
    if isinstance(slabs, dict):
        return {index: swap(slab, "dp", index) if index else slab for index, slab in slabs.items()}
    return [lax.all_to_all(slabs[0], "dp", split_axis=0, concat_axis=0, tiled=True)]


def attend(projected_ref, bias_ref, output_ref, attended_ref, chunk, half, width_part):
    span = slice(chunk * half, (chunk + 1) * half)
    pieces = []
    for head in range(width_part // HEAD):
        at = head * HEAD
        queries = projected_ref[span, at : at + HEAD]
        keys = projected_ref[:, width_part + at : width_part + at + HEAD]
        values = projected_ref[:, 2 * width_part + at : 2 * width_part + at + HEAD]
        scores = dot(queries, keys, ((1,), (1,))) * scale + bias_ref[span, :]
        spread = jnp.exp(scores - jnp.max(scores, axis=1, keepdims=True))
        probs = spread * (1.0 / jnp.sum(spread, axis=1, keepdims=True))
        pieces.append(dot(probs.astype(low), values))
    attended = jnp.concatenate(pieces, axis=1).astype(low)
    attended_ref[...] = attended
    return dot(attended, output_ref[...])


def entry_kernel(
    lane_ref,
    big_ref,
    piece_0,
    piece_1,
    piece_2,
    piece_3,
    mask_ref,
    entry_ref,
    bias_ref,
    output_ref,
    chosen_ref,
    spatial_ref,
    normed_ref,
    projected_ref,
    attended_ref,
    part_0,
    part_1,
    gathered,
    table,
):
    lane = lane_ref[0]
    block, width = spatial_ref.shape
    width_part = width // QUARTERS
    group = block - SPARE
    half = 2 * block
    pieces = (piece_0, piece_1, piece_2, piece_3)
    for index, piece in enumerate(pieces):
        at = pl.multiple_of((lane ^ index) * width_part, 16)
        gathered[pl.ds(at, width_part), :] = piece[:width_part, :]
    summed = pieces[0][width_part:, :].astype(full)
    for piece in pieces[1:]:
        summed = summed + piece[width_part:, :].astype(full)
    span = summed.shape[1]
    steps = summed.shape[0] // QUARTERS
    for row in range(QUARTERS):
        for step in range(steps):
            from_row = row * steps + step
            table[row : row + 1, step * span : (step + 1) * span] = summed[from_row : from_row + 1]
    for index in range(QUARTERS):
        row = jnp.where(big_ref[0] == 1, 0, lane ^ index)
        chosen_ref[index : index + 1, :] = table[pl.ds(row, 1), : 6 * width]
    spare_id = lax.broadcasted_iota(jnp.int32, (SPARE, width), 0)
    spare = jnp.where(spare_id == 0, mask_ref[...].astype(full), 0.0)
    for chunk in (1, 0):
        span = slice(chunk * half, (chunk + 1) * half)
        normed = []
        for index in (2 * chunk, 2 * chunk + 1):
            at = pl.multiple_of((lane ^ index) * group, 128)
            kept = jnp.transpose(gathered[:, pl.ds(at, group)].astype(full))
            rows = jnp.concatenate([kept, spare], axis=0)
            if index == 0:
                spatial_ref[...] = rows.astype(low)
            unit, inverse = normalize(rows)
            shift = chosen_ref[index : index + 1, :width]
            gain = chosen_ref[index : index + 1, width : 2 * width]
            normed.append(unit * (1.0 + gain) + shift)
        normed = jnp.concatenate(normed, axis=0).astype(low)
        normed_ref[span, :] = normed
        projected_ref[span, :] = dot(normed, entry_ref[...], ((1,), (1,))).astype(low)
    part = attend(projected_ref, bias_ref, output_ref, attended_ref, 1, half, width_part)
    part_0[...] = part[:block].astype(low)
    part_1[...] = part[block:].astype(low)


def attend_kernel(projected_ref, bias_ref, output_ref, attended_ref, part_0, part_1):
    block = part_0.shape[0]
    part = attend(
        projected_ref, bias_ref, output_ref, attended_ref, 0, 2 * block, output_ref.shape[0]
    )
    part_0[...] = part[:block].astype(low)
    part_1[...] = part[block:].astype(low)


def middle_kernel(
    part_0, part_1, part_2, spatial_ref, chosen_ref, branch_ref, middle_ref, normed_ref
):
    width = spatial_ref.shape[1]
    branch = part_0[...].astype(full) + part_1[...].astype(full) + part_2[...].astype(full)
    branch_ref[...] = branch
    middle = spatial_ref[...].astype(full) + chosen_ref[0:1, 2 * width : 3 * width] * branch
    middle_ref[...] = middle
    unit, inverse = normalize(middle)
    shift = chosen_ref[0:1, 3 * width : 4 * width]
    gain = chosen_ref[0:1, 4 * width : 5 * width]
    normed_ref[...] = (unit * (1.0 + gain) + shift).astype(low)


def feed_kernel(
    piece_0,
    piece_1,
    back_ref,
    expand_ref,
    normed_ref,
    activated_ref,
    hidden_grad_ref,
    part_0,
    part_1,
):
    block = piece_0.shape[0]
    normed = jnp.concatenate([piece_0[...].astype(full), piece_1[...].astype(full)], axis=0)
    normed = normed.astype(low)
    normed_ref[...] = normed
    hidden = dot(normed, expand_ref[...])
    activated, slope = gelu_both(hidden)
    activated_ref[...] = activated.astype(low)
    hidden_grad = (back_ref[...] * slope).astype(low)
    hidden_grad_ref[...] = hidden_grad
    part = dot(hidden_grad, expand_ref[...], ((1,), (1,)))
    part_0[...] = part[:block].astype(low)
    part_1[...] = part[block:].astype(low)


def middle_back_kernel(
    part_0,
    part_1,
    part_2,
    middle_ref,
    branch_ref,
    upstream_ref,
    chosen_ref,
    middle_grad_ref,
    branch_grad_ref,
    sums_ref,
):
    width = middle_ref.shape[1]
    normed_grad = part_0[...].astype(full) + part_1[...].astype(full) + part_2[...].astype(full)
    unit, inverse = normalize(middle_ref[...])
    gain = chosen_ref[0:1, 4 * width : 5 * width]
    middle_grad = upstream_ref[...] + normalize_back(unit, inverse, normed_grad * (1.0 + gain))
    middle_grad_ref[...] = middle_grad
    branch_grad_ref[...] = (chosen_ref[0:1, 2 * width : 3 * width] * middle_grad).astype(low)
    sums_ref[0:1, :] = jnp.sum(middle_grad * branch_ref[...], axis=0, keepdims=True)
    sums_ref[1:2, :] = jnp.sum(normed_grad, axis=0, keepdims=True)
    sums_ref[2:3, :] = jnp.sum(normed_grad * unit, axis=0, keepdims=True)


def probs_kernel(projected_ref, bias_ref, probs_ref):
    width_part = projected_ref.shape[1] // 3
    for head in range(width_part // HEAD):
        at = head * HEAD
        queries = projected_ref[:, at : at + HEAD]
        keys = projected_ref[:, width_part + at : width_part + at + HEAD]
        scores = dot(keys, queries, ((1,), (1,))) * scale + bias_ref[...]
        spread = jnp.exp(scores - jnp.max(scores, axis=0, keepdims=True))
        probs = spread * (1.0 / jnp.sum(spread, axis=0, keepdims=True))
        probs_ref[head] = probs.astype(low)


def attend_back_kernel(
    projected_ref,
    probs_ref,
    output_ref,
    piece_0,
    piece_1,
    piece_2,
    piece_3,
    branch_grad_ref,
    grad_ref,
):
    rows, width_all = projected_ref.shape
    width_part = width_all // 3
    block = piece_0.shape[0]
    half = 2 * block
    for chunk, pair in enumerate(((piece_0, piece_1), (piece_2, piece_3))):
        branch_grad_ref[chunk * half : (chunk + 1) * half, :] = jnp.concatenate(
            [piece[...].astype(full) for piece in pair], axis=0
        ).astype(low)
    attended_grad = dot(branch_grad_ref[...], output_ref[...], ((1,), (1,))).astype(low)
    pieces = [[], [], []]
    for head in range(width_part // HEAD):
        at = head * HEAD
        queries = projected_ref[:, at : at + HEAD]
        keys = projected_ref[:, width_part + at : width_part + at + HEAD]
        values = projected_ref[:, 2 * width_part + at : 2 * width_part + at + HEAD]
        grad = attended_grad[:, at : at + HEAD]
        probs = probs_ref[head]
        pieces[2].append(dot(probs, grad))
        probs = probs.astype(full)
        prob_grad = dot(values, grad, ((1,), (1,)))
        delta = jnp.sum(probs * prob_grad, axis=0, keepdims=True)
        score_grad = (probs * (prob_grad - delta)).astype(low)
        pieces[1].append(dot(score_grad, queries) * scale)
        pieces[0].append(dot(score_grad, keys, ((0,), (0,))) * scale)
    grad_ref[...] = jnp.concatenate(pieces[0] + pieces[1] + pieces[2], axis=1).astype(low)


def entry_back_kernel(chunk, grad_ref, entry_ref, part_0, part_1):
    block = part_0.shape[0]
    part = dot(grad_ref[2 * chunk * block : 2 * (chunk + 1) * block, :], entry_ref[...])
    part_0[...] = part[:block].astype(low)
    part_1[...] = part[block:].astype(low)


def pack_kernel(owners, chosen, shift, me_ref, kept_ref, spot_ref, riders_ref, *out_refs):
    slot_ref = out_refs[-1]
    extra, capacity = riders_ref.shape
    kept_count = kept_ref.shape[1]
    owner_local = (spot_ref[...] >> shift) ^ me_ref[0]
    owner_id = lax.broadcasted_iota(jnp.int32, (owners, kept_count), 0)
    hot = (owner_id == owner_local).astype(full)
    row_id = lax.broadcasted_iota(jnp.int32, (kept_count, kept_count), 0)
    column_id = lax.broadcasted_iota(jnp.int32, (kept_count, kept_count), 1)
    before = dot(hot.astype(low), (row_id < column_id).astype(full).astype(low))
    rank = jnp.sum(hot * before, axis=0, keepdims=True).astype(jnp.int32)
    slot = owner_local * capacity + rank
    slot_ref[...] = slot
    coded = (spot_ref[...] & ((1 << shift) - 1)) + 1
    tag_id = lax.broadcasted_iota(jnp.int32, (extra, kept_count), 0)
    tags = jnp.where(tag_id == 0, coded >> 5, jnp.where(tag_id == 1, coded & 31, 0))
    rows = jnp.concatenate([kept_ref[...], tags.astype(full).astype(low)], axis=0)
    slot_id = lax.broadcasted_iota(jnp.int32, (capacity, kept_count), 0)
    for number, index in enumerate(chosen):
        matrix = (slot_id + index * capacity == slot).astype(full).astype(low)
        slab = dot(rows, matrix, ((1,), (1,)))
        split = kept_ref.shape[0]
        slab = jnp.concatenate([slab[:split], slab[split:] + riders_ref[...].astype(full)], axis=0)
        if len(out_refs) == 2:
            out_refs[0][me_ref[0] ^ index] = slab.astype(low)
        else:
            out_refs[number][...] = slab.astype(low)


def places(owners, me_ref, slab_refs, arrived, width_part):
    slots_all = arrived.shape[1]
    capacity = slots_all // owners
    for index in range(owners):
        if len(slab_refs) == 1:
            slab = slab_refs[0][me_ref[0] ^ index]
        else:
            slab = slab_refs[(FAR + NEAR).index(index)][...]
        rows = arrived.shape[0]
        arrived[:, index * capacity : (index + 1) * capacity] = slab[slab.shape[0] - rows :]
    tags = arrived[width_part : width_part + 16, :].astype(full)
    place = tags[0:1] * 32.0 + tags[1:2] - 1.0
    turned = jnp.transpose(jnp.broadcast_to(place, (8, slots_all)))[:, 0:1]
    return tags, place, jnp.where(turned < 0.0, 1e9, turned)


def unpack_kernel(owners, me_ref, table_ref, *refs):
    slab_refs, (compact_ref, slot_rank_ref, arrived) = refs[:-3], refs[-3:]
    arrived_count = compact_ref.shape[1]
    width_part = compact_ref.shape[0] - table_ref.shape[0]
    _, place, turned = places(owners, me_ref, slab_refs, arrived, width_part)
    slot_rank = jnp.sum(jnp.where(turned < place, 1.0, 0.0), axis=0, keepdims=True)
    slot_rank = jnp.where(place < 0.0, -1.0, slot_rank).astype(jnp.int32)
    slot_rank_ref[...] = slot_rank
    rank_id = lax.broadcasted_iota(jnp.int32, (arrived_count, arrived.shape[1]), 0)
    matrix = (rank_id == slot_rank).astype(full).astype(low)
    compact_ref[:width_part, :] = dot(arrived[:width_part, :], matrix, ((1,), (1,))).astype(low)
    compact_ref[width_part:, :] = table_ref[...]


def spots_kernel(owners, me_ref, *refs):
    slab_refs, (token_rank_ref, lifted_ref, arrived) = refs[:-3], refs[-3:]
    own_tokens = token_rank_ref.shape[1]
    capacity = arrived.shape[1] // owners
    tags, _, turned = places(owners, me_ref, slab_refs, arrived, 0)
    spot = lax.broadcasted_iota(jnp.int32, (1, own_tokens), 1).astype(full)
    token_rank = jnp.sum(jnp.where(turned < spot, 1.0, 0.0), axis=0, keepdims=True)
    filled = jnp.sum(jnp.where(turned == spot, 1.0, 0.0), axis=0, keepdims=True)
    token_rank_ref[...] = jnp.where(filled > 0.0, token_rank, -1.0).astype(jnp.int32)
    if len(slab_refs) > 1:
        chunks = lifted_ref.shape[1] // capacity
        for index in range(owners):
            for row in range(QUARTERS):
                for chunk in range(chunks):
                    lifted_ref[
                        index * QUARTERS + row : index * QUARTERS + row + 1,
                        chunk * capacity : (chunk + 1) * capacity,
                    ] = tags[
                        2 + row * chunks + chunk : 3 + row * chunks + chunk,
                        index * capacity : (index + 1) * capacity,
                    ]
    else:
        lifted_ref[...] = jnp.zeros_like(lifted_ref)


def back_kernel(
    lane_ref,
    part_0,
    part_1,
    part_2,
    spatial_ref,
    middle_grad_ref,
    chosen_ref,
    sums_ref,
    feed_0,
    feed_1,
    feed_2,
    upstream_ref,
    piece_0,
    piece_1,
    piece_2,
    piece_3,
    turned,
    riders,
):
    lane = lane_ref[0]
    block, width = spatial_ref.shape
    group = block - SPARE
    width_part = width // QUARTERS
    normed_grad = part_0[...].astype(full) + part_1[...].astype(full) + part_2[...].astype(full)
    unit, inverse = normalize(spatial_ref[...].astype(full))
    gain = chosen_ref[0:1, width : 2 * width]
    grad = middle_grad_ref[...] + normalize_back(unit, inverse, normed_grad * (1.0 + gain))
    turned[...] = jnp.transpose(grad[:group]).astype(low)
    feed = feed_0[...].astype(full) + feed_1[...].astype(full) + feed_2[...].astype(full)
    mask_sum = grad[group : group + 1]
    mask_high = mask_sum.astype(low).astype(full)
    fields = [
        jnp.sum(normed_grad, axis=0, keepdims=True),
        jnp.sum(normed_grad * unit, axis=0, keepdims=True),
        sums_ref[0:1, :],
        sums_ref[1:2, :],
        sums_ref[2:3, :],
        jnp.sum(feed * upstream_ref[...], axis=0, keepdims=True),
        mask_high,
        mask_sum - mask_high,
    ]
    chunks = width // 128
    riders[...] = jnp.zeros_like(riders)
    for number, field in enumerate(fields):
        for chunk in range(chunks):
            at = number * chunks + chunk
            riders[at : at + 1, :] = field[:, chunk * 128 : (chunk + 1) * 128]
    rider_rows = riders[...].astype(low)
    for index, piece in enumerate((piece_0, piece_1, piece_2, piece_3)):
        at = pl.multiple_of((lane ^ index) * width_part, 16)
        piece[:width_part, :] = turned[pl.ds(at, width_part), :]
        piece[width_part:, :] = rider_rows


def slots_kernel(
    owners,
    lane_ref,
    me_ref,
    big_ref,
    rank_ref,
    piece_0,
    piece_1,
    piece_2,
    piece_3,
    slabs_ref,
    table_ref,
    table,
    mask_total,
):
    lane = lane_ref[0]
    me = me_ref[0]
    group = piece_0.shape[1]
    slots_all = rank_ref.shape[1]
    capacity = slots_all // owners
    chunks = table_ref.shape[1]
    width_part = slabs_ref.shape[1] - RIDERS
    pieces = [piece_0, piece_1, piece_2, piece_3]
    rows = jnp.concatenate([piece[:width_part, :] for piece in pieces], axis=1)
    row_id = lax.broadcasted_iota(jnp.int32, (group, slots_all), 0)
    matrix = jnp.concatenate(
        [
            (row_id + (lane ^ index) * group == rank_ref[...]).astype(full).astype(low)
            for index in range(QUARTERS)
        ],
        axis=0,
    )
    slots = dot(rows, matrix)
    table[...] = jnp.zeros_like(table)
    summed = jnp.zeros((chunks, 128), full)
    mask_sum = jnp.zeros((16, 128), full)
    mask_rows = chunks // 6
    for index, piece in enumerate(pieces):
        field = piece[width_part : width_part + chunks, :].astype(full)
        summed = summed + field
        rest = piece[width_part + chunks - chunks % 16 :, :].astype(full)
        table[lane ^ index, :chunks, :] = field
        at = chunks % 16
        mask_sum = mask_sum + jnp.concatenate(
            [
                rest[at : at + mask_rows] + rest[at + mask_rows : at + 2 * mask_rows],
                jnp.zeros((16 - mask_rows, 128), full),
            ],
            axis=0,
        )
    mask_total[...] = mask_sum

    @pl.when(big_ref[0] == 1)
    def _():
        table[...] = jnp.zeros_like(table)
        table[0, :chunks, :] = summed

    table_ref[...] = table[:, :chunks, :].astype(low)
    for index in range(owners):
        owner = me ^ index
        start = (owner * chunks) // owners
        fields = [table[row, pl.ds(start, 8), :] for row in range(QUARTERS)]
        mask_start = (owner * mask_rows) // owners
        mask_part = mask_total[pl.ds(mask_start, 2), :]
        mask_high = mask_part.astype(low).astype(full)
        fields += [mask_high, mask_part - mask_high, jnp.zeros((RIDERS - 36, 128), full)]
        slab = jnp.concatenate([slots[:, index * capacity : (index + 1) * capacity]] + fields, axis=0)
        slabs_ref[owner] = slab.astype(low)


def kept_kernel(
    owners, me_ref, slot_ref, lifted_ref, slabs_ref, kept_ref, modulate_ref, mask_ref, table
):
    width_part, kept_count = kept_ref.shape
    capacity = slabs_ref.shape[2]
    table_part = modulate_ref.shape[1]
    mask_part = mask_ref.shape[1]
    me = me_ref[0]
    slabs = [slabs_ref[me ^ index] for index in range(owners)]
    rows = jnp.concatenate([slab[:width_part] for slab in slabs], axis=1)
    slot_id = lax.broadcasted_iota(jnp.int32, (owners * capacity, kept_count), 0)
    matrix = (slot_id == slot_ref[...]).astype(full).astype(low)
    kept_ref[...] = dot(rows, matrix).astype(low)
    mask_sum = jnp.zeros((1, 256), full)
    for index, slab in enumerate(slabs):
        rider = slab[width_part:].astype(full)
        for row in range(QUARTERS):
            at = index * QUARTERS + row
            for chunk in range(8):
                from_row = row * 8 + chunk
                table[at : at + 1, chunk * 128 : (chunk + 1) * 128] = rider[
                    from_row : from_row + 1
                ]
        high, rest = rider[32:34], rider[34:36]
        both = high + rest
        mask_sum = mask_sum + jnp.concatenate([both[0:1], both[1:2]], axis=1)
    shift = (me * table_part) % 128
    field = pltpu.roll(table[...], (1024 - shift) % 1024, 1)[:, :table_part]
    lifted = lifted_ref[...].astype(low)[:, :width_part]
    modulate_ref[...] = dot(lifted, field.astype(low), ((0,), (0,)))
    shift = (me * mask_part) % 128
    mask_sum = jnp.broadcast_to(mask_sum, (8, 256))
    mask_ref[...] = pltpu.roll(mask_sum, (256 - shift) % 256, 1)[0:1, :mask_part]


def out_kernel(
    lane_ref,
    part_0,
    part_1,
    part_2,
    middle_ref,
    chosen_ref,
    piece_0,
    piece_1,
    piece_2,
    piece_3,
    turned,
    riders,
):
    lane = lane_ref[0]
    block, width = middle_ref.shape
    group = block - SPARE
    width_part = width // QUARTERS
    feed = part_0[...].astype(full) + part_1[...].astype(full) + part_2[...].astype(full)
    out = middle_ref[...] + chosen_ref[0:1, 5 * width : 6 * width] * feed
    turned[...] = jnp.transpose(out[:group]).astype(low)
    riders[...] = jnp.zeros_like(riders)
    for chunk in range(width // 128):
        riders[chunk : chunk + 1, :] = out[group : group + 1, chunk * 128 : (chunk + 1) * 128]
    rider_rows = riders[...].astype(low)
    for index, piece in enumerate((piece_0, piece_1, piece_2, piece_3)):
        at = pl.multiple_of((lane ^ index) * width_part, 16)
        piece[:width_part, :] = turned[pl.ds(at, width_part), :]
        piece[width_part:, :] = rider_rows


def layer_kernel(
    lane_ref, rank_ref, piece_0, piece_1, piece_2, piece_3, out_ref, spare, turned
):
    lane = lane_ref[0]
    width_part, own_tokens = out_ref.shape
    group = piece_0.shape[1]
    quarter = own_tokens // QUARTERS
    pieces = (piece_0, piece_1, piece_2, piece_3)
    rows = jnp.concatenate([piece[:width_part, :] for piece in pieces], axis=1)
    row_id = lax.broadcasted_iota(jnp.int32, (group, own_tokens), 0)
    matrix = jnp.concatenate(
        [
            (row_id + (lane ^ index) * group == rank_ref[...]).astype(full).astype(low)
            for index in range(QUARTERS)
        ],
        axis=0,
    )
    spare[...] = jnp.zeros_like(spare)
    for index, piece in enumerate(pieces):
        rider = piece[width_part:, :].astype(full)
        for chunk in range(spare.shape[1] // 128):
            spare[index : index + 1, chunk * 128 : (chunk + 1) * 128] = rider[chunk : chunk + 1]
    turned[...] = jnp.transpose(spare[...])
    columns = turned[pl.ds(pl.multiple_of(lane * width_part, 16), width_part), :].astype(low)
    spare_id = lax.broadcasted_iota(jnp.int32, (8, own_tokens), 0)
    spot = lax.broadcasted_iota(jnp.int32, (8, own_tokens), 1) // quarter
    empty = rank_ref[...] < 0
    spots = jnp.where(((spare_id ^ lane) == spot) & (spare_id < QUARTERS) & empty, 1.0, 0.0)
    out_ref[...] = (dot(rows, matrix) + dot(columns, spots.astype(low))).astype(low)


def table_kernel(big_ref, lifted_ref, modulate_ref, table_ref, bias_ref, turned_ref, table):
    span = table_ref.shape[1]
    steps = table_ref.shape[0] // QUARTERS
    table[...] = jnp.zeros_like(table)
    table[:QUARTERS, : modulate_ref.shape[1]] = dot(lifted_ref[...], modulate_ref[...])
    table_ref[...] = jnp.concatenate(
        [
            table[row : row + 1, step * span : (step + 1) * span]
            for row in range(QUARTERS)
            for step in range(steps)
        ],
        axis=0,
    ).astype(low)
    rows = bias_ref.shape[0]
    block = rows // QUARTERS
    group = block - SPARE
    big = big_ref[0] == 1
    spare_small = jnp.log(jnp.full((1, 1), float(group), full))
    spare_big = jnp.log(jnp.full((1, 1), float(QUARTERS * group), full))

    def bias_of(query, key):
        query_block, key_block, key_inner = query // block, key // block, key % block
        small = jnp.where(key_inner < group, 0.0, jnp.where(key_inner == group, spare_small, -1e30))
        small = jnp.where(query_block == key_block, small, -1e30)
        large = jnp.where(key_inner < group, 0.0, jnp.where(key == group, spare_big, -1e30))
        return jnp.where(big, large, small)

    row_id = lax.broadcasted_iota(jnp.int32, (rows, rows), 0)
    column_id = lax.broadcasted_iota(jnp.int32, (rows, rows), 1)
    bias_ref[...] = bias_of(row_id, column_id)
    turned_ref[...] = bias_of(column_id, row_id)


def add_kernel(left_ref, right_ref, out_ref):
    out_ref[...] = (left_ref[...].astype(full) + right_ref[...].astype(full)).astype(low)


def copy_kernel(*refs):
    for index in range(len(refs) // 2):
        refs[len(refs) // 2 + index][...] = refs[index][...]


def upstream_kernel(
    lane_ref,
    rank_ref,
    chosen_ref,
    cotangent_ref,
    shrink_ref,
    grad_near,
    grad_far,
    upstream_ref,
    back_near,
    back_far,
):
    lane = lane_ref[0]
    block, width = upstream_ref.shape
    own_tokens = rank_ref.shape[1]
    group = block - SPARE
    rank = rank_ref[...]
    row_id = lax.broadcasted_iota(jnp.int32, (group, own_tokens), 0)
    spare_id = lax.broadcasted_iota(jnp.int32, (SPARE, own_tokens), 0)
    spot = lax.broadcasted_iota(jnp.int32, (SPARE, own_tokens), 1) // (own_tokens // QUARTERS)
    for chunk, back, grad_ref in ((0, back_near, grad_near), (1, back_far, grad_far)):
        matrix = []
        for index in (2 * chunk, 2 * chunk + 1):
            matrix.append(jnp.where(row_id + (lane ^ index) * group == rank, 1.0, 0.0))
            matrix.append(
                jnp.where((spare_id == 0) & (spot == (lane ^ index)) & (rank < 0), 1.0, 0.0)
            )
        upstream = dot(jnp.concatenate(matrix, axis=0).astype(low), cotangent_ref[...])
        if chunk == 0:
            upstream_ref[...] = upstream[:block]
        gates = [chosen_ref[index : index + 1, 5 * width :] for index in (2 * chunk, 2 * chunk + 1)]
        feed_grad = jnp.concatenate(
            [gates[0] * upstream[:block], gates[1] * upstream[block:]], axis=0
        ).astype(low)
        grad_ref[...] = feed_grad
        back[...] = dot(feed_grad, shrink_ref[...], ((1,), (1,)))


def feed_out_kernel(near_ref, far_ref, shrink_ref, part_0, part_1, part_2, part_3):
    block = part_0.shape[0]
    for activated, pair in ((far_ref, (part_2, part_3)), (near_ref, (part_0, part_1))):
        part = dot(activated[...], shrink_ref[...])
        pair[0][...] = part[:block].astype(low)
        pair[1][...] = part[block:].astype(low)


def partial_kernel(lhs_0, rhs_0, lhs_1, rhs_1, out_0, out_1):
    for lhs, rhs, out in ((lhs_0, rhs_0, out_0), (lhs_1, rhs_1, out_1)):
        chunk = lhs.shape[1] // 3
        for number in range(3):
            span = slice(number * chunk, (number + 1) * chunk)
            out[span, :] = dot(lhs[:, span], rhs[...], ((0,), (0,))).astype(low)


def weight_kernel(counts, bases, me_ref, *refs):
    given_0, given_1, kept_0, kept_1, product = refs[-5:]
    operands = list(refs[:-5])
    base_refs = [operands.pop() for _ in range(bases)][::-1]
    rows = given_0.shape[1] + given_1.shape[1]
    chunk = product.shape[0] // 3
    for group, pairs in enumerate(counts):
        products = []
        for lefts, rights in pairs:
            lhs = [operands.pop(0) for _ in range(lefts)]
            right = jnp.concatenate([operands.pop(0)[...] for _ in range(rights)], axis=0)
            products.append((lhs, right))
        for number in range(3):
            span = slice(number * chunk, (number + 1) * chunk)
            parts = [
                dot(jnp.concatenate([ref[:, span] for ref in lhs], axis=0), right, ((0,), (0,)))
                for lhs, right in products
            ]
            value = jnp.concatenate(parts, axis=1)
            if bases:
                value = value + base_refs[group][span, :].astype(full)
            product[span, :] = value
        for bit, start, given, kept in (
            (0, 0, given_0, kept_0),
            (1, given_0.shape[1], given_1, kept_1),
        ):
            mine = (me_ref[0] >> bit) & 1
            for index in range(4):
                for value, ref in ((1 - mine, given), (mine, kept)):
                    above = (index >> bit) << (bit + 1)
                    at = (above + (value << bit) + (index & bit)) * rows + start
                    at = pl.multiple_of(at, 8)
                    ref[4 * group + index] = product[pl.ds(at, ref.shape[1]), :].astype(low)


def halve_kernel(
    me_ref, held_0, held_1, got_0, got_1, given_0, given_1, kept_0, kept_1
):
    for bit, held, got, given, kept in (
        (1, held_0, got_0, given_0, kept_0),
        (0, held_1, got_1, given_1, kept_1),
    ):
        mine = (me_ref[0] >> bit) & 1
        for index in range(given.shape[0]):
            for value, ref in ((1 - mine, given), (mine, kept)):
                at = 2 * index + value
                ref[index] = (held[at].astype(full) + got[at].astype(full)).astype(low)


def join_kernel(me_ref, held_0, held_1, got_0, got_1, given, kept):
    mine = (me_ref[0] >> 2) & 1
    for index in range(given.shape[0]):
        for value, ref in ((1 - mine, given), (mine, kept)):
            at = 2 * index + value
            upper = held_0[at].astype(full) + got_0[at].astype(full)
            lower = held_1[at].astype(full) + got_1[at].astype(full)
            ref[index] = jnp.concatenate([upper, lower], axis=0).astype(low)


def total_kernel(held_ref, got_ref, *out_refs):
    if len(out_refs[0].shape) == 2:
        for index, out_ref in enumerate(out_refs):
            out_ref[...] = held_ref[index].astype(full) + got_ref[index].astype(full)
        return
    entry_ref, output_ref = out_refs
    total = held_ref[0].astype(full) + got_ref[0].astype(full)
    parts, _, columns = entry_ref.shape
    for index in range(parts):
        entry_ref[index] = total[:, index * columns : (index + 1) * columns]
    output_ref[...] = total[:, parts * columns :]


def call(
    kernel, outs, *operands, words=0, deps=(), time=1.0, scratch=(), token=False, loose=False
):
    count = len(operands)
    deps = tuple(deps)
    outs = tuple(outs)
    if token:
        outs += (((8, 128), full),)

    def run(*refs):
        outs_at = count + len(deps)
        rest = list(refs[outs_at:])
        if token:
            last = rest.pop(len(outs) - 1)
            last[...] = jnp.zeros_like(last)
        kernel(*refs[:count], *rest)

    return pl.pallas_call(
        run,
        out_shape=tuple(jax.ShapeDtypeStruct(shape, kind) for shape, kind in outs),
        in_specs=[SMALL] * words
        + [pl.BlockSpec() if loose else PLAIN] * (count - words)
        + [pl.BlockSpec(memory_space=pl.ANY)] * len(deps),
        scratch_shapes=list(scratch),
        compiler_params=pltpu.CompilerParams(vmem_limit_bytes=VMEM_ASK),
        cost_estimate=pl.CostEstimate(
            flops=int(time * 1.15e9), bytes_accessed=1024, transcendentals=0
        ),
    )(*operands, *deps)


def turn(token):
    return swap(token, "tensor", 1)


def body(
    kept_rows,
    owner_index,
    kept_position,
    resolution,
    mask_token,
    condition,
    modulate_weight,
    entry_weight,
    output_weight,
    expand_weight,
    shrink_weight,
    cotangent,
):
    owners = lax.axis_size("dp")
    me = lax.axis_index("dp")
    lane = lax.axis_index("tensor")
    kept_count, width_part = kept_rows.shape
    width = mask_token.shape[0]
    own_tokens = cotangent.shape[0]
    ff_part = expand_weight.shape[1]
    quarter = own_tokens // QUARTERS
    group = quarter // 2
    arrived_count = own_tokens // 2
    block = group + SPARE
    rows = QUARTERS * block
    capacity = 2 * kept_count // owners
    slots_all = owners * capacity
    direct = owners == SWAP_OWNERS
    lane_word = lane.reshape(1).astype(jnp.int32)
    me_word = me.reshape(1).astype(jnp.int32)
    big_word = resolution[:1]
    context_part = lax.dynamic_slice_in_dim(
        condition.astype(full), lane * width_part, width_part, 1
    )
    lifted = jax.nn.silu(context_part).astype(low)
    if direct:
        padded = -(-width_part // capacity) * capacity
        riders = jnp.pad(lifted, ((0, 0), (0, padded - width_part))).reshape(-1, capacity)
    else:
        padded = 128
        riders = lifted.reshape(-1, capacity)
    rider_count = riders.shape[0]
    extra = -(-(rider_count + 2) // 16) * 16
    riders = jnp.pad(riders, ((2, extra - 2 - rider_count), (0, 0)))
    slab_rows = width_part + extra
    slab_shape = (slab_rows, capacity)
    if not direct:
        slab_shape = (owners,) + slab_shape
    *slabs, slot_index = call(
        partial(
            pack_kernel,
            owners,
            FAR + NEAR if direct else range(owners),
            own_tokens.bit_length() - 1,
        ),
        ((slab_shape, low),) * (owners if direct else 1) + (((1, kept_count), jnp.int32),),
        me_word,
        kept_rows.T,
        (owner_index * own_tokens + kept_position)[None, :],
        riders,
        words=1,
        time=1.0,
        loose=direct,
    )

    steps = -(-6 * width // arrived_count)
    table, bias, bias_turned = call(
        table_kernel,
        (
            ((QUARTERS * steps, arrived_count), low),
            ((rows, rows), full),
            ((rows, rows), full),
        ),
        big_word,
        lifted,
        modulate_weight,
        words=1,
        deps=[slot_index],
        time=2.0,
        scratch=[pltpu.VMEM((8, steps * arrived_count), full)],
    )
    if direct:
        slabs = exchange_owners(dict(zip(FAR + NEAR, slabs)))
        slabs = list(slabs.values())
    else:
        slabs = exchange_owners(slabs)
    compact, slot_rank, event = call(
        partial(unpack_kernel, owners),
        (
            ((width_part + QUARTERS * steps, arrived_count), low),
            ((1, slots_all), jnp.int32),
        ),
        me_word,
        table,
        *slabs,
        words=1,
        time=1.2,
        token=True,
        scratch=[pltpu.VMEM((slab_rows, slots_all), low)],
    )
    token_rank, lifted_all = call(
        partial(spots_kernel, owners),
        (((1, own_tokens), jnp.int32), ((owners * QUARTERS, padded), full)),
        me_word,
        *slabs,
        words=1,
        deps=[event],
        time=1.2,
        scratch=[pltpu.VMEM((extra, slots_all), low)],
    )
    if not direct:
        owner_order = jnp.arange(owners, dtype=jnp.int32) ^ me
        lifted_all = slabs[0][:, width_part + 2 : width_part + 2 + rider_count]
        lifted_all = lifted_all.reshape(owners * QUARTERS, width_part)
    spatial_pieces = gather_blocks(compact)
    entry_flat = jnp.transpose(entry_weight, (1, 2, 0)).reshape(3 * width_part, width)
    token_shape = ((block, width), low)
    half = 2 * block
    chosen, spatial_own, normed_one, projected, attended_far, part_2, part_3 = call(
        entry_kernel,
        (
            ((QUARTERS, 6 * width), full),
            token_shape,
            ((rows, width), low),
            ((rows, 3 * width_part), low),
            ((half, width_part), low),
            token_shape,
            token_shape,
        ),
        lane_word,
        big_word,
        *spatial_pieces,
        mask_token[None, :],
        entry_flat,
        bias,
        output_weight,
        words=2,
        deps=[token_rank],
        time=5.0,
        scratch=[
            pltpu.VMEM((width, arrived_count), low),
            pltpu.VMEM((8, steps * arrived_count), full),
        ],
    )
    far, across, start = sum_far(part_2, part_3)
    attended_near, part_0, part_1 = call(
        attend_kernel,
        (((half, width_part), low), token_shape, token_shape),
        projected,
        bias,
        output_weight,
        deps=[start],
        time=3.0,
    )
    got = swap(part_1, "tensor", 1)
    feed_grad_near, feed_grad_far, upstream_own, back_near, back_far = call(
        upstream_kernel,
        (
            ((half, width), low),
            ((half, width), low),
            ((block, width), full),
            ((half, width), full),
            ((half, width), full),
        ),
        lane_word,
        token_rank,
        chosen,
        cotangent,
        shrink_weight,
        words=1,
        deps=[part_1],
        time=3.6,
    )
    branch, middle, normed_two_own = call(
        middle_kernel,
        (((block, width), full), ((block, width), full), token_shape),
        part_0,
        got,
        across,
        spatial_own,
        chosen,
        deps=[back_far],
        time=0.6,
    )

    def feed_call(piece_0, piece_1, back, *deps):
        return call(
            feed_kernel,
            (((half, width), low), ((half, width), low), ((half, width), low))
            + (token_shape, token_shape),
            piece_0,
            piece_1,
            back,
            expand_weight,
            deps=deps,
            time=2.4,
        )

    near_piece = swap(normed_two_own, "tensor", 1)
    across = swap(normed_two_own, "tensor", 2)
    normed_near, activated_near, hidden_near, part_0, part_1 = feed_call(
        normed_two_own, near_piece, back_near
    )
    *partials, event = call(
        partial_kernel,
        (((width, ff_part), low),) * 2,
        feed_grad_near,
        activated_near,
        normed_near,
        hidden_near,
        time=2.5,
        token=True,
    )
    (across,) = call(copy_kernel, (token_shape,), across, deps=[event], time=0.3)
    last_piece = swap(across, "tensor", 1)
    normed_far, activated_far, hidden_far, part_2, part_3 = feed_call(
        across, last_piece, back_far
    )
    feed_groups = [
        [([feed_grad_far], [activated_far])],
        [([normed_far], [hidden_far])],
    ]
    event = part_0
    if direct:
        feed_given, feed_kept, event = start_sums(feed_groups, FEED_SPLIT, (), 3.5, partials)
        feed_got = cross(feed_given, 1, 2)
    far, across, start = sum_far(part_2, part_3, [event])
    got = swap(part_1, "tensor", 1)
    middle_grad, branch_grad_own, sums, start = call(
        middle_back_kernel,
        (((block, width), full), token_shape, ((SPARE, width), full)),
        part_0,
        got,
        across,
        middle,
        branch,
        upstream_own,
        chosen,
        deps=[start],
        time=0.7,
        token=True,
    )
    branch_near = swap(branch_grad_own, "tensor", 1)
    branch_across = swap(branch_grad_own, "tensor", 2)
    feed_parts = call(
        feed_out_kernel,
        (token_shape,) * QUARTERS,
        activated_near,
        activated_far,
        shrink_weight,
        deps=[turn(start)],
        time=0.1,
    )
    feed_far = swap(feed_parts[3], "tensor", 1)
    feed_near = swap(feed_parts[1], "tensor", 1)
    probs, event = call(
        probs_kernel,
        (((width_part // HEAD, rows, rows), low),),
        projected,
        bias_turned,
        deps=[feed_parts[0]],
        time=0.1,
        token=True,
    )
    (branch_across,) = call(copy_kernel, (token_shape,), branch_across, deps=[event], time=0.1)
    branch_pieces = [
        branch_grad_own,
        branch_near,
        branch_across,
        swap(branch_across, "tensor", 1),
    ]
    feed_far, start = call(
        add_kernel,
        (token_shape,),
        feed_parts[2],
        feed_far,
        deps=[branch_pieces[2]],
        time=0.1,
        token=True,
    )
    branch_grad, projected_grad, event = call(
        attend_back_kernel,
        (((rows, width), low), ((rows, 3 * width_part), low)),
        projected,
        probs,
        output_weight,
        *branch_pieces,
        deps=[turn(start)],
        time=0.1,
        token=True,
    )
    feed_across = swap(feed_far, "tensor", 2)
    if direct:
        feed_given, feed_kept, event = halve_sums(feed_kept, feed_got, [event])
        feed_got = cross(feed_given, 2, 1)
    part_2, part_3 = call(
        partial(entry_back_kernel, 1),
        (token_shape, token_shape),
        projected_grad,
        entry_flat,
        deps=[feed_across, feed_near, event],
        time=0.1,
    )
    far, across, start = sum_far(part_2, part_3)
    part_0, part_1 = call(
        partial(entry_back_kernel, 0),
        (token_shape, token_shape),
        projected_grad,
        entry_flat,
        deps=[start],
        time=0.2,
    )
    got = swap(part_1, "tensor", 1)
    entry_groups = [
        [([normed_one], [projected_grad]), ([branch_grad], [attended_near, attended_far])]
    ]
    event = part_1
    if direct:
        entry_given, entry_kept, event = start_sums(entry_groups, ENTRY_SPLIT, [got], 0.2)
        entry_got = cross(entry_given, 1, 2)
    *back_pieces, back_token = call(
        back_kernel,
        (((width_part + 80, group), low),) * QUARTERS,
        lane_word,
        part_0,
        got,
        across,
        spatial_own,
        middle_grad,
        chosen,
        sums,
        feed_parts[0],
        feed_near,
        feed_across,
        upstream_own,
        words=1,
        deps=[event],
        time=BACK_TIME,
        token=True,
        scratch=[pltpu.VMEM((width, group), low), pltpu.VMEM((80, 128), full)],
    )
    if direct:
        feed_got, feed_kept, joined = join_sums(feed_kept, feed_got, [back_token])
    back_pieces = [
        back_pieces[0],
        swap(back_pieces[1], "tensor", 1),
        *swap_pair(back_pieces[2:]),
    ]
    chunks = 6 * width // 128
    logistic = jax.nn.sigmoid(context_part)
    logistic = logistic * (1.0 + context_part * (1.0 - logistic))
    if direct:
        entry_given, entry_kept, halved = halve_sums(entry_kept, entry_got, [back_token], HALVE_TIME)
        entry_got = cross(entry_given, 2, 1)
        shrink_grad, expand_grad, total_token = call(
            total_kernel,
            (((width // owners, ff_part), full),) * 2,
            feed_kept,
            feed_got,
            deps=[halved],
            time=TOTAL_TIME,
            token=True,
        )
        slabs, table_grad, event = call(
            partial(slots_kernel, owners),
            (
                ((owners, width_part + RIDERS, capacity), low),
                ((QUARTERS, chunks, 128), low),
            ),
            lane_word,
            me_word,
            big_word,
            slot_rank,
            *back_pieces,
            words=3,
            time=0.1,
            token=True,
            scratch=[
                pltpu.VMEM((QUARTERS, chunks + 2, 128), full),
                pltpu.VMEM((16, 128), full),
            ],
        )
        (slabs,) = exchange_owners([slabs])
        table_grad = table_grad.reshape(QUARTERS, 6 * width)
        entry_got, entry_kept, event = join_sums(entry_kept, entry_got, [total_token])
        out_pieces = call(
            out_kernel,
            (((width_part + 16, group), low),) * QUARTERS,
            lane_word,
            feed_parts[0],
            feed_near,
            feed_across,
            middle,
            chosen,
            words=1,
            deps=[event],
            time=0.1,
            scratch=[pltpu.VMEM((width, group), low), pltpu.VMEM((16, 128), full)],
        )
        out_pieces = [
            out_pieces[0],
            swap(out_pieces[1], "tensor", 1),
            *swap_pair(out_pieces[2:]),
        ]
        layer_out, layer_token = call(
            layer_kernel,
            (((width_part, own_tokens), low),),
            lane_word,
            token_rank,
            *out_pieces,
            words=1,
            deps=[event],
            time=0.1,
            token=True,
            scratch=[pltpu.VMEM((8, width), full), pltpu.VMEM((width, 8), full)],
        )
        kept_grad, modulate_grad, mask_grad, kept_token = call(
            partial(kept_kernel, owners),
            (
                ((width_part, kept_count), low),
                ((width_part, 6 * width // owners), full),
                ((1, width // owners), full),
            ),
            me_word,
            slot_index,
            lifted_all,
            slabs,
            words=1,
            deps=[layer_token],
            time=KEPT_TIME,
            token=True,
            scratch=[pltpu.VMEM((owners * QUARTERS, 1024), full)],
        )
        mask_grad = mask_grad[0]
    else:
        event = back_pieces[1]
        rows_back = jnp.concatenate([piece[:width_part] for piece in back_pieces], axis=1)
        rank_ids = jnp.arange(arrived_count, dtype=jnp.int32)
        rank_ids = ((rank_ids // group) ^ lane) * group + rank_ids % group
        matrix = (rank_ids[:, None] == slot_rank).astype(low)
        slabs = dot(rows_back, matrix).astype(low).reshape(width_part, owners, capacity)
        slabs = jnp.take(jnp.transpose(slabs, (1, 0, 2)), owner_order, axis=0)
        slabs = jnp.take(exchange_owners([slabs])[0], owner_order, axis=0)
        slabs = jnp.transpose(slabs, (1, 0, 2)).reshape(width_part, slots_all)
        slot_ids = jnp.arange(slots_all, dtype=jnp.int32)[:, None]
        kept_grad = dot(slabs, (slot_ids == slot_index).astype(low)).astype(low)
        riders = jnp.stack(
            [piece[width_part : width_part + 8 * width // 128] for piece in back_pieces]
        )
        riders = riders.reshape(QUARTERS, 8, width).astype(full)
        mask_total = jnp.sum(riders[:, 6] + riders[:, 7], axis=0)
        table_local = riders[:, :6].reshape(QUARTERS, 6 * width)
        table_small = jnp.take(table_local, jnp.arange(QUARTERS, dtype=jnp.int32) ^ lane, axis=0)
        first = jnp.arange(QUARTERS, dtype=jnp.int32)[:, None] == 0
        table_big = jnp.where(first, jnp.sum(table_local, axis=0, keepdims=True), 0.0)
        table_grad = jnp.where(big_word[0] == 1, table_big, table_small).astype(low)
        sent = jnp.transpose(table_grad.reshape(QUARTERS, owners, -1), (1, 0, 2))
        table_all = exchange_owners([sent])[0].reshape(owners * QUARTERS, -1)
        modulate_grad = dot(lifted_all, table_all, ((0,), (0,)))
        mask_grad = lax.psum_scatter(mask_total, "dp", scatter_dimension=0, tiled=True)
    condition_grad = dot(table_grad, modulate_weight, ((1,), (1,))) * logistic
    if not direct:
        out_pieces = call(
            out_kernel,
            (((width_part + 16, group), low),) * QUARTERS,
            lane_word,
            feed_parts[0],
            feed_near,
            feed_across,
            middle,
            chosen,
            words=1,
            deps=[],
            time=0.1,
            scratch=[pltpu.VMEM((width, group), low), pltpu.VMEM((16, 128), full)],
        )
        out_pieces = [
            out_pieces[0],
            swap(out_pieces[1], "tensor", 1),
            *swap_pair(out_pieces[2:]),
        ]
        layer_out, layer_token = call(
            layer_kernel,
            (((width_part, own_tokens), low),),
            lane_word,
            token_rank,
            *out_pieces,
            words=1,
            deps=[],
            time=0.1,
            token=True,
            scratch=[pltpu.VMEM((8, width), full), pltpu.VMEM((width, 8), full)],
        )
    rows_part = width // owners
    if direct:
        entry_grad, output_grad = call(
            total_kernel,
            (((3, rows_part, width_part), full), ((rows_part, width_part), full)),
            entry_kept,
            entry_got,
            deps=[kept_token],
            time=0.8,
        )
    else:
        totals = []
        for number, pairs in enumerate(feed_groups + entry_groups):
            total = [
                dot(jnp.concatenate(lhs), jnp.concatenate(rhs), ((0,), (0,))) for lhs, rhs in pairs
            ]
            total = jnp.concatenate(total, axis=1)
            if number < len(partials):
                total = total + partials[number].astype(full)
            totals.append(sum_owners(total.astype(low).reshape(owners, rows_part, -1)))
        shrink_grad, expand_grad, entry_grad = totals
        output_grad = entry_grad[:, 3 * width_part :]
        entry_grad = entry_grad[:, : 3 * width_part].reshape(rows_part, 3, width_part)
        entry_grad = jnp.transpose(entry_grad, (1, 0, 2))

    return (
        layer_out.T,
        kept_grad.T,
        mask_grad,
        condition_grad,
        modulate_grad,
        jnp.transpose(entry_grad, (1, 0, 2)),
        output_grad.T,
        expand_grad,
        shrink_grad.T,
    )


def solution(mesh):
    return jax.shard_map(
        body,
        mesh=mesh,
        in_specs=(
            P("dp", "tensor"),
            P("dp"),
            P("dp"),
            P("dp"),
            P(),
            P("dp", None),
            P("tensor", None),
            P(None, None, "tensor"),
            P("tensor", None),
            P(None, "tensor"),
            P("tensor", None),
            P("dp", None),
        ),
        out_specs=(
            P("dp", "tensor"),
            P("dp", "tensor"),
            P("dp"),
            P("dp", "tensor"),
            P("tensor", "dp"),
            P("dp", None, "tensor"),
            P("tensor", "dp"),
            P("dp", "tensor"),
            P("tensor", "dp"),
        ),
        check_vma=False,
    )
```

```python
from functools import partial

import jax
import jax.numpy as jnp
from jax import lax
from jax.experimental import pallas as pl
from jax.experimental.pallas import tpu as pltpu
from jax.sharding import PartitionSpec as P

HEAD = 72
QUARTERS = 4
SPARE = 8
scale = HEAD ** (-0.5)
epsilon = 1e-06
gelu_coeff = 0.7978845608028654
low = jnp.bfloat16
full = jnp.float32
VMEM_ASK = 12 * 1024 * 1024
RIDERS = 48
SWAP_OWNERS = 8
FEED_SPLIT = 72
ENTRY_SPLIT = 72
FAR = (6, 7, 4, 5)
NEAR = (2, 3, 1, 0)
JOIN_TIME = 0.1
KEPT_TIME = 0.1
TOTAL_TIME = 14.0
HALVE_TIME = 0.35
BACK_TIME = 0.1
SMALL = pl.BlockSpec(memory_space=pltpu.SMEM)
PLAIN = pl.BlockSpec(memory_space=pltpu.VMEM)


def dot(a, b, dims=((1,), (0,))):
    return lax.dot_general(a, b, (dims, ((), ())), preferred_element_type=full)


def normalize(rows):
    centered = rows - jnp.mean(rows, axis=-1, keepdims=True)
    inverse = lax.rsqrt(jnp.mean(centered * centered, axis=-1, keepdims=True) + epsilon)
    return (centered * inverse, inverse)


def normalize_back(unit, inverse, grad):
    return inverse * (
        grad
        - jnp.mean(grad, axis=-1, keepdims=True)
        - unit * jnp.mean(grad * unit, axis=-1, keepdims=True)
    )


def gelu_both(value):
    square = value * value
    inner = value * (gelu_coeff + 0.044715 * gelu_coeff * square)
    half = 0.5 + 0.5 * jnp.tanh(inner)
    activated = value * half
    outer = 2.0 * gelu_coeff + 6.0 * 0.044715 * gelu_coeff * square
    return (activated, half + activated * (1.0 - half) * outer)


def swap(value, axis, bit):
    size = lax.axis_size(axis)
    return lax.ppermute(value, axis, [(index, index ^ bit) for index in range(size)])


def swap_pair(pieces):
    came = swap(jnp.stack(pieces), "tensor", 2)
    return came[0], swap(came[1], "tensor", 1)


def gather_blocks(own):
    near = swap(own, "tensor", 1)
    across = swap(own, "tensor", 2)
    return [own, near, across, swap(across, "tensor", 1)]


def sum_far(part_2, part_3, deps=()):
    got = swap(part_3, "tensor", 1)
    far, token = call(
        add_kernel, ((part_2.shape, low),), part_2, got, deps=deps, time=0.1, token=True
    )
    return far, swap(far, "tensor", 2), turn(token)


def sum_owners(total):
    owners, rows, columns = total.shape
    me = lax.axis_index("dp")
    step = 1
    while step < owners:
        pairs = total.reshape(-1, 2, rows, columns)
        mine = (me // step) % 2
        given = lax.dynamic_index_in_dim(pairs, 1 - mine, 1, keepdims=False)
        kept = lax.dynamic_index_in_dim(pairs, mine, 1, keepdims=False)
        total = kept.astype(full) + swap(given, "dp", step).astype(full)
        step *= 2
        total = total if step == owners else total.astype(low)
    return total[0]


def part_shapes(count, upper, lower, columns):
    return [((count, upper, columns), low), ((count, lower, columns), low)]


def start_sums(groups, split, deps=(), time=3.0, bases=()):
    width = groups[0][0][0][0].shape[1]
    columns = sum(rhs[0].shape[1] for _, rhs in groups[0])
    rows = width // 8
    shapes = part_shapes(4 * len(groups), split, rows - split, columns)
    counts = [[(len(lhs), len(rhs)) for lhs, rhs in pairs] for pairs in groups]
    given_0, given_1, kept_0, kept_1, token = call(
        partial(weight_kernel, counts, len(bases)),
        shapes + shapes,
        lax.axis_index("dp").reshape(1).astype(jnp.int32),
        *[value for pairs in groups for lhs, rhs in pairs for value in (*lhs, *rhs)],
        *bases,
        words=1,
        deps=deps,
        time=time,
        scratch=[pltpu.VMEM((width, columns), full)],
        token=True,
    )
    return (given_0, given_1), (kept_0, kept_1), token


def cross(given, first, second):
    return swap(given[0], "dp", first), swap(given[1], "dp", second)


def halve_sums(kept, got, deps=(), time=0.1):
    count, _, columns = kept[0].shape
    shapes = part_shapes(count // 2, kept[0].shape[1], kept[1].shape[1], columns)
    given_0, given_1, kept_0, kept_1, token = call(
        halve_kernel,
        shapes + shapes,
        lax.axis_index("dp").reshape(1).astype(jnp.int32),
        *kept,
        *got,
        words=1,
        deps=deps,
        time=time,
        token=True,
    )
    return (given_0, given_1), (kept_0, kept_1), token


def join_sums(kept, got, deps=()):
    count, _, columns = kept[0].shape
    shape = ((count // 2, kept[0].shape[1] + kept[1].shape[1], columns), low)
    given, kept, token = call(
        join_kernel,
        (shape, shape),
        lax.axis_index("dp").reshape(1).astype(jnp.int32),
        *kept,
        *got,
        words=1,
        deps=deps,
        time=JOIN_TIME,
        token=True,
    )
    return swap(given, "dp", 4), kept, token


def exchange_owners(slabs):
    if isinstance(slabs, dict):
        return {index: swap(slab, "dp", index) if index else slab for index, slab in slabs.items()}
    return [lax.all_to_all(slabs[0], "dp", split_axis=0, concat_axis=0, tiled=True)]


def attend(projected_ref, bias_ref, output_ref, attended_ref, chunk, half, width_part):
    span = slice(chunk * half, (chunk + 1) * half)
    pieces = []
    for head in range(width_part // HEAD):
        at = head * HEAD
        queries = projected_ref[span, at : at + HEAD]
        keys = projected_ref[:, width_part + at : width_part + at + HEAD]
        values = projected_ref[:, 2 * width_part + at : 2 * width_part + at + HEAD]
        scores = dot(queries, keys, ((1,), (1,))) * scale + bias_ref[span, :]
        spread = jnp.exp(scores - jnp.max(scores, axis=1, keepdims=True))
        probs = spread * (1.0 / jnp.sum(spread, axis=1, keepdims=True))
        pieces.append(dot(probs.astype(low), values))
    attended = jnp.concatenate(pieces, axis=1).astype(low)
    attended_ref[...] = attended
    return dot(attended, output_ref[...])


def entry_kernel(
    lane_ref,
    big_ref,
    piece_0,
    piece_1,
    piece_2,
    piece_3,
    mask_ref,
    entry_ref,
    bias_ref,
    output_ref,
    chosen_ref,
    spatial_ref,
    normed_ref,
    projected_ref,
    attended_ref,
    part_0,
    part_1,
    gathered,
    table,
):
    lane = lane_ref[0]
    block, width = spatial_ref.shape
    width_part = width // QUARTERS
    group = block - SPARE
    half = 2 * block
    pieces = (piece_0, piece_1, piece_2, piece_3)
    for index, piece in enumerate(pieces):
        at = pl.multiple_of((lane ^ index) * width_part, 16)
        gathered[pl.ds(at, width_part), :] = piece[:width_part, :]
    summed = pieces[0][width_part:, :].astype(full)
    for piece in pieces[1:]:
        summed = summed + piece[width_part:, :].astype(full)
    span = summed.shape[1]
    steps = summed.shape[0] // QUARTERS
    for row in range(QUARTERS):
        for step in range(steps):
            from_row = row * steps + step
            table[row : row + 1, step * span : (step + 1) * span] = summed[from_row : from_row + 1]
    for index in range(QUARTERS):
        row = jnp.where(big_ref[0] == 1, 0, lane ^ index)
        chosen_ref[index : index + 1, :] = table[pl.ds(row, 1), : 6 * width]
    spare_id = lax.broadcasted_iota(jnp.int32, (SPARE, width), 0)
    spare = jnp.where(spare_id == 0, mask_ref[...].astype(full), 0.0)
    for chunk in (1, 0):
        span = slice(chunk * half, (chunk + 1) * half)
        normed = []
        for index in (2 * chunk, 2 * chunk + 1):
            at = pl.multiple_of((lane ^ index) * group, 128)
            kept = jnp.transpose(gathered[:, pl.ds(at, group)].astype(full))
            rows = jnp.concatenate([kept, spare], axis=0)
            if index == 0:
                spatial_ref[...] = rows.astype(low)
            unit, inverse = normalize(rows)
            shift = chosen_ref[index : index + 1, :width]
            gain = chosen_ref[index : index + 1, width : 2 * width]
            normed.append(unit * (1.0 + gain) + shift)
        normed = jnp.concatenate(normed, axis=0).astype(low)
        normed_ref[span, :] = normed
        projected_ref[span, :] = dot(normed, entry_ref[...], ((1,), (1,))).astype(low)
    part = attend(projected_ref, bias_ref, output_ref, attended_ref, 1, half, width_part)
    part_0[...] = part[:block].astype(low)
    part_1[...] = part[block:].astype(low)


def attend_kernel(projected_ref, bias_ref, output_ref, attended_ref, part_0, part_1):
    block = part_0.shape[0]
    part = attend(
        projected_ref, bias_ref, output_ref, attended_ref, 0, 2 * block, output_ref.shape[0]
    )
    part_0[...] = part[:block].astype(low)
    part_1[...] = part[block:].astype(low)


def middle_kernel(
    part_0, part_1, part_2, spatial_ref, chosen_ref, branch_ref, middle_ref, normed_ref
):
    width = spatial_ref.shape[1]
    branch = part_0[...].astype(full) + part_1[...].astype(full) + part_2[...].astype(full)
    branch_ref[...] = branch
    middle = spatial_ref[...].astype(full) + chosen_ref[0:1, 2 * width : 3 * width] * branch
    middle_ref[...] = middle
    unit, inverse = normalize(middle)
    shift = chosen_ref[0:1, 3 * width : 4 * width]
    gain = chosen_ref[0:1, 4 * width : 5 * width]
    normed_ref[...] = (unit * (1.0 + gain) + shift).astype(low)


def feed_kernel(
    piece_0,
    piece_1,
    back_ref,
    expand_ref,
    normed_ref,
    activated_ref,
    hidden_grad_ref,
    part_0,
    part_1,
):
    block = piece_0.shape[0]
    normed = jnp.concatenate([piece_0[...].astype(full), piece_1[...].astype(full)], axis=0)
    normed = normed.astype(low)
    normed_ref[...] = normed
    hidden = dot(normed, expand_ref[...])
    activated, slope = gelu_both(hidden)
    activated_ref[...] = activated.astype(low)
    hidden_grad = (back_ref[...] * slope).astype(low)
    hidden_grad_ref[...] = hidden_grad
    part = dot(hidden_grad, expand_ref[...], ((1,), (1,)))
    part_0[...] = part[:block].astype(low)
    part_1[...] = part[block:].astype(low)


def middle_back_kernel(
    part_0,
    part_1,
    part_2,
    middle_ref,
    branch_ref,
    upstream_ref,
    chosen_ref,
    middle_grad_ref,
    branch_grad_ref,
    sums_ref,
):
    width = middle_ref.shape[1]
    normed_grad = part_0[...].astype(full) + part_1[...].astype(full) + part_2[...].astype(full)
    unit, inverse = normalize(middle_ref[...])
    gain = chosen_ref[0:1, 4 * width : 5 * width]
    middle_grad = upstream_ref[...] + normalize_back(unit, inverse, normed_grad * (1.0 + gain))
    middle_grad_ref[...] = middle_grad
    branch_grad_ref[...] = (chosen_ref[0:1, 2 * width : 3 * width] * middle_grad).astype(low)
    sums_ref[0:1, :] = jnp.sum(middle_grad * branch_ref[...], axis=0, keepdims=True)
    sums_ref[1:2, :] = jnp.sum(normed_grad, axis=0, keepdims=True)
    sums_ref[2:3, :] = jnp.sum(normed_grad * unit, axis=0, keepdims=True)


def probs_kernel(projected_ref, bias_ref, probs_ref):
    width_part = projected_ref.shape[1] // 3
    for head in range(width_part // HEAD):
        at = head * HEAD
        queries = projected_ref[:, at : at + HEAD]
        keys = projected_ref[:, width_part + at : width_part + at + HEAD]
        scores = dot(keys, queries, ((1,), (1,))) * scale + bias_ref[...]
        spread = jnp.exp(scores - jnp.max(scores, axis=0, keepdims=True))
        probs = spread * (1.0 / jnp.sum(spread, axis=0, keepdims=True))
        probs_ref[head] = probs.astype(low)


def attend_back_kernel(
    projected_ref,
    probs_ref,
    output_ref,
    piece_0,
    piece_1,
    piece_2,
    piece_3,
    branch_grad_ref,
    grad_ref,
):
    rows, width_all = projected_ref.shape
    width_part = width_all // 3
    block = piece_0.shape[0]
    half = 2 * block
    for chunk, pair in enumerate(((piece_0, piece_1), (piece_2, piece_3))):
        branch_grad_ref[chunk * half : (chunk + 1) * half, :] = jnp.concatenate(
            [piece[...].astype(full) for piece in pair], axis=0
        ).astype(low)
    attended_grad = dot(branch_grad_ref[...], output_ref[...], ((1,), (1,))).astype(low)
    pieces = [[], [], []]
    for head in range(width_part // HEAD):
        at = head * HEAD
        queries = projected_ref[:, at : at + HEAD]
        keys = projected_ref[:, width_part + at : width_part + at + HEAD]
        values = projected_ref[:, 2 * width_part + at : 2 * width_part + at + HEAD]
        grad = attended_grad[:, at : at + HEAD]
        probs = probs_ref[head]
        pieces[2].append(dot(probs, grad))
        probs = probs.astype(full)
        prob_grad = dot(values, grad, ((1,), (1,)))
        delta = jnp.sum(probs * prob_grad, axis=0, keepdims=True)
        score_grad = (probs * (prob_grad - delta)).astype(low)
        pieces[1].append(dot(score_grad, queries) * scale)
        pieces[0].append(dot(score_grad, keys, ((0,), (0,))) * scale)
    grad_ref[...] = jnp.concatenate(pieces[0] + pieces[1] + pieces[2], axis=1).astype(low)


def entry_back_kernel(chunk, grad_ref, entry_ref, part_0, part_1):
    block = part_0.shape[0]
    part = dot(grad_ref[2 * chunk * block : 2 * (chunk + 1) * block, :], entry_ref[...])
    part_0[...] = part[:block].astype(low)
    part_1[...] = part[block:].astype(low)


def pack_kernel(owners, chosen, shift, extra, capacity, me_ref, kept_ref, spot_ref, *refs):
    direct = len(refs) == owners + 1
    out_refs = refs if direct else refs[1:]
    slot_ref = out_refs[-1]
    kept_count = kept_ref.shape[1]
    owner_local = (spot_ref[...] >> shift) ^ me_ref[0]
    owner_id = lax.broadcasted_iota(jnp.int32, (owners, kept_count), 0)
    hot = (owner_id == owner_local).astype(full)
    row_id = lax.broadcasted_iota(jnp.int32, (kept_count, kept_count), 0)
    column_id = lax.broadcasted_iota(jnp.int32, (kept_count, kept_count), 1)
    before = dot(hot.astype(low), (row_id < column_id).astype(full).astype(low))
    rank = jnp.sum(hot * before, axis=0, keepdims=True).astype(jnp.int32)
    slot = owner_local * capacity + rank
    slot_ref[...] = slot
    coded = (spot_ref[...] & ((1 << shift) - 1)) + 1
    tag_id = lax.broadcasted_iota(jnp.int32, (extra, kept_count), 0)
    tags = jnp.where(tag_id == 0, coded >> 5, jnp.where(tag_id == 1, coded & 31, 0))
    rows = jnp.concatenate([kept_ref[...], tags.astype(full).astype(low)], axis=0)
    slot_id = lax.broadcasted_iota(jnp.int32, (capacity, kept_count), 0)
    for number, index in enumerate(chosen):
        matrix = (slot_id + index * capacity == slot).astype(full).astype(low)
        slab = dot(rows, matrix, ((1,), (1,)))
        split = kept_ref.shape[0]
        if not direct:
            lower = slab[split:] + refs[0][...].astype(full)
            slab = jnp.concatenate([slab[:split], lower], axis=0)
            out_refs[0][me_ref[0] ^ index] = slab.astype(low)
        else:
            out_refs[number][...] = slab.astype(low)


def places(owners, me_ref, slab_refs, arrived, width_part):
    slots_all = arrived.shape[1]
    capacity = slots_all // owners
    for index in range(owners):
        if len(slab_refs) == 1:
            slab = slab_refs[0][me_ref[0] ^ index]
        else:
            slab = slab_refs[(FAR + NEAR).index(index)][...]
        rows = arrived.shape[0]
        arrived[:, index * capacity : (index + 1) * capacity] = slab[slab.shape[0] - rows :]
    tags = arrived[width_part : width_part + 16, :].astype(full)
    place = tags[0:1] * 32.0 + tags[1:2] - 1.0
    turned = jnp.transpose(jnp.broadcast_to(place, (8, slots_all)))[:, 0:1]
    return place, jnp.where(turned < 0.0, 1e9, turned)


def unpack_kernel(owners, me_ref, table_ref, *refs):
    slab_refs, (compact_ref, slot_rank_ref, arrived) = refs[:-3], refs[-3:]
    arrived_count = compact_ref.shape[1]
    width_part = compact_ref.shape[0] - table_ref.shape[0]
    place, turned = places(owners, me_ref, slab_refs, arrived, width_part)
    slot_rank = jnp.sum(jnp.where(turned < place, 1.0, 0.0), axis=0, keepdims=True)
    slot_rank = jnp.where(place < 0.0, -1.0, slot_rank).astype(jnp.int32)
    slot_rank_ref[...] = slot_rank
    rank_id = lax.broadcasted_iota(jnp.int32, (arrived_count, arrived.shape[1]), 0)
    matrix = (rank_id == slot_rank).astype(full).astype(low)
    compact_ref[:width_part, :] = dot(arrived[:width_part, :], matrix, ((1,), (1,))).astype(low)
    compact_ref[width_part:, :] = table_ref[...]


def spots_kernel(owners, me_ref, *refs):
    slab_refs, (token_rank_ref, arrived) = refs[:-2], refs[-2:]
    own_tokens = token_rank_ref.shape[1]
    _, turned = places(owners, me_ref, slab_refs, arrived, 0)
    spot = lax.broadcasted_iota(jnp.int32, (1, own_tokens), 1).astype(full)
    token_rank = jnp.sum(jnp.where(turned < spot, 1.0, 0.0), axis=0, keepdims=True)
    filled = jnp.sum(jnp.where(turned == spot, 1.0, 0.0), axis=0, keepdims=True)
    token_rank_ref[...] = jnp.where(filled > 0.0, token_rank, -1.0).astype(jnp.int32)


def back_kernel(
    lane_ref,
    part_0,
    part_1,
    part_2,
    spatial_ref,
    middle_grad_ref,
    chosen_ref,
    sums_ref,
    feed_0,
    feed_1,
    feed_2,
    upstream_ref,
    piece_0,
    piece_1,
    piece_2,
    piece_3,
    turned,
    riders,
):
    lane = lane_ref[0]
    block, width = spatial_ref.shape
    group = block - SPARE
    width_part = width // QUARTERS
    normed_grad = part_0[...].astype(full) + part_1[...].astype(full) + part_2[...].astype(full)
    unit, inverse = normalize(spatial_ref[...].astype(full))
    gain = chosen_ref[0:1, width : 2 * width]
    grad = middle_grad_ref[...] + normalize_back(unit, inverse, normed_grad * (1.0 + gain))
    turned[...] = jnp.transpose(grad[:group]).astype(low)
    feed = feed_0[...].astype(full) + feed_1[...].astype(full) + feed_2[...].astype(full)
    mask_sum = grad[group : group + 1]
    mask_high = mask_sum.astype(low).astype(full)
    fields = [
        jnp.sum(normed_grad, axis=0, keepdims=True),
        jnp.sum(normed_grad * unit, axis=0, keepdims=True),
        sums_ref[0:1, :],
        sums_ref[1:2, :],
        sums_ref[2:3, :],
        jnp.sum(feed * upstream_ref[...], axis=0, keepdims=True),
        mask_high,
        mask_sum - mask_high,
    ]
    chunks = width // 128
    riders[...] = jnp.zeros_like(riders)
    for number, field in enumerate(fields):
        for chunk in range(chunks):
            at = number * chunks + chunk
            riders[at : at + 1, :] = field[:, chunk * 128 : (chunk + 1) * 128]
    rider_rows = riders[...].astype(low)
    for index, piece in enumerate((piece_0, piece_1, piece_2, piece_3)):
        at = pl.multiple_of((lane ^ index) * width_part, 16)
        piece[:width_part, :] = turned[pl.ds(at, width_part), :]
        piece[width_part:, :] = rider_rows


def slots_kernel(
    owners,
    lane_ref,
    me_ref,
    big_ref,
    rank_ref,
    lifted_ref,
    piece_0,
    piece_1,
    piece_2,
    piece_3,
    slabs_ref,
    table_ref,
    table,
    mask_total,
):
    lane = lane_ref[0]
    me = me_ref[0]
    group = piece_0.shape[1]
    slots_all = rank_ref.shape[1]
    capacity = slots_all // owners
    chunks = table_ref.shape[1]
    width_part = slabs_ref.shape[1] - RIDERS
    pieces = [piece_0, piece_1, piece_2, piece_3]
    rows = jnp.concatenate([piece[:width_part, :] for piece in pieces], axis=1)
    row_id = lax.broadcasted_iota(jnp.int32, (group, slots_all), 0)
    matrix = jnp.concatenate(
        [
            (row_id + (lane ^ index) * group == rank_ref[...]).astype(full).astype(low)
            for index in range(QUARTERS)
        ],
        axis=0,
    )
    slots = dot(rows, matrix)
    table[...] = jnp.zeros_like(table)
    summed = jnp.zeros((chunks, 128), full)
    mask_sum = jnp.zeros((16, 128), full)
    mask_rows = chunks // 6
    for index, piece in enumerate(pieces):
        field = piece[width_part : width_part + chunks, :].astype(full)
        summed = summed + field
        rest = piece[width_part + chunks - chunks % 16 :, :].astype(full)
        table[lane ^ index, :chunks, :] = field
        at = chunks % 16
        mask_sum = mask_sum + jnp.concatenate(
            [
                rest[at : at + mask_rows] + rest[at + mask_rows : at + 2 * mask_rows],
                jnp.zeros((16 - mask_rows, 128), full),
            ],
            axis=0,
        )
    mask_total[...] = mask_sum

    @pl.when(big_ref[0] == 1)
    def _():
        table[...] = jnp.zeros_like(table)
        table[0, :chunks, :] = summed

    table_ref[...] = table[:, :chunks, :].astype(low)
    for index in range(owners):
        owner = me ^ index
        start = (owner * chunks) // owners
        fields = [table[row, pl.ds(start, 8), :] for row in range(QUARTERS)]
        mask_start = (owner * mask_rows) // owners
        mask_part = mask_total[pl.ds(mask_start, 2), :]
        mask_high = mask_part.astype(low).astype(full)
        fields += [mask_high, mask_part - mask_high, lifted_ref[...].astype(full)]
        slab = jnp.concatenate([slots[:, index * capacity : (index + 1) * capacity]] + fields, axis=0)
        slabs_ref[owner] = slab.astype(low)


def kept_kernel(
    owners, me_ref, slot_ref, slabs_ref, kept_ref, modulate_ref, mask_ref, table, lifted_all
):
    width_part, kept_count = kept_ref.shape
    capacity = slabs_ref.shape[2]
    table_part = modulate_ref.shape[1]
    mask_part = mask_ref.shape[1]
    me = me_ref[0]
    slabs = [slabs_ref[me ^ index] for index in range(owners)]
    rows = jnp.concatenate([slab[:width_part] for slab in slabs], axis=1)
    slot_id = lax.broadcasted_iota(jnp.int32, (owners * capacity, kept_count), 0)
    matrix = (slot_id == slot_ref[...]).astype(full).astype(low)
    kept_ref[...] = dot(rows, matrix).astype(low)
    mask_sum = jnp.zeros((1, 256), full)
    for index, slab in enumerate(slabs):
        rider = slab[width_part:].astype(full)
        for row in range(QUARTERS):
            at = index * QUARTERS + row
            for chunk in range(8):
                from_row = row * 8 + chunk
                table[at : at + 1, chunk * 128 : (chunk + 1) * 128] = rider[
                    from_row : from_row + 1
                ]
        for row in range(QUARTERS):
            for chunk in range(3):
                from_row = 36 + row * 3 + chunk
                lifted_all[
                    index * QUARTERS + row : index * QUARTERS + row + 1,
                    chunk * 128 : (chunk + 1) * 128,
                ] = rider[from_row : from_row + 1]
        high, rest = rider[32:34], rider[34:36]
        both = high + rest
        mask_sum = mask_sum + jnp.concatenate([both[0:1], both[1:2]], axis=1)
    shift = (me * table_part) % 128
    field = pltpu.roll(table[...], (1024 - shift) % 1024, 1)[:, :table_part]
    lifted = lifted_all[...].astype(low)[:, :width_part]
    modulate_ref[...] = dot(lifted, field.astype(low), ((0,), (0,)))
    shift = (me * mask_part) % 128
    mask_sum = jnp.broadcast_to(mask_sum, (8, 256))
    mask_ref[...] = pltpu.roll(mask_sum, (256 - shift) % 256, 1)[0:1, :mask_part]


def out_kernel(
    lane_ref,
    part_0,
    part_1,
    part_2,
    middle_ref,
    chosen_ref,
    piece_0,
    piece_1,
    piece_2,
    piece_3,
    turned,
    riders,
):
    lane = lane_ref[0]
    block, width = middle_ref.shape
    group = block - SPARE
    width_part = width // QUARTERS
    feed = part_0[...].astype(full) + part_1[...].astype(full) + part_2[...].astype(full)
    out = middle_ref[...] + chosen_ref[0:1, 5 * width : 6 * width] * feed
    turned[...] = jnp.transpose(out[:group]).astype(low)
    riders[...] = jnp.zeros_like(riders)
    for chunk in range(width // 128):
        riders[chunk : chunk + 1, :] = out[group : group + 1, chunk * 128 : (chunk + 1) * 128]
    rider_rows = riders[...].astype(low)
    for index, piece in enumerate((piece_0, piece_1, piece_2, piece_3)):
        at = pl.multiple_of((lane ^ index) * width_part, 16)
        piece[:width_part, :] = turned[pl.ds(at, width_part), :]
        piece[width_part:, :] = rider_rows


def layer_kernel(
    lane_ref, rank_ref, piece_0, piece_1, piece_2, piece_3, out_ref, spare, turned
):
    lane = lane_ref[0]
    width_part, own_tokens = out_ref.shape
    group = piece_0.shape[1]
    quarter = own_tokens // QUARTERS
    pieces = (piece_0, piece_1, piece_2, piece_3)
    rows = jnp.concatenate([piece[:width_part, :] for piece in pieces], axis=1)
    row_id = lax.broadcasted_iota(jnp.int32, (group, own_tokens), 0)
    matrix = jnp.concatenate(
        [
            (row_id + (lane ^ index) * group == rank_ref[...]).astype(full).astype(low)
            for index in range(QUARTERS)
        ],
        axis=0,
    )
    spare[...] = jnp.zeros_like(spare)
    for index, piece in enumerate(pieces):
        rider = piece[width_part:, :].astype(full)
        for chunk in range(spare.shape[1] // 128):
            spare[index : index + 1, chunk * 128 : (chunk + 1) * 128] = rider[chunk : chunk + 1]
    turned[...] = jnp.transpose(spare[...])
    columns = turned[pl.ds(pl.multiple_of(lane * width_part, 16), width_part), :].astype(low)
    spare_id = lax.broadcasted_iota(jnp.int32, (8, own_tokens), 0)
    spot = lax.broadcasted_iota(jnp.int32, (8, own_tokens), 1) // quarter
    empty = rank_ref[...] < 0
    spots = jnp.where(((spare_id ^ lane) == spot) & (spare_id < QUARTERS) & empty, 1.0, 0.0)
    out_ref[...] = (dot(rows, matrix) + dot(columns, spots.astype(low))).astype(low)


def table_kernel(big_ref, lifted_ref, modulate_ref, table_ref, bias_ref, turned_ref, table):
    span = table_ref.shape[1]
    steps = table_ref.shape[0] // QUARTERS
    table[...] = jnp.zeros_like(table)
    table[:QUARTERS, : modulate_ref.shape[1]] = dot(lifted_ref[...], modulate_ref[...])
    table_ref[...] = jnp.concatenate(
        [
            table[row : row + 1, step * span : (step + 1) * span]
            for row in range(QUARTERS)
            for step in range(steps)
        ],
        axis=0,
    ).astype(low)
    rows = bias_ref.shape[0]
    block = rows // QUARTERS
    group = block - SPARE
    big = big_ref[0] == 1
    spare_small = jnp.log(jnp.full((1, 1), float(group), full))
    spare_big = jnp.log(jnp.full((1, 1), float(QUARTERS * group), full))

    def bias_of(query, key):
        query_block, key_block, key_inner = query // block, key // block, key % block
        small = jnp.where(key_inner < group, 0.0, jnp.where(key_inner == group, spare_small, -1e30))
        small = jnp.where(query_block == key_block, small, -1e30)
        large = jnp.where(key_inner < group, 0.0, jnp.where(key == group, spare_big, -1e30))
        return jnp.where(big, large, small)

    row_id = lax.broadcasted_iota(jnp.int32, (rows, rows), 0)
    column_id = lax.broadcasted_iota(jnp.int32, (rows, rows), 1)
    bias_ref[...] = bias_of(row_id, column_id)
    turned_ref[...] = bias_of(column_id, row_id)


def add_kernel(left_ref, right_ref, out_ref):
    out_ref[...] = (left_ref[...].astype(full) + right_ref[...].astype(full)).astype(low)


def copy_kernel(*refs):
    for index in range(len(refs) // 2):
        refs[len(refs) // 2 + index][...] = refs[index][...]


def upstream_kernel(
    lane_ref,
    rank_ref,
    chosen_ref,
    cotangent_ref,
    shrink_ref,
    grad_near,
    grad_far,
    upstream_ref,
    back_near,
    back_far,
):
    lane = lane_ref[0]
    block, width = upstream_ref.shape
    own_tokens = rank_ref.shape[1]
    group = block - SPARE
    rank = rank_ref[...]
    row_id = lax.broadcasted_iota(jnp.int32, (group, own_tokens), 0)
    spare_id = lax.broadcasted_iota(jnp.int32, (SPARE, own_tokens), 0)
    spot = lax.broadcasted_iota(jnp.int32, (SPARE, own_tokens), 1) // (own_tokens // QUARTERS)
    for chunk, back, grad_ref in ((0, back_near, grad_near), (1, back_far, grad_far)):
        matrix = []
        for index in (2 * chunk, 2 * chunk + 1):
            matrix.append(jnp.where(row_id + (lane ^ index) * group == rank, 1.0, 0.0))
            matrix.append(
                jnp.where((spare_id == 0) & (spot == (lane ^ index)) & (rank < 0), 1.0, 0.0)
            )
        upstream = dot(jnp.concatenate(matrix, axis=0).astype(low), cotangent_ref[...])
        if chunk == 0:
            upstream_ref[...] = upstream[:block]
        gates = [chosen_ref[index : index + 1, 5 * width :] for index in (2 * chunk, 2 * chunk + 1)]
        feed_grad = jnp.concatenate(
            [gates[0] * upstream[:block], gates[1] * upstream[block:]], axis=0
        ).astype(low)
        grad_ref[...] = feed_grad
        back[...] = dot(feed_grad, shrink_ref[...], ((1,), (1,)))


def feed_out_kernel(near_ref, far_ref, shrink_ref, part_0, part_1, part_2, part_3):
    block = part_0.shape[0]
    for activated, pair in ((far_ref, (part_2, part_3)), (near_ref, (part_0, part_1))):
        part = dot(activated[...], shrink_ref[...])
        pair[0][...] = part[:block].astype(low)
        pair[1][...] = part[block:].astype(low)


def partial_kernel(lhs_0, rhs_0, lhs_1, rhs_1, out_0, out_1):
    for lhs, rhs, out in ((lhs_0, rhs_0, out_0), (lhs_1, rhs_1, out_1)):
        chunk = lhs.shape[1] // 3
        for number in range(3):
            span = slice(number * chunk, (number + 1) * chunk)
            out[span, :] = dot(lhs[:, span], rhs[...], ((0,), (0,))).astype(low)


def weight_kernel(counts, bases, me_ref, *refs):
    given_0, given_1, kept_0, kept_1, product = refs[-5:]
    operands = list(refs[:-5])
    base_refs = [operands.pop() for _ in range(bases)][::-1]
    rows = given_0.shape[1] + given_1.shape[1]
    chunk = product.shape[0] // 3
    for group, pairs in enumerate(counts):
        products = []
        for lefts, rights in pairs:
            lhs = [operands.pop(0) for _ in range(lefts)]
            right = jnp.concatenate([operands.pop(0)[...] for _ in range(rights)], axis=0)
            products.append((lhs, right))
        for number in range(3):
            span = slice(number * chunk, (number + 1) * chunk)
            parts = [
                dot(jnp.concatenate([ref[:, span] for ref in lhs], axis=0), right, ((0,), (0,)))
                for lhs, right in products
            ]
            value = jnp.concatenate(parts, axis=1)
            if bases:
                value = value + base_refs[group][span, :].astype(full)
            product[span, :] = value
        for bit, start, given, kept in (
            (0, 0, given_0, kept_0),
            (1, given_0.shape[1], given_1, kept_1),
        ):
            mine = (me_ref[0] >> bit) & 1
            for index in range(4):
                for value, ref in ((1 - mine, given), (mine, kept)):
                    above = (index >> bit) << (bit + 1)
                    at = (above + (value << bit) + (index & bit)) * rows + start
                    at = pl.multiple_of(at, 8)
                    ref[4 * group + index] = product[pl.ds(at, ref.shape[1]), :].astype(low)


def halve_kernel(
    me_ref, held_0, held_1, got_0, got_1, given_0, given_1, kept_0, kept_1
):
    for bit, held, got, given, kept in (
        (1, held_0, got_0, given_0, kept_0),
        (0, held_1, got_1, given_1, kept_1),
    ):
        mine = (me_ref[0] >> bit) & 1
        for index in range(given.shape[0]):
            for value, ref in ((1 - mine, given), (mine, kept)):
                at = 2 * index + value
                ref[index] = (held[at].astype(full) + got[at].astype(full)).astype(low)


def join_kernel(me_ref, held_0, held_1, got_0, got_1, given, kept):
    mine = (me_ref[0] >> 2) & 1
    for index in range(given.shape[0]):
        for value, ref in ((1 - mine, given), (mine, kept)):
            at = 2 * index + value
            upper = held_0[at].astype(full) + got_0[at].astype(full)
            lower = held_1[at].astype(full) + got_1[at].astype(full)
            ref[index] = jnp.concatenate([upper, lower], axis=0).astype(low)


def total_kernel(held_ref, got_ref, *out_refs):
    if len(out_refs[0].shape) == 2:
        for index, out_ref in enumerate(out_refs):
            out_ref[...] = held_ref[index].astype(full) + got_ref[index].astype(full)
        return
    entry_ref, output_ref = out_refs
    total = held_ref[0].astype(full) + got_ref[0].astype(full)
    parts, _, columns = entry_ref.shape
    for index in range(parts):
        entry_ref[index] = total[:, index * columns : (index + 1) * columns]
    output_ref[...] = total[:, parts * columns :]


def call(
    kernel, outs, *operands, words=0, deps=(), time=1.0, scratch=(), token=False, loose=False
):
    count = len(operands)
    deps = tuple(deps)
    outs = tuple(outs)
    if token:
        outs += (((8, 128), full),)

    def run(*refs):
        outs_at = count + len(deps)
        rest = list(refs[outs_at:])
        if token:
            last = rest.pop(len(outs) - 1)
            last[...] = jnp.zeros_like(last)
        kernel(*refs[:count], *rest)

    return pl.pallas_call(
        run,
        out_shape=tuple(jax.ShapeDtypeStruct(shape, kind) for shape, kind in outs),
        in_specs=[SMALL] * words
        + [pl.BlockSpec() if loose else PLAIN] * (count - words)
        + [pl.BlockSpec(memory_space=pl.ANY)] * len(deps),
        scratch_shapes=list(scratch),
        compiler_params=pltpu.CompilerParams(vmem_limit_bytes=VMEM_ASK),
        cost_estimate=pl.CostEstimate(
            flops=int(time * 1.15e9), bytes_accessed=1024, transcendentals=0
        ),
    )(*operands, *deps)


def turn(token):
    return swap(token, "tensor", 1)


def body(
    kept_rows,
    owner_index,
    kept_position,
    resolution,
    mask_token,
    condition,
    modulate_weight,
    entry_weight,
    output_weight,
    expand_weight,
    shrink_weight,
    cotangent,
):
    owners = lax.axis_size("dp")
    me = lax.axis_index("dp")
    lane = lax.axis_index("tensor")
    kept_count, width_part = kept_rows.shape
    width = mask_token.shape[0]
    own_tokens = cotangent.shape[0]
    ff_part = expand_weight.shape[1]
    quarter = own_tokens // QUARTERS
    group = quarter // 2
    arrived_count = own_tokens // 2
    block = group + SPARE
    rows = QUARTERS * block
    capacity = 2 * kept_count // owners
    slots_all = owners * capacity
    direct = owners == SWAP_OWNERS
    lane_word = lane.reshape(1).astype(jnp.int32)
    me_word = me.reshape(1).astype(jnp.int32)
    big_word = resolution[:1]
    context_part = lax.dynamic_slice_in_dim(
        condition.astype(full), lane * width_part, width_part, 1
    )
    lifted = jax.nn.silu(context_part).astype(low)
    if direct:
        padded = -(-width_part // capacity) * capacity
        riders = jnp.pad(lifted, ((0, 0), (0, padded - width_part))).reshape(-1, capacity)
        extra = 16
    else:
        riders = lifted.reshape(-1, capacity)
        rider_count = riders.shape[0]
        extra = -(-(rider_count + 2) // 16) * 16
        riders = jnp.pad(riders, ((2, extra - 2 - rider_count), (0, 0)))
    slab_rows = width_part + extra
    slab_shape = (slab_rows, capacity)
    if not direct:
        slab_shape = (owners,) + slab_shape
    *slabs, slot_index = call(
        partial(
            pack_kernel,
            owners,
            FAR + NEAR if direct else range(owners),
            own_tokens.bit_length() - 1,
            extra,
            capacity,
        ),
        ((slab_shape, low),) * (owners if direct else 1) + (((1, kept_count), jnp.int32),),
        me_word,
        kept_rows.T,
        (owner_index * own_tokens + kept_position)[None, :],
        *([] if direct else [riders]),
        words=1,
        time=1.0,
        loose=direct,
    )

    steps = -(-6 * width // arrived_count)
    table, bias, bias_turned = call(
        table_kernel,
        (
            ((QUARTERS * steps, arrived_count), low),
            ((rows, rows), full),
            ((rows, rows), full),
        ),
        big_word,
        lifted,
        modulate_weight,
        words=1,
        deps=[slot_index],
        time=2.0,
        scratch=[pltpu.VMEM((8, steps * arrived_count), full)],
    )
    if direct:
        slabs = exchange_owners(dict(zip(FAR + NEAR, slabs)))
        slabs = list(slabs.values())
    else:
        slabs = exchange_owners(slabs)
    compact, slot_rank, event = call(
        partial(unpack_kernel, owners),
        (
            ((width_part + QUARTERS * steps, arrived_count), low),
            ((1, slots_all), jnp.int32),
        ),
        me_word,
        table,
        *slabs,
        words=1,
        time=1.2,
        token=True,
        scratch=[pltpu.VMEM((slab_rows, slots_all), low)],
    )
    (token_rank,) = call(
        partial(spots_kernel, owners),
        (((1, own_tokens), jnp.int32),),
        me_word,
        *slabs,
        words=1,
        deps=[event],
        time=1.2,
        scratch=[pltpu.VMEM((extra, slots_all), low)],
    )
    if not direct:
        owner_order = jnp.arange(owners, dtype=jnp.int32) ^ me
        lifted_all = slabs[0][:, width_part + 2 : width_part + 2 + rider_count]
        lifted_all = lifted_all.reshape(owners * QUARTERS, width_part)
    spatial_pieces = gather_blocks(compact)
    entry_flat = jnp.transpose(entry_weight, (1, 2, 0)).reshape(3 * width_part, width)
    token_shape = ((block, width), low)
    half = 2 * block
    chosen, spatial_own, normed_one, projected, attended_far, part_2, part_3 = call(
        entry_kernel,
        (
            ((QUARTERS, 6 * width), full),
            token_shape,
            ((rows, width), low),
            ((rows, 3 * width_part), low),
            ((half, width_part), low),
            token_shape,
            token_shape,
        ),
        lane_word,
        big_word,
        *spatial_pieces,
        mask_token[None, :],
        entry_flat,
        bias,
        output_weight,
        words=2,
        deps=[token_rank],
        time=5.0,
        scratch=[
            pltpu.VMEM((width, arrived_count), low),
            pltpu.VMEM((8, steps * arrived_count), full),
        ],
    )
    far, across, start = sum_far(part_2, part_3)
    attended_near, part_0, part_1 = call(
        attend_kernel,
        (((half, width_part), low), token_shape, token_shape),
        projected,
        bias,
        output_weight,
        deps=[start],
        time=3.0,
    )
    got = swap(part_1, "tensor", 1)
    feed_grad_near, feed_grad_far, upstream_own, back_near, back_far = call(
        upstream_kernel,
        (
            ((half, width), low),
            ((half, width), low),
            ((block, width), full),
            ((half, width), full),
            ((half, width), full),
        ),
        lane_word,
        token_rank,
        chosen,
        cotangent,
        shrink_weight,
        words=1,
        deps=[part_1],
        time=3.6,
    )
    branch, middle, normed_two_own = call(
        middle_kernel,
        (((block, width), full), ((block, width), full), token_shape),
        part_0,
        got,
        across,
        spatial_own,
        chosen,
        deps=[back_far],
        time=0.6,
    )

    def feed_call(piece_0, piece_1, back, *deps):
        return call(
            feed_kernel,
            (((half, width), low), ((half, width), low), ((half, width), low))
            + (token_shape, token_shape),
            piece_0,
            piece_1,
            back,
            expand_weight,
            deps=deps,
            time=2.4,
        )

    near_piece = swap(normed_two_own, "tensor", 1)
    across = swap(normed_two_own, "tensor", 2)
    normed_near, activated_near, hidden_near, part_0, part_1 = feed_call(
        normed_two_own, near_piece, back_near
    )
    *partials, event = call(
        partial_kernel,
        (((width, ff_part), low),) * 2,
        feed_grad_near,
        activated_near,
        normed_near,
        hidden_near,
        time=2.5,
        token=True,
    )
    (across,) = call(copy_kernel, (token_shape,), across, deps=[event], time=0.3)
    last_piece = swap(across, "tensor", 1)
    normed_far, activated_far, hidden_far, part_2, part_3 = feed_call(
        across, last_piece, back_far
    )
    feed_groups = [
        [([feed_grad_far], [activated_far])],
        [([normed_far], [hidden_far])],
    ]
    event = part_0
    if direct:
        feed_given, feed_kept, event = start_sums(feed_groups, FEED_SPLIT, (), 3.5, partials)
        feed_got = cross(feed_given, 1, 2)
    far, across, start = sum_far(part_2, part_3, [event])
    got = swap(part_1, "tensor", 1)
    middle_grad, branch_grad_own, sums, start = call(
        middle_back_kernel,
        (((block, width), full), token_shape, ((SPARE, width), full)),
        part_0,
        got,
        across,
        middle,
        branch,
        upstream_own,
        chosen,
        deps=[start],
        time=0.7,
        token=True,
    )
    branch_near = swap(branch_grad_own, "tensor", 1)
    branch_across = swap(branch_grad_own, "tensor", 2)
    feed_parts = call(
        feed_out_kernel,
        (token_shape,) * QUARTERS,
        activated_near,
        activated_far,
        shrink_weight,
        deps=[turn(start)],
        time=0.1,
    )
    feed_far = swap(feed_parts[3], "tensor", 1)
    feed_near = swap(feed_parts[1], "tensor", 1)
    probs, event = call(
        probs_kernel,
        (((width_part // HEAD, rows, rows), low),),
        projected,
        bias_turned,
        deps=[feed_parts[0]],
        time=0.1,
        token=True,
    )
    (branch_across,) = call(copy_kernel, (token_shape,), branch_across, deps=[event], time=0.1)
    branch_pieces = [
        branch_grad_own,
        branch_near,
        branch_across,
        swap(branch_across, "tensor", 1),
    ]
    feed_far, start = call(
        add_kernel,
        (token_shape,),
        feed_parts[2],
        feed_far,
        deps=[branch_pieces[2]],
        time=0.1,
        token=True,
    )
    branch_grad, projected_grad, event = call(
        attend_back_kernel,
        (((rows, width), low), ((rows, 3 * width_part), low)),
        projected,
        probs,
        output_weight,
        *branch_pieces,
        deps=[turn(start)],
        time=0.1,
        token=True,
    )
    feed_across = swap(feed_far, "tensor", 2)
    if direct:
        feed_given, feed_kept, event = halve_sums(feed_kept, feed_got, [event])
        feed_got = cross(feed_given, 2, 1)
    part_2, part_3 = call(
        partial(entry_back_kernel, 1),
        (token_shape, token_shape),
        projected_grad,
        entry_flat,
        deps=[feed_across, feed_near, event],
        time=0.1,
    )
    far, across, start = sum_far(part_2, part_3)
    part_0, part_1 = call(
        partial(entry_back_kernel, 0),
        (token_shape, token_shape),
        projected_grad,
        entry_flat,
        deps=[start],
        time=0.2,
    )
    got = swap(part_1, "tensor", 1)
    entry_groups = [
        [([normed_one], [projected_grad]), ([branch_grad], [attended_near, attended_far])]
    ]
    event = part_1
    if direct:
        entry_given, entry_kept, event = start_sums(entry_groups, ENTRY_SPLIT, [got], 0.2)
        entry_got = cross(entry_given, 1, 2)
    *back_pieces, back_token = call(
        back_kernel,
        (((width_part + 80, group), low),) * QUARTERS,
        lane_word,
        part_0,
        got,
        across,
        spatial_own,
        middle_grad,
        chosen,
        sums,
        feed_parts[0],
        feed_near,
        feed_across,
        upstream_own,
        words=1,
        deps=[event],
        time=BACK_TIME,
        token=True,
        scratch=[pltpu.VMEM((width, group), low), pltpu.VMEM((80, 128), full)],
    )
    if direct:
        feed_got, feed_kept, joined = join_sums(feed_kept, feed_got, [back_token])
    back_pieces = [
        back_pieces[0],
        swap(back_pieces[1], "tensor", 1),
        *swap_pair(back_pieces[2:]),
    ]
    chunks = 6 * width // 128
    logistic = jax.nn.sigmoid(context_part)
    logistic = logistic * (1.0 + context_part * (1.0 - logistic))
    if direct:
        entry_given, entry_kept, halved = halve_sums(entry_kept, entry_got, [back_token], HALVE_TIME)
        entry_got = cross(entry_given, 2, 1)
        shrink_grad, expand_grad, total_token = call(
            total_kernel,
            (((width // owners, ff_part), full),) * 2,
            feed_kept,
            feed_got,
            deps=[halved],
            time=TOTAL_TIME,
            token=True,
        )
        slabs, table_grad, event = call(
            partial(slots_kernel, owners),
            (
                ((owners, width_part + RIDERS, capacity), low),
                ((QUARTERS, chunks, 128), low),
            ),
            lane_word,
            me_word,
            big_word,
            slot_rank,
            riders,
            *back_pieces,
            words=3,
            time=0.1,
            token=True,
            scratch=[
                pltpu.VMEM((QUARTERS, chunks + 2, 128), full),
                pltpu.VMEM((16, 128), full),
            ],
        )
        (slabs,) = exchange_owners([slabs])
        table_grad = table_grad.reshape(QUARTERS, 6 * width)
        entry_got, entry_kept, event = join_sums(entry_kept, entry_got, [total_token])
        out_pieces = call(
            out_kernel,
            (((width_part + 16, group), low),) * QUARTERS,
            lane_word,
            feed_parts[0],
            feed_near,
            feed_across,
            middle,
            chosen,
            words=1,
            deps=[event],
            time=0.1,
            scratch=[pltpu.VMEM((width, group), low), pltpu.VMEM((16, 128), full)],
        )
        out_pieces = [
            out_pieces[0],
            swap(out_pieces[1], "tensor", 1),
            *swap_pair(out_pieces[2:]),
        ]
        layer_out, layer_token = call(
            layer_kernel,
            (((width_part, own_tokens), low),),
            lane_word,
            token_rank,
            *out_pieces,
            words=1,
            deps=[event],
            time=0.1,
            token=True,
            scratch=[pltpu.VMEM((8, width), full), pltpu.VMEM((width, 8), full)],
        )
        kept_grad, modulate_grad, mask_grad, kept_token = call(
            partial(kept_kernel, owners),
            (
                ((width_part, kept_count), low),
                ((width_part, 6 * width // owners), full),
                ((1, width // owners), full),
            ),
            me_word,
            slot_index,
            slabs,
            words=1,
            deps=[layer_token],
            time=KEPT_TIME,
            token=True,
            scratch=[
                pltpu.VMEM((owners * QUARTERS, 1024), full),
                pltpu.VMEM((owners * QUARTERS, padded), full),
            ],
        )
        mask_grad = mask_grad[0]
    else:
        event = back_pieces[1]
        rows_back = jnp.concatenate([piece[:width_part] for piece in back_pieces], axis=1)
        rank_ids = jnp.arange(arrived_count, dtype=jnp.int32)
        rank_ids = ((rank_ids // group) ^ lane) * group + rank_ids % group
        matrix = (rank_ids[:, None] == slot_rank).astype(low)
        slabs = dot(rows_back, matrix).astype(low).reshape(width_part, owners, capacity)
        slabs = jnp.take(jnp.transpose(slabs, (1, 0, 2)), owner_order, axis=0)
        slabs = jnp.take(exchange_owners([slabs])[0], owner_order, axis=0)
        slabs = jnp.transpose(slabs, (1, 0, 2)).reshape(width_part, slots_all)
        slot_ids = jnp.arange(slots_all, dtype=jnp.int32)[:, None]
        kept_grad = dot(slabs, (slot_ids == slot_index).astype(low)).astype(low)
        riders = jnp.stack(
            [piece[width_part : width_part + 8 * width // 128] for piece in back_pieces]
        )
        riders = riders.reshape(QUARTERS, 8, width).astype(full)
        mask_total = jnp.sum(riders[:, 6] + riders[:, 7], axis=0)
        table_local = riders[:, :6].reshape(QUARTERS, 6 * width)
        table_small = jnp.take(table_local, jnp.arange(QUARTERS, dtype=jnp.int32) ^ lane, axis=0)
        first = jnp.arange(QUARTERS, dtype=jnp.int32)[:, None] == 0
        table_big = jnp.where(first, jnp.sum(table_local, axis=0, keepdims=True), 0.0)
        table_grad = jnp.where(big_word[0] == 1, table_big, table_small).astype(low)
        sent = jnp.transpose(table_grad.reshape(QUARTERS, owners, -1), (1, 0, 2))
        table_all = exchange_owners([sent])[0].reshape(owners * QUARTERS, -1)
        modulate_grad = dot(lifted_all, table_all, ((0,), (0,)))
        mask_grad = lax.psum_scatter(mask_total, "dp", scatter_dimension=0, tiled=True)
    condition_grad = dot(table_grad, modulate_weight, ((1,), (1,))) * logistic
    if not direct:
        out_pieces = call(
            out_kernel,
            (((width_part + 16, group), low),) * QUARTERS,
            lane_word,
            feed_parts[0],
            feed_near,
            feed_across,
            middle,
            chosen,
            words=1,
            deps=[],
            time=0.1,
            scratch=[pltpu.VMEM((width, group), low), pltpu.VMEM((16, 128), full)],
        )
        out_pieces = [
            out_pieces[0],
            swap(out_pieces[1], "tensor", 1),
            *swap_pair(out_pieces[2:]),
        ]
        layer_out, layer_token = call(
            layer_kernel,
            (((width_part, own_tokens), low),),
            lane_word,
            token_rank,
            *out_pieces,
            words=1,
            deps=[],
            time=0.1,
            token=True,
            scratch=[pltpu.VMEM((8, width), full), pltpu.VMEM((width, 8), full)],
        )
    rows_part = width // owners
    if direct:
        entry_grad, output_grad = call(
            total_kernel,
            (((3, rows_part, width_part), full), ((rows_part, width_part), full)),
            entry_kept,
            entry_got,
            deps=[kept_token],
            time=0.8,
        )
    else:
        totals = []
        for number, pairs in enumerate(feed_groups + entry_groups):
            total = [
                dot(jnp.concatenate(lhs), jnp.concatenate(rhs), ((0,), (0,))) for lhs, rhs in pairs
            ]
            total = jnp.concatenate(total, axis=1)
            if number < len(partials):
                total = total + partials[number].astype(full)
            totals.append(sum_owners(total.astype(low).reshape(owners, rows_part, -1)))
        shrink_grad, expand_grad, entry_grad = totals
        output_grad = entry_grad[:, 3 * width_part :]
        entry_grad = entry_grad[:, : 3 * width_part].reshape(rows_part, 3, width_part)
        entry_grad = jnp.transpose(entry_grad, (1, 0, 2))

    return (
        layer_out.T,
        kept_grad.T,
        mask_grad,
        condition_grad,
        modulate_grad,
        jnp.transpose(entry_grad, (1, 0, 2)),
        output_grad.T,
        expand_grad,
        shrink_grad.T,
    )


def solution(mesh):
    return jax.shard_map(
        body,
        mesh=mesh,
        in_specs=(
            P("dp", "tensor"),
            P("dp"),
            P("dp"),
            P("dp"),
            P(),
            P("dp", None),
            P("tensor", None),
            P(None, None, "tensor"),
            P("tensor", None),
            P(None, "tensor"),
            P("tensor", None),
            P("dp", None),
        ),
        out_specs=(
            P("dp", "tensor"),
            P("dp", "tensor"),
            P("dp"),
            P("dp", "tensor"),
            P("tensor", "dp"),
            P("dp", None, "tensor"),
            P("tensor", "dp"),
            P("dp", "tensor"),
            P("tensor", "dp"),
        ),
        check_vma=False,
    )
```

```python
from functools import partial

import jax
import jax.numpy as jnp
from jax import lax
from jax.experimental import pallas as pl
from jax.experimental.pallas import tpu as pltpu
from jax.sharding import PartitionSpec as P

HEAD = 72
QUARTERS = 4
SPARE = 8
scale = HEAD ** (-0.5)
epsilon = 1e-06
gelu_coeff = 0.7978845608028654
low = jnp.bfloat16
full = jnp.float32
VMEM_ASK = 12 * 1024 * 1024
RIDERS = 48
SWAP_OWNERS = 8
FEED_SPLIT = 72
ENTRY_SPLIT = 72
FAR = (6, 7, 4, 5)
NEAR = (2, 3, 1, 0)
JOIN_TIME = 0.1
KEPT_TIME = 0.1
TOTAL_TIME = 14.0
HALVE_TIME = 0.35
BACK_TIME = 0.1
SINGLE_TIME = 1.0
SMALL = pl.BlockSpec(memory_space=pltpu.SMEM)
PLAIN = pl.BlockSpec(memory_space=pltpu.VMEM)


def dot(a, b, dims=((1,), (0,))):
    return lax.dot_general(a, b, (dims, ((), ())), preferred_element_type=full)


def normalize(rows):
    centered = rows - jnp.mean(rows, axis=-1, keepdims=True)
    inverse = lax.rsqrt(jnp.mean(centered * centered, axis=-1, keepdims=True) + epsilon)
    return (centered * inverse, inverse)


def normalize_back(unit, inverse, grad):
    return inverse * (
        grad
        - jnp.mean(grad, axis=-1, keepdims=True)
        - unit * jnp.mean(grad * unit, axis=-1, keepdims=True)
    )


def gelu_both(value):
    square = value * value
    inner = value * (gelu_coeff + 0.044715 * gelu_coeff * square)
    half = 0.5 + 0.5 * jnp.tanh(inner)
    activated = value * half
    outer = 2.0 * gelu_coeff + 6.0 * 0.044715 * gelu_coeff * square
    return (activated, half + activated * (1.0 - half) * outer)


def swap(value, axis, bit):
    size = lax.axis_size(axis)
    return lax.ppermute(value, axis, [(index, index ^ bit) for index in range(size)])


def swap_pair(pieces):
    came = swap(jnp.stack(pieces), "tensor", 2)
    return came[0], swap(came[1], "tensor", 1)


def gather_blocks(own):
    near = swap(own, "tensor", 1)
    across = swap(own, "tensor", 2)
    return [own, near, across, swap(across, "tensor", 1)]


def sum_far(part_2, part_3, deps=()):
    got = swap(part_3, "tensor", 1)
    far, token = call(
        add_kernel, ((part_2.shape, low),), part_2, got, deps=deps, time=0.1, token=True
    )
    return far, swap(far, "tensor", 2), turn(token)


def sum_owners(total):
    owners, rows, columns = total.shape
    me = lax.axis_index("dp")
    step = 1
    while step < owners:
        pairs = total.reshape(-1, 2, rows, columns)
        mine = (me // step) % 2
        given = lax.dynamic_index_in_dim(pairs, 1 - mine, 1, keepdims=False)
        kept = lax.dynamic_index_in_dim(pairs, mine, 1, keepdims=False)
        total = kept.astype(full) + swap(given, "dp", step).astype(full)
        step *= 2
        total = total if step == owners else total.astype(low)
    return total[0]


def part_shapes(count, upper, lower, columns):
    return [((count, upper, columns), low), ((count, lower, columns), low)]


def start_sums(groups, split, deps=(), time=3.0, bases=()):
    width = groups[0][0][0][0].shape[1]
    columns = sum(rhs[0].shape[1] for _, rhs in groups[0])
    rows = width // 8
    shapes = part_shapes(4 * len(groups), split, rows - split, columns)
    counts = [[(len(lhs), len(rhs)) for lhs, rhs in pairs] for pairs in groups]
    given_0, given_1, kept_0, kept_1, token = call(
        partial(weight_kernel, counts, len(bases)),
        shapes + shapes,
        lax.axis_index("dp").reshape(1).astype(jnp.int32),
        *[value for pairs in groups for lhs, rhs in pairs for value in (*lhs, *rhs)],
        *bases,
        words=1,
        deps=deps,
        time=time,
        scratch=[pltpu.VMEM((width, columns), full)],
        token=True,
    )
    return (given_0, given_1), (kept_0, kept_1), token


def cross(given, first, second):
    return swap(given[0], "dp", first), swap(given[1], "dp", second)


def halve_sums(kept, got, deps=(), time=0.1):
    count, _, columns = kept[0].shape
    shapes = part_shapes(count // 2, kept[0].shape[1], kept[1].shape[1], columns)
    given_0, given_1, kept_0, kept_1, token = call(
        halve_kernel,
        shapes + shapes,
        lax.axis_index("dp").reshape(1).astype(jnp.int32),
        *kept,
        *got,
        words=1,
        deps=deps,
        time=time,
        token=True,
    )
    return (given_0, given_1), (kept_0, kept_1), token


def join_sums(kept, got, deps=()):
    count, _, columns = kept[0].shape
    shape = ((count // 2, kept[0].shape[1] + kept[1].shape[1], columns), low)
    given, kept, token = call(
        join_kernel,
        (shape, shape),
        lax.axis_index("dp").reshape(1).astype(jnp.int32),
        *kept,
        *got,
        words=1,
        deps=deps,
        time=JOIN_TIME,
        token=True,
    )
    return swap(given, "dp", 4), kept, token


def exchange_owners(slabs):
    if isinstance(slabs, dict):
        return {index: swap(slab, "dp", index) if index else slab for index, slab in slabs.items()}
    return [lax.all_to_all(slabs[0], "dp", split_axis=0, concat_axis=0, tiled=True)]


def attend(projected_ref, bias_ref, output_ref, attended_ref, chunk, half, width_part):
    span = slice(chunk * half, (chunk + 1) * half)
    pieces = []
    for head in range(width_part // HEAD):
        at = head * HEAD
        queries = projected_ref[span, at : at + HEAD]
        keys = projected_ref[:, width_part + at : width_part + at + HEAD]
        values = projected_ref[:, 2 * width_part + at : 2 * width_part + at + HEAD]
        scores = dot(queries, keys, ((1,), (1,))) * scale + bias_ref[span, :]
        spread = jnp.exp(scores - jnp.max(scores, axis=1, keepdims=True))
        probs = spread * (1.0 / jnp.sum(spread, axis=1, keepdims=True))
        pieces.append(dot(probs.astype(low), values))
    attended = jnp.concatenate(pieces, axis=1).astype(low)
    attended_ref[...] = attended
    return dot(attended, output_ref[...])


def entry_kernel(
    lane_ref,
    big_ref,
    piece_0,
    piece_1,
    piece_2,
    piece_3,
    mask_ref,
    entry_ref,
    bias_ref,
    output_ref,
    chosen_ref,
    spatial_ref,
    normed_ref,
    projected_ref,
    attended_ref,
    part_0,
    part_1,
    gathered,
    table,
):
    lane = lane_ref[0]
    block, width = spatial_ref.shape
    width_part = width // QUARTERS
    group = block - SPARE
    half = 2 * block
    pieces = (piece_0, piece_1, piece_2, piece_3)
    for index, piece in enumerate(pieces):
        at = pl.multiple_of((lane ^ index) * width_part, 16)
        gathered[pl.ds(at, width_part), :] = piece[:width_part, :]
    summed = pieces[0][width_part:, :].astype(full)
    for piece in pieces[1:]:
        summed = summed + piece[width_part:, :].astype(full)
    span = summed.shape[1]
    steps = summed.shape[0] // QUARTERS
    for row in range(QUARTERS):
        for step in range(steps):
            from_row = row * steps + step
            table[row : row + 1, step * span : (step + 1) * span] = summed[from_row : from_row + 1]
    for index in range(QUARTERS):
        row = jnp.where(big_ref[0] == 1, 0, lane ^ index)
        chosen_ref[index : index + 1, :] = table[pl.ds(row, 1), : 6 * width]
    spare_id = lax.broadcasted_iota(jnp.int32, (SPARE, width), 0)
    spare = jnp.where(spare_id == 0, mask_ref[...].astype(full), 0.0)
    for chunk in (1, 0):
        span = slice(chunk * half, (chunk + 1) * half)
        normed = []
        for index in (2 * chunk, 2 * chunk + 1):
            at = pl.multiple_of((lane ^ index) * group, 128)
            kept = jnp.transpose(gathered[:, pl.ds(at, group)].astype(full))
            rows = jnp.concatenate([kept, spare], axis=0)
            if index == 0:
                spatial_ref[...] = rows.astype(low)
            unit, inverse = normalize(rows)
            shift = chosen_ref[index : index + 1, :width]
            gain = chosen_ref[index : index + 1, width : 2 * width]
            normed.append(unit * (1.0 + gain) + shift)
        normed = jnp.concatenate(normed, axis=0).astype(low)
        normed_ref[span, :] = normed
        projected_ref[span, :] = dot(normed, entry_ref[...], ((1,), (1,))).astype(low)
    part = attend(projected_ref, bias_ref, output_ref, attended_ref, 1, half, width_part)
    part_0[...] = part[:block].astype(low)
    part_1[...] = part[block:].astype(low)


def attend_kernel(projected_ref, bias_ref, output_ref, attended_ref, part_0, part_1):
    block = part_0.shape[0]
    part = attend(
        projected_ref, bias_ref, output_ref, attended_ref, 0, 2 * block, output_ref.shape[0]
    )
    part_0[...] = part[:block].astype(low)
    part_1[...] = part[block:].astype(low)


def middle_kernel(
    part_0, part_1, part_2, spatial_ref, chosen_ref, branch_ref, middle_ref, normed_ref
):
    width = spatial_ref.shape[1]
    branch = part_0[...].astype(full) + part_1[...].astype(full) + part_2[...].astype(full)
    branch_ref[...] = branch
    middle = spatial_ref[...].astype(full) + chosen_ref[0:1, 2 * width : 3 * width] * branch
    middle_ref[...] = middle
    unit, inverse = normalize(middle)
    shift = chosen_ref[0:1, 3 * width : 4 * width]
    gain = chosen_ref[0:1, 4 * width : 5 * width]
    normed_ref[...] = (unit * (1.0 + gain) + shift).astype(low)


def feed_kernel(
    piece_0,
    piece_1,
    back_ref,
    expand_ref,
    normed_ref,
    activated_ref,
    hidden_grad_ref,
    part_0,
    part_1,
):
    block = piece_0.shape[0]
    normed = jnp.concatenate([piece_0[...].astype(full), piece_1[...].astype(full)], axis=0)
    normed = normed.astype(low)
    normed_ref[...] = normed
    hidden = dot(normed, expand_ref[...])
    activated, slope = gelu_both(hidden)
    activated_ref[...] = activated.astype(low)
    hidden_grad = (back_ref[...] * slope).astype(low)
    hidden_grad_ref[...] = hidden_grad
    part = dot(hidden_grad, expand_ref[...], ((1,), (1,)))
    part_0[...] = part[:block].astype(low)
    part_1[...] = part[block:].astype(low)


def middle_back_kernel(
    part_0,
    part_1,
    part_2,
    middle_ref,
    branch_ref,
    upstream_ref,
    chosen_ref,
    middle_grad_ref,
    branch_grad_ref,
    sums_ref,
):
    width = middle_ref.shape[1]
    normed_grad = part_0[...].astype(full) + part_1[...].astype(full) + part_2[...].astype(full)
    unit, inverse = normalize(middle_ref[...])
    gain = chosen_ref[0:1, 4 * width : 5 * width]
    middle_grad = upstream_ref[...] + normalize_back(unit, inverse, normed_grad * (1.0 + gain))
    middle_grad_ref[...] = middle_grad
    branch_grad_ref[...] = (chosen_ref[0:1, 2 * width : 3 * width] * middle_grad).astype(low)
    sums_ref[0:1, :] = jnp.sum(middle_grad * branch_ref[...], axis=0, keepdims=True)
    sums_ref[1:2, :] = jnp.sum(normed_grad, axis=0, keepdims=True)
    sums_ref[2:3, :] = jnp.sum(normed_grad * unit, axis=0, keepdims=True)


def probs_kernel(projected_ref, bias_ref, probs_ref):
    width_part = projected_ref.shape[1] // 3
    for head in range(width_part // HEAD):
        at = head * HEAD
        queries = projected_ref[:, at : at + HEAD]
        keys = projected_ref[:, width_part + at : width_part + at + HEAD]
        scores = dot(keys, queries, ((1,), (1,))) * scale + bias_ref[...]
        spread = jnp.exp(scores - jnp.max(scores, axis=0, keepdims=True))
        probs = spread * (1.0 / jnp.sum(spread, axis=0, keepdims=True))
        probs_ref[head] = probs.astype(low)


def attend_back_kernel(
    projected_ref,
    probs_ref,
    output_ref,
    piece_0,
    piece_1,
    piece_2,
    piece_3,
    branch_grad_ref,
    grad_ref,
):
    rows, width_all = projected_ref.shape
    width_part = width_all // 3
    block = piece_0.shape[0]
    half = 2 * block
    for chunk, pair in enumerate(((piece_0, piece_1), (piece_2, piece_3))):
        branch_grad_ref[chunk * half : (chunk + 1) * half, :] = jnp.concatenate(
            [piece[...].astype(full) for piece in pair], axis=0
        ).astype(low)
    attended_grad = dot(branch_grad_ref[...], output_ref[...], ((1,), (1,))).astype(low)
    pieces = [[], [], []]
    for head in range(width_part // HEAD):
        at = head * HEAD
        queries = projected_ref[:, at : at + HEAD]
        keys = projected_ref[:, width_part + at : width_part + at + HEAD]
        values = projected_ref[:, 2 * width_part + at : 2 * width_part + at + HEAD]
        grad = attended_grad[:, at : at + HEAD]
        probs = probs_ref[head]
        pieces[2].append(dot(probs, grad))
        probs = probs.astype(full)
        prob_grad = dot(values, grad, ((1,), (1,)))
        delta = jnp.sum(probs * prob_grad, axis=0, keepdims=True)
        score_grad = (probs * (prob_grad - delta)).astype(low)
        pieces[1].append(dot(score_grad, queries) * scale)
        pieces[0].append(dot(score_grad, keys, ((0,), (0,))) * scale)
    grad_ref[...] = jnp.concatenate(pieces[0] + pieces[1] + pieces[2], axis=1).astype(low)


def entry_back_kernel(chunk, grad_ref, entry_ref, part_0, part_1):
    block = part_0.shape[0]
    part = dot(grad_ref[2 * chunk * block : 2 * (chunk + 1) * block, :], entry_ref[...])
    part_0[...] = part[:block].astype(low)
    part_1[...] = part[block:].astype(low)


def pack_kernel(owners, chosen, shift, extra, capacity, me_ref, kept_ref, spot_ref, *refs):
    direct = len(refs) == owners + 1
    out_refs = refs if direct else refs[1:]
    slot_ref = out_refs[-1]
    kept_count = kept_ref.shape[1]
    owner_local = (spot_ref[...] >> shift) ^ me_ref[0]
    owner_id = lax.broadcasted_iota(jnp.int32, (owners, kept_count), 0)
    hot = (owner_id == owner_local).astype(full)
    row_id = lax.broadcasted_iota(jnp.int32, (kept_count, kept_count), 0)
    column_id = lax.broadcasted_iota(jnp.int32, (kept_count, kept_count), 1)
    before = dot(hot.astype(low), (row_id < column_id).astype(full).astype(low))
    rank = jnp.sum(hot * before, axis=0, keepdims=True).astype(jnp.int32)
    slot = owner_local * capacity + rank
    slot_ref[...] = slot
    coded = (spot_ref[...] & ((1 << shift) - 1)) + 1
    tag_id = lax.broadcasted_iota(jnp.int32, (extra, kept_count), 0)
    tags = jnp.where(tag_id == 0, coded >> 5, jnp.where(tag_id == 1, coded & 31, 0))
    rows = jnp.concatenate([kept_ref[...], tags.astype(full).astype(low)], axis=0)
    slot_id = lax.broadcasted_iota(jnp.int32, (capacity, kept_count), 0)
    for number, index in enumerate(chosen):
        matrix = (slot_id + index * capacity == slot).astype(full).astype(low)
        slab = dot(rows, matrix, ((1,), (1,)))
        split = kept_ref.shape[0]
        if not direct:
            lower = slab[split:] + refs[0][...].astype(full)
            slab = jnp.concatenate([slab[:split], lower], axis=0)
            out_refs[0][me_ref[0] ^ index] = slab.astype(low)
        else:
            out_refs[number][...] = slab.astype(low)


def places(owners, me_ref, slab_refs, arrived, width_part):
    slots_all = arrived.shape[1]
    capacity = slots_all // owners
    for index in range(owners):
        if len(slab_refs) == 1:
            slab = slab_refs[0][me_ref[0] ^ index]
        else:
            slab = slab_refs[(FAR + NEAR).index(index)][...]
        rows = arrived.shape[0]
        arrived[:, index * capacity : (index + 1) * capacity] = slab[slab.shape[0] - rows :]
    tags = arrived[width_part : width_part + 16, :].astype(full)
    place = tags[0:1] * 32.0 + tags[1:2] - 1.0
    turned = jnp.transpose(jnp.broadcast_to(place, (8, slots_all)))[:, 0:1]
    return place, jnp.where(turned < 0.0, 1e9, turned)


def unpack_kernel(owners, me_ref, table_ref, *refs):
    slab_refs, (compact_ref, slot_rank_ref, arrived) = refs[:-3], refs[-3:]
    arrived_count = compact_ref.shape[1]
    width_part = compact_ref.shape[0] - table_ref.shape[0]
    place, turned = places(owners, me_ref, slab_refs, arrived, width_part)
    slot_rank = jnp.sum(jnp.where(turned < place, 1.0, 0.0), axis=0, keepdims=True)
    slot_rank = jnp.where(place < 0.0, -1.0, slot_rank).astype(jnp.int32)
    slot_rank_ref[...] = slot_rank
    rank_id = lax.broadcasted_iota(jnp.int32, (arrived_count, arrived.shape[1]), 0)
    matrix = (rank_id == slot_rank).astype(full).astype(low)
    compact_ref[:width_part, :] = dot(arrived[:width_part, :], matrix, ((1,), (1,))).astype(low)
    compact_ref[width_part:, :] = table_ref[...]


def spots_kernel(owners, me_ref, *refs):
    slab_refs, (token_rank_ref, arrived) = refs[:-2], refs[-2:]
    own_tokens = token_rank_ref.shape[1]
    _, turned = places(owners, me_ref, slab_refs, arrived, 0)
    spot = lax.broadcasted_iota(jnp.int32, (1, own_tokens), 1).astype(full)
    token_rank = jnp.sum(jnp.where(turned < spot, 1.0, 0.0), axis=0, keepdims=True)
    filled = jnp.sum(jnp.where(turned == spot, 1.0, 0.0), axis=0, keepdims=True)
    token_rank_ref[...] = jnp.where(filled > 0.0, token_rank, -1.0).astype(jnp.int32)


def back_kernel(
    lane_ref,
    part_0,
    part_1,
    part_2,
    spatial_ref,
    middle_grad_ref,
    chosen_ref,
    sums_ref,
    feed_0,
    feed_1,
    feed_2,
    upstream_ref,
    piece_0,
    piece_1,
    piece_2,
    piece_3,
    turned,
    riders,
):
    lane = lane_ref[0]
    block, width = spatial_ref.shape
    group = block - SPARE
    width_part = width // QUARTERS
    normed_grad = part_0[...].astype(full) + part_1[...].astype(full) + part_2[...].astype(full)
    unit, inverse = normalize(spatial_ref[...].astype(full))
    gain = chosen_ref[0:1, width : 2 * width]
    grad = middle_grad_ref[...] + normalize_back(unit, inverse, normed_grad * (1.0 + gain))
    turned[...] = jnp.transpose(grad[:group]).astype(low)
    feed = feed_0[...].astype(full) + feed_1[...].astype(full) + feed_2[...].astype(full)
    mask_sum = grad[group : group + 1]
    mask_high = mask_sum.astype(low).astype(full)
    fields = [
        jnp.sum(normed_grad, axis=0, keepdims=True),
        jnp.sum(normed_grad * unit, axis=0, keepdims=True),
        sums_ref[0:1, :],
        sums_ref[1:2, :],
        sums_ref[2:3, :],
        jnp.sum(feed * upstream_ref[...], axis=0, keepdims=True),
        mask_high,
        mask_sum - mask_high,
    ]
    chunks = width // 128
    riders[...] = jnp.zeros_like(riders)
    for number, field in enumerate(fields):
        for chunk in range(chunks):
            at = number * chunks + chunk
            riders[at : at + 1, :] = field[:, chunk * 128 : (chunk + 1) * 128]
    rider_rows = riders[...].astype(low)
    for index, piece in enumerate((piece_0, piece_1, piece_2, piece_3)):
        at = pl.multiple_of((lane ^ index) * width_part, 16)
        piece[:width_part, :] = turned[pl.ds(at, width_part), :]
        piece[width_part:, :] = rider_rows


def slots_kernel(
    owners,
    lane_ref,
    me_ref,
    big_ref,
    rank_ref,
    lifted_ref,
    piece_0,
    piece_1,
    piece_2,
    piece_3,
    slabs_ref,
    table_ref,
    table,
    mask_total,
):
    lane = lane_ref[0]
    me = me_ref[0]
    group = piece_0.shape[1]
    slots_all = rank_ref.shape[1]
    capacity = slots_all // owners
    chunks = table_ref.shape[1]
    width_part = slabs_ref.shape[1] - RIDERS
    pieces = [piece_0, piece_1, piece_2, piece_3]
    rows = jnp.concatenate([piece[:width_part, :] for piece in pieces], axis=1)
    row_id = lax.broadcasted_iota(jnp.int32, (group, slots_all), 0)
    matrix = jnp.concatenate(
        [
            (row_id + (lane ^ index) * group == rank_ref[...]).astype(full).astype(low)
            for index in range(QUARTERS)
        ],
        axis=0,
    )
    slots = dot(rows, matrix)
    table[...] = jnp.zeros_like(table)
    summed = jnp.zeros((chunks, 128), full)
    mask_sum = jnp.zeros((16, 128), full)
    mask_rows = chunks // 6
    for index, piece in enumerate(pieces):
        field = piece[width_part : width_part + chunks, :].astype(full)
        summed = summed + field
        rest = piece[width_part + chunks - chunks % 16 :, :].astype(full)
        table[lane ^ index, :chunks, :] = field
        at = chunks % 16
        mask_sum = mask_sum + jnp.concatenate(
            [
                rest[at : at + mask_rows] + rest[at + mask_rows : at + 2 * mask_rows],
                jnp.zeros((16 - mask_rows, 128), full),
            ],
            axis=0,
        )
    mask_total[...] = mask_sum

    @pl.when(big_ref[0] == 1)
    def _():
        table[...] = jnp.zeros_like(table)
        table[0, :chunks, :] = summed

    table_ref[...] = table[:, :chunks, :].astype(low)
    for index in range(owners):
        owner = me ^ index
        start = (owner * chunks) // owners
        fields = [table[row, pl.ds(start, 8), :] for row in range(QUARTERS)]
        mask_start = (owner * mask_rows) // owners
        mask_part = mask_total[pl.ds(mask_start, 2), :]
        mask_high = mask_part.astype(low).astype(full)
        fields += [mask_high, mask_part - mask_high, lifted_ref[...].astype(full)]
        slab = jnp.concatenate([slots[:, index * capacity : (index + 1) * capacity]] + fields, axis=0)
        slabs_ref[owner] = slab.astype(low)


def kept_kernel(
    owners, me_ref, slot_ref, slabs_ref, kept_ref, modulate_ref, mask_ref, table, lifted_all
):
    width_part, kept_count = kept_ref.shape
    capacity = slabs_ref.shape[2]
    table_part = modulate_ref.shape[1]
    mask_part = mask_ref.shape[1]
    me = me_ref[0]
    slabs = [slabs_ref[me ^ index] for index in range(owners)]
    rows = jnp.concatenate([slab[:width_part] for slab in slabs], axis=1)
    slot_id = lax.broadcasted_iota(jnp.int32, (owners * capacity, kept_count), 0)
    matrix = (slot_id == slot_ref[...]).astype(full).astype(low)
    kept_ref[...] = dot(rows, matrix).astype(low)
    mask_sum = jnp.zeros((1, 256), full)
    for index, slab in enumerate(slabs):
        rider = slab[width_part:].astype(full)
        for row in range(QUARTERS):
            at = index * QUARTERS + row
            for chunk in range(8):
                from_row = row * 8 + chunk
                table[at : at + 1, chunk * 128 : (chunk + 1) * 128] = rider[
                    from_row : from_row + 1
                ]
        for row in range(QUARTERS):
            for chunk in range(3):
                from_row = 36 + row * 3 + chunk
                lifted_all[
                    index * QUARTERS + row : index * QUARTERS + row + 1,
                    chunk * 128 : (chunk + 1) * 128,
                ] = rider[from_row : from_row + 1]
        high, rest = rider[32:34], rider[34:36]
        both = high + rest
        mask_sum = mask_sum + jnp.concatenate([both[0:1], both[1:2]], axis=1)
    shift = (me * table_part) % 128
    field = pltpu.roll(table[...], (1024 - shift) % 1024, 1)[:, :table_part]
    lifted = lifted_all[...].astype(low)[:, :width_part]
    modulate_ref[...] = dot(lifted, field.astype(low), ((0,), (0,)))
    shift = (me * mask_part) % 128
    mask_sum = jnp.broadcast_to(mask_sum, (8, 256))
    mask_ref[...] = pltpu.roll(mask_sum, (256 - shift) % 256, 1)[0:1, :mask_part]


def out_kernel(
    lane_ref,
    part_0,
    part_1,
    part_2,
    middle_ref,
    chosen_ref,
    piece_0,
    piece_1,
    piece_2,
    piece_3,
    turned,
    riders,
):
    lane = lane_ref[0]
    block, width = middle_ref.shape
    group = block - SPARE
    width_part = width // QUARTERS
    feed = part_0[...].astype(full) + part_1[...].astype(full) + part_2[...].astype(full)
    out = middle_ref[...] + chosen_ref[0:1, 5 * width : 6 * width] * feed
    turned[...] = jnp.transpose(out[:group]).astype(low)
    riders[...] = jnp.zeros_like(riders)
    for chunk in range(width // 128):
        riders[chunk : chunk + 1, :] = out[group : group + 1, chunk * 128 : (chunk + 1) * 128]
    rider_rows = riders[...].astype(low)
    for index, piece in enumerate((piece_0, piece_1, piece_2, piece_3)):
        at = pl.multiple_of((lane ^ index) * width_part, 16)
        piece[:width_part, :] = turned[pl.ds(at, width_part), :]
        piece[width_part:, :] = rider_rows


def layer_kernel(
    lane_ref, rank_ref, piece_0, piece_1, piece_2, piece_3, out_ref, spare, turned
):
    lane = lane_ref[0]
    width_part, own_tokens = out_ref.shape
    group = piece_0.shape[1]
    quarter = own_tokens // QUARTERS
    pieces = (piece_0, piece_1, piece_2, piece_3)
    rows = jnp.concatenate([piece[:width_part, :] for piece in pieces], axis=1)
    row_id = lax.broadcasted_iota(jnp.int32, (group, own_tokens), 0)
    matrix = jnp.concatenate(
        [
            (row_id + (lane ^ index) * group == rank_ref[...]).astype(full).astype(low)
            for index in range(QUARTERS)
        ],
        axis=0,
    )
    spare[...] = jnp.zeros_like(spare)
    for index, piece in enumerate(pieces):
        rider = piece[width_part:, :].astype(full)
        for chunk in range(spare.shape[1] // 128):
            spare[index : index + 1, chunk * 128 : (chunk + 1) * 128] = rider[chunk : chunk + 1]
    turned[...] = jnp.transpose(spare[...])
    columns = turned[pl.ds(pl.multiple_of(lane * width_part, 16), width_part), :].astype(low)
    spare_id = lax.broadcasted_iota(jnp.int32, (8, own_tokens), 0)
    spot = lax.broadcasted_iota(jnp.int32, (8, own_tokens), 1) // quarter
    empty = rank_ref[...] < 0
    spots = jnp.where(((spare_id ^ lane) == spot) & (spare_id < QUARTERS) & empty, 1.0, 0.0)
    out_ref[...] = (dot(rows, matrix) + dot(columns, spots.astype(low))).astype(low)


def table_kernel(big_ref, lifted_ref, modulate_ref, table_ref, bias_ref, turned_ref, table):
    span = table_ref.shape[1]
    steps = table_ref.shape[0] // QUARTERS
    table[...] = jnp.zeros_like(table)
    table[:QUARTERS, : modulate_ref.shape[1]] = dot(lifted_ref[...], modulate_ref[...])
    table_ref[...] = jnp.concatenate(
        [
            table[row : row + 1, step * span : (step + 1) * span]
            for row in range(QUARTERS)
            for step in range(steps)
        ],
        axis=0,
    ).astype(low)
    rows = bias_ref.shape[0]
    block = rows // QUARTERS
    group = block - SPARE
    big = big_ref[0] == 1
    spare_small = jnp.log(jnp.full((1, 1), float(group), full))
    spare_big = jnp.log(jnp.full((1, 1), float(QUARTERS * group), full))

    def bias_of(query, key):
        query_block, key_block, key_inner = query // block, key // block, key % block
        small = jnp.where(key_inner < group, 0.0, jnp.where(key_inner == group, spare_small, -1e30))
        small = jnp.where(query_block == key_block, small, -1e30)
        large = jnp.where(key_inner < group, 0.0, jnp.where(key == group, spare_big, -1e30))
        return jnp.where(big, large, small)

    row_id = lax.broadcasted_iota(jnp.int32, (rows, rows), 0)
    column_id = lax.broadcasted_iota(jnp.int32, (rows, rows), 1)
    bias_ref[...] = bias_of(row_id, column_id)
    turned_ref[...] = bias_of(column_id, row_id)


def add_kernel(left_ref, right_ref, out_ref):
    out_ref[...] = (left_ref[...].astype(full) + right_ref[...].astype(full)).astype(low)


def copy_kernel(*refs):
    for index in range(len(refs) // 2):
        refs[len(refs) // 2 + index][...] = refs[index][...]


def upstream_kernel(
    lane_ref,
    rank_ref,
    chosen_ref,
    cotangent_ref,
    shrink_ref,
    grad_near,
    grad_far,
    upstream_ref,
    back_near,
    back_far,
):
    lane = lane_ref[0]
    block, width = upstream_ref.shape
    own_tokens = rank_ref.shape[1]
    group = block - SPARE
    rank = rank_ref[...]
    row_id = lax.broadcasted_iota(jnp.int32, (group, own_tokens), 0)
    spare_id = lax.broadcasted_iota(jnp.int32, (SPARE, own_tokens), 0)
    spot = lax.broadcasted_iota(jnp.int32, (SPARE, own_tokens), 1) // (own_tokens // QUARTERS)
    for chunk, back, grad_ref in ((0, back_near, grad_near), (1, back_far, grad_far)):
        matrix = []
        for index in (2 * chunk, 2 * chunk + 1):
            matrix.append(jnp.where(row_id + (lane ^ index) * group == rank, 1.0, 0.0))
            matrix.append(
                jnp.where((spare_id == 0) & (spot == (lane ^ index)) & (rank < 0), 1.0, 0.0)
            )
        upstream = dot(jnp.concatenate(matrix, axis=0).astype(low), cotangent_ref[...])
        if chunk == 0:
            upstream_ref[...] = upstream[:block]
        gates = [chosen_ref[index : index + 1, 5 * width :] for index in (2 * chunk, 2 * chunk + 1)]
        feed_grad = jnp.concatenate(
            [gates[0] * upstream[:block], gates[1] * upstream[block:]], axis=0
        ).astype(low)
        grad_ref[...] = feed_grad
        back[...] = dot(feed_grad, shrink_ref[...], ((1,), (1,)))


def feed_out_kernel(near_ref, far_ref, shrink_ref, part_0, part_1, part_2, part_3):
    block = part_0.shape[0]
    for activated, pair in ((far_ref, (part_2, part_3)), (near_ref, (part_0, part_1))):
        part = dot(activated[...], shrink_ref[...])
        pair[0][...] = part[:block].astype(low)
        pair[1][...] = part[block:].astype(low)


def partial_kernel(lhs_0, rhs_0, lhs_1, rhs_1, out_0, out_1):
    for lhs, rhs, out in ((lhs_0, rhs_0, out_0), (lhs_1, rhs_1, out_1)):
        chunk = lhs.shape[1] // 3
        for number in range(3):
            span = slice(number * chunk, (number + 1) * chunk)
            out[span, :] = dot(lhs[:, span], rhs[...], ((0,), (0,))).astype(low)


def weight_kernel(counts, bases, me_ref, *refs):
    given_0, given_1, kept_0, kept_1, product = refs[-5:]
    operands = list(refs[:-5])
    base_refs = [operands.pop() for _ in range(bases)][::-1]
    rows = given_0.shape[1] + given_1.shape[1]
    chunk = product.shape[0] // 3
    for group, pairs in enumerate(counts):
        products = []
        for lefts, rights in pairs:
            lhs = [operands.pop(0) for _ in range(lefts)]
            right = jnp.concatenate([operands.pop(0)[...] for _ in range(rights)], axis=0)
            products.append((lhs, right))
        for number in range(3):
            span = slice(number * chunk, (number + 1) * chunk)
            parts = [
                dot(jnp.concatenate([ref[:, span] for ref in lhs], axis=0), right, ((0,), (0,)))
                for lhs, right in products
            ]
            value = jnp.concatenate(parts, axis=1)
            if bases:
                value = value + base_refs[group][span, :].astype(full)
            product[span, :] = value
        for bit, start, given, kept in (
            (0, 0, given_0, kept_0),
            (1, given_0.shape[1], given_1, kept_1),
        ):
            mine = (me_ref[0] >> bit) & 1
            for index in range(4):
                for value, ref in ((1 - mine, given), (mine, kept)):
                    above = (index >> bit) << (bit + 1)
                    at = (above + (value << bit) + (index & bit)) * rows + start
                    at = pl.multiple_of(at, 8)
                    ref[4 * group + index] = product[pl.ds(at, ref.shape[1]), :].astype(low)


def single_kernel(bit, me_ref, lhs_ref, rhs_ref, base_ref, given_ref, kept_ref, product):
    rows = given_ref.shape[1]
    chunk = product.shape[0] // 3
    for number in range(3):
        span = slice(number * chunk, (number + 1) * chunk)
        value = dot(lhs_ref[:, span], rhs_ref[...], ((0,), (0,)))
        product[span, :] = (value + base_ref[span, :].astype(full)).astype(low)
    mine = (me_ref[0] >> bit) & 1
    for index in range(given_ref.shape[0]):
        for value, ref in ((1 - mine, given_ref), (mine, kept_ref)):
            above = (index >> bit) << (bit + 1)
            at = (above + (value << bit) + (index & bit)) * rows
            ref[index] = product[pl.ds(pl.multiple_of(at, 16), rows), :]


def feed_join_kernel(me_ref, held_0, held_1, got_0, got_1, given, kept):
    mine = (me_ref[0] >> 2) & 1
    for index, (held, got) in enumerate(((held_0, got_0), (held_1, got_1))):
        for at, ref in ((1 - mine, given), (mine, kept)):
            ref[index] = (held[at].astype(full) + got[at].astype(full)).astype(low)


def halve_kernel(
    me_ref, held_0, held_1, got_0, got_1, given_0, given_1, kept_0, kept_1
):
    for bit, held, got, given, kept in (
        (1, held_0, got_0, given_0, kept_0),
        (0, held_1, got_1, given_1, kept_1),
    ):
        mine = (me_ref[0] >> bit) & 1
        for index in range(given.shape[0]):
            for value, ref in ((1 - mine, given), (mine, kept)):
                at = 2 * index + value
                ref[index] = (held[at].astype(full) + got[at].astype(full)).astype(low)


def join_kernel(me_ref, held_0, held_1, got_0, got_1, given, kept):
    mine = (me_ref[0] >> 2) & 1
    for index in range(given.shape[0]):
        for value, ref in ((1 - mine, given), (mine, kept)):
            at = 2 * index + value
            upper = held_0[at].astype(full) + got_0[at].astype(full)
            lower = held_1[at].astype(full) + got_1[at].astype(full)
            ref[index] = jnp.concatenate([upper, lower], axis=0).astype(low)


def total_kernel(held_ref, got_ref, *out_refs):
    if len(out_refs[0].shape) == 2:
        for index, out_ref in enumerate(out_refs):
            out_ref[...] = held_ref[index].astype(full) + got_ref[index].astype(full)
        return
    entry_ref, output_ref = out_refs
    total = held_ref[0].astype(full) + got_ref[0].astype(full)
    parts, _, columns = entry_ref.shape
    for index in range(parts):
        entry_ref[index] = total[:, index * columns : (index + 1) * columns]
    output_ref[...] = total[:, parts * columns :]


def call(
    kernel, outs, *operands, words=0, deps=(), time=1.0, scratch=(), token=False, loose=False
):
    count = len(operands)
    deps = tuple(deps)
    outs = tuple(outs)
    if token:
        outs += (((8, 128), full),)

    def run(*refs):
        outs_at = count + len(deps)
        rest = list(refs[outs_at:])
        if token:
            last = rest.pop(len(outs) - 1)
            last[...] = jnp.zeros_like(last)
        kernel(*refs[:count], *rest)

    return pl.pallas_call(
        run,
        out_shape=tuple(jax.ShapeDtypeStruct(shape, kind) for shape, kind in outs),
        in_specs=[SMALL] * words
        + [pl.BlockSpec() if loose else PLAIN] * (count - words)
        + [pl.BlockSpec(memory_space=pl.ANY)] * len(deps),
        scratch_shapes=list(scratch),
        compiler_params=pltpu.CompilerParams(vmem_limit_bytes=VMEM_ASK),
        cost_estimate=pl.CostEstimate(
            flops=int(time * 1.15e9), bytes_accessed=1024, transcendentals=0
        ),
    )(*operands, *deps)


def turn(token):
    return swap(token, "tensor", 1)


def body(
    kept_rows,
    owner_index,
    kept_position,
    resolution,
    mask_token,
    condition,
    modulate_weight,
    entry_weight,
    output_weight,
    expand_weight,
    shrink_weight,
    cotangent,
):
    owners = lax.axis_size("dp")
    me = lax.axis_index("dp")
    lane = lax.axis_index("tensor")
    kept_count, width_part = kept_rows.shape
    width = mask_token.shape[0]
    own_tokens = cotangent.shape[0]
    ff_part = expand_weight.shape[1]
    quarter = own_tokens // QUARTERS
    group = quarter // 2
    arrived_count = own_tokens // 2
    block = group + SPARE
    rows = QUARTERS * block
    capacity = 2 * kept_count // owners
    slots_all = owners * capacity
    direct = owners == SWAP_OWNERS
    lane_word = lane.reshape(1).astype(jnp.int32)
    me_word = me.reshape(1).astype(jnp.int32)
    big_word = resolution[:1]
    context_part = lax.dynamic_slice_in_dim(
        condition.astype(full), lane * width_part, width_part, 1
    )
    lifted = jax.nn.silu(context_part).astype(low)
    if direct:
        padded = -(-width_part // capacity) * capacity
        riders = jnp.pad(lifted, ((0, 0), (0, padded - width_part))).reshape(-1, capacity)
        extra = 16
    else:
        riders = lifted.reshape(-1, capacity)
        rider_count = riders.shape[0]
        extra = -(-(rider_count + 2) // 16) * 16
        riders = jnp.pad(riders, ((2, extra - 2 - rider_count), (0, 0)))
    slab_rows = width_part + extra
    slab_shape = (slab_rows, capacity)
    if not direct:
        slab_shape = (owners,) + slab_shape
    *slabs, slot_index = call(
        partial(
            pack_kernel,
            owners,
            FAR + NEAR if direct else range(owners),
            own_tokens.bit_length() - 1,
            extra,
            capacity,
        ),
        ((slab_shape, low),) * (owners if direct else 1) + (((1, kept_count), jnp.int32),),
        me_word,
        kept_rows.T,
        (owner_index * own_tokens + kept_position)[None, :],
        *([] if direct else [riders]),
        words=1,
        time=1.0,
        loose=direct,
    )

    steps = -(-6 * width // arrived_count)
    table, bias, bias_turned = call(
        table_kernel,
        (
            ((QUARTERS * steps, arrived_count), low),
            ((rows, rows), full),
            ((rows, rows), full),
        ),
        big_word,
        lifted,
        modulate_weight,
        words=1,
        deps=[slot_index],
        time=2.0,
        scratch=[pltpu.VMEM((8, steps * arrived_count), full)],
    )
    if direct:
        slabs = exchange_owners(dict(zip(FAR + NEAR, slabs)))
        slabs = list(slabs.values())
    else:
        slabs = exchange_owners(slabs)
    compact, slot_rank, event = call(
        partial(unpack_kernel, owners),
        (
            ((width_part + QUARTERS * steps, arrived_count), low),
            ((1, slots_all), jnp.int32),
        ),
        me_word,
        table,
        *slabs,
        words=1,
        time=1.2,
        token=True,
        scratch=[pltpu.VMEM((slab_rows, slots_all), low)],
    )
    (token_rank,) = call(
        partial(spots_kernel, owners),
        (((1, own_tokens), jnp.int32),),
        me_word,
        *slabs,
        words=1,
        deps=[event],
        time=1.2,
        scratch=[pltpu.VMEM((extra, slots_all), low)],
    )
    if not direct:
        owner_order = jnp.arange(owners, dtype=jnp.int32) ^ me
        lifted_all = slabs[0][:, width_part + 2 : width_part + 2 + rider_count]
        lifted_all = lifted_all.reshape(owners * QUARTERS, width_part)
    spatial_pieces = gather_blocks(compact)
    entry_flat = jnp.transpose(entry_weight, (1, 2, 0)).reshape(3 * width_part, width)
    token_shape = ((block, width), low)
    half = 2 * block
    chosen, spatial_own, normed_one, projected, attended_far, part_2, part_3 = call(
        entry_kernel,
        (
            ((QUARTERS, 6 * width), full),
            token_shape,
            ((rows, width), low),
            ((rows, 3 * width_part), low),
            ((half, width_part), low),
            token_shape,
            token_shape,
        ),
        lane_word,
        big_word,
        *spatial_pieces,
        mask_token[None, :],
        entry_flat,
        bias,
        output_weight,
        words=2,
        deps=[token_rank],
        time=5.0,
        scratch=[
            pltpu.VMEM((width, arrived_count), low),
            pltpu.VMEM((8, steps * arrived_count), full),
        ],
    )
    far, across, start = sum_far(part_2, part_3)
    attended_near, part_0, part_1 = call(
        attend_kernel,
        (((half, width_part), low), token_shape, token_shape),
        projected,
        bias,
        output_weight,
        deps=[start],
        time=3.0,
    )
    got = swap(part_1, "tensor", 1)
    feed_grad_near, feed_grad_far, upstream_own, back_near, back_far = call(
        upstream_kernel,
        (
            ((half, width), low),
            ((half, width), low),
            ((block, width), full),
            ((half, width), full),
            ((half, width), full),
        ),
        lane_word,
        token_rank,
        chosen,
        cotangent,
        shrink_weight,
        words=1,
        deps=[part_1],
        time=3.6,
    )
    branch, middle, normed_two_own = call(
        middle_kernel,
        (((block, width), full), ((block, width), full), token_shape),
        part_0,
        got,
        across,
        spatial_own,
        chosen,
        deps=[back_far],
        time=0.6,
    )

    def feed_call(piece_0, piece_1, back, *deps):
        return call(
            feed_kernel,
            (((half, width), low), ((half, width), low), ((half, width), low))
            + (token_shape, token_shape),
            piece_0,
            piece_1,
            back,
            expand_weight,
            deps=deps,
            time=2.4,
        )

    near_piece = swap(normed_two_own, "tensor", 1)
    across = swap(normed_two_own, "tensor", 2)
    normed_near, activated_near, hidden_near, part_0, part_1 = feed_call(
        normed_two_own, near_piece, back_near
    )
    *partials, event = call(
        partial_kernel,
        (((width, ff_part), low),) * 2,
        feed_grad_near,
        activated_near,
        normed_near,
        hidden_near,
        time=2.5,
        token=True,
    )
    (across,) = call(copy_kernel, (token_shape,), across, deps=[event], time=0.3)
    last_piece = swap(across, "tensor", 1)
    normed_far, activated_far, hidden_far, part_2, part_3 = feed_call(
        across, last_piece, back_far
    )
    feed_groups = [
        [([feed_grad_far], [activated_far])],
        [([normed_far], [hidden_far])],
    ]
    event = part_0
    if direct:
        me_now = lax.axis_index("dp").reshape(1).astype(jnp.int32)
        shape = ((owners // 2, width // owners, ff_part), low)
        sums = []
        for bit, lhs, rhs, base, waits in (
            (1, normed_far, hidden_far, partials[1], 0),
            (0, feed_grad_far, activated_far, partials[0], 1),
        ):
            given, kept, event = call(
                partial(single_kernel, bit),
                (shape, shape),
                me_now,
                lhs,
                rhs,
                base,
                words=1,
                deps=[turn(event)] if waits else (),
                time=SINGLE_TIME,
                scratch=[pltpu.VMEM((width, ff_part), low)],
                token=True,
            )
            sums.append((swap(given, "dp", 1 << bit), kept))
        feed_got = [sums[1][0], sums[0][0]]
        feed_kept = [sums[1][1], sums[0][1]]
    far, across, start = sum_far(part_2, part_3, [event])
    got = swap(part_1, "tensor", 1)
    middle_grad, branch_grad_own, sums, start = call(
        middle_back_kernel,
        (((block, width), full), token_shape, ((SPARE, width), full)),
        part_0,
        got,
        across,
        middle,
        branch,
        upstream_own,
        chosen,
        deps=[start],
        time=0.7,
        token=True,
    )
    branch_near = swap(branch_grad_own, "tensor", 1)
    branch_across = swap(branch_grad_own, "tensor", 2)
    feed_parts = call(
        feed_out_kernel,
        (token_shape,) * QUARTERS,
        activated_near,
        activated_far,
        shrink_weight,
        deps=[turn(start)],
        time=0.1,
    )
    feed_far = swap(feed_parts[3], "tensor", 1)
    feed_near = swap(feed_parts[1], "tensor", 1)
    probs, event = call(
        probs_kernel,
        (((width_part // HEAD, rows, rows), low),),
        projected,
        bias_turned,
        deps=[feed_parts[0]],
        time=0.1,
        token=True,
    )
    (branch_across,) = call(copy_kernel, (token_shape,), branch_across, deps=[event], time=0.1)
    branch_pieces = [
        branch_grad_own,
        branch_near,
        branch_across,
        swap(branch_across, "tensor", 1),
    ]
    feed_far, start = call(
        add_kernel,
        (token_shape,),
        feed_parts[2],
        feed_far,
        deps=[branch_pieces[2]],
        time=0.1,
        token=True,
    )
    branch_grad, projected_grad, event = call(
        attend_back_kernel,
        (((rows, width), low), ((rows, 3 * width_part), low)),
        projected,
        probs,
        output_weight,
        *branch_pieces,
        deps=[turn(start)],
        time=0.1,
        token=True,
    )
    feed_across = swap(feed_far, "tensor", 2)
    if direct:
        feed_given, feed_kept, event = halve_sums(feed_kept, feed_got, [event])
        feed_got = cross(feed_given, 2, 1)
    part_2, part_3 = call(
        partial(entry_back_kernel, 1),
        (token_shape, token_shape),
        projected_grad,
        entry_flat,
        deps=[feed_across, feed_near, event],
        time=0.1,
    )
    far, across, start = sum_far(part_2, part_3)
    part_0, part_1 = call(
        partial(entry_back_kernel, 0),
        (token_shape, token_shape),
        projected_grad,
        entry_flat,
        deps=[start],
        time=0.2,
    )
    got = swap(part_1, "tensor", 1)
    entry_groups = [
        [([normed_one], [projected_grad]), ([branch_grad], [attended_near, attended_far])]
    ]
    event = part_1
    if direct:
        entry_given, entry_kept, event = start_sums(entry_groups, ENTRY_SPLIT, [got], 0.2)
        entry_got = cross(entry_given, 1, 2)
    *back_pieces, back_token = call(
        back_kernel,
        (((width_part + 80, group), low),) * QUARTERS,
        lane_word,
        part_0,
        got,
        across,
        spatial_own,
        middle_grad,
        chosen,
        sums,
        feed_parts[0],
        feed_near,
        feed_across,
        upstream_own,
        words=1,
        deps=[event],
        time=BACK_TIME,
        token=True,
        scratch=[pltpu.VMEM((width, group), low), pltpu.VMEM((80, 128), full)],
    )
    if direct:
        feed_given, feed_kept, joined = call(
            feed_join_kernel,
            (((2, width // owners, ff_part), low),) * 2,
            me_word,
            *feed_kept,
            *feed_got,
            words=1,
            deps=[back_token],
            time=JOIN_TIME,
            token=True,
        )
        feed_got = swap(feed_given, "dp", 4)
    back_pieces = [
        back_pieces[0],
        swap(back_pieces[1], "tensor", 1),
        *swap_pair(back_pieces[2:]),
    ]
    chunks = 6 * width // 128
    logistic = jax.nn.sigmoid(context_part)
    logistic = logistic * (1.0 + context_part * (1.0 - logistic))
    if direct:
        entry_given, entry_kept, halved = halve_sums(entry_kept, entry_got, [back_token], HALVE_TIME)
        entry_got = cross(entry_given, 2, 1)
        shrink_grad, expand_grad, total_token = call(
            total_kernel,
            (((width // owners, ff_part), full),) * 2,
            feed_kept,
            feed_got,
            deps=[halved],
            time=TOTAL_TIME,
            token=True,
        )
        slabs, table_grad, event = call(
            partial(slots_kernel, owners),
            (
                ((owners, width_part + RIDERS, capacity), low),
                ((QUARTERS, chunks, 128), low),
            ),
            lane_word,
            me_word,
            big_word,
            slot_rank,
            riders,
            *back_pieces,
            words=3,
            time=0.1,
            token=True,
            scratch=[
                pltpu.VMEM((QUARTERS, chunks + 2, 128), full),
                pltpu.VMEM((16, 128), full),
            ],
        )
        (slabs,) = exchange_owners([slabs])
        table_grad = table_grad.reshape(QUARTERS, 6 * width)
        entry_got, entry_kept, event = join_sums(entry_kept, entry_got, [total_token])
        out_pieces = call(
            out_kernel,
            (((width_part + 16, group), low),) * QUARTERS,
            lane_word,
            feed_parts[0],
            feed_near,
            feed_across,
            middle,
            chosen,
            words=1,
            deps=[event],
            time=0.1,
            scratch=[pltpu.VMEM((width, group), low), pltpu.VMEM((16, 128), full)],
        )
        out_pieces = [
            out_pieces[0],
            swap(out_pieces[1], "tensor", 1),
            *swap_pair(out_pieces[2:]),
        ]
        layer_out, layer_token = call(
            layer_kernel,
            (((width_part, own_tokens), low),),
            lane_word,
            token_rank,
            *out_pieces,
            words=1,
            deps=[event],
            time=0.1,
            token=True,
            scratch=[pltpu.VMEM((8, width), full), pltpu.VMEM((width, 8), full)],
        )
        kept_grad, modulate_grad, mask_grad, kept_token = call(
            partial(kept_kernel, owners),
            (
                ((width_part, kept_count), low),
                ((width_part, 6 * width // owners), full),
                ((1, width // owners), full),
            ),
            me_word,
            slot_index,
            slabs,
            words=1,
            deps=[layer_token],
            time=KEPT_TIME,
            token=True,
            scratch=[
                pltpu.VMEM((owners * QUARTERS, 1024), full),
                pltpu.VMEM((owners * QUARTERS, padded), full),
            ],
        )
        mask_grad = mask_grad[0]
    else:
        event = back_pieces[1]
        rows_back = jnp.concatenate([piece[:width_part] for piece in back_pieces], axis=1)
        rank_ids = jnp.arange(arrived_count, dtype=jnp.int32)
        rank_ids = ((rank_ids // group) ^ lane) * group + rank_ids % group
        matrix = (rank_ids[:, None] == slot_rank).astype(low)
        slabs = dot(rows_back, matrix).astype(low).reshape(width_part, owners, capacity)
        slabs = jnp.take(jnp.transpose(slabs, (1, 0, 2)), owner_order, axis=0)
        slabs = jnp.take(exchange_owners([slabs])[0], owner_order, axis=0)
        slabs = jnp.transpose(slabs, (1, 0, 2)).reshape(width_part, slots_all)
        slot_ids = jnp.arange(slots_all, dtype=jnp.int32)[:, None]
        kept_grad = dot(slabs, (slot_ids == slot_index).astype(low)).astype(low)
        riders = jnp.stack(
            [piece[width_part : width_part + 8 * width // 128] for piece in back_pieces]
        )
        riders = riders.reshape(QUARTERS, 8, width).astype(full)
        mask_total = jnp.sum(riders[:, 6] + riders[:, 7], axis=0)
        table_local = riders[:, :6].reshape(QUARTERS, 6 * width)
        table_small = jnp.take(table_local, jnp.arange(QUARTERS, dtype=jnp.int32) ^ lane, axis=0)
        first = jnp.arange(QUARTERS, dtype=jnp.int32)[:, None] == 0
        table_big = jnp.where(first, jnp.sum(table_local, axis=0, keepdims=True), 0.0)
        table_grad = jnp.where(big_word[0] == 1, table_big, table_small).astype(low)
        sent = jnp.transpose(table_grad.reshape(QUARTERS, owners, -1), (1, 0, 2))
        table_all = exchange_owners([sent])[0].reshape(owners * QUARTERS, -1)
        modulate_grad = dot(lifted_all, table_all, ((0,), (0,)))
        mask_grad = lax.psum_scatter(mask_total, "dp", scatter_dimension=0, tiled=True)
    condition_grad = dot(table_grad, modulate_weight, ((1,), (1,))) * logistic
    if not direct:
        out_pieces = call(
            out_kernel,
            (((width_part + 16, group), low),) * QUARTERS,
            lane_word,
            feed_parts[0],
            feed_near,
            feed_across,
            middle,
            chosen,
            words=1,
            deps=[],
            time=0.1,
            scratch=[pltpu.VMEM((width, group), low), pltpu.VMEM((16, 128), full)],
        )
        out_pieces = [
            out_pieces[0],
            swap(out_pieces[1], "tensor", 1),
            *swap_pair(out_pieces[2:]),
        ]
        layer_out, layer_token = call(
            layer_kernel,
            (((width_part, own_tokens), low),),
            lane_word,
            token_rank,
            *out_pieces,
            words=1,
            deps=[],
            time=0.1,
            token=True,
            scratch=[pltpu.VMEM((8, width), full), pltpu.VMEM((width, 8), full)],
        )
    rows_part = width // owners
    if direct:
        entry_grad, output_grad = call(
            total_kernel,
            (((3, rows_part, width_part), full), ((rows_part, width_part), full)),
            entry_kept,
            entry_got,
            deps=[kept_token],
            time=0.8,
        )
    else:
        totals = []
        for number, pairs in enumerate(feed_groups + entry_groups):
            total = [
                dot(jnp.concatenate(lhs), jnp.concatenate(rhs), ((0,), (0,))) for lhs, rhs in pairs
            ]
            total = jnp.concatenate(total, axis=1)
            if number < len(partials):
                total = total + partials[number].astype(full)
            totals.append(sum_owners(total.astype(low).reshape(owners, rows_part, -1)))
        shrink_grad, expand_grad, entry_grad = totals
        output_grad = entry_grad[:, 3 * width_part :]
        entry_grad = entry_grad[:, : 3 * width_part].reshape(rows_part, 3, width_part)
        entry_grad = jnp.transpose(entry_grad, (1, 0, 2))

    return (
        layer_out.T,
        kept_grad.T,
        mask_grad,
        condition_grad,
        modulate_grad,
        jnp.transpose(entry_grad, (1, 0, 2)),
        output_grad.T,
        expand_grad,
        shrink_grad.T,
    )


def solution(mesh):
    return jax.shard_map(
        body,
        mesh=mesh,
        in_specs=(
            P("dp", "tensor"),
            P("dp"),
            P("dp"),
            P("dp"),
            P(),
            P("dp", None),
            P("tensor", None),
            P(None, None, "tensor"),
            P("tensor", None),
            P(None, "tensor"),
            P("tensor", None),
            P("dp", None),
        ),
        out_specs=(
            P("dp", "tensor"),
            P("dp", "tensor"),
            P("dp"),
            P("dp", "tensor"),
            P("tensor", "dp"),
            P("dp", None, "tensor"),
            P("tensor", "dp"),
            P("dp", "tensor"),
            P("tensor", "dp"),
        ),
        check_vma=False,
    )
```

```python
from functools import partial

import jax
import jax.numpy as jnp
from jax import lax
from jax.experimental import pallas as pl
from jax.experimental.pallas import tpu as pltpu
from jax.sharding import PartitionSpec as P

HEAD = 72
QUARTERS = 4
SPARE = 8
scale = HEAD ** (-0.5)
epsilon = 1e-06
gelu_coeff = 0.7978845608028654
low = jnp.bfloat16
full = jnp.float32
VMEM_ASK = 12 * 1024 * 1024
RIDERS = 48
SWAP_OWNERS = 8
FEED_SPLIT = 72
ENTRY_SPLIT = 72
FAR = (6, 7, 4, 5)
NEAR = (2, 3, 1, 0)
JOIN_TIME = 0.1
KEPT_TIME = 0.1
TOTAL_TIME = 14.0
HALVE_TIME = 0.35
BACK_TIME = 0.1
SINGLE_TIME = 1.0
SMALL = pl.BlockSpec(memory_space=pltpu.SMEM)
PLAIN = pl.BlockSpec(memory_space=pltpu.VMEM)


def dot(a, b, dims=((1,), (0,))):
    return lax.dot_general(a, b, (dims, ((), ())), preferred_element_type=full)


def normalize(rows):
    centered = rows - jnp.mean(rows, axis=-1, keepdims=True)
    inverse = lax.rsqrt(jnp.mean(centered * centered, axis=-1, keepdims=True) + epsilon)
    return (centered * inverse, inverse)


def normalize_back(unit, inverse, grad):
    return inverse * (
        grad
        - jnp.mean(grad, axis=-1, keepdims=True)
        - unit * jnp.mean(grad * unit, axis=-1, keepdims=True)
    )


def gelu_both(value):
    square = value * value
    inner = value * (gelu_coeff + 0.044715 * gelu_coeff * square)
    half = 0.5 + 0.5 * jnp.tanh(inner)
    activated = value * half
    outer = 2.0 * gelu_coeff + 6.0 * 0.044715 * gelu_coeff * square
    return (activated, half + activated * (1.0 - half) * outer)


def swap(value, axis, bit):
    size = lax.axis_size(axis)
    return lax.ppermute(value, axis, [(index, index ^ bit) for index in range(size)])


def swap_pair(pieces):
    came = swap(jnp.stack(pieces), "tensor", 2)
    return came[0], swap(came[1], "tensor", 1)


def gather_blocks(own):
    near = swap(own, "tensor", 1)
    across = swap(own, "tensor", 2)
    return [own, near, across, swap(across, "tensor", 1)]


def sum_far(part_2, part_3, deps=()):
    got = swap(part_3, "tensor", 1)
    far, token = call(
        add_kernel, ((part_2.shape, low),), part_2, got, deps=deps, time=0.1, token=True
    )
    return far, swap(far, "tensor", 2), turn(token)


def sum_owners(total):
    owners, rows, columns = total.shape
    me = lax.axis_index("dp")
    step = 1
    while step < owners:
        pairs = total.reshape(-1, 2, rows, columns)
        mine = (me // step) % 2
        given = lax.dynamic_index_in_dim(pairs, 1 - mine, 1, keepdims=False)
        kept = lax.dynamic_index_in_dim(pairs, mine, 1, keepdims=False)
        total = kept.astype(full) + swap(given, "dp", step).astype(full)
        step *= 2
        total = total if step == owners else total.astype(low)
    return total[0]


def part_shapes(count, upper, lower, columns):
    return [((count, upper, columns), low), ((count, lower, columns), low)]


def start_sums(groups, split, deps=(), time=3.0, bases=()):
    width = groups[0][0][0][0].shape[1]
    columns = sum(rhs[0].shape[1] for _, rhs in groups[0])
    rows = width // 8
    shapes = part_shapes(4 * len(groups), split, rows - split, columns)
    counts = [[(len(lhs), len(rhs)) for lhs, rhs in pairs] for pairs in groups]
    given_0, given_1, kept_0, kept_1, token = call(
        partial(weight_kernel, counts, len(bases)),
        shapes + shapes,
        lax.axis_index("dp").reshape(1).astype(jnp.int32),
        *[value for pairs in groups for lhs, rhs in pairs for value in (*lhs, *rhs)],
        *bases,
        words=1,
        deps=deps,
        time=time,
        scratch=[pltpu.VMEM((width, columns), full)],
        token=True,
    )
    return (given_0, given_1), (kept_0, kept_1), token


def cross(given, first, second):
    return swap(given[0], "dp", first), swap(given[1], "dp", second)


def halve_sums(kept, got, deps=(), time=0.1):
    count, _, columns = kept[0].shape
    shapes = part_shapes(count // 2, kept[0].shape[1], kept[1].shape[1], columns)
    given_0, given_1, kept_0, kept_1, token = call(
        halve_kernel,
        shapes + shapes,
        lax.axis_index("dp").reshape(1).astype(jnp.int32),
        *kept,
        *got,
        words=1,
        deps=deps,
        time=time,
        token=True,
    )
    return (given_0, given_1), (kept_0, kept_1), token


def join_sums(kept, got, deps=()):
    count, _, columns = kept[0].shape
    shape = ((count // 2, kept[0].shape[1] + kept[1].shape[1], columns), low)
    given, kept, token = call(
        join_kernel,
        (shape, shape),
        lax.axis_index("dp").reshape(1).astype(jnp.int32),
        *kept,
        *got,
        words=1,
        deps=deps,
        time=JOIN_TIME,
        token=True,
    )
    return swap(given, "dp", 4), kept, token


def exchange_owners(slabs):
    if isinstance(slabs, dict):
        return {index: swap(slab, "dp", index) if index else slab for index, slab in slabs.items()}
    return [lax.all_to_all(slabs[0], "dp", split_axis=0, concat_axis=0, tiled=True)]


def attend(projected_ref, bias_ref, output_ref, attended_ref, chunk, half, width_part):
    span = slice(chunk * half, (chunk + 1) * half)
    pieces = []
    for head in range(width_part // HEAD):
        at = head * HEAD
        queries = projected_ref[span, at : at + HEAD]
        keys = projected_ref[:, width_part + at : width_part + at + HEAD]
        values = projected_ref[:, 2 * width_part + at : 2 * width_part + at + HEAD]
        scores = dot(queries, keys, ((1,), (1,))) * scale + bias_ref[span, :]
        spread = jnp.exp(scores - jnp.max(scores, axis=1, keepdims=True))
        probs = spread * (1.0 / jnp.sum(spread, axis=1, keepdims=True))
        pieces.append(dot(probs.astype(low), values))
    attended = jnp.concatenate(pieces, axis=1).astype(low)
    attended_ref[...] = attended
    return dot(attended, output_ref[...])


def entry_kernel(
    lane_ref,
    big_ref,
    piece_0,
    piece_1,
    piece_2,
    piece_3,
    mask_ref,
    entry_ref,
    bias_ref,
    output_ref,
    chosen_ref,
    spatial_ref,
    normed_ref,
    projected_ref,
    attended_ref,
    part_0,
    part_1,
    gathered,
    table,
):
    lane = lane_ref[0]
    block, width = spatial_ref.shape
    width_part = width // QUARTERS
    group = block - SPARE
    half = 2 * block
    pieces = (piece_0, piece_1, piece_2, piece_3)
    for index, piece in enumerate(pieces):
        at = pl.multiple_of((lane ^ index) * width_part, 16)
        gathered[pl.ds(at, width_part), :] = piece[:width_part, :]
    summed = pieces[0][width_part:, :].astype(full)
    for piece in pieces[1:]:
        summed = summed + piece[width_part:, :].astype(full)
    span = summed.shape[1]
    steps = summed.shape[0] // QUARTERS
    for row in range(QUARTERS):
        for step in range(steps):
            from_row = row * steps + step
            table[row : row + 1, step * span : (step + 1) * span] = summed[from_row : from_row + 1]
    for index in range(QUARTERS):
        row = jnp.where(big_ref[0] == 1, 0, lane ^ index)
        chosen_ref[index : index + 1, :] = table[pl.ds(row, 1), : 6 * width]
    spare_id = lax.broadcasted_iota(jnp.int32, (SPARE, width), 0)
    spare = jnp.where(spare_id == 0, mask_ref[...].astype(full), 0.0)
    for chunk in (1, 0):
        span = slice(chunk * half, (chunk + 1) * half)
        normed = []
        for index in (2 * chunk, 2 * chunk + 1):
            at = pl.multiple_of((lane ^ index) * group, 128)
            kept = jnp.transpose(gathered[:, pl.ds(at, group)].astype(full))
            rows = jnp.concatenate([kept, spare], axis=0)
            if index == 0:
                spatial_ref[...] = rows.astype(low)
            unit, inverse = normalize(rows)
            shift = chosen_ref[index : index + 1, :width]
            gain = chosen_ref[index : index + 1, width : 2 * width]
            normed.append(unit * (1.0 + gain) + shift)
        normed = jnp.concatenate(normed, axis=0).astype(low)
        normed_ref[span, :] = normed
        projected_ref[span, :] = dot(normed, entry_ref[...], ((1,), (1,))).astype(low)
    part = attend(projected_ref, bias_ref, output_ref, attended_ref, 1, half, width_part)
    part_0[...] = part[:block].astype(low)
    part_1[...] = part[block:].astype(low)


def attend_kernel(projected_ref, bias_ref, output_ref, attended_ref, part_0, part_1):
    block = part_0.shape[0]
    part = attend(
        projected_ref, bias_ref, output_ref, attended_ref, 0, 2 * block, output_ref.shape[0]
    )
    part_0[...] = part[:block].astype(low)
    part_1[...] = part[block:].astype(low)


def middle_kernel(
    part_0, part_1, part_2, spatial_ref, chosen_ref, branch_ref, middle_ref, normed_ref
):
    width = spatial_ref.shape[1]
    branch = part_0[...].astype(full) + part_1[...].astype(full) + part_2[...].astype(full)
    branch_ref[...] = branch
    middle = spatial_ref[...].astype(full) + chosen_ref[0:1, 2 * width : 3 * width] * branch
    middle_ref[...] = middle
    unit, inverse = normalize(middle)
    shift = chosen_ref[0:1, 3 * width : 4 * width]
    gain = chosen_ref[0:1, 4 * width : 5 * width]
    normed_ref[...] = (unit * (1.0 + gain) + shift).astype(low)


def feed_kernel(
    piece_0,
    piece_1,
    back_ref,
    expand_ref,
    normed_ref,
    activated_ref,
    hidden_grad_ref,
    *parts,
):
    normed = jnp.concatenate([piece_0[...].astype(full), piece_1[...].astype(full)], axis=0)
    normed = normed.astype(low)
    normed_ref[...] = normed
    hidden = dot(normed, expand_ref[...])
    activated, slope = gelu_both(hidden)
    activated_ref[...] = activated.astype(low)
    hidden_grad = (back_ref[...] * slope).astype(low)
    hidden_grad_ref[...] = hidden_grad
    if parts:
        feed_part_kernel(hidden_grad_ref, expand_ref, *parts)


def feed_part_kernel(hidden_grad_ref, expand_ref, part_0, part_1):
    block = part_0.shape[0]
    part = dot(hidden_grad_ref[...], expand_ref[...], ((1,), (1,)))
    part_0[...] = part[:block].astype(low)
    part_1[...] = part[block:].astype(low)


def middle_back_kernel(
    part_0,
    part_1,
    part_2,
    middle_ref,
    branch_ref,
    upstream_ref,
    chosen_ref,
    middle_grad_ref,
    branch_grad_ref,
    sums_ref,
):
    width = middle_ref.shape[1]
    normed_grad = part_0[...].astype(full) + part_1[...].astype(full) + part_2[...].astype(full)
    unit, inverse = normalize(middle_ref[...])
    gain = chosen_ref[0:1, 4 * width : 5 * width]
    middle_grad = upstream_ref[...] + normalize_back(unit, inverse, normed_grad * (1.0 + gain))
    middle_grad_ref[...] = middle_grad
    branch_grad_ref[...] = (chosen_ref[0:1, 2 * width : 3 * width] * middle_grad).astype(low)
    sums_ref[0:1, :] = jnp.sum(middle_grad * branch_ref[...], axis=0, keepdims=True)
    sums_ref[1:2, :] = jnp.sum(normed_grad, axis=0, keepdims=True)
    sums_ref[2:3, :] = jnp.sum(normed_grad * unit, axis=0, keepdims=True)


def probs_kernel(projected_ref, bias_ref, probs_ref):
    width_part = projected_ref.shape[1] // 3
    for head in range(width_part // HEAD):
        at = head * HEAD
        queries = projected_ref[:, at : at + HEAD]
        keys = projected_ref[:, width_part + at : width_part + at + HEAD]
        scores = dot(keys, queries, ((1,), (1,))) * scale + bias_ref[...]
        spread = jnp.exp(scores - jnp.max(scores, axis=0, keepdims=True))
        probs = spread * (1.0 / jnp.sum(spread, axis=0, keepdims=True))
        probs_ref[head] = probs.astype(low)


def attend_back_kernel(
    projected_ref,
    probs_ref,
    output_ref,
    piece_0,
    piece_1,
    piece_2,
    piece_3,
    branch_grad_ref,
    grad_ref,
):
    rows, width_all = projected_ref.shape
    width_part = width_all // 3
    block = piece_0.shape[0]
    half = 2 * block
    for chunk, pair in enumerate(((piece_0, piece_1), (piece_2, piece_3))):
        branch_grad_ref[chunk * half : (chunk + 1) * half, :] = jnp.concatenate(
            [piece[...].astype(full) for piece in pair], axis=0
        ).astype(low)
    attended_grad = dot(branch_grad_ref[...], output_ref[...], ((1,), (1,))).astype(low)
    pieces = [[], [], []]
    for head in range(width_part // HEAD):
        at = head * HEAD
        queries = projected_ref[:, at : at + HEAD]
        keys = projected_ref[:, width_part + at : width_part + at + HEAD]
        values = projected_ref[:, 2 * width_part + at : 2 * width_part + at + HEAD]
        grad = attended_grad[:, at : at + HEAD]
        probs = probs_ref[head]
        pieces[2].append(dot(probs, grad))
        probs = probs.astype(full)
        prob_grad = dot(values, grad, ((1,), (1,)))
        delta = jnp.sum(probs * prob_grad, axis=0, keepdims=True)
        score_grad = (probs * (prob_grad - delta)).astype(low)
        pieces[1].append(dot(score_grad, queries) * scale)
        pieces[0].append(dot(score_grad, keys, ((0,), (0,))) * scale)
    grad_ref[...] = jnp.concatenate(pieces[0] + pieces[1] + pieces[2], axis=1).astype(low)


def entry_back_kernel(chunk, grad_ref, entry_ref, part_0, part_1):
    block = part_0.shape[0]
    part = dot(grad_ref[2 * chunk * block : 2 * (chunk + 1) * block, :], entry_ref[...])
    part_0[...] = part[:block].astype(low)
    part_1[...] = part[block:].astype(low)


def pack_kernel(owners, chosen, shift, extra, capacity, me_ref, kept_ref, spot_ref, *refs):
    direct = len(refs) == owners + 1
    out_refs = refs if direct else refs[1:]
    slot_ref = out_refs[-1]
    kept_count = kept_ref.shape[1]
    owner_local = (spot_ref[...] >> shift) ^ me_ref[0]
    owner_id = lax.broadcasted_iota(jnp.int32, (owners, kept_count), 0)
    hot = (owner_id == owner_local).astype(full)
    row_id = lax.broadcasted_iota(jnp.int32, (kept_count, kept_count), 0)
    column_id = lax.broadcasted_iota(jnp.int32, (kept_count, kept_count), 1)
    before = dot(hot.astype(low), (row_id < column_id).astype(full).astype(low))
    rank = jnp.sum(hot * before, axis=0, keepdims=True).astype(jnp.int32)
    slot = owner_local * capacity + rank
    slot_ref[...] = slot
    coded = (spot_ref[...] & ((1 << shift) - 1)) + 1
    tag_id = lax.broadcasted_iota(jnp.int32, (extra, kept_count), 0)
    tags = jnp.where(tag_id == 0, coded >> 5, jnp.where(tag_id == 1, coded & 31, 0))
    rows = jnp.concatenate([kept_ref[...], tags.astype(full).astype(low)], axis=0)
    slot_id = lax.broadcasted_iota(jnp.int32, (capacity, kept_count), 0)
    for number, index in enumerate(chosen):
        matrix = (slot_id + index * capacity == slot).astype(full).astype(low)
        slab = dot(rows, matrix, ((1,), (1,)))
        split = kept_ref.shape[0]
        if not direct:
            lower = slab[split:] + refs[0][...].astype(full)
            slab = jnp.concatenate([slab[:split], lower], axis=0)
            out_refs[0][me_ref[0] ^ index] = slab.astype(low)
        else:
            out_refs[number][...] = slab.astype(low)


def places(owners, me_ref, slab_refs, arrived, width_part):
    slots_all = arrived.shape[1]
    capacity = slots_all // owners
    for index in range(owners):
        if len(slab_refs) == 1:
            slab = slab_refs[0][me_ref[0] ^ index]
        else:
            slab = slab_refs[(FAR + NEAR).index(index)][...]
        rows = arrived.shape[0]
        arrived[:, index * capacity : (index + 1) * capacity] = slab[slab.shape[0] - rows :]
    tags = arrived[width_part : width_part + 16, :].astype(full)
    place = tags[0:1] * 32.0 + tags[1:2] - 1.0
    turned = jnp.transpose(jnp.broadcast_to(place, (8, slots_all)))[:, 0:1]
    return place, jnp.where(turned < 0.0, 1e9, turned)


def unpack_kernel(owners, me_ref, table_ref, *refs):
    slab_refs, (compact_ref, slot_rank_ref, arrived) = refs[:-3], refs[-3:]
    arrived_count = compact_ref.shape[1]
    width_part = compact_ref.shape[0] - table_ref.shape[0]
    place, turned = places(owners, me_ref, slab_refs, arrived, width_part)
    slot_rank = jnp.sum(jnp.where(turned < place, 1.0, 0.0), axis=0, keepdims=True)
    slot_rank = jnp.where(place < 0.0, -1.0, slot_rank).astype(jnp.int32)
    slot_rank_ref[...] = slot_rank
    rank_id = lax.broadcasted_iota(jnp.int32, (arrived_count, arrived.shape[1]), 0)
    matrix = (rank_id == slot_rank).astype(full).astype(low)
    compact_ref[:width_part, :] = dot(arrived[:width_part, :], matrix, ((1,), (1,))).astype(low)
    compact_ref[width_part:, :] = table_ref[...]


def spots_kernel(owners, me_ref, *refs):
    slab_refs, (token_rank_ref, arrived) = refs[:-2], refs[-2:]
    own_tokens = token_rank_ref.shape[1]
    _, turned = places(owners, me_ref, slab_refs, arrived, 0)
    spot = lax.broadcasted_iota(jnp.int32, (1, own_tokens), 1).astype(full)
    token_rank = jnp.sum(jnp.where(turned < spot, 1.0, 0.0), axis=0, keepdims=True)
    filled = jnp.sum(jnp.where(turned == spot, 1.0, 0.0), axis=0, keepdims=True)
    token_rank_ref[...] = jnp.where(filled > 0.0, token_rank, -1.0).astype(jnp.int32)


def back_kernel(
    lane_ref,
    part_0,
    part_1,
    part_2,
    spatial_ref,
    middle_grad_ref,
    chosen_ref,
    sums_ref,
    feed_0,
    feed_1,
    feed_2,
    upstream_ref,
    piece_0,
    piece_1,
    piece_2,
    piece_3,
    turned,
    riders,
):
    lane = lane_ref[0]
    block, width = spatial_ref.shape
    group = block - SPARE
    width_part = width // QUARTERS
    normed_grad = part_0[...].astype(full) + part_1[...].astype(full) + part_2[...].astype(full)
    unit, inverse = normalize(spatial_ref[...].astype(full))
    gain = chosen_ref[0:1, width : 2 * width]
    grad = middle_grad_ref[...] + normalize_back(unit, inverse, normed_grad * (1.0 + gain))
    turned[...] = jnp.transpose(grad[:group]).astype(low)
    feed = feed_0[...].astype(full) + feed_1[...].astype(full) + feed_2[...].astype(full)
    mask_sum = grad[group : group + 1]
    mask_high = mask_sum.astype(low).astype(full)
    fields = [
        jnp.sum(normed_grad, axis=0, keepdims=True),
        jnp.sum(normed_grad * unit, axis=0, keepdims=True),
        sums_ref[0:1, :],
        sums_ref[1:2, :],
        sums_ref[2:3, :],
        jnp.sum(feed * upstream_ref[...], axis=0, keepdims=True),
        mask_high,
        mask_sum - mask_high,
    ]
    chunks = width // 128
    riders[...] = jnp.zeros_like(riders)
    for number, field in enumerate(fields):
        for chunk in range(chunks):
            at = number * chunks + chunk
            riders[at : at + 1, :] = field[:, chunk * 128 : (chunk + 1) * 128]
    rider_rows = riders[...].astype(low)
    for index, piece in enumerate((piece_0, piece_1, piece_2, piece_3)):
        at = pl.multiple_of((lane ^ index) * width_part, 16)
        piece[:width_part, :] = turned[pl.ds(at, width_part), :]
        piece[width_part:, :] = rider_rows


def slots_kernel(
    owners,
    lane_ref,
    me_ref,
    big_ref,
    rank_ref,
    lifted_ref,
    piece_0,
    piece_1,
    piece_2,
    piece_3,
    slabs_ref,
    table_ref,
    table,
    mask_total,
):
    lane = lane_ref[0]
    me = me_ref[0]
    group = piece_0.shape[1]
    slots_all = rank_ref.shape[1]
    capacity = slots_all // owners
    chunks = table_ref.shape[1]
    width_part = slabs_ref.shape[1] - RIDERS
    pieces = [piece_0, piece_1, piece_2, piece_3]
    rows = jnp.concatenate([piece[:width_part, :] for piece in pieces], axis=1)
    row_id = lax.broadcasted_iota(jnp.int32, (group, slots_all), 0)
    matrix = jnp.concatenate(
        [
            (row_id + (lane ^ index) * group == rank_ref[...]).astype(full).astype(low)
            for index in range(QUARTERS)
        ],
        axis=0,
    )
    slots = dot(rows, matrix)
    table[...] = jnp.zeros_like(table)
    summed = jnp.zeros((chunks, 128), full)
    mask_sum = jnp.zeros((16, 128), full)
    mask_rows = chunks // 6
    for index, piece in enumerate(pieces):
        field = piece[width_part : width_part + chunks, :].astype(full)
        summed = summed + field
        rest = piece[width_part + chunks - chunks % 16 :, :].astype(full)
        table[lane ^ index, :chunks, :] = field
        at = chunks % 16
        mask_sum = mask_sum + jnp.concatenate(
            [
                rest[at : at + mask_rows] + rest[at + mask_rows : at + 2 * mask_rows],
                jnp.zeros((16 - mask_rows, 128), full),
            ],
            axis=0,
        )
    mask_total[...] = mask_sum

    @pl.when(big_ref[0] == 1)
    def _():
        table[...] = jnp.zeros_like(table)
        table[0, :chunks, :] = summed

    table_ref[...] = table[:, :chunks, :].astype(low)
    for index in range(owners):
        owner = me ^ index
        start = (owner * chunks) // owners
        fields = [table[row, pl.ds(start, 8), :] for row in range(QUARTERS)]
        mask_start = (owner * mask_rows) // owners
        mask_part = mask_total[pl.ds(mask_start, 2), :]
        mask_high = mask_part.astype(low).astype(full)
        fields += [mask_high, mask_part - mask_high, lifted_ref[...].astype(full)]
        slab = jnp.concatenate([slots[:, index * capacity : (index + 1) * capacity]] + fields, axis=0)
        slabs_ref[owner] = slab.astype(low)


def kept_kernel(
    owners, me_ref, slot_ref, slabs_ref, kept_ref, modulate_ref, mask_ref, table, lifted_all
):
    width_part, kept_count = kept_ref.shape
    capacity = slabs_ref.shape[2]
    table_part = modulate_ref.shape[1]
    mask_part = mask_ref.shape[1]
    me = me_ref[0]
    slabs = [slabs_ref[me ^ index] for index in range(owners)]
    rows = jnp.concatenate([slab[:width_part] for slab in slabs], axis=1)
    slot_id = lax.broadcasted_iota(jnp.int32, (owners * capacity, kept_count), 0)
    matrix = (slot_id == slot_ref[...]).astype(full).astype(low)
    kept_ref[...] = dot(rows, matrix).astype(low)
    mask_sum = jnp.zeros((1, 256), full)
    for index, slab in enumerate(slabs):
        rider = slab[width_part:].astype(full)
        for row in range(QUARTERS):
            at = index * QUARTERS + row
            for chunk in range(8):
                from_row = row * 8 + chunk
                table[at : at + 1, chunk * 128 : (chunk + 1) * 128] = rider[
                    from_row : from_row + 1
                ]
        for row in range(QUARTERS):
            for chunk in range(3):
                from_row = 36 + row * 3 + chunk
                lifted_all[
                    index * QUARTERS + row : index * QUARTERS + row + 1,
                    chunk * 128 : (chunk + 1) * 128,
                ] = rider[from_row : from_row + 1]
        high, rest = rider[32:34], rider[34:36]
        both = high + rest
        mask_sum = mask_sum + jnp.concatenate([both[0:1], both[1:2]], axis=1)
    shift = (me * table_part) % 128
    field = pltpu.roll(table[...], (1024 - shift) % 1024, 1)[:, :table_part]
    lifted = lifted_all[...].astype(low)[:, :width_part]
    modulate_ref[...] = dot(lifted, field.astype(low), ((0,), (0,)))
    shift = (me * mask_part) % 128
    mask_sum = jnp.broadcast_to(mask_sum, (8, 256))
    mask_ref[...] = pltpu.roll(mask_sum, (256 - shift) % 256, 1)[0:1, :mask_part]


def out_kernel(
    lane_ref,
    part_0,
    part_1,
    part_2,
    middle_ref,
    chosen_ref,
    piece_0,
    piece_1,
    piece_2,
    piece_3,
    turned,
    riders,
):
    lane = lane_ref[0]
    block, width = middle_ref.shape
    group = block - SPARE
    width_part = width // QUARTERS
    feed = part_0[...].astype(full) + part_1[...].astype(full) + part_2[...].astype(full)
    out = middle_ref[...] + chosen_ref[0:1, 5 * width : 6 * width] * feed
    turned[...] = jnp.transpose(out[:group]).astype(low)
    riders[...] = jnp.zeros_like(riders)
    for chunk in range(width // 128):
        riders[chunk : chunk + 1, :] = out[group : group + 1, chunk * 128 : (chunk + 1) * 128]
    rider_rows = riders[...].astype(low)
    for index, piece in enumerate((piece_0, piece_1, piece_2, piece_3)):
        at = pl.multiple_of((lane ^ index) * width_part, 16)
        piece[:width_part, :] = turned[pl.ds(at, width_part), :]
        piece[width_part:, :] = rider_rows


def layer_kernel(
    lane_ref, rank_ref, piece_0, piece_1, piece_2, piece_3, out_ref, spare, turned
):
    lane = lane_ref[0]
    width_part, own_tokens = out_ref.shape
    group = piece_0.shape[1]
    quarter = own_tokens // QUARTERS
    pieces = (piece_0, piece_1, piece_2, piece_3)
    rows = jnp.concatenate([piece[:width_part, :] for piece in pieces], axis=1)
    row_id = lax.broadcasted_iota(jnp.int32, (group, own_tokens), 0)
    matrix = jnp.concatenate(
        [
            (row_id + (lane ^ index) * group == rank_ref[...]).astype(full).astype(low)
            for index in range(QUARTERS)
        ],
        axis=0,
    )
    spare[...] = jnp.zeros_like(spare)
    for index, piece in enumerate(pieces):
        rider = piece[width_part:, :].astype(full)
        for chunk in range(spare.shape[1] // 128):
            spare[index : index + 1, chunk * 128 : (chunk + 1) * 128] = rider[chunk : chunk + 1]
    turned[...] = jnp.transpose(spare[...])
    columns = turned[pl.ds(pl.multiple_of(lane * width_part, 16), width_part), :].astype(low)
    spare_id = lax.broadcasted_iota(jnp.int32, (8, own_tokens), 0)
    spot = lax.broadcasted_iota(jnp.int32, (8, own_tokens), 1) // quarter
    empty = rank_ref[...] < 0
    spots = jnp.where(((spare_id ^ lane) == spot) & (spare_id < QUARTERS) & empty, 1.0, 0.0)
    out_ref[...] = (dot(rows, matrix) + dot(columns, spots.astype(low))).astype(low)


def table_kernel(big_ref, lifted_ref, modulate_ref, table_ref, bias_ref, turned_ref, table):
    span = table_ref.shape[1]
    steps = table_ref.shape[0] // QUARTERS
    table[...] = jnp.zeros_like(table)
    table[:QUARTERS, : modulate_ref.shape[1]] = dot(lifted_ref[...], modulate_ref[...])
    table_ref[...] = jnp.concatenate(
        [
            table[row : row + 1, step * span : (step + 1) * span]
            for row in range(QUARTERS)
            for step in range(steps)
        ],
        axis=0,
    ).astype(low)
    rows = bias_ref.shape[0]
    block = rows // QUARTERS
    group = block - SPARE
    big = big_ref[0] == 1
    spare_small = jnp.log(jnp.full((1, 1), float(group), full))
    spare_big = jnp.log(jnp.full((1, 1), float(QUARTERS * group), full))

    def bias_of(query, key):
        query_block, key_block, key_inner = query // block, key // block, key % block
        small = jnp.where(key_inner < group, 0.0, jnp.where(key_inner == group, spare_small, -1e30))
        small = jnp.where(query_block == key_block, small, -1e30)
        large = jnp.where(key_inner < group, 0.0, jnp.where(key == group, spare_big, -1e30))
        return jnp.where(big, large, small)

    row_id = lax.broadcasted_iota(jnp.int32, (rows, rows), 0)
    column_id = lax.broadcasted_iota(jnp.int32, (rows, rows), 1)
    bias_ref[...] = bias_of(row_id, column_id)
    turned_ref[...] = bias_of(column_id, row_id)


def add_kernel(left_ref, right_ref, out_ref):
    out_ref[...] = (left_ref[...].astype(full) + right_ref[...].astype(full)).astype(low)


def copy_kernel(*refs):
    for index in range(len(refs) // 2):
        refs[len(refs) // 2 + index][...] = refs[index][...]


def upstream_kernel(
    lane_ref,
    rank_ref,
    chosen_ref,
    cotangent_ref,
    shrink_ref,
    grad_near,
    grad_far,
    upstream_ref,
    back_near,
    back_far,
):
    lane = lane_ref[0]
    block, width = upstream_ref.shape
    own_tokens = rank_ref.shape[1]
    group = block - SPARE
    rank = rank_ref[...]
    row_id = lax.broadcasted_iota(jnp.int32, (group, own_tokens), 0)
    spare_id = lax.broadcasted_iota(jnp.int32, (SPARE, own_tokens), 0)
    spot = lax.broadcasted_iota(jnp.int32, (SPARE, own_tokens), 1) // (own_tokens // QUARTERS)
    for chunk, back, grad_ref in ((0, back_near, grad_near), (1, back_far, grad_far)):
        matrix = []
        for index in (2 * chunk, 2 * chunk + 1):
            matrix.append(jnp.where(row_id + (lane ^ index) * group == rank, 1.0, 0.0))
            matrix.append(
                jnp.where((spare_id == 0) & (spot == (lane ^ index)) & (rank < 0), 1.0, 0.0)
            )
        upstream = dot(jnp.concatenate(matrix, axis=0).astype(low), cotangent_ref[...])
        if chunk == 0:
            upstream_ref[...] = upstream[:block]
        gates = [chosen_ref[index : index + 1, 5 * width :] for index in (2 * chunk, 2 * chunk + 1)]
        feed_grad = jnp.concatenate(
            [gates[0] * upstream[:block], gates[1] * upstream[block:]], axis=0
        ).astype(low)
        grad_ref[...] = feed_grad
        back[...] = dot(feed_grad, shrink_ref[...], ((1,), (1,)))


def feed_out_kernel(near_ref, far_ref, shrink_ref, part_0, part_1, part_2, part_3):
    block = part_0.shape[0]
    for activated, pair in ((far_ref, (part_2, part_3)), (near_ref, (part_0, part_1))):
        part = dot(activated[...], shrink_ref[...])
        pair[0][...] = part[:block].astype(low)
        pair[1][...] = part[block:].astype(low)


def partial_kernel(lhs_0, rhs_0, lhs_1, rhs_1, out_0, out_1):
    for lhs, rhs, out in ((lhs_0, rhs_0, out_0), (lhs_1, rhs_1, out_1)):
        chunk = lhs.shape[1] // 3
        for number in range(3):
            span = slice(number * chunk, (number + 1) * chunk)
            out[span, :] = dot(lhs[:, span], rhs[...], ((0,), (0,))).astype(low)


def weight_kernel(counts, bases, me_ref, *refs):
    given_0, given_1, kept_0, kept_1, product = refs[-5:]
    operands = list(refs[:-5])
    base_refs = [operands.pop() for _ in range(bases)][::-1]
    rows = given_0.shape[1] + given_1.shape[1]
    chunk = product.shape[0] // 3
    for group, pairs in enumerate(counts):
        products = []
        for lefts, rights in pairs:
            lhs = [operands.pop(0) for _ in range(lefts)]
            right = jnp.concatenate([operands.pop(0)[...] for _ in range(rights)], axis=0)
            products.append((lhs, right))
        for number in range(3):
            span = slice(number * chunk, (number + 1) * chunk)
            parts = [
                dot(jnp.concatenate([ref[:, span] for ref in lhs], axis=0), right, ((0,), (0,)))
                for lhs, right in products
            ]
            value = jnp.concatenate(parts, axis=1)
            if bases:
                value = value + base_refs[group][span, :].astype(full)
            product[span, :] = value
        for bit, start, given, kept in (
            (0, 0, given_0, kept_0),
            (1, given_0.shape[1], given_1, kept_1),
        ):
            mine = (me_ref[0] >> bit) & 1
            for index in range(4):
                for value, ref in ((1 - mine, given), (mine, kept)):
                    above = (index >> bit) << (bit + 1)
                    at = (above + (value << bit) + (index & bit)) * rows + start
                    at = pl.multiple_of(at, 8)
                    ref[4 * group + index] = product[pl.ds(at, ref.shape[1]), :].astype(low)


def single_kernel(bit, me_ref, lhs_ref, rhs_ref, base_ref, given_ref, kept_ref, product):
    rows = given_ref.shape[1]
    chunk = product.shape[0] // 3
    for number in range(3):
        span = slice(number * chunk, (number + 1) * chunk)
        value = dot(lhs_ref[:, span], rhs_ref[...], ((0,), (0,)))
        product[span, :] = (value + base_ref[span, :].astype(full)).astype(low)
    mine = (me_ref[0] >> bit) & 1
    for index in range(given_ref.shape[0]):
        for value, ref in ((1 - mine, given_ref), (mine, kept_ref)):
            above = (index >> bit) << (bit + 1)
            at = (above + (value << bit) + (index & bit)) * rows
            ref[index] = product[pl.ds(pl.multiple_of(at, 16), rows), :]


def feed_join_kernel(me_ref, held_0, held_1, got_0, got_1, given, kept):
    mine = (me_ref[0] >> 2) & 1
    for index, (held, got) in enumerate(((held_0, got_0), (held_1, got_1))):
        for at, ref in ((1 - mine, given), (mine, kept)):
            ref[index] = (held[at].astype(full) + got[at].astype(full)).astype(low)


def halve_kernel(
    me_ref, held_0, held_1, got_0, got_1, given_0, given_1, kept_0, kept_1
):
    for bit, held, got, given, kept in (
        (1, held_0, got_0, given_0, kept_0),
        (0, held_1, got_1, given_1, kept_1),
    ):
        mine = (me_ref[0] >> bit) & 1
        for index in range(given.shape[0]):
            for value, ref in ((1 - mine, given), (mine, kept)):
                at = 2 * index + value
                ref[index] = (held[at].astype(full) + got[at].astype(full)).astype(low)


def join_kernel(me_ref, held_0, held_1, got_0, got_1, given, kept):
    mine = (me_ref[0] >> 2) & 1
    for index in range(given.shape[0]):
        for value, ref in ((1 - mine, given), (mine, kept)):
            at = 2 * index + value
            upper = held_0[at].astype(full) + got_0[at].astype(full)
            lower = held_1[at].astype(full) + got_1[at].astype(full)
            ref[index] = jnp.concatenate([upper, lower], axis=0).astype(low)


def total_kernel(held_ref, got_ref, *out_refs):
    if len(out_refs[0].shape) == 2:
        for index, out_ref in enumerate(out_refs):
            out_ref[...] = held_ref[index].astype(full) + got_ref[index].astype(full)
        return
    entry_ref, output_ref = out_refs
    total = held_ref[0].astype(full) + got_ref[0].astype(full)
    parts, _, columns = entry_ref.shape
    for index in range(parts):
        entry_ref[index] = total[:, index * columns : (index + 1) * columns]
    output_ref[...] = total[:, parts * columns :]


def call(
    kernel, outs, *operands, words=0, deps=(), time=1.0, scratch=(), token=False, loose=False
):
    count = len(operands)
    deps = tuple(deps)
    outs = tuple(outs)
    if token:
        outs += (((8, 128), full),)

    def run(*refs):
        outs_at = count + len(deps)
        rest = list(refs[outs_at:])
        if token:
            last = rest.pop(len(outs) - 1)
            last[...] = jnp.zeros_like(last)
        kernel(*refs[:count], *rest)

    return pl.pallas_call(
        run,
        out_shape=tuple(jax.ShapeDtypeStruct(shape, kind) for shape, kind in outs),
        in_specs=[SMALL] * words
        + [pl.BlockSpec() if loose else PLAIN] * (count - words)
        + [pl.BlockSpec(memory_space=pl.ANY)] * len(deps),
        scratch_shapes=list(scratch),
        compiler_params=pltpu.CompilerParams(vmem_limit_bytes=VMEM_ASK),
        cost_estimate=pl.CostEstimate(
            flops=int(time * 1.15e9), bytes_accessed=1024, transcendentals=0
        ),
    )(*operands, *deps)


def turn(token):
    return swap(token, "tensor", 1)


def body(
    kept_rows,
    owner_index,
    kept_position,
    resolution,
    mask_token,
    condition,
    modulate_weight,
    entry_weight,
    output_weight,
    expand_weight,
    shrink_weight,
    cotangent,
):
    owners = lax.axis_size("dp")
    me = lax.axis_index("dp")
    lane = lax.axis_index("tensor")
    kept_count, width_part = kept_rows.shape
    width = mask_token.shape[0]
    own_tokens = cotangent.shape[0]
    ff_part = expand_weight.shape[1]
    quarter = own_tokens // QUARTERS
    group = quarter // 2
    arrived_count = own_tokens // 2
    block = group + SPARE
    rows = QUARTERS * block
    capacity = 2 * kept_count // owners
    slots_all = owners * capacity
    direct = owners == SWAP_OWNERS
    lane_word = lane.reshape(1).astype(jnp.int32)
    me_word = me.reshape(1).astype(jnp.int32)
    big_word = resolution[:1]
    context_part = lax.dynamic_slice_in_dim(
        condition.astype(full), lane * width_part, width_part, 1
    )
    lifted = jax.nn.silu(context_part).astype(low)
    if direct:
        padded = -(-width_part // capacity) * capacity
        riders = jnp.pad(lifted, ((0, 0), (0, padded - width_part))).reshape(-1, capacity)
        extra = 16
    else:
        riders = lifted.reshape(-1, capacity)
        rider_count = riders.shape[0]
        extra = -(-(rider_count + 2) // 16) * 16
        riders = jnp.pad(riders, ((2, extra - 2 - rider_count), (0, 0)))
    slab_rows = width_part + extra
    slab_shape = (slab_rows, capacity)
    if not direct:
        slab_shape = (owners,) + slab_shape
    *slabs, slot_index = call(
        partial(
            pack_kernel,
            owners,
            FAR + NEAR if direct else range(owners),
            own_tokens.bit_length() - 1,
            extra,
            capacity,
        ),
        ((slab_shape, low),) * (owners if direct else 1) + (((1, kept_count), jnp.int32),),
        me_word,
        kept_rows.T,
        (owner_index * own_tokens + kept_position)[None, :],
        *([] if direct else [riders]),
        words=1,
        time=1.0,
        loose=direct,
    )

    steps = -(-6 * width // arrived_count)
    table, bias, bias_turned = call(
        table_kernel,
        (
            ((QUARTERS * steps, arrived_count), low),
            ((rows, rows), full),
            ((rows, rows), full),
        ),
        big_word,
        lifted,
        modulate_weight,
        words=1,
        deps=[slot_index],
        time=2.0,
        scratch=[pltpu.VMEM((8, steps * arrived_count), full)],
    )
    if direct:
        slabs = exchange_owners(dict(zip(FAR + NEAR, slabs)))
        slabs = list(slabs.values())
    else:
        slabs = exchange_owners(slabs)
    compact, slot_rank, event = call(
        partial(unpack_kernel, owners),
        (
            ((width_part + QUARTERS * steps, arrived_count), low),
            ((1, slots_all), jnp.int32),
        ),
        me_word,
        table,
        *slabs,
        words=1,
        time=1.2,
        token=True,
        scratch=[pltpu.VMEM((slab_rows, slots_all), low)],
    )
    (token_rank,) = call(
        partial(spots_kernel, owners),
        (((1, own_tokens), jnp.int32),),
        me_word,
        *slabs,
        words=1,
        deps=[event],
        time=1.2,
        scratch=[pltpu.VMEM((extra, slots_all), low)],
    )
    if not direct:
        owner_order = jnp.arange(owners, dtype=jnp.int32) ^ me
        lifted_all = slabs[0][:, width_part + 2 : width_part + 2 + rider_count]
        lifted_all = lifted_all.reshape(owners * QUARTERS, width_part)
    spatial_pieces = gather_blocks(compact)
    entry_flat = jnp.transpose(entry_weight, (1, 2, 0)).reshape(3 * width_part, width)
    token_shape = ((block, width), low)
    half = 2 * block
    chosen, spatial_own, normed_one, projected, attended_far, part_2, part_3 = call(
        entry_kernel,
        (
            ((QUARTERS, 6 * width), full),
            token_shape,
            ((rows, width), low),
            ((rows, 3 * width_part), low),
            ((half, width_part), low),
            token_shape,
            token_shape,
        ),
        lane_word,
        big_word,
        *spatial_pieces,
        mask_token[None, :],
        entry_flat,
        bias,
        output_weight,
        words=2,
        deps=[token_rank],
        time=5.0,
        scratch=[
            pltpu.VMEM((width, arrived_count), low),
            pltpu.VMEM((8, steps * arrived_count), full),
        ],
    )
    far, across, start = sum_far(part_2, part_3)
    attended_near, part_0, part_1 = call(
        attend_kernel,
        (((half, width_part), low), token_shape, token_shape),
        projected,
        bias,
        output_weight,
        deps=[start],
        time=3.0,
    )
    got = swap(part_1, "tensor", 1)
    feed_grad_near, feed_grad_far, upstream_own, back_near, back_far = call(
        upstream_kernel,
        (
            ((half, width), low),
            ((half, width), low),
            ((block, width), full),
            ((half, width), full),
            ((half, width), full),
        ),
        lane_word,
        token_rank,
        chosen,
        cotangent,
        shrink_weight,
        words=1,
        deps=[part_1],
        time=3.6,
    )
    branch, middle, normed_two_own = call(
        middle_kernel,
        (((block, width), full), ((block, width), full), token_shape),
        part_0,
        got,
        across,
        spatial_own,
        chosen,
        deps=[back_far],
        time=0.6,
    )

    def feed_call(piece_0, piece_1, back, parts):
        return call(
            feed_kernel,
            (((half, width), low), ((half, width), low), ((half, width), low))
            + parts,
            piece_0,
            piece_1,
            back,
            expand_weight,
            time=2.4,
        )

    near_piece = swap(normed_two_own, "tensor", 1)
    across = swap(normed_two_own, "tensor", 2)
    normed_near, activated_near, hidden_near, part_0, part_1 = feed_call(
        normed_two_own, near_piece, back_near, (token_shape, token_shape)
    )
    *partials, event = call(
        partial_kernel,
        (((width, ff_part), low),) * 2,
        feed_grad_near,
        activated_near,
        normed_near,
        hidden_near,
        time=2.5,
        token=True,
    )
    (across,) = call(copy_kernel, (token_shape,), across, deps=[event], time=0.3)
    last_piece = swap(across, "tensor", 1)
    normed_far, activated_far, hidden_far = feed_call(across, last_piece, back_far, ())
    feed_groups = [
        [([feed_grad_far], [activated_far])],
        [([normed_far], [hidden_far])],
    ]
    event = hidden_far
    if direct:
        me_now = lax.axis_index("dp").reshape(1).astype(jnp.int32)
        shape = ((owners // 2, width // owners, ff_part), low)
        sums = []
        for bit, lhs, rhs, base, waits in (
            (1, normed_far, hidden_far, partials[1], 0),
            (0, feed_grad_far, activated_far, partials[0], 1),
        ):
            given, kept, event = call(
                partial(single_kernel, bit),
                (shape, shape),
                me_now,
                lhs,
                rhs,
                base,
                words=1,
                deps=[event] if waits else (),
                time=SINGLE_TIME,
                scratch=[pltpu.VMEM((width, ff_part), low)],
                token=True,
            )
            sums.append((swap(given, "dp", 1 << bit), kept))
            if not waits:
                part_2, part_3, event = call(
                    feed_part_kernel,
                    (token_shape, token_shape),
                    hidden_far,
                    expand_weight,
                    deps=[event],
                    time=0.1,
                    token=True,
                )
        feed_got = [sums[1][0], sums[0][0]]
        feed_kept = [sums[1][1], sums[0][1]]
    if not direct:
        part_2, part_3 = call(
            feed_part_kernel, (token_shape, token_shape), hidden_far, expand_weight
        )
    far, across, start = sum_far(part_2, part_3, [event])
    got = swap(part_1, "tensor", 1)
    middle_grad, branch_grad_own, sums, start = call(
        middle_back_kernel,
        (((block, width), full), token_shape, ((SPARE, width), full)),
        part_0,
        got,
        across,
        middle,
        branch,
        upstream_own,
        chosen,
        deps=[start],
        time=0.7,
        token=True,
    )
    branch_near = swap(branch_grad_own, "tensor", 1)
    branch_across = swap(branch_grad_own, "tensor", 2)
    feed_parts = call(
        feed_out_kernel,
        (token_shape,) * QUARTERS,
        activated_near,
        activated_far,
        shrink_weight,
        deps=[turn(start)],
        time=0.1,
    )
    feed_far = swap(feed_parts[3], "tensor", 1)
    feed_near = swap(feed_parts[1], "tensor", 1)
    probs, event = call(
        probs_kernel,
        (((width_part // HEAD, rows, rows), low),),
        projected,
        bias_turned,
        deps=[feed_parts[0]],
        time=0.1,
        token=True,
    )
    (branch_across,) = call(copy_kernel, (token_shape,), branch_across, deps=[event], time=0.1)
    branch_pieces = [
        branch_grad_own,
        branch_near,
        branch_across,
        swap(branch_across, "tensor", 1),
    ]
    feed_far, start = call(
        add_kernel,
        (token_shape,),
        feed_parts[2],
        feed_far,
        deps=[branch_pieces[2]],
        time=0.1,
        token=True,
    )
    branch_grad, projected_grad, event = call(
        attend_back_kernel,
        (((rows, width), low), ((rows, 3 * width_part), low)),
        projected,
        probs,
        output_weight,
        *branch_pieces,
        deps=[turn(start)],
        time=0.1,
        token=True,
    )
    feed_across = swap(feed_far, "tensor", 2)
    if direct:
        feed_given, feed_kept, event = halve_sums(feed_kept, feed_got, [event])
        feed_got = cross(feed_given, 2, 1)
    part_2, part_3 = call(
        partial(entry_back_kernel, 1),
        (token_shape, token_shape),
        projected_grad,
        entry_flat,
        deps=[feed_across, feed_near, event],
        time=0.1,
    )
    far, across, start = sum_far(part_2, part_3)
    part_0, part_1 = call(
        partial(entry_back_kernel, 0),
        (token_shape, token_shape),
        projected_grad,
        entry_flat,
        deps=[start],
        time=0.2,
    )
    got = swap(part_1, "tensor", 1)
    entry_groups = [
        [([normed_one], [projected_grad]), ([branch_grad], [attended_near, attended_far])]
    ]
    event = part_1
    if direct:
        entry_given, entry_kept, event = start_sums(entry_groups, ENTRY_SPLIT, [got], 0.2)
        entry_got = cross(entry_given, 1, 2)
    *back_pieces, back_token = call(
        back_kernel,
        (((width_part + 80, group), low),) * QUARTERS,
        lane_word,
        part_0,
        got,
        across,
        spatial_own,
        middle_grad,
        chosen,
        sums,
        feed_parts[0],
        feed_near,
        feed_across,
        upstream_own,
        words=1,
        deps=[event],
        time=BACK_TIME,
        token=True,
        scratch=[pltpu.VMEM((width, group), low), pltpu.VMEM((80, 128), full)],
    )
    if direct:
        feed_given, feed_kept, joined = call(
            feed_join_kernel,
            (((2, width // owners, ff_part), low),) * 2,
            me_word,
            *feed_kept,
            *feed_got,
            words=1,
            deps=[back_token],
            time=JOIN_TIME,
            token=True,
        )
        feed_got = swap(feed_given, "dp", 4)
    back_pieces = [
        back_pieces[0],
        swap(back_pieces[1], "tensor", 1),
        *swap_pair(back_pieces[2:]),
    ]
    chunks = 6 * width // 128
    logistic = jax.nn.sigmoid(context_part)
    logistic = logistic * (1.0 + context_part * (1.0 - logistic))
    if direct:
        entry_given, entry_kept, halved = halve_sums(entry_kept, entry_got, [back_token], HALVE_TIME)
        entry_got = cross(entry_given, 2, 1)
        shrink_grad, expand_grad, total_token = call(
            total_kernel,
            (((width // owners, ff_part), full),) * 2,
            feed_kept,
            feed_got,
            deps=[halved],
            time=TOTAL_TIME,
            token=True,
        )
        slabs, table_grad, event = call(
            partial(slots_kernel, owners),
            (
                ((owners, width_part + RIDERS, capacity), low),
                ((QUARTERS, chunks, 128), low),
            ),
            lane_word,
            me_word,
            big_word,
            slot_rank,
            riders,
            *back_pieces,
            words=3,
            time=0.1,
            token=True,
            scratch=[
                pltpu.VMEM((QUARTERS, chunks + 2, 128), full),
                pltpu.VMEM((16, 128), full),
            ],
        )
        (slabs,) = exchange_owners([slabs])
        table_grad = table_grad.reshape(QUARTERS, 6 * width)
        entry_got, entry_kept, event = join_sums(entry_kept, entry_got, [total_token])
        out_pieces = call(
            out_kernel,
            (((width_part + 16, group), low),) * QUARTERS,
            lane_word,
            feed_parts[0],
            feed_near,
            feed_across,
            middle,
            chosen,
            words=1,
            deps=[event],
            time=0.1,
            scratch=[pltpu.VMEM((width, group), low), pltpu.VMEM((16, 128), full)],
        )
        out_pieces = [
            out_pieces[0],
            swap(out_pieces[1], "tensor", 1),
            *swap_pair(out_pieces[2:]),
        ]
        layer_out, layer_token = call(
            layer_kernel,
            (((width_part, own_tokens), low),),
            lane_word,
            token_rank,
            *out_pieces,
            words=1,
            deps=[event],
            time=0.1,
            token=True,
            scratch=[pltpu.VMEM((8, width), full), pltpu.VMEM((width, 8), full)],
        )
        kept_grad, modulate_grad, mask_grad, kept_token = call(
            partial(kept_kernel, owners),
            (
                ((width_part, kept_count), low),
                ((width_part, 6 * width // owners), full),
                ((1, width // owners), full),
            ),
            me_word,
            slot_index,
            slabs,
            words=1,
            deps=[layer_token],
            time=KEPT_TIME,
            token=True,
            scratch=[
                pltpu.VMEM((owners * QUARTERS, 1024), full),
                pltpu.VMEM((owners * QUARTERS, padded), full),
            ],
        )
        mask_grad = mask_grad[0]
    else:
        event = back_pieces[1]
        rows_back = jnp.concatenate([piece[:width_part] for piece in back_pieces], axis=1)
        rank_ids = jnp.arange(arrived_count, dtype=jnp.int32)
        rank_ids = ((rank_ids // group) ^ lane) * group + rank_ids % group
        matrix = (rank_ids[:, None] == slot_rank).astype(low)
        slabs = dot(rows_back, matrix).astype(low).reshape(width_part, owners, capacity)
        slabs = jnp.take(jnp.transpose(slabs, (1, 0, 2)), owner_order, axis=0)
        slabs = jnp.take(exchange_owners([slabs])[0], owner_order, axis=0)
        slabs = jnp.transpose(slabs, (1, 0, 2)).reshape(width_part, slots_all)
        slot_ids = jnp.arange(slots_all, dtype=jnp.int32)[:, None]
        kept_grad = dot(slabs, (slot_ids == slot_index).astype(low)).astype(low)
        riders = jnp.stack(
            [piece[width_part : width_part + 8 * width // 128] for piece in back_pieces]
        )
        riders = riders.reshape(QUARTERS, 8, width).astype(full)
        mask_total = jnp.sum(riders[:, 6] + riders[:, 7], axis=0)
        table_local = riders[:, :6].reshape(QUARTERS, 6 * width)
        table_small = jnp.take(table_local, jnp.arange(QUARTERS, dtype=jnp.int32) ^ lane, axis=0)
        first = jnp.arange(QUARTERS, dtype=jnp.int32)[:, None] == 0
        table_big = jnp.where(first, jnp.sum(table_local, axis=0, keepdims=True), 0.0)
        table_grad = jnp.where(big_word[0] == 1, table_big, table_small).astype(low)
        sent = jnp.transpose(table_grad.reshape(QUARTERS, owners, -1), (1, 0, 2))
        table_all = exchange_owners([sent])[0].reshape(owners * QUARTERS, -1)
        modulate_grad = dot(lifted_all, table_all, ((0,), (0,)))
        mask_grad = lax.psum_scatter(mask_total, "dp", scatter_dimension=0, tiled=True)
    condition_grad = dot(table_grad, modulate_weight, ((1,), (1,))) * logistic
    if not direct:
        out_pieces = call(
            out_kernel,
            (((width_part + 16, group), low),) * QUARTERS,
            lane_word,
            feed_parts[0],
            feed_near,
            feed_across,
            middle,
            chosen,
            words=1,
            deps=[],
            time=0.1,
            scratch=[pltpu.VMEM((width, group), low), pltpu.VMEM((16, 128), full)],
        )
        out_pieces = [
            out_pieces[0],
            swap(out_pieces[1], "tensor", 1),
            *swap_pair(out_pieces[2:]),
        ]
        layer_out, layer_token = call(
            layer_kernel,
            (((width_part, own_tokens), low),),
            lane_word,
            token_rank,
            *out_pieces,
            words=1,
            deps=[],
            time=0.1,
            token=True,
            scratch=[pltpu.VMEM((8, width), full), pltpu.VMEM((width, 8), full)],
        )
    rows_part = width // owners
    if direct:
        entry_grad, output_grad = call(
            total_kernel,
            (((3, rows_part, width_part), full), ((rows_part, width_part), full)),
            entry_kept,
            entry_got,
            deps=[kept_token],
            time=0.8,
        )
    else:
        totals = []
        for number, pairs in enumerate(feed_groups + entry_groups):
            total = [
                dot(jnp.concatenate(lhs), jnp.concatenate(rhs), ((0,), (0,))) for lhs, rhs in pairs
            ]
            total = jnp.concatenate(total, axis=1)
            if number < len(partials):
                total = total + partials[number].astype(full)
            totals.append(sum_owners(total.astype(low).reshape(owners, rows_part, -1)))
        shrink_grad, expand_grad, entry_grad = totals
        output_grad = entry_grad[:, 3 * width_part :]
        entry_grad = entry_grad[:, : 3 * width_part].reshape(rows_part, 3, width_part)
        entry_grad = jnp.transpose(entry_grad, (1, 0, 2))

    return (
        layer_out.T,
        kept_grad.T,
        mask_grad,
        condition_grad,
        modulate_grad,
        jnp.transpose(entry_grad, (1, 0, 2)),
        output_grad.T,
        expand_grad,
        shrink_grad.T,
    )


def solution(mesh):
    return jax.shard_map(
        body,
        mesh=mesh,
        in_specs=(
            P("dp", "tensor"),
            P("dp"),
            P("dp"),
            P("dp"),
            P(),
            P("dp", None),
            P("tensor", None),
            P(None, None, "tensor"),
            P("tensor", None),
            P(None, "tensor"),
            P("tensor", None),
            P("dp", None),
        ),
        out_specs=(
            P("dp", "tensor"),
            P("dp", "tensor"),
            P("dp"),
            P("dp", "tensor"),
            P("tensor", "dp"),
            P("dp", None, "tensor"),
            P("tensor", "dp"),
            P("dp", "tensor"),
            P("tensor", "dp"),
        ),
        check_vma=False,
    )
```
